32 devices in a mesh: task: 4 (over y, x), dp: 4 (over z), tensor: 2 (over core).
Axes of the slice: x: 2, y: 2, z: 4, core: 2. Of those that a mesh axis runs over, the one named last changes fastest.
Arguments:
- queries: bfloat16 [4, 2400, 768], P('task', 'dp'), may hold values from -6 to 6
- memory: bfloat16 [4, 28800, 768], P('task', 'dp'), may hold values from -6 to 6
- cotangent: bfloat16 [4, 2400, 768], P('task', 'dp'), may hold values from -6 to 6
- matches: int32 [4, 24, 100], P('task', 'dp'), may hold values from 0 to 99, each once within a row
- counts: int32 [4, 24], P('task', 'dp'), may hold values from 1 to 100
- task_order: int32 [4], replicated, may hold values from 0 to 3, each once
- params: bfloat16 [768, 16, 768], P(None, None, 'tensor'), may hold values from -1.875 to 1.875
- head_bias: bfloat16 [8, 768], P(None, 'tensor'), may hold values from -3 to 3
- row_bias: bfloat16 [3, 2, 768], replicated, may hold values from -3 to 3
- norm_gain: bfloat16 [3, 768], replicated, may hold values from 0.5 to 1.5
Outputs:
- block_out: bfloat16 [4, 2400, 768], P('task', 'dp')
- query_grad: bfloat16 [4, 2400, 768], P('task', ('dp', 'tensor'))
- memory_grad: bfloat16 [4, 28800, 768], P('task', ('dp', 'tensor'))
- param_update: float32 [768, 16, 768], P('dp', None, 'tensor')
- head_bias_update: float32 [8, 768], P(None, 'tensor')
- row_bias_update: float32 [3, 2, 768], replicated
- gain_update: float32 [3, 768], replicated
- gram: float32 [4, 4], replicated
The draws below stay inside these ranges and needn't reach their ends.
Inputs may be any that keep to these rules, and one draw needn't show every extreme that they name: `matches`: for each image, a permutation of the 100 query slots; only the first counts entries name matched queries. `task_order`: a permutation of the indices 0 to 3.
All inputs are finite; a program needn't handle non-finite values.
Results may differ from the reference program's by a relative error of at most 0.015.
Values may be sent and summed in bfloat16 or wider, within the bound.
A program may use at most 256 MiB of HBM per device.

```python
import math
import jax
import jax.numpy as jnp
from jax import lax

D = 768
HD = 64
FF = 3072
NQ = 100
MEM = 1200
IMAGES = 6
TASKS = 4
ROWS = 2400
MEM_ROWS = 28800
N_DP = 4


def draw_params(key, part):
    key = jax.random.fold_in(key, 7)
    base_draw = jnp.clip(jax.random.normal(key, (D, 16, D), jnp.float32), -6.0, 6.0)
    inner_scale = D ** (-0.5)
    outer_scale = FF ** (-0.5)
    self_factor = math.sqrt(NQ) / 2.0
    cross_factor = math.sqrt(MEM) / 4.0
    factors = jnp.array([inner_scale] * 3 + [inner_scale * self_factor] + [inner_scale] * 3 + [inner_scale * cross_factor] + [inner_scale] * 4 + [outer_scale] * 4, jnp.float32)
    return (base_draw * factors[None, :, None]).astype(jnp.bfloat16)


def unit_field(key, shape):
    return jnp.clip(jax.random.normal(key, shape, jnp.float32), -4.0, 4.0)


def shared_rows(key, row_count, signs):
    common_key, own_key = jax.random.split(key)
    common_part = unit_field(common_key, (1, row_count, D))
    own_part = unit_field(own_key, (TASKS, row_count, D))
    return 0.9 * signs[:, None, None] * common_part + 0.45 * own_part


def draw_queries(key, part):
    key = jax.random.fold_in(key, 11)
    signs = jnp.ones((TASKS,), jnp.float32)
    return shared_rows(key, ROWS, signs).astype(jnp.bfloat16)


def draw_memory(key, part):
    key = jax.random.fold_in(key, 13)
    signs = jnp.ones((TASKS,), jnp.float32)
    return shared_rows(key, MEM_ROWS, signs).astype(jnp.bfloat16)


def draw_cotangent(key, part):
    key = jax.random.fold_in(key, 17)
    sign_key, field_key = jax.random.split(key)
    order_draw = jax.random.permutation(sign_key, jnp.arange(TASKS, dtype=jnp.int32))
    signs = (2 * (order_draw % 2) - 1).astype(jnp.float32)
    return shared_rows(field_key, ROWS, signs).astype(jnp.bfloat16)


def place_ends(values, rng, low, high):
    index_at = [jax.random.randint(jax.random.fold_in(rng, axis), (), 0, length) for axis, length in enumerate(values.shape)]
    main_axis = values.shape.index(max(values.shape))
    neighbour = index_at[:main_axis] + [(index_at[main_axis] + 1) % values.shape[main_axis]] + index_at[main_axis + 1:]
    return values.at[tuple(index_at)].set(low).at[tuple(neighbour)].set(high)


def block_scale(key, shape, cuts, least, largest):
    factor_of = 1.0
    for dim, parts in cuts:
        draws = jax.random.uniform(jax.random.fold_in(jax.random.fold_in(key, 6), dim), (parts,), jnp.float32, least / len(cuts), largest / len(cuts))
        factor_of = factor_of * jnp.repeat(jnp.exp(draws), shape[dim] // parts).reshape((-1,) + (1,) * (len(shape) - 1 - dim))
    return factor_of


def noise(stream_key, shape, deviation, reach, cuts=(), held_as=jnp.bfloat16):
    gain = block_scale(stream_key, shape, cuts, -0.22, 0.18) if cuts else 1.0
    entries = jax.random.normal(stream_key, shape, jnp.float32) * deviation * gain
    return jnp.minimum(jnp.maximum(entries, -reach), reach).astype(held_as)


def setup_inputs(seed: int = 0) -> dict:
    arg_keys = jax.random.split(jax.random.key(seed), 11)
    queries = draw_queries(jax.random.fold_in(arg_keys[10], 71), 0)
    memory = draw_memory(jax.random.fold_in(arg_keys[10], 71), 0)
    cotangent = draw_cotangent(jax.random.fold_in(arg_keys[10], 71), 0)
    matches = jax.vmap(lambda own: jax.random.permutation(own, NQ))(jax.random.split(arg_keys[3], TASKS * (N_DP * IMAGES))).reshape((TASKS, N_DP * IMAGES, NQ)).astype(jnp.int32)
    counts = place_ends(jax.random.randint(arg_keys[4], (TASKS, N_DP * IMAGES), 1, NQ + 1), jax.random.fold_in(arg_keys[4], 1), 1, NQ).astype(jnp.int32)
    task_order = jax.random.permutation(arg_keys[5], TASKS).astype(jnp.int32)
    params = draw_params(jax.random.fold_in(arg_keys[10], 71), 0)
    head_bias = noise(arg_keys[7], (8, D), 0.5, 3.0, ((1, 2),))
    row_bias = noise(arg_keys[8], (3, 2, D), 0.5, 3.0)
    norm_gain = jnp.clip(1.0 + 0.1 * jax.random.normal(arg_keys[9], (3, D), jnp.float32), 0.5, 1.5).astype(jnp.bfloat16)
    return {"queries": queries, "memory": memory, "cotangent": cotangent, "matches": matches, "counts": counts, "task_order": task_order, "params": params, "head_bias": head_bias, "row_bias": row_bias, "norm_gain": norm_gain}


highest = lax.Precision.HIGHEST

@jax.custom_vjp
def low(v):
    return lax.optimization_barrier(v.astype(jnp.bfloat16)).astype(jnp.float32)

@jax.custom_vjp
def low_back(v):
    return v

def low_keep(v):
    return (low(v), None)

def low_pass(kept, grad):
    return (grad,)

def back_keep(v):
    return (v, None)

def back_low(kept, grad):
    return (low(grad),)
low.defvjp(low_keep, low_pass)
low_back.defvjp(back_keep, back_low)

def layer_norm(residual, gain_row, shift_row):
    row_mean = lax.optimization_barrier(jnp.mean(residual, axis=-1, keepdims=True))
    centred = residual - row_mean
    variance = lax.optimization_barrier(jnp.mean(centred * centred, axis=-1, keepdims=True))
    return centred * lax.rsqrt(variance + 1e-05) * gain_row + shift_row

def gelu_tanh(hidden):
    return 0.5 * hidden * (1.0 + jnp.tanh(0.7978845608028654 * (hidden + 0.044715 * hidden * hidden * hidden)))

def linear(activations, matrix):
    return jnp.einsum('nld,de->nle', activations, matrix, precision=highest)

def linear_out(activations, matrix):
    return jnp.einsum('nld,ed->nle', activations, matrix, precision=highest)

def attend(query_act, key_act, value_act):
    image_count, query_rows, model_width = query_act.shape
    key_rows = key_act.shape[1]
    head_count = model_width // HD
    query_heads = query_act.reshape(image_count, query_rows, head_count, HD)
    key_heads = key_act.reshape(image_count, key_rows, head_count, HD)
    value_heads = value_act.reshape(image_count, key_rows, head_count, HD)
    scores = low_back(jnp.einsum('nqhd,nkhd->nhqk', query_heads, key_heads, precision=highest) * HD ** (-0.5))
    row_max = lax.optimization_barrier(jnp.max(scores, axis=-1, keepdims=True))
    log_total = row_max + jnp.log(lax.optimization_barrier(jnp.sum(jnp.exp(scores - row_max), axis=-1, keepdims=True)))
    attn_probs = low(jnp.exp(scores - log_total))
    attended = jnp.einsum('nhqk,nkhd->nqhd', attn_probs, value_heads, precision=highest)
    return low(low_back(attended.reshape(image_count, query_rows, model_width)))

def layer(tokens, memory, params, head_bias, row_bias, norm_gain):
    model_width = tokens.shape[-1]
    self_query = low(low_back(linear(tokens, params[:, 0]) + head_bias[0]))
    self_key = low(low_back(linear(tokens, params[:, 1])))
    self_value = low(low_back(linear(tokens, params[:, 2]) + head_bias[1]))
    self_mixed = attend(self_query, self_key, self_value)
    first_sum = tokens + low_back(linear_out(self_mixed, params[:, 3])) + row_bias[0, 0]
    first_out = layer_norm(first_sum, norm_gain[0], row_bias[0, 1])
    first_low = low(first_out)
    cross_query = low(low_back(linear(first_low, params[:, 4]) + head_bias[2]))
    cross_key = low(low_back(linear(memory, params[:, 5])))
    cross_value = low(low_back(linear(memory, params[:, 6]) + head_bias[3]))
    cross_mixed = attend(cross_query, cross_key, cross_value)
    second_sum = first_out + low_back(linear_out(cross_mixed, params[:, 7])) + row_bias[1, 0]
    second_out = layer_norm(second_sum, norm_gain[1], row_bias[1, 1])
    second_low = low(second_out)
    weight_in = params[:, 8:12].reshape(model_width, 4 * model_width)
    weight_out = params[:, 12:16].reshape(model_width, 4 * model_width)
    hidden = low_back(linear(second_low, weight_in) + head_bias[4:8].reshape(4 * model_width))
    activated = low(gelu_tanh(hidden))
    third_sum = second_out + low_back(linear_out(activated, weight_out)) + row_bias[2, 0]
    return layer_norm(third_sum, norm_gain[2], row_bias[2, 1])

def live_rows(match_rows, box_counts):
    query_count = match_rows.shape[-1]
    slot_index = jnp.arange(query_count, dtype=jnp.int32)
    box_live = slot_index[None, :] < box_counts[:, None]
    matched = (match_rows[:, :, None] == slot_index[None, None, :]) & box_live[:, :, None]
    return lax.optimization_barrier(jnp.sum(matched.astype(jnp.float32), axis=1))

def combine_weights(gram_matrix, order_list):
    task_count = gram_matrix.shape[0]
    task_index = jnp.arange(task_count, dtype=jnp.int32)
    summed = jnp.zeros((task_count,), jnp.float32)
    for own_task in range(task_count):
        coeffs = (task_index == own_task).astype(jnp.float32)
        for position in range(task_count):
            chosen = (task_index == order_list[position]).astype(jnp.float32)
            column = jnp.dot(gram_matrix, chosen, precision=highest)
            inner_dot = jnp.sum(coeffs * column)
            square = jnp.sum(chosen * column)
            others = (order_list[position] != own_task).astype(jnp.float32)
            coeffs = coeffs - others * jnp.minimum(inner_dot, 0.0) / (square + 1e-06) * chosen
        summed = summed + coeffs
    return summed

def reference(queries, memory, cotangent, matches, counts, task_order, params, head_bias, row_bias, norm_gain):
    params_f = params.astype(jnp.float32)
    head_f = head_bias.astype(jnp.float32)
    row_f = row_bias.astype(jnp.float32)
    gain_f = norm_gain.astype(jnp.float32)

    def one_group(totals, group):
        token_block, memory_block, cot_block, match_block, count_block = group
        outputs, pullback = jax.vjp(layer, token_block.astype(jnp.float32), memory_block.astype(jnp.float32), params_f, head_f, row_f, gain_f)
        live_mask = live_rows(match_block, count_block)
        gradients = pullback(cot_block.astype(jnp.float32) * live_mask[:, :, None])
        totals = tuple((total_part + grad_part for total_part, grad_part in zip(totals, gradients[2:])))
        return (totals, (outputs.astype(jnp.bfloat16), gradients[0].astype(jnp.bfloat16), gradients[1].astype(jnp.bfloat16)))

    def one_task(task_inputs):
        token_all, memory_all, cot_all, match_all, count_all = task_inputs
        groups = (token_all.reshape(N_DP, IMAGES, NQ, D), memory_all.reshape(N_DP, IMAGES, MEM, D), cot_all.reshape(N_DP, IMAGES, NQ, D), match_all.reshape(N_DP, IMAGES, NQ), count_all.reshape(N_DP, IMAGES))
        zero_grads = (jnp.zeros_like(params_f), jnp.zeros_like(head_f), jnp.zeros_like(row_f), jnp.zeros_like(gain_f))
        totals, (outputs, token_grads, memory_grads) = lax.scan(one_group, zero_grads, groups)
        return (outputs.reshape(N_DP * IMAGES * NQ, D), token_grads.reshape(N_DP * IMAGES * NQ, D), memory_grads.reshape(N_DP * IMAGES * MEM, D), totals)
    block_out, query_grad, memory_grad, task_grads = lax.map(one_task, (queries, memory, cotangent, matches, counts))
    flats = [grad_array.reshape(TASKS, -1) for grad_array in task_grads]
    gram = jnp.zeros((TASKS, TASKS), jnp.float32)
    for flat_grad in flats:
        gram = gram + jnp.einsum('ax,bx->ab', flat_grad, flat_grad, precision=highest)
    task_weights = combine_weights(gram, task_order)
    updates = [jnp.einsum('a,ax->x', task_weights, flat_grad, precision=highest).reshape(grad_array.shape[1:]) for flat_grad, grad_array in zip(flats, task_grads)]
    return (block_out, query_grad, memory_grad, updates[0], updates[1], updates[2], updates[3], gram)
```

```python
import functools

import jax
import jax.numpy as jnp
from jax import lax
from jax.experimental import pallas as pl
from jax.experimental.pallas import tpu as pltpu
from jax.sharding import PartitionSpec as P

HD = 64
GROUP = 4
SLAB = GROUP * HD
BF = jnp.bfloat16
F32 = jnp.float32
MESH_ID = pl.DeviceIdType.MESH
highest = lax.Precision.HIGHEST
VMEM_LIMIT = 60 * 2**20


def combine_weights(gram_matrix, order_list):
    task_count = gram_matrix.shape[0]
    task_index = jnp.arange(task_count, dtype=jnp.int32)
    summed = jnp.zeros((task_count,), F32)
    for own_task in range(task_count):
        coeffs = (task_index == own_task).astype(F32)
        for position in range(task_count):
            chosen = (task_index == order_list[position]).astype(F32)
            column = jnp.sum(gram_matrix * chosen[None, :], axis=1)
            inner_dot = jnp.sum(coeffs * column)
            square = jnp.sum(chosen * column)
            others = (order_list[position] != own_task).astype(F32)
            coeffs = coeffs - others * jnp.minimum(inner_dot, 0.0) / (square + 1e-06) * chosen
        summed = summed + coeffs
    return summed


def mm(a, b):
    return jnp.dot(a, b, preferred_element_type=F32)


def mm_nt(a, b):
    return lax.dot_general(a, b, (((1,), (1,)), ((), ())), preferred_element_type=F32)


def mm_tn(a, b):
    return lax.dot_general(a, b, (((0,), (0,)), ((), ())), preferred_element_type=F32)


def norm_parts(residual):
    row_mean = jnp.mean(residual, axis=-1, keepdims=True)
    centred = residual - row_mean
    variance = jnp.mean(centred * centred, axis=-1, keepdims=True)
    scale = lax.rsqrt(variance + 1e-05)
    return centred * scale, scale


def norm_back(normed, scale, gain_row, grad):
    scaled = grad * gain_row
    first = jnp.mean(scaled, axis=-1, keepdims=True)
    second = jnp.mean(scaled * normed, axis=-1, keepdims=True)
    return scale * (scaled - first - normed * second)


def rows_sum(value):
    return jnp.sum(value, axis=0, keepdims=True)


def gelu_tanh(hidden):
    return (
        0.5
        * hidden
        * (1.0 + jnp.tanh(0.7978845608028654 * (hidden + 0.044715 * hidden * hidden * hidden)))
    )


def gelu_slope(hidden):
    square = hidden * hidden
    tanh = jnp.tanh(0.7978845608028654 * (hidden + 0.044715 * hidden * square))
    inner = 0.7978845608028654 * (1.0 + 3 * 0.044715 * square)
    return 0.5 * (1.0 + tanh) + 0.5 * hidden * (1.0 - tanh * tanh) * inner


def head_mask(head, rows, dtype):
    lane = lax.broadcasted_iota(jnp.int32, (rows, SLAB), 1)
    return (lane // HD == head).astype(F32).astype(dtype)


def stack_heads(slab):
    return jnp.concatenate(
        [slab * head_mask(head, slab.shape[0], slab.dtype) for head in range(GROUP)], axis=0
    )


def unstack_heads(stacked):
    rows = stacked.shape[0] // GROUP
    total = None
    for head in range(GROUP):
        part = stacked[head * rows : (head + 1) * rows] * head_mask(head, rows, stacked.dtype)
        total = part if total is None else total + part
    return total


def scores_of(query_stack, key_slab, valid):
    scores = mm_nt(key_slab, query_stack)
    if valid < key_slab.shape[0]:
        row = lax.broadcasted_iota(jnp.int32, scores.shape, 0)
        scores = jnp.where(row < valid, scores, -1e30)
    return scores


def attend(query_slab, key_slab, value_slab, valid):
    scores = scores_of(stack_heads(query_slab * HD ** (-0.5)), key_slab, valid)
    row_max = jnp.max(scores, axis=0, keepdims=True)
    exps = jnp.exp(scores - row_max)
    total = jnp.sum(exps, axis=0, keepdims=True)
    probs = (exps * (1.0 / total)).astype(BF)
    mixed = unstack_heads(mm_tn(value_slab, probs).T)
    return mixed, row_max + jnp.log(total)


def attend_back(query_slab, key_slab, value_slab, log_total, grad_slab, valid):
    query_stack = stack_heads(query_slab * HD ** (-0.5))
    grad_stack = stack_heads(grad_slab)
    probs = jnp.exp(scores_of(query_stack, key_slab, valid) - log_total)
    grad_value = mm(probs.astype(BF), grad_stack)
    grad_probs = mm_nt(value_slab, grad_stack)
    inner = jnp.sum(probs * grad_probs, axis=0, keepdims=True)
    grad_scores = (probs * (grad_probs - inner)).astype(BF)
    grad_key = mm(grad_scores, query_stack)
    grad_query = unstack_heads(mm_tn(key_slab, grad_scores).T) * HD ** (-0.5)
    return grad_query.astype(BF), grad_key.astype(BF), grad_value.astype(BF)


def gather_kernel(own_ref, bias_ref, full_ref, full_bias_ref, turned, bias_own, remote_send,
                  remote_recv, local_sem):
    step, steps = pl.program_id(0), pl.num_programs(0)
    other = 1 - lax.axis_index("tensor")
    rows, _, width = own_ref.shape
    near, far = pl.ds(0, width), pl.ds(width, width)

    def copies(chunk):
        at = pl.ds(pl.multiple_of(chunk * rows, rows), rows)
        source = turned.at[:, at]
        return (
            pltpu.make_async_remote_copy(
                source, full_ref.at[:, at, far], remote_send.at[chunk], remote_recv.at[chunk],
                device_id={"tensor": other}, device_id_type=MESH_ID,
            ),
            pltpu.make_async_copy(source, full_ref.at[:, at, near], local_sem.at[chunk]),
        )

    def bias_copies():
        return (
            pltpu.make_async_remote_copy(
                bias_own, full_bias_ref.at[:, far], remote_send.at[steps], remote_recv.at[steps],
                device_id={"tensor": other}, device_id_type=MESH_ID,
            ),
            pltpu.make_async_copy(bias_own, full_bias_ref.at[:, near], local_sem.at[steps]),
        )

    @pl.when(step == 0)
    def _():
        barrier = pltpu.get_barrier_semaphore()
        pl.semaphore_signal(barrier, inc=1, device_id={"tensor": other}, device_id_type=MESH_ID)
        pl.semaphore_wait(barrier, 1)
        bias_own[...] = bias_ref[...]
        for copy in bias_copies():
            copy.start()

    turned[:, pl.ds(pl.multiple_of(step * rows, rows), rows)] = jnp.swapaxes(own_ref[...], 0, 1)
    for copy in copies(step):
        copy.start()

    @pl.when(step == steps - 1)
    def _():
        for copy in bias_copies():
            copy.wait()

        def finish(chunk, carry):
            for copy in copies(chunk):
                copy.wait()
            return carry

        lax.fori_loop(0, steps, finish, 0)


def any_spec():
    return pl.BlockSpec(memory_space=pl.ANY)


def whole_spec():
    return pl.BlockSpec(memory_space=pltpu.VMEM)


def params_for(**keys):
    return pltpu.CompilerParams(vmem_limit_bytes=VMEM_LIMIT, **keys)


def self_kernel(images, valid, tokens_ref, weight_ref, head_ref, row_ref, gain_ref, qkv_ref,
                mixed_ref, total_ref, sum_ref, cross_query_ref):
    tokens = tokens_ref[...]
    rows = tokens.shape[0] // images
    width = tokens.shape[1]
    qkv_ref[0] = (mm(tokens, weight_ref[0]) + head_ref[0:1]).astype(BF)
    qkv_ref[1] = mm(tokens, weight_ref[1]).astype(BF)
    qkv_ref[2] = (mm(tokens, weight_ref[2]) + head_ref[1:2]).astype(BF)
    for image in range(images):
        at = slice(image * rows, (image + 1) * rows)
        for group in range(width // SLAB):
            lanes = slice(group * SLAB, (group + 1) * SLAB)
            mixed, log_total = attend(
                qkv_ref[0, at, lanes], qkv_ref[1, at, lanes], qkv_ref[2, at, lanes], valid
            )
            mixed_ref[at, lanes] = mixed.astype(BF)
            total_ref[image * (width // SLAB) + group] = jnp.broadcast_to(
                log_total, total_ref.shape[1:]
            )
    first_sum = tokens.astype(F32) + mm_nt(mixed_ref[...], weight_ref[3]) + row_ref[0:1]
    sum_ref[...] = first_sum
    first_low = (norm_parts(first_sum)[0] * gain_ref[0:1] + row_ref[1:2]).astype(BF)
    cross_query_ref[...] = (mm(first_low, weight_ref[4]) + head_ref[2:3]).astype(BF)


def cross_kernel(context_ref, query_ref, key_w_ref, value_w_ref, head_ref, key_ref, value_ref,
                 mixed_ref, total_ref):
    context = context_ref[...]
    key_ref[...] = mm(context, key_w_ref[0]).astype(BF)
    value_ref[...] = (mm(context, value_w_ref[0]) + head_ref[3:4]).astype(BF)
    mixed, log_total = attend(query_ref[...], key_ref[...], value_ref[...], key_ref.shape[0])
    mixed_ref[...] = mixed.astype(BF)
    total_ref[0] = jnp.broadcast_to(log_total, total_ref.shape[1:])


def ffn_kernel(
    images, blocks, sum_ref, mixed_ref, cotangent_ref, matches_ref, counts_ref, cross_w_ref, in_ref,
    out_ref, head_ref, row_ref, gain_ref,
    block_ref, grad_in_ref, grad_out_ref, cross_grad_ref, mixed_grad_ref, residual_ref, small_ref,
    second_sum, second_low_t, low_t, hidden, activated, branch, third_grad,
):
    step = pl.program_id(0)
    rows = sum_ref.shape[0] // images

    @pl.when(step == 0)
    def _():
        first_out = norm_parts(sum_ref[...])[0] * gain_ref[0:1] + row_ref[1:2]
        second_sum[...] = first_out + mm_nt(mixed_ref[...], cross_w_ref[0]) + row_ref[2:3]
        branch[...] = jnp.zeros_like(branch)
        small_ref[...] = jnp.zeros_like(small_ref)

    def second_out():
        return norm_parts(second_sum[...])[0] * gain_ref[1:2] + row_ref[3:4]

    @pl.when(step < blocks)
    def _():
        second_low = second_out().astype(BF)
        pre = mm(second_low, in_ref[0]) + head_ref[pl.ds(4 + step, 1)]
        hidden[step] = pre
        act = gelu_tanh(pre).astype(BF)
        activated[step] = act
        branch[...] += mm_nt(act, out_ref[0])

    @pl.when(step == blocks - 1)
    def _():
        second = second_out()
        second_low_t[...] = second.astype(BF).T
        third_sum = second + branch[...] + row_ref[4:5]
        normed, scale = norm_parts(third_sum)
        block_ref[...] = (normed * gain_ref[2:3] + row_ref[5:6]).astype(BF)
        count = matches_ref.shape[2]
        slot = lax.broadcasted_iota(jnp.int32, (rows, count), 0)
        box = lax.broadcasted_iota(jnp.int32, (rows, count), 1)
        grads = []
        for image in range(images):
            live = (matches_ref[image] == slot) & (box < counts_ref[image])
            mask = jnp.sum(jnp.where(live, 1.0, 0.0), axis=1, keepdims=True)
            cot = cotangent_ref[image * rows : (image + 1) * rows].astype(F32)
            grads.append(cot * mask)
        out_grad = jnp.concatenate(grads, axis=0)
        grad = norm_back(normed, scale, gain_ref[2:3], out_grad)
        third_grad[...] = grad
        low_t[...] = grad.astype(BF).T
        small_ref[12:13] = rows_sum(grad)
        small_ref[13:14] = rows_sum(out_grad)
        small_ref[16:17] = rows_sum(out_grad * normed)
        branch[...] = jnp.zeros_like(branch)

    @pl.when(step >= blocks)
    def _():
        block = step - blocks
        ffn_low = third_grad[...].astype(BF)
        grad_out_ref[0] = mm(low_t[...], activated[block]).astype(BF)
        grad_hidden = mm(ffn_low, out_ref[0]) * gelu_slope(hidden[block])
        grad_low = grad_hidden.astype(BF)
        small_ref[pl.ds(4 + block, 1)] = rows_sum(grad_low.astype(F32))
        grad_in_ref[0] = mm(second_low_t[...], grad_low).astype(BF)
        branch[...] += mm_nt(grad_low, in_ref[0])

    @pl.when(step == 2 * blocks - 1)
    def _():
        second_in = third_grad[...] + branch[...]
        normed, scale = norm_parts(second_sum[...])
        grad = norm_back(normed, scale, gain_ref[1:2], second_in)
        residual_ref[...] = grad
        small_ref[10:11] = rows_sum(grad)
        small_ref[11:12] = rows_sum(second_in)
        small_ref[15:16] = rows_sum(second_in * normed)
        cross_low = grad.astype(BF)
        cross_grad_ref[...] = mm(cross_low.T, mixed_ref[...]).astype(BF)
        mixed_grad_ref[...] = mm(cross_low, cross_w_ref[0]).astype(BF)


def cross_back_kernel(
    context_ref, query_ref, key_ref, value_ref, total_ref, mixed_grad_ref, key_w_ref, value_w_ref,
    query_grad_ref, context_grad_ref, key_wg_ref, value_wg_ref, small_ref,
    context_t, acc, key_acc, value_acc,
):
    image, group = pl.program_id(0), pl.program_id(1)
    last_image, last_group = pl.num_programs(0) - 1, pl.num_programs(1) - 1

    @pl.when(group == 0)
    def _():
        context_t[...] = context_ref[...].T

    @pl.when((image == 0) & (group == 0))
    def _():
        small_ref[...] = jnp.zeros_like(small_ref)

    grad_query, grad_key, grad_value = attend_back(
        query_ref[...], key_ref[...], value_ref[...], total_ref[0, 0:1], mixed_grad_ref[...],
        key_ref.shape[0],
    )
    query_grad_ref[...] = grad_query
    lanes = pl.ds(pl.multiple_of(group * SLAB, SLAB), SLAB)
    small_ref[0:1, lanes] += rows_sum(grad_query.astype(F32))
    small_ref[1:2, lanes] += rows_sum(grad_value.astype(F32))
    key_wg = mm(context_t[...], grad_key)
    value_wg = mm(context_t[...], grad_value)
    context_part = mm_nt(grad_key, key_w_ref[0]) + mm_nt(grad_value, value_w_ref[0])

    @pl.when(group == 0)
    def _():
        acc[...] = context_part

    @pl.when((group > 0) & (group < last_group))
    def _():
        acc[...] += context_part

    @pl.when(group == last_group)
    def _():
        context_grad_ref[...] = (acc[...] + context_part).astype(BF)

    @pl.when(image == 0)
    def _():
        key_acc[:, lanes] = key_wg
        value_acc[:, lanes] = value_wg

    @pl.when(image > 0)
    def _():
        key_acc[:, lanes] += key_wg
        value_acc[:, lanes] += value_wg

    @pl.when(image == last_image)
    def _():
        key_wg_ref[:, lanes] = key_acc[:, lanes].astype(BF)
        value_wg_ref[:, lanes] = value_acc[:, lanes].astype(BF)


def self_back_kernel(
    images, valid, tokens_ref, weight_ref, row_ref, gain_ref, qkv_ref, mixed_ref, total_ref, sum_ref,
    residual_ref, cross_query_grad_ref,
    query_grad_ref, cross_wg_ref, self_wg_ref, small_ref, qkv_grad,
):
    small_ref[...] = jnp.zeros_like(small_ref)
    tokens = tokens_ref[...]
    rows = tokens.shape[0] // images
    width = tokens.shape[1]
    normed, scale = norm_parts(sum_ref[...])
    first_low = (normed * gain_ref[0:1] + row_ref[1:2]).astype(BF)
    cross_query_grad = cross_query_grad_ref[...]
    cross_wg_ref[...] = mm(first_low.T, cross_query_grad).astype(BF)
    first_in = residual_ref[...] + mm_nt(cross_query_grad, weight_ref[4])
    first_grad = norm_back(normed, scale, gain_ref[0:1], first_in)
    small_ref[2:3] = rows_sum(first_grad)
    small_ref[3:4] = rows_sum(first_in)
    small_ref[4:5] = rows_sum(first_in * normed)
    self_low = first_grad.astype(BF)
    self_wg_ref[3] = mm(self_low.T, mixed_ref[...]).astype(BF)
    mixed_grad = mm(self_low, weight_ref[3]).astype(BF)
    for image in range(images):
        at = slice(image * rows, (image + 1) * rows)
        for group in range(width // SLAB):
            lanes = slice(group * SLAB, (group + 1) * SLAB)
            grads = attend_back(
                qkv_ref[0, at, lanes], qkv_ref[1, at, lanes], qkv_ref[2, at, lanes],
                total_ref[image * (width // SLAB) + group, 0:1], mixed_grad[at, lanes], valid,
            )
            for which in range(3):
                qkv_grad[which, at, lanes] = grads[which]
    tokens_t = tokens.T
    total = first_grad
    for which in range(3):
        grad = qkv_grad[which]
        self_wg_ref[which] = mm(tokens_t, grad).astype(BF)
        total = total + mm_nt(grad, weight_ref[which])
    small_ref[0:1] = rows_sum(qkv_grad[0].astype(F32))
    small_ref[1:2] = rows_sum(qkv_grad[2].astype(F32))
    query_grad_ref[...] = total.astype(BF)


def gram_kernel(parts_ref, gram_ref):
    tasks = parts_ref.shape[0]

    @pl.when(pl.program_id(0) == 0)
    def _():
        gram_ref[...] = jnp.zeros_like(gram_ref)

    shares = [parts_ref[task, 0].astype(F32) for task in range(tasks)]
    for a in range(tasks):
        for b in range(a, tasks):
            gram_ref[a * tasks + b : a * tasks + b + 1] += rows_sum(shares[a] * shares[b])


def update_kernel(weights_ref, parts_ref, update_ref):
    tasks, blocks = parts_ref.shape[:2]
    for block in range(blocks):
        total = weights_ref[0] * parts_ref[0, block].astype(F32)
        for task in range(1, tasks):
            total += weights_ref[task] * parts_ref[task, block].astype(F32)
        update_ref[:, block, :] = total


def body(
    queries, memory, cotangent, matches, counts, task_order, params, head_bias, row_bias, norm_gain
):
    all_images = matches.shape[1]
    valid = matches.shape[2]
    width = queries.shape[2]
    half = params.shape[2]
    block_count = params.shape[1]
    blocks = (block_count - 8) // 2
    cores = lax.axis_size("tensor")
    images = all_images // cores
    keys = memory.shape[1] // all_images
    padded = -(-valid // 16) * 16
    rows = images * padded
    groups = width // SLAB
    stack = GROUP * padded
    core = lax.axis_index("tensor")

    def own_rows(array):
        split = array[0].reshape(all_images, valid, width)
        mine = lax.dynamic_slice_in_dim(split, core * images, images, 0)
        return jnp.pad(mine, ((0, 0), (0, padded - valid), (0, 0))).reshape(rows, width)

    tokens = own_rows(queries)
    own_cotangent = own_rows(cotangent)
    own_matches = lax.dynamic_slice_in_dim(matches[0], core * images, images, 0)[:, None, :]
    own_counts = lax.dynamic_slice_in_dim(counts[0], core * images, images, 0)
    context = memory[0]
    row_f = jnp.pad(row_bias.astype(F32).reshape(6, width), ((0, 2), (0, 0)))
    gain_f = jnp.pad(norm_gain.astype(F32), ((0, 5), (0, 0)))
    own_bias = jnp.pad(head_bias, ((0, 8), (0, 0)))
    chunk = 96
    weights, full_bias = pl.pallas_call(
        gather_kernel,
        grid=(width // chunk,),
        out_shape=(
            jax.ShapeDtypeStruct((block_count, width, cores * half), BF),
            jax.ShapeDtypeStruct((16, cores * half), BF),
        ),
        in_specs=[
            pl.BlockSpec((chunk, block_count, half), lambda i: (i, 0, 0)),
            pl.BlockSpec((16, half), lambda i: (0, 0)),
        ],
        out_specs=(any_spec(), any_spec()),
        scratch_shapes=[
            pltpu.VMEM((block_count, width, half), BF),
            pltpu.VMEM((16, half), BF),
            pltpu.SemaphoreType.DMA((width // chunk + 1,)),
            pltpu.SemaphoreType.DMA((width // chunk + 1,)),
            pltpu.SemaphoreType.DMA((width // chunk + 1,)),
        ],
        compiler_params=params_for(collective_id=0, has_side_effects=True),
        name="gather_weights",
    )(params, own_bias)
    head_f = full_bias.astype(F32)

    def const(shape, *index):
        return pl.BlockSpec(shape, lambda *_: index)

    total_shape = jax.ShapeDtypeStruct((images * groups, 8, stack), F32)
    low_rows = jax.ShapeDtypeStruct((rows, width), BF)
    full_rows = jax.ShapeDtypeStruct((rows, width), F32)
    small_shape = jax.ShapeDtypeStruct((24, width), F32)
    one_block = jax.ShapeDtypeStruct((width, width), BF)
    small_spec = const((24, width), 0, 0)
    vec8 = const((8, width), 0, 0)
    head_spec = const((16, width), 0, 0)
    rows_spec = const((rows, width), 0, 0)

    qkv, self_mixed, self_total, first_sum, cross_query = pl.pallas_call(
        functools.partial(self_kernel, images, valid),
        grid=(1,),
        out_shape=(
            jax.ShapeDtypeStruct((3, rows, width), BF), low_rows, total_shape, full_rows, low_rows,
        ),
        in_specs=[rows_spec, const((5, width, width), 0, 0, 0), head_spec, vec8, vec8],
        out_specs=(
            const((3, rows, width), 0, 0, 0), rows_spec, const(total_shape.shape, 0, 0, 0),
            rows_spec, rows_spec,
        ),
        compiler_params=params_for(),
        name="self_forward",
    )(tokens, weights, head_f, row_f, gain_f)

    start = (core * images).astype(jnp.int32).reshape(1)
    context_all = pl.BlockSpec((keys, width), lambda i, g, s: (s[0] + i, 0))
    slab_q = pl.BlockSpec((padded, SLAB), lambda i, g, *_: (i, g))
    slab_k = pl.BlockSpec((keys, SLAB), lambda i, g, *_: (i, g))
    slab_t = pl.BlockSpec((1, 8, stack), lambda i, g, *_: (i * groups + g, 0, 0))

    def slab_w(block):
        return pl.BlockSpec((1, width, SLAB), lambda i, g, *_: (block, 0, g))

    def with_start(kernel):
        return lambda start_ref, *refs: kernel(*refs)

    key_rows = jax.ShapeDtypeStruct((images * keys, width), BF)
    keys_act, values_act, cross_mixed, cross_total = pl.pallas_call(
        with_start(cross_kernel),
        grid_spec=pltpu.PrefetchScalarGridSpec(
            num_scalar_prefetch=1,
            grid=(images, groups),
            in_specs=[
                context_all, slab_q, slab_w(5), slab_w(6),
                pl.BlockSpec((16, SLAB), lambda i, g, *_: (0, g)),
            ],
            out_specs=(slab_k, slab_k, slab_q, slab_t),
        ),
        out_shape=(key_rows, key_rows, low_rows, total_shape),
        compiler_params=params_for(),
        name="cross_forward",
    )(start, context, cross_query, weights, weights, head_f)

    (
        block_rows, grad_in, grad_out, cross_out_wg, mixed_grad, second_grad, ffn_small,
    ) = pl.pallas_call(
        functools.partial(ffn_kernel, images, blocks),
        grid=(2 * blocks,),
        out_shape=(
            low_rows,
            jax.ShapeDtypeStruct((blocks, width, width), BF),
            jax.ShapeDtypeStruct((blocks, width, width), BF),
            one_block, low_rows, full_rows, small_shape,
        ),
        in_specs=[
            rows_spec, rows_spec, rows_spec,
            const(own_matches.shape, 0, 0, 0),
            pl.BlockSpec(memory_space=pltpu.SMEM),
            const((1, width, width), 7, 0, 0),
            pl.BlockSpec((1, width, width), lambda s: (8 + s % blocks, 0, 0)),
            pl.BlockSpec((1, width, width), lambda s: (8 + blocks + s % blocks, 0, 0)),
            head_spec, vec8, vec8,
        ],
        out_specs=(
            rows_spec,
            pl.BlockSpec((1, width, width), lambda s: (jnp.maximum(s - blocks, 0), 0, 0)),
            pl.BlockSpec((1, width, width), lambda s: (jnp.maximum(s - blocks, 0), 0, 0)),
            const((width, width), 0, 0), rows_spec, rows_spec, small_spec,
        ),
        scratch_shapes=[
            pltpu.VMEM((rows, width), F32),
            pltpu.VMEM((width, rows), BF),
            pltpu.VMEM((width, rows), BF),
            pltpu.VMEM((blocks, rows, width), F32),
            pltpu.VMEM((blocks, rows, width), BF),
            pltpu.VMEM((rows, width), F32),
            pltpu.VMEM((rows, width), F32),
        ],
        compiler_params=params_for(),
        name="ffn",
    )(
        first_sum, cross_mixed, own_cotangent, own_matches, own_counts, weights, weights, weights,
        head_f, row_f, gain_f,
    )

    cross_query_grad, context_grad, key_wg, value_wg, cross_small = pl.pallas_call(
        with_start(cross_back_kernel),
        grid_spec=pltpu.PrefetchScalarGridSpec(
            num_scalar_prefetch=1,
            grid=(images, groups),
            in_specs=[
                context_all, slab_q, slab_k, slab_k, slab_t, slab_q, slab_w(5), slab_w(6),
            ],
            out_specs=(
                slab_q,
                pl.BlockSpec((keys, width), lambda i, g, *_: (i, 0)),
                const((width, width), 0, 0), const((width, width), 0, 0), small_spec,
            ),
            scratch_shapes=[
                pltpu.VMEM((width, keys), BF),
                pltpu.VMEM((keys, width), F32),
                pltpu.VMEM((width, width), F32),
                pltpu.VMEM((width, width), F32),
            ],
        ),
        out_shape=(low_rows, key_rows, one_block, one_block, small_shape),
        compiler_params=params_for(),
        name="cross_backward",
    )(start, context, cross_query, keys_act, values_act, cross_total, mixed_grad, weights, weights)

    token_grad, cross_query_wg, self_wg, self_small = pl.pallas_call(
        functools.partial(self_back_kernel, images, valid),
        grid=(1,),
        out_shape=(
            low_rows, one_block, jax.ShapeDtypeStruct((4, width, width), BF), small_shape,
        ),
        in_specs=[
            rows_spec, const((5, width, width), 0, 0, 0), vec8, vec8,
            const((3, rows, width), 0, 0, 0), rows_spec, const(total_shape.shape, 0, 0, 0),
            rows_spec, rows_spec, rows_spec,
        ],
        out_specs=(
            rows_spec, const((width, width), 0, 0), const((4, width, width), 0, 0, 0), small_spec,
        ),
        scratch_shapes=[pltpu.VMEM((3, rows, width), BF)],
        compiler_params=params_for(),
        name="self_backward",
    )(
        tokens, weights, row_f, gain_f, qkv, self_mixed, self_total, first_sum, second_grad,
        cross_query_grad,
    )

    def unpad(array):
        return array.reshape(images, padded, width)[:, :valid].reshape(1, images * valid, width)

    block_out = lax.all_gather(unpad(block_rows), "tensor", axis=1, tiled=True)
    query_grad = unpad(token_grad)
    memory_grad = context_grad[None]

    small = jnp.concatenate(
        [
            self_small[0:2], cross_small[0:2], ffn_small[4:8],
            self_small[2:4], ffn_small[10:14], self_small[4:5], ffn_small[15:17],
        ],
        axis=0,
    )
    grads = jnp.concatenate(
        [
            self_wg,
            jnp.stack([cross_query_wg, key_wg, value_wg, cross_out_wg]),
            grad_in,
            grad_out,
        ],
        axis=0,
    )
    swap = [(0, 1), (1, 0)]
    grads = (
        grads[:, :, :half].astype(F32) + lax.ppermute(grads[:, :, half:], "tensor", swap).astype(F32)
    ).astype(BF)
    head_small = small[:8, :half] + lax.ppermute(small[:8, half:], "tensor", swap)
    row_small = lax.psum(small[8:], ("dp", "tensor"))
    head_small = lax.psum(head_small, "dp")
    shard = lax.psum_scatter(grads, "dp", scatter_dimension=1, tiled=True)
    all_shards = lax.all_gather(shard, "task", axis=0, tiled=False)
    all_head = lax.all_gather(head_small, "task", axis=0, tiled=False)
    all_row = lax.all_gather(row_small, "task", axis=0, tiled=False)
    tasks = all_shards.shape[0]
    share_rows = shard.shape[1]
    sums = pl.pallas_call(
        gram_kernel,
        grid=(block_count,),
        out_shape=jax.ShapeDtypeStruct((tasks * tasks, half), F32),
        in_specs=[pl.BlockSpec((tasks, 1, share_rows, half), lambda k: (0, k, 0, 0))],
        out_specs=const((tasks * tasks, half), 0, 0),
        compiler_params=params_for(),
        name="gram",
    )(all_shards)
    upper = jnp.sum(sums, axis=1).reshape(tasks, tasks)
    gram_weights = upper + upper.T - jnp.diag(jnp.diag(upper))
    gram_weights = lax.psum(gram_weights, ("dp", "tensor"))
    gram_heads = jnp.einsum("axy,bxy->ab", all_head, all_head, precision=highest)
    gram_heads = lax.psum(gram_heads, "tensor")
    gram = gram_weights + gram_heads + jnp.einsum(
        "axy,bxy->ab", all_row, all_row, precision=highest
    )
    task_weights = combine_weights(gram, task_order)
    tile = 64 if share_rows % 64 == 0 else share_rows
    param_update = pl.pallas_call(
        update_kernel,
        grid=(share_rows // tile,),
        out_shape=jax.ShapeDtypeStruct((share_rows, block_count, half), F32),
        in_specs=[
            pl.BlockSpec(memory_space=pltpu.SMEM),
            pl.BlockSpec((tasks, block_count, tile, half), lambda r: (0, 0, r, 0)),
        ],
        out_specs=pl.BlockSpec((tile, block_count, half), lambda r: (r, 0, 0)),
        compiler_params=params_for(),
        name="update",
    )(task_weights, all_shards)
    head_bias_update = jnp.einsum("a,axy->xy", task_weights, all_head, precision=highest)
    row_update = jnp.einsum("a,axy->xy", task_weights, all_row, precision=highest)
    return (
        block_out, query_grad, memory_grad, param_update, head_bias_update,
        row_update[:6].reshape(3, 2, width), row_update[6:9], gram,
    )


def solution(mesh):
    return jax.shard_map(
        body,
        mesh=mesh,
        in_specs=(
            P("task", "dp", None),
            P("task", "dp", None),
            P("task", "dp", None),
            P("task", "dp", None),
            P("task", "dp"),
            P(),
            P(None, None, "tensor"),
            P(None, "tensor"),
            P(),
            P(),
        ),
        out_specs=(
            P("task", "dp", None),
            P("task", ("dp", "tensor"), None),
            P("task", ("dp", "tensor"), None),
            P("dp", None, "tensor"),
            P(None, "tensor"),
            P(),
            P(),
            P(),
        ),
        check_vma=False,
    )
```

```python
import functools

import jax
import jax.numpy as jnp
from jax import lax
from jax.experimental import pallas as pl
from jax.experimental.pallas import tpu as pltpu
from jax.sharding import PartitionSpec as P

HD = 64
GROUP = 4
SLAB = GROUP * HD
BF = jnp.bfloat16
F32 = jnp.float32
MESH_ID = pl.DeviceIdType.MESH
highest = lax.Precision.HIGHEST
VMEM_LIMIT = 60 * 2**20


def combine_weights(gram_matrix, order_list):
    task_count = gram_matrix.shape[0]
    task_index = jnp.arange(task_count, dtype=jnp.int32)
    summed = jnp.zeros((task_count,), F32)
    for own_task in range(task_count):
        coeffs = (task_index == own_task).astype(F32)
        for position in range(task_count):
            chosen = (task_index == order_list[position]).astype(F32)
            column = jnp.sum(gram_matrix * chosen[None, :], axis=1)
            inner_dot = jnp.sum(coeffs * column)
            square = jnp.sum(chosen * column)
            others = (order_list[position] != own_task).astype(F32)
            coeffs = coeffs - others * jnp.minimum(inner_dot, 0.0) / (square + 1e-06) * chosen
        summed = summed + coeffs
    return summed


def mm(a, b):
    return jnp.dot(a, b, preferred_element_type=F32)


def mm_nt(a, b):
    return lax.dot_general(a, b, (((1,), (1,)), ((), ())), preferred_element_type=F32)


def mm_tn(a, b):
    return lax.dot_general(a, b, (((0,), (0,)), ((), ())), preferred_element_type=F32)


def norm_parts(residual):
    row_mean = jnp.mean(residual, axis=-1, keepdims=True)
    centred = residual - row_mean
    variance = jnp.mean(centred * centred, axis=-1, keepdims=True)
    scale = lax.rsqrt(variance + 1e-05)
    return centred * scale, scale


def norm_back(normed, scale, gain_row, grad):
    scaled = grad * gain_row
    first = jnp.mean(scaled, axis=-1, keepdims=True)
    second = jnp.mean(scaled * normed, axis=-1, keepdims=True)
    return scale * (scaled - first - normed * second)


def rows_sum(value):
    return jnp.sum(value, axis=0, keepdims=True)


def gelu_tanh(hidden):
    return (
        0.5
        * hidden
        * (1.0 + jnp.tanh(0.7978845608028654 * (hidden + 0.044715 * hidden * hidden * hidden)))
    )


def gelu_slope(hidden):
    square = hidden * hidden
    tanh = jnp.tanh(0.7978845608028654 * (hidden + 0.044715 * hidden * square))
    inner = 0.7978845608028654 * (1.0 + 3 * 0.044715 * square)
    return 0.5 * (1.0 + tanh) + 0.5 * hidden * (1.0 - tanh * tanh) * inner


def head_mask(head, rows, dtype):
    lane = lax.broadcasted_iota(jnp.int32, (rows, SLAB), 1)
    return (lane // HD == head).astype(F32).astype(dtype)


def stack_heads(slab):
    return jnp.concatenate(
        [slab * head_mask(head, slab.shape[0], slab.dtype) for head in range(GROUP)], axis=0
    )


def unstack_heads(stacked):
    rows = stacked.shape[0] // GROUP
    total = None
    for head in range(GROUP):
        part = stacked[head * rows : (head + 1) * rows] * head_mask(head, rows, stacked.dtype)
        total = part if total is None else total + part
    return total


def scores_of(query_stack, key_slab, valid):
    scores = mm_nt(key_slab, query_stack)
    if valid < key_slab.shape[0]:
        row = lax.broadcasted_iota(jnp.int32, scores.shape, 0)
        scores = jnp.where(row < valid, scores, -1e30)
    return scores


def attend(query_slab, key_slab, value_slab, valid):
    scores = scores_of(stack_heads(query_slab * HD ** (-0.5)), key_slab, valid)
    row_max = jnp.max(scores, axis=0, keepdims=True)
    exps = jnp.exp(scores - row_max)
    total = jnp.sum(exps, axis=0, keepdims=True)
    probs = (exps * (1.0 / total)).astype(BF)
    mixed = unstack_heads(mm_tn(value_slab, probs).T)
    return mixed, row_max + jnp.log(total)


def attend_back(query_slab, key_slab, value_slab, log_total, grad_slab, valid):
    query_stack = stack_heads(query_slab * HD ** (-0.5))
    grad_stack = stack_heads(grad_slab)
    probs = jnp.exp(scores_of(query_stack, key_slab, valid) - log_total)
    grad_value = mm(probs.astype(BF), grad_stack)
    grad_probs = mm_nt(value_slab, grad_stack)
    inner = jnp.sum(probs * grad_probs, axis=0, keepdims=True)
    grad_scores = (probs * (grad_probs - inner)).astype(BF)
    grad_key = mm(grad_scores, query_stack)
    grad_query = unstack_heads(mm_tn(key_slab, grad_scores).T) * HD ** (-0.5)
    return grad_query.astype(BF), grad_key.astype(BF), grad_value.astype(BF)


def gather_kernel(own_ref, bias_ref, full_ref, full_bias_ref, turned, bias_own, remote_send,
                  remote_recv, local_sem):
    step, steps = pl.program_id(0), pl.num_programs(0)
    other = 1 - lax.axis_index("tensor")
    rows, _, width = own_ref.shape
    near, far = pl.ds(0, width), pl.ds(width, width)

    def copies(chunk):
        at = pl.ds(pl.multiple_of(chunk * rows, rows), rows)
        source = turned.at[:, at]
        return (
            pltpu.make_async_remote_copy(
                source, full_ref.at[:, at, far], remote_send.at[chunk], remote_recv.at[chunk],
                device_id={"tensor": other}, device_id_type=MESH_ID,
            ),
            pltpu.make_async_copy(source, full_ref.at[:, at, near], local_sem.at[chunk]),
        )

    def bias_copies():
        return (
            pltpu.make_async_remote_copy(
                bias_own, full_bias_ref.at[:, far], remote_send.at[steps], remote_recv.at[steps],
                device_id={"tensor": other}, device_id_type=MESH_ID,
            ),
            pltpu.make_async_copy(bias_own, full_bias_ref.at[:, near], local_sem.at[steps]),
        )

    @pl.when(step == 0)
    def _():
        barrier = pltpu.get_barrier_semaphore()
        pl.semaphore_signal(barrier, inc=1, device_id={"tensor": other}, device_id_type=MESH_ID)
        pl.semaphore_wait(barrier, 1)
        bias_own[...] = bias_ref[...]
        for copy in bias_copies():
            copy.start()

    turned[:, pl.ds(pl.multiple_of(step * rows, rows), rows)] = jnp.swapaxes(own_ref[...], 0, 1)
    for copy in copies(step):
        copy.start()

    @pl.when(step == steps - 1)
    def _():
        for copy in bias_copies():
            copy.wait()

        def finish(chunk, carry):
            for copy in copies(chunk):
                copy.wait()
            return carry

        lax.fori_loop(0, steps, finish, 0)


def any_spec():
    return pl.BlockSpec(memory_space=pl.ANY)


def whole_spec():
    return pl.BlockSpec(memory_space=pltpu.VMEM)


def params_for(**keys):
    return pltpu.CompilerParams(vmem_limit_bytes=VMEM_LIMIT, **keys)


def self_kernel(images, valid, tokens_ref, weight_ref, head_ref, row_ref, gain_ref, qkv_ref,
                mixed_ref, total_ref, sum_ref, cross_query_ref):
    tokens = tokens_ref[...]
    rows = tokens.shape[0] // images
    width = tokens.shape[1]
    qkv_ref[0] = (mm(tokens, weight_ref[0]) + head_ref[0:1]).astype(BF)
    qkv_ref[1] = mm(tokens, weight_ref[1]).astype(BF)
    qkv_ref[2] = (mm(tokens, weight_ref[2]) + head_ref[1:2]).astype(BF)
    for image in range(images):
        at = slice(image * rows, (image + 1) * rows)
        for group in range(width // SLAB):
            lanes = slice(group * SLAB, (group + 1) * SLAB)
            mixed, log_total = attend(
                qkv_ref[0, at, lanes], qkv_ref[1, at, lanes], qkv_ref[2, at, lanes], valid
            )
            mixed_ref[at, lanes] = mixed.astype(BF)
            total_ref[image * (width // SLAB) + group] = jnp.broadcast_to(
                log_total, total_ref.shape[1:]
            )
    first_sum = tokens.astype(F32) + mm_nt(mixed_ref[...], weight_ref[3]) + row_ref[0:1]
    sum_ref[...] = first_sum
    first_low = (norm_parts(first_sum)[0] * gain_ref[0:1] + row_ref[1:2]).astype(BF)
    cross_query_ref[...] = (mm(first_low, weight_ref[4]) + head_ref[2:3]).astype(BF)


def cross_kernel(context_ref, query_ref, key_w_ref, value_w_ref, head_ref, key_ref, value_ref,
                 mixed_ref, total_ref):
    context = context_ref[...]
    key_ref[...] = mm(context, key_w_ref[0]).astype(BF)
    value_ref[...] = (mm(context, value_w_ref[0]) + head_ref[3:4]).astype(BF)
    mixed, log_total = attend(query_ref[...], key_ref[...], value_ref[...], key_ref.shape[0])
    mixed_ref[...] = mixed.astype(BF)
    total_ref[0] = jnp.broadcast_to(log_total, total_ref.shape[1:])


def ffn_kernel(
    images, blocks, sum_ref, mixed_ref, cotangent_ref, matches_ref, counts_ref, cross_w_ref, in_ref,
    out_ref, head_ref, row_ref, gain_ref,
    block_ref, grad_in_ref, grad_out_ref, cross_grad_ref, mixed_grad_ref, residual_ref, small_ref,
    second_sum, second_low_t, low_t, hidden, activated, branch, third_grad,
):
    step = pl.program_id(0)
    rows = sum_ref.shape[0] // images

    @pl.when(step == 0)
    def _():
        first_out = norm_parts(sum_ref[...])[0] * gain_ref[0:1] + row_ref[1:2]
        second_sum[...] = first_out + mm_nt(mixed_ref[...], cross_w_ref[0]) + row_ref[2:3]
        branch[...] = jnp.zeros_like(branch)
        small_ref[...] = jnp.zeros_like(small_ref)

    def second_out():
        return norm_parts(second_sum[...])[0] * gain_ref[1:2] + row_ref[3:4]

    @pl.when(step < blocks)
    def _():
        second_low = second_out().astype(BF)
        pre = mm(second_low, in_ref[0]) + head_ref[pl.ds(4 + step, 1)]
        hidden[step] = pre
        act = gelu_tanh(pre).astype(BF)
        activated[step] = act
        branch[...] += mm_nt(act, out_ref[0])

    @pl.when(step == blocks - 1)
    def _():
        second = second_out()
        second_low_t[...] = second.astype(BF).T
        third_sum = second + branch[...] + row_ref[4:5]
        normed, scale = norm_parts(third_sum)
        block_ref[...] = (normed * gain_ref[2:3] + row_ref[5:6]).astype(BF)
        count = matches_ref.shape[2]
        slot = lax.broadcasted_iota(jnp.int32, (rows, count), 0)
        box = lax.broadcasted_iota(jnp.int32, (rows, count), 1)
        grads = []
        for image in range(images):
            live = (matches_ref[image] == slot) & (box < counts_ref[image])
            mask = jnp.sum(jnp.where(live, 1.0, 0.0), axis=1, keepdims=True)
            cot = cotangent_ref[image * rows : (image + 1) * rows].astype(F32)
            grads.append(cot * mask)
        out_grad = jnp.concatenate(grads, axis=0)
        grad = norm_back(normed, scale, gain_ref[2:3], out_grad)
        third_grad[...] = grad
        low_t[...] = grad.astype(BF).T
        small_ref[12:13] = rows_sum(grad)
        small_ref[13:14] = rows_sum(out_grad)
        small_ref[16:17] = rows_sum(out_grad * normed)
        branch[...] = jnp.zeros_like(branch)

    @pl.when(step >= blocks)
    def _():
        block = step - blocks
        ffn_low = third_grad[...].astype(BF)
        grad_out_ref[0] = mm(low_t[...], activated[block]).astype(BF)
        grad_hidden = mm(ffn_low, out_ref[0]) * gelu_slope(hidden[block])
        grad_low = grad_hidden.astype(BF)
        small_ref[pl.ds(4 + block, 1)] = rows_sum(grad_low.astype(F32))
        grad_in_ref[0] = mm(second_low_t[...], grad_low).astype(BF)
        branch[...] += mm_nt(grad_low, in_ref[0])

    @pl.when(step == 2 * blocks - 1)
    def _():
        second_in = third_grad[...] + branch[...]
        normed, scale = norm_parts(second_sum[...])
        grad = norm_back(normed, scale, gain_ref[1:2], second_in)
        residual_ref[...] = grad
        small_ref[10:11] = rows_sum(grad)
        small_ref[11:12] = rows_sum(second_in)
        small_ref[15:16] = rows_sum(second_in * normed)
        cross_low = grad.astype(BF)
        cross_grad_ref[...] = mm(cross_low.T, mixed_ref[...]).astype(BF)
        mixed_grad_ref[...] = mm(cross_low, cross_w_ref[0]).astype(BF)


def cross_back_kernel(
    context_ref, query_ref, key_ref, value_ref, total_ref, mixed_grad_ref, key_w_ref, value_w_ref,
    query_grad_ref, context_grad_ref, key_wg_ref, value_wg_ref, small_ref,
    context_t, acc, key_acc, value_acc,
):
    image, group = pl.program_id(0), pl.program_id(1)
    last_image, last_group = pl.num_programs(0) - 1, pl.num_programs(1) - 1

    @pl.when(group == 0)
    def _():
        context_t[...] = context_ref[...].T

    @pl.when((image == 0) & (group == 0))
    def _():
        small_ref[...] = jnp.zeros_like(small_ref)

    grad_query, grad_key, grad_value = attend_back(
        query_ref[...], key_ref[...], value_ref[...], total_ref[0, 0:1], mixed_grad_ref[...],
        key_ref.shape[0],
    )
    query_grad_ref[...] = grad_query
    lanes = pl.ds(pl.multiple_of(group * SLAB, SLAB), SLAB)
    small_ref[0:1, lanes] += rows_sum(grad_query.astype(F32))
    small_ref[1:2, lanes] += rows_sum(grad_value.astype(F32))
    key_wg = mm(context_t[...], grad_key)
    value_wg = mm(context_t[...], grad_value)
    context_part = mm_nt(grad_key, key_w_ref[0]) + mm_nt(grad_value, value_w_ref[0])

    @pl.when(group == 0)
    def _():
        acc[...] = context_part

    @pl.when((group > 0) & (group < last_group))
    def _():
        acc[...] += context_part

    @pl.when(group == last_group)
    def _():
        context_grad_ref[...] = (acc[...] + context_part).astype(BF)

    @pl.when(image == 0)
    def _():
        key_acc[:, lanes] = key_wg
        value_acc[:, lanes] = value_wg

    @pl.when(image > 0)
    def _():
        key_acc[:, lanes] += key_wg
        value_acc[:, lanes] += value_wg

    @pl.when(image == last_image)
    def _():
        key_wg_ref[:, lanes] = key_acc[:, lanes].astype(BF)
        value_wg_ref[:, lanes] = value_acc[:, lanes].astype(BF)


def self_back_kernel(
    images, valid, tokens_ref, weight_ref, row_ref, gain_ref, qkv_ref, mixed_ref, total_ref, sum_ref,
    residual_ref, cross_query_grad_ref,
    query_grad_ref, cross_wg_ref, self_wg_ref, small_ref, qkv_grad,
):
    small_ref[...] = jnp.zeros_like(small_ref)
    tokens = tokens_ref[...]
    rows = tokens.shape[0] // images
    width = tokens.shape[1]
    normed, scale = norm_parts(sum_ref[...])
    first_low = (normed * gain_ref[0:1] + row_ref[1:2]).astype(BF)
    cross_query_grad = cross_query_grad_ref[...]
    cross_wg_ref[...] = mm(first_low.T, cross_query_grad).astype(BF)
    first_in = residual_ref[...] + mm_nt(cross_query_grad, weight_ref[4])
    first_grad = norm_back(normed, scale, gain_ref[0:1], first_in)
    small_ref[2:3] = rows_sum(first_grad)
    small_ref[3:4] = rows_sum(first_in)
    small_ref[4:5] = rows_sum(first_in * normed)
    self_low = first_grad.astype(BF)
    self_wg_ref[3] = mm(self_low.T, mixed_ref[...]).astype(BF)
    mixed_grad = mm(self_low, weight_ref[3]).astype(BF)
    for image in range(images):
        at = slice(image * rows, (image + 1) * rows)
        for group in range(width // SLAB):
            lanes = slice(group * SLAB, (group + 1) * SLAB)
            grads = attend_back(
                qkv_ref[0, at, lanes], qkv_ref[1, at, lanes], qkv_ref[2, at, lanes],
                total_ref[image * (width // SLAB) + group, 0:1], mixed_grad[at, lanes], valid,
            )
            for which in range(3):
                qkv_grad[which, at, lanes] = grads[which]
    tokens_t = tokens.T
    total = first_grad
    for which in range(3):
        grad = qkv_grad[which]
        self_wg_ref[which] = mm(tokens_t, grad).astype(BF)
        total = total + mm_nt(grad, weight_ref[which])
    small_ref[0:1] = rows_sum(qkv_grad[0].astype(F32))
    small_ref[1:2] = rows_sum(qkv_grad[2].astype(F32))
    query_grad_ref[...] = total.astype(BF)


def task_peers(tasks):
    me = lax.axis_index("task")
    return [lax.rem(me + shift, tasks) for shift in range(1, tasks)]


def task_senders(tasks):
    me = lax.axis_index("task")
    return [lax.rem(me + tasks - shift, tasks) for shift in range(1, tasks)]


def send(source, target, send_sem, recv_sem, **device):
    return pltpu.make_async_remote_copy(
        source, target, send_sem, recv_sem, device_id=device, device_id_type=MESH_ID
    )


def greet(depth, tasks):
    me = lax.axis_index("dp")
    barrier = pltpu.get_barrier_semaphore()
    for peer in task_peers(tasks):
        pl.semaphore_signal(barrier, inc=1, device_id={"task": peer}, device_id_type=MESH_ID)
    for shift in range(1, depth):
        pl.semaphore_signal(
            barrier, inc=1, device_id={"dp": lax.rem(me + shift, depth)}, device_id_type=MESH_ID
        )
    pl.semaphore_signal(
        barrier, inc=1, device_id={"tensor": 1 - lax.axis_index("tensor")}, device_id_type=MESH_ID
    )
    pl.semaphore_wait(barrier, tasks + depth - 1)


class Chain:
    def __init__(self, depth, tasks, near, far, passed, parts, sems):
        self.depth, self.tasks = depth, tasks
        self.near, self.far, self.passed, self.parts = near, far, passed, parts
        (self.near_sem, self.far_send, self.far_recv, self.pass_send, self.pass_recv,
         self.part_send, self.part_recv) = sems
        self.chunks = passed.shape[1]
        self.rows, self.half = passed.shape[2:]
        self.me = lax.axis_index("dp")
        self.task = lax.axis_index("task")
        self.is_end = (self.me == 0) | (self.me == depth - 1)

    @staticmethod
    def scratch(blocks, rows, half, tasks):
        chunks = 2 * blocks
        return [
            pltpu.VMEM((2, blocks, 2 * rows, half), BF),
            pltpu.VMEM((2, blocks, 2 * rows, half), BF),
            pltpu.VMEM((2, chunks, rows, half), BF),
            pltpu.VMEM((tasks, chunks, rows // tasks, half), BF),
            pltpu.SemaphoreType.DMA((2, blocks)),
            pltpu.SemaphoreType.DMA((2, blocks)),
            pltpu.SemaphoreType.DMA((2, blocks)),
            pltpu.SemaphoreType.DMA((2, chunks, 2)),
            pltpu.SemaphoreType.DMA((2, chunks, 2)),
            pltpu.SemaphoreType.DMA((chunks, tasks - 1)),
            pltpu.SemaphoreType.DMA((chunks, tasks - 1)),
        ]

    def near_copy(self, source, way, block):
        return pltpu.make_async_copy(
            source, self.near.at[way, block], self.near_sem.at[way, block]
        )

    def far_copy(self, source, way, block):
        return send(
            source, self.far.at[way, block], self.far_send.at[way, block],
            self.far_recv.at[way, block], tensor=1 - lax.axis_index("tensor"),
        )

    def load(self, block, source):
        for way in range(2):
            rows = pl.ds(way * 2 * self.rows, 2 * self.rows)
            self.near_copy(source.at[rows, pl.ds(0, self.half)], way, block).start()
            self.far_copy(source.at[rows, pl.ds(self.half, self.half)], way, block).start()

    def pass_copy(self, way, chunk, sub):
        rows = pl.ds(sub * (self.rows // 2), self.rows // 2)
        piece = self.passed.at[way, chunk, rows]
        target = self.me - 1 if way == 0 else self.me + 1
        return send(
            piece, piece, self.pass_send.at[way, chunk, sub], self.pass_recv.at[way, chunk, sub],
            dp=target,
        )

    def part_rows(self, peer):
        size = self.rows // self.tasks
        return pl.ds(pl.multiple_of(peer * size, size), size)

    def part_copy(self, way, chunk, shift, peer):
        return send(
            self.passed.at[way, chunk, self.part_rows(peer)], self.parts.at[self.task, chunk],
            self.part_send.at[chunk, shift], self.part_recv.at[chunk, shift], task=peer,
        )

    def lag(self, way):
        return self.depth - 1 - self.me if way == 0 else self.me

    def steps(self):
        return self.chunks + self.depth - 1

    def step(self, index):
        for way in range(2):
            chunk = index - self.lag(way)

            @pl.when((chunk >= 0) & (chunk < self.chunks))
            def _(way=way, chunk=chunk):
                self.chunk_step(way, chunk)

    def chunk_step(self, way, chunk):
        block = chunk // 2
        part = chunk - 2 * block
        first, last = self.lag(way) == 0, self.lag(way) == self.depth - 1

        @pl.when(part == 0)
        def _():
            piece = self.near.at[way, block]
            self.near_copy(piece, way, block).wait()
            self.far_copy(piece, way, block).wait_recv()

        sub_rows = self.rows // 2
        for sub in range(2):
            at = pl.ds(pl.multiple_of(part * self.rows + sub * sub_rows, sub_rows), sub_rows)
            rows = pl.ds(sub * sub_rows, sub_rows)

            def own():
                return self.near[way, block, at].astype(F32) + self.far[way, block, at].astype(F32)

            @pl.when(first)
            def _():
                self.passed[way, chunk, rows] = own().astype(BF)

            @pl.when(jnp.logical_not(first))
            def _():
                self.pass_copy(way, chunk, sub).wait_recv()
                self.passed[way, chunk, rows] = (
                    own() + self.passed[way, chunk, rows].astype(F32)
                ).astype(BF)

            @pl.when(jnp.logical_not(last))
            def _():
                self.pass_copy(way, chunk, sub).start()

        @pl.when(last)
        def _():
            for shift, peer in enumerate(task_peers(self.tasks)):
                self.part_copy(way, chunk, shift, peer).start()
            self.parts[self.task, chunk] = self.passed[way, chunk, self.part_rows(self.task)]

    def wait_parts(self, chunk):
        for shift, peer in enumerate(task_senders(self.tasks)):
            landed = self.parts.at[peer, chunk]
            send(
                landed, landed, self.part_send.at[chunk, shift], self.part_recv.at[chunk, shift],
                task=peer,
            ).wait_recv()

    def finish(self):
        def blocks(block, carry):
            for way in range(2):
                self.far_copy(self.near.at[way, block], way, block).wait_send()
            return carry

        lax.fori_loop(0, self.chunks // 2, blocks, 0)

        def chunks(chunk, carry):
            for way in range(2):

                @pl.when(self.lag(way) != self.depth - 1)
                def _(way=way):
                    for sub in range(2):
                        self.pass_copy(way, chunk, sub).wait_send()

                @pl.when(self.lag(way) == self.depth - 1)
                def _(way=way):
                    for shift, peer in enumerate(task_peers(self.tasks)):
                        self.part_copy(way, chunk, shift, peer).wait_send()

            return carry

        lax.fori_loop(0, self.chunks, chunks, 0)


def pairs_of(tasks):
    return [(a, b) for a in range(tasks) for b in range(a, tasks)]


def weights_of(gram, order_ref, tasks):
    totals = [0.0] * tasks
    for own in range(tasks):
        coeffs = [jnp.full_like(gram[0, 0], 1.0 if t == own else 0.0) for t in range(tasks)]
        for position in range(tasks):
            chosen = [
                jnp.where(order_ref[position] == t, 1.0, 0.0).astype(F32) for t in range(tasks)
            ]
            column = [sum(gram[t, j] * chosen[j] for j in range(tasks)) for t in range(tasks)]
            inner = sum(coeffs[t] * column[t] for t in range(tasks))
            square = sum(chosen[t] * column[t] for t in range(tasks))
            others = 1.0 - chosen[own]
            share = others * jnp.minimum(inner, 0.0) / (square + 1e-06)
            coeffs = [coeffs[t] - share * chosen[t] for t in range(tasks)]
        totals = [total + coeff for total, coeff in zip(totals, coeffs)]
    return totals


GROUPS = 4


def reduce_kernel(depth, tasks, layout, order_ref, small_ref, *refs):
    sources, refs = refs[: len(layout)], refs[len(layout) :]
    (update_ref, small_out_ref, gram_ref), refs = refs[:3], refs[3:]
    chain = Chain(depth, tasks, *refs[:4], refs[4:11])
    (
        small_far, small_pass, small_all, small_both, gram_acc, gram_task, gram_core, gram_end,
        hop, out,
        small_far_sem, small_pass_sem, small_task_sem, small_dp_sem, small_core_sem,
        gram_task_sem, gram_core_sem, gram_dp_sem, hop_sem, out_sem,
    ) = refs[11:]
    me, task, core = (lax.axis_index(axis) for axis in ("dp", "task", "tensor"))
    half = chain.half
    is_end = chain.is_end
    top = me == 0
    greet(depth, tasks)
    small_copy = send(
        small_ref.at[:, pl.ds(half, half)], small_far, small_far_sem.at[0], small_far_sem.at[1],
        tensor=1 - core,
    )
    small_copy.start()
    for index, (source, blocks) in enumerate(zip(sources, layout)):
        base = sum(len(entry) for entry in layout[:index])
        for block in range(len(blocks)):
            chain.load(base + block, source.at[block])
    block_order = [block for blocks in layout for block in blocks]

    def small_hop():
        return send(
            small_pass, small_pass, small_pass_sem.at[0], small_pass_sem.at[1], dp=me - 1
        )

    def small_task_copy(shift, peer):
        return send(
            small_pass, small_all.at[task], small_task_sem.at[0, shift],
            small_task_sem.at[1, shift], task=peer,
        )

    gram_acc[...] = jnp.zeros_like(gram_acc)
    pairs = pairs_of(tasks)

    def add_products(shares):
        for index, (a, b) in enumerate(pairs):
            product = shares[a] * shares[b]
            total = product[0:8]
            for row in range(8, product.shape[0], 8):
                total = total + product[row : row + 8]
            gram_acc[index * 8 : index * 8 + 8] += total

    def step(index, carry):
        chain.step(index)

        @pl.when(index == chain.lag(0))
        def _():
            small_copy.wait_recv()
            total = small_ref[:, pl.ds(0, half)] + small_far[...]

            @pl.when(me == depth - 1)
            def _():
                small_pass[...] = total

            @pl.when(me < depth - 1)
            def _():
                small_hop().wait_recv()
                small_pass[...] += total

            @pl.when(me > 0)
            def _():
                small_hop().start()

            @pl.when(top)
            def _():
                for shift, peer in enumerate(task_peers(tasks)):
                    small_task_copy(shift, peer).start()
                small_all[task] = small_pass[...]

        landed = index - (depth - 1) - 2

        @pl.when(is_end & (landed >= 0))
        def _():
            chain.wait_parts(landed)
            add_products([chain.parts[t, landed].astype(F32) for t in range(tasks)])

        return carry

    lax.fori_loop(0, chain.steps() + 2, step, 0)

    @pl.when(top)
    def _():
        for shift, peer in enumerate(task_senders(tasks)):
            landed = small_all.at[peer]
            send(
                landed, landed, small_task_sem.at[0, shift], small_task_sem.at[1, shift], task=peer
            ).wait_recv()

    lanes = gram_task.shape[2]

    def gram_task_copy(shift, peer):
        return send(
            gram_task.at[task], gram_task.at[task], gram_task_sem.at[0, shift],
            gram_task_sem.at[1, shift], task=peer,
        )

    def gram_core_copy(which):
        return send(
            gram_core.at[which], gram_core.at[which], gram_core_sem.at[0], gram_core_sem.at[1],
            tensor=1 - core,
        )

    def gram_dp_copy(end, shift):
        return send(
            gram_end.at[end], gram_end.at[end], gram_dp_sem.at[0, end, shift],
            gram_dp_sem.at[1, end, shift], dp=lax.rem((depth - 1) * end + shift + 1, depth),
        )

    def one_number(values):
        return jnp.sum(jnp.sum(values, axis=0, keepdims=True), axis=1, keepdims=True)

    @pl.when(is_end)
    def _():
        gram_task[task] = jnp.zeros(gram_task.shape[1:], F32)
        for index in range(len(pairs)):
            gram_task[task, index : index + 1] = jnp.broadcast_to(
                one_number(gram_acc[index * 8 : index * 8 + 8]), (1, lanes)
            )
        for shift, peer in enumerate(task_peers(tasks)):
            gram_task_copy(shift, peer).start()

    @pl.when(top)
    def _():
        small_all_values = [small_all[t] for t in range(tasks)]
        for index, (a, b) in enumerate(pairs):
            gram_end[0, index : index + 1] = jnp.broadcast_to(
                one_number(small_all_values[a] * small_all_values[b]), (1, lanes)
            )

    @pl.when(is_end)
    def _():
        for shift, peer in enumerate(task_senders(tasks)):
            landed = gram_task.at[peer]
            send(
                landed, landed, gram_task_sem.at[0, shift], gram_task_sem.at[1, shift], task=peer
            ).wait_recv()
        total = gram_task[0]
        for t in range(1, tasks):
            total = total + gram_task[t]

        @pl.when(top)
        def _():
            gram_core[core] = total + gram_end[0]

        @pl.when(jnp.logical_not(top))
        def _():
            gram_core[core] = total

        gram_core_copy(core).start()
        gram_core_copy(1 - core).wait_recv()

    for end in range(2):

        @pl.when(me == (depth - 1) * end)
        def _(end=end):
            gram_end[end] = gram_core[0] + gram_core[1]
            for shift in range(depth - 1):
                gram_dp_copy(end, shift).start()

    for end in range(2):
        for shift in range(depth - 1):

            @pl.when(me == ((depth - 1) * end + shift + 1) % depth)
            def _(end=end, shift=shift):
                gram_dp_copy(end, shift).wait_recv()

    gram = {}
    for index, (a, b) in enumerate(pairs):
        row = slice(index, index + 1)
        gram[a, b] = gram[b, a] = gram_end[0, row] + gram_end[1, row]
    for a in range(tasks):
        for b in range(tasks):
            gram_ref[a * tasks + b : a * tasks + b + 1] = gram[a, b]
    weights = [
        jnp.concatenate([weight] * (half // lanes), axis=1)
        for weight in weights_of(gram, order_ref, tasks)
    ]

    blocks = chain.chunks // 2
    group = blocks // GROUPS
    share = chain.rows // tasks
    mine = pl.ds(pl.multiple_of(task * share, share), share)
    own_part = jnp.minimum(me, 1)

    def hop_copy(index):
        return send(
            hop.at[pl.ds(index * group, group)], out.at[pl.ds(index * group, group), mine],
            hop_sem.at[0, index], hop_sem.at[1, index],
            dp=jnp.where(top, 1, depth - 2),
        )

    def out_copy(index, shift, peer):
        piece = out.at[pl.ds(index * group, group), mine]
        return send(piece, piece, out_sem.at[0, index, shift], out_sem.at[1, index, shift], task=peer)

    def weighted(chunk):
        total = weights[0] * chain.parts[0, chunk].astype(F32)
        for t in range(1, tasks):
            total = total + weights[t] * chain.parts[t, chunk].astype(F32)
        return total.astype(BF)

    def small_dp_copy(shift):
        return send(
            small_both.at[0], small_both.at[0], small_dp_sem.at[0, shift],
            small_dp_sem.at[1, shift], dp=shift + 1,
        )

    def small_core_copy():
        return send(
            small_both.at[0], small_both.at[1], small_core_sem.at[0], small_core_sem.at[1],
            tensor=1 - core,
        )

    @pl.when(top)
    def _():
        total = weights[0] * small_all[0]
        for t in range(1, tasks):
            total = total + weights[t] * small_all[t]
        small_both[0] = total
        for shift in range(depth - 1):
            small_dp_copy(shift).start()

    @pl.when(is_end)
    def _():
        for index in range(GROUPS):

            def other(block, carry):
                hop[block] = weighted(2 * block + 1 - own_part)
                return carry

            lax.fori_loop(index * group, (index + 1) * group, other, 0)
            hop_copy(index).start()

            def own(block, carry):
                out[block, mine] = weighted(2 * block + own_part)
                return carry

            lax.fori_loop(index * group, (index + 1) * group, own, 0)
            for shift, peer in enumerate(task_peers(tasks)):
                out_copy(index, shift, peer).start()

    @pl.when(jnp.logical_not(is_end))
    def _():
        for index in range(GROUPS):
            hop_copy(index).wait_recv()
            for shift, peer in enumerate(task_peers(tasks)):
                out_copy(index, shift, peer).start()

    for shift in range(depth - 1):

        @pl.when(me == shift + 1)
        def _(shift=shift):
            small_dp_copy(shift).wait_recv()

    small_core_copy().start()

    for index in range(GROUPS):
        for shift, peer in enumerate(task_senders(tasks)):
            piece = out.at[
                pl.ds(index * group, group), pl.ds(pl.multiple_of(peer * share, share), share)
            ]
            send(
                piece, piece, out_sem.at[0, index, shift], out_sem.at[1, index, shift], task=peer
            ).wait_recv()
        for block in range(index * group, (index + 1) * group):
            update_ref[:, block_order[block], :] = out[block].astype(F32)

    small_core_copy().wait_recv()
    small_out_ref[...] = small_both[...]

    small_copy.wait_send()
    small_core_copy().wait_send()
    chain.finish()

    @pl.when(me > 0)
    def _():
        small_hop().wait_send()

    @pl.when(top)
    def _():
        for shift, peer in enumerate(task_peers(tasks)):
            small_task_copy(shift, peer).wait_send()
        for shift in range(depth - 1):
            small_dp_copy(shift).wait_send()

    for end in range(2):

        @pl.when(me == (depth - 1) * end)
        def _(end=end):
            for shift in range(depth - 1):
                gram_dp_copy(end, shift).wait_send()

    @pl.when(is_end)
    def _():
        gram_core_copy(core).wait_send()
        for shift, peer in enumerate(task_peers(tasks)):
            gram_task_copy(shift, peer).wait_send()
        for index in range(GROUPS):
            hop_copy(index).wait_send()

    for index in range(GROUPS):
        for shift, peer in enumerate(task_peers(tasks)):
            out_copy(index, shift, peer).wait_send()


def reduce_by_chain(order, small, sources, layout, depth, tasks, half):
    blocks = sum(len(entry) for entry in layout)
    rows = sources[0].shape[1] // 4
    pair_rows = 8 * len(pairs_of(tasks))
    dma = pltpu.SemaphoreType.DMA
    return pl.pallas_call(
        functools.partial(reduce_kernel, depth, tasks, layout),
        out_shape=(
            jax.ShapeDtypeStruct((rows, blocks, half), F32),
            jax.ShapeDtypeStruct((2, *small.shape[:1], half), F32),
            jax.ShapeDtypeStruct((16, 128), F32),
        ),
        in_specs=[pl.BlockSpec(memory_space=pltpu.SMEM), whole_spec()]
        + [any_spec()] * len(sources),
        out_specs=(whole_spec(), whole_spec(), whole_spec()),
        scratch_shapes=Chain.scratch(blocks, rows, half, tasks)
        + [
            pltpu.VMEM((small.shape[0], half), F32),
            pltpu.VMEM((small.shape[0], half), F32),
            pltpu.VMEM((tasks, small.shape[0], half), F32),
            pltpu.VMEM((2, small.shape[0], half), F32),
            pltpu.VMEM((pair_rows, half), F32),
            pltpu.VMEM((tasks, 16, 128), F32),
            pltpu.VMEM((2, 16, 128), F32),
            pltpu.VMEM((2, 16, 128), F32),
            pltpu.VMEM((blocks, rows // tasks, half), BF),
            pltpu.VMEM((blocks, rows, half), BF),
            dma((2,)),
            dma((2,)),
            dma((2, tasks - 1)),
            dma((2, depth - 1)),
            dma((2,)),
            dma((2, tasks - 1)),
            dma((2,)),
            dma((2, 2, depth - 1)),
            dma((2, GROUPS)),
            dma((2, GROUPS, tasks - 1)),
        ],
        compiler_params=params_for(collective_id=1, has_side_effects=True),
        name="reduce",
    )(order, small, *sources)


def gram_kernel(parts_ref, gram_ref):
    tasks = parts_ref.shape[0]

    @pl.when(pl.program_id(0) == 0)
    def _():
        gram_ref[...] = jnp.zeros_like(gram_ref)

    shares = [parts_ref[task, 0].astype(F32) for task in range(tasks)]
    for a in range(tasks):
        for b in range(a, tasks):
            gram_ref[a * tasks + b : a * tasks + b + 1] += rows_sum(shares[a] * shares[b])


def update_kernel(weights_ref, parts_ref, update_ref):
    tasks, blocks = parts_ref.shape[:2]
    for block in range(blocks):
        total = weights_ref[0] * parts_ref[0, block].astype(F32)
        for task in range(1, tasks):
            total += weights_ref[task] * parts_ref[task, block].astype(F32)
        update_ref[:, block, :] = total


def body(
    queries, memory, cotangent, matches, counts, task_order, params, head_bias, row_bias, norm_gain
):
    all_images = matches.shape[1]
    valid = matches.shape[2]
    width = queries.shape[2]
    half = params.shape[2]
    block_count = params.shape[1]
    blocks = (block_count - 8) // 2
    cores = lax.axis_size("tensor")
    images = all_images // cores
    keys = memory.shape[1] // all_images
    padded = -(-valid // 16) * 16
    rows = images * padded
    groups = width // SLAB
    stack = GROUP * padded
    core = lax.axis_index("tensor")

    def own_rows(array):
        split = array[0].reshape(all_images, valid, width)
        mine = lax.dynamic_slice_in_dim(split, core * images, images, 0)
        return jnp.pad(mine, ((0, 0), (0, padded - valid), (0, 0))).reshape(rows, width)

    tokens = own_rows(queries)
    own_cotangent = own_rows(cotangent)
    own_matches = lax.dynamic_slice_in_dim(matches[0], core * images, images, 0)[:, None, :]
    own_counts = lax.dynamic_slice_in_dim(counts[0], core * images, images, 0)
    context = memory[0]
    row_f = jnp.pad(row_bias.astype(F32).reshape(6, width), ((0, 2), (0, 0)))
    gain_f = jnp.pad(norm_gain.astype(F32), ((0, 5), (0, 0)))
    own_bias = jnp.pad(head_bias, ((0, 8), (0, 0)))
    chunk = 96
    weights, full_bias = pl.pallas_call(
        gather_kernel,
        grid=(width // chunk,),
        out_shape=(
            jax.ShapeDtypeStruct((block_count, width, cores * half), BF),
            jax.ShapeDtypeStruct((16, cores * half), BF),
        ),
        in_specs=[
            pl.BlockSpec((chunk, block_count, half), lambda i: (i, 0, 0)),
            pl.BlockSpec((16, half), lambda i: (0, 0)),
        ],
        out_specs=(any_spec(), any_spec()),
        scratch_shapes=[
            pltpu.VMEM((block_count, width, half), BF),
            pltpu.VMEM((16, half), BF),
            pltpu.SemaphoreType.DMA((width // chunk + 1,)),
            pltpu.SemaphoreType.DMA((width // chunk + 1,)),
            pltpu.SemaphoreType.DMA((width // chunk + 1,)),
        ],
        compiler_params=params_for(collective_id=0, has_side_effects=True),
        name="gather_weights",
    )(params, own_bias)
    head_f = full_bias.astype(F32)

    def const(shape, *index):
        return pl.BlockSpec(shape, lambda *_: index)

    total_shape = jax.ShapeDtypeStruct((images * groups, 8, stack), F32)
    low_rows = jax.ShapeDtypeStruct((rows, width), BF)
    full_rows = jax.ShapeDtypeStruct((rows, width), F32)
    small_shape = jax.ShapeDtypeStruct((24, width), F32)
    one_block = jax.ShapeDtypeStruct((width, width), BF)
    small_spec = const((24, width), 0, 0)
    vec8 = const((8, width), 0, 0)
    head_spec = const((16, width), 0, 0)
    rows_spec = const((rows, width), 0, 0)

    qkv, self_mixed, self_total, first_sum, cross_query = pl.pallas_call(
        functools.partial(self_kernel, images, valid),
        grid=(1,),
        out_shape=(
            jax.ShapeDtypeStruct((3, rows, width), BF), low_rows, total_shape, full_rows, low_rows,
        ),
        in_specs=[rows_spec, const((5, width, width), 0, 0, 0), head_spec, vec8, vec8],
        out_specs=(
            const((3, rows, width), 0, 0, 0), rows_spec, const(total_shape.shape, 0, 0, 0),
            rows_spec, rows_spec,
        ),
        compiler_params=params_for(),
        name="self_forward",
    )(tokens, weights, head_f, row_f, gain_f)

    start = (core * images).astype(jnp.int32).reshape(1)
    context_all = pl.BlockSpec((keys, width), lambda i, g, s: (s[0] + i, 0))
    slab_q = pl.BlockSpec((padded, SLAB), lambda i, g, *_: (i, g))
    slab_k = pl.BlockSpec((keys, SLAB), lambda i, g, *_: (i, g))
    slab_t = pl.BlockSpec((1, 8, stack), lambda i, g, *_: (i * groups + g, 0, 0))

    def slab_w(block):
        return pl.BlockSpec((1, width, SLAB), lambda i, g, *_: (block, 0, g))

    def with_start(kernel):
        return lambda start_ref, *refs: kernel(*refs)

    key_rows = jax.ShapeDtypeStruct((images * keys, width), BF)
    keys_act, values_act, cross_mixed, cross_total = pl.pallas_call(
        with_start(cross_kernel),
        grid_spec=pltpu.PrefetchScalarGridSpec(
            num_scalar_prefetch=1,
            grid=(images, groups),
            in_specs=[
                context_all, slab_q, slab_w(5), slab_w(6),
                pl.BlockSpec((16, SLAB), lambda i, g, *_: (0, g)),
            ],
            out_specs=(slab_k, slab_k, slab_q, slab_t),
        ),
        out_shape=(key_rows, key_rows, low_rows, total_shape),
        compiler_params=params_for(),
        name="cross_forward",
    )(start, context, cross_query, weights, weights, head_f)

    (
        block_rows, grad_in, grad_out, cross_out_wg, mixed_grad, second_grad, ffn_small,
    ) = pl.pallas_call(
        functools.partial(ffn_kernel, images, blocks),
        grid=(2 * blocks,),
        out_shape=(
            low_rows,
            jax.ShapeDtypeStruct((blocks, width, width), BF),
            jax.ShapeDtypeStruct((blocks, width, width), BF),
            one_block, low_rows, full_rows, small_shape,
        ),
        in_specs=[
            rows_spec, rows_spec, rows_spec,
            const(own_matches.shape, 0, 0, 0),
            pl.BlockSpec(memory_space=pltpu.SMEM),
            const((1, width, width), 7, 0, 0),
            pl.BlockSpec((1, width, width), lambda s: (8 + s % blocks, 0, 0)),
            pl.BlockSpec((1, width, width), lambda s: (8 + blocks + s % blocks, 0, 0)),
            head_spec, vec8, vec8,
        ],
        out_specs=(
            rows_spec,
            pl.BlockSpec((1, width, width), lambda s: (jnp.maximum(s - blocks, 0), 0, 0)),
            pl.BlockSpec((1, width, width), lambda s: (jnp.maximum(s - blocks, 0), 0, 0)),
            const((width, width), 0, 0), rows_spec, rows_spec, small_spec,
        ),
        scratch_shapes=[
            pltpu.VMEM((rows, width), F32),
            pltpu.VMEM((width, rows), BF),
            pltpu.VMEM((width, rows), BF),
            pltpu.VMEM((blocks, rows, width), F32),
            pltpu.VMEM((blocks, rows, width), BF),
            pltpu.VMEM((rows, width), F32),
            pltpu.VMEM((rows, width), F32),
        ],
        compiler_params=params_for(),
        name="ffn",
    )(
        first_sum, cross_mixed, own_cotangent, own_matches, own_counts, weights, weights, weights,
        head_f, row_f, gain_f,
    )

    cross_query_grad, context_grad, key_wg, value_wg, cross_small = pl.pallas_call(
        with_start(cross_back_kernel),
        grid_spec=pltpu.PrefetchScalarGridSpec(
            num_scalar_prefetch=1,
            grid=(images, groups),
            in_specs=[
                context_all, slab_q, slab_k, slab_k, slab_t, slab_q, slab_w(5), slab_w(6),
            ],
            out_specs=(
                slab_q,
                pl.BlockSpec((keys, width), lambda i, g, *_: (i, 0)),
                const((width, width), 0, 0), const((width, width), 0, 0), small_spec,
            ),
            scratch_shapes=[
                pltpu.VMEM((width, keys), BF),
                pltpu.VMEM((keys, width), F32),
                pltpu.VMEM((width, width), F32),
                pltpu.VMEM((width, width), F32),
            ],
        ),
        out_shape=(low_rows, key_rows, one_block, one_block, small_shape),
        compiler_params=params_for(),
        name="cross_backward",
    )(start, context, cross_query, keys_act, values_act, cross_total, mixed_grad, weights, weights)

    token_grad, cross_query_wg, self_wg, self_small = pl.pallas_call(
        functools.partial(self_back_kernel, images, valid),
        grid=(1,),
        out_shape=(
            low_rows, one_block, jax.ShapeDtypeStruct((4, width, width), BF), small_shape,
        ),
        in_specs=[
            rows_spec, const((5, width, width), 0, 0, 0), vec8, vec8,
            const((3, rows, width), 0, 0, 0), rows_spec, const(total_shape.shape, 0, 0, 0),
            rows_spec, rows_spec, rows_spec,
        ],
        out_specs=(
            rows_spec, const((width, width), 0, 0), const((4, width, width), 0, 0, 0), small_spec,
        ),
        scratch_shapes=[pltpu.VMEM((3, rows, width), BF)],
        compiler_params=params_for(),
        name="self_backward",
    )(
        tokens, weights, row_f, gain_f, qkv, self_mixed, self_total, first_sum, second_grad,
        cross_query_grad,
    )

    def unpad(array):
        return array.reshape(images, padded, width)[:, :valid].reshape(1, images * valid, width)

    block_out = lax.all_gather(unpad(block_rows), "tensor", axis=1, tiled=True)
    query_grad = unpad(token_grad)
    memory_grad = context_grad[None]

    def by_halves(array):
        halves = array.reshape(array.shape[0], cores, half)
        return jnp.where(core == 0, halves, halves[:, ::-1]).reshape(array.shape)

    small = jnp.concatenate(
        [
            self_small[0:2], cross_small[0:2], ffn_small[4:8],
            by_halves(
                jnp.concatenate(
                    [self_small[2:4], ffn_small[10:14], self_small[4:5], ffn_small[15:17]], axis=0
                )
            ),
            jnp.zeros((7, width), F32),
        ],
        axis=0,
    )
    depth, tasks = lax.axis_size("dp"), lax.axis_size("task")
    if depth == 4 and tasks == 4 and cores == 2:
        param_update, small_update, gram_rows = reduce_by_chain(
            task_order, small,
            [grad_in, grad_out, self_wg, cross_query_wg[None], key_wg[None], value_wg[None],
             cross_out_wg[None]],
            [range(8, 8 + blocks), range(8 + blocks, block_count), range(4), [4], [5], [6], [7]],
            depth, tasks, half,
        )
        row_update = by_halves(
            jnp.concatenate([small_update[0, 8:17], small_update[1, 8:17]], axis=1)
        )
        return (
            block_out, query_grad, memory_grad, param_update, small_update[0, :8],
            row_update[:6].reshape(3, 2, width), row_update[6:9],
            gram_rows[: tasks * tasks, 0].reshape(tasks, tasks),
        )
    grads = jnp.concatenate(
        [
            self_wg,
            jnp.stack([cross_query_wg, key_wg, value_wg, cross_out_wg]),
            grad_in,
            grad_out,
        ],
        axis=0,
    )
    swap = [(0, 1), (1, 0)]
    grads = (
        grads[:, :, :half].astype(F32) + lax.ppermute(grads[:, :, half:], "tensor", swap).astype(F32)
    ).astype(BF)
    head_small = small[:8, :half] + lax.ppermute(small[:8, half:], "tensor", swap)
    row_small = lax.psum(by_halves(small[8:17]), ("dp", "tensor"))
    head_small = lax.psum(head_small, "dp")
    shard = lax.psum_scatter(grads, "dp", scatter_dimension=1, tiled=True)
    all_shards = lax.all_gather(shard, "task", axis=0, tiled=False)
    all_head = lax.all_gather(head_small, "task", axis=0, tiled=False)
    all_row = lax.all_gather(row_small, "task", axis=0, tiled=False)
    tasks = all_shards.shape[0]
    share_rows = shard.shape[1]
    sums = pl.pallas_call(
        gram_kernel,
        grid=(block_count,),
        out_shape=jax.ShapeDtypeStruct((tasks * tasks, half), F32),
        in_specs=[pl.BlockSpec((tasks, 1, share_rows, half), lambda k: (0, k, 0, 0))],
        out_specs=const((tasks * tasks, half), 0, 0),
        compiler_params=params_for(),
        name="gram",
    )(all_shards)
    upper = jnp.sum(sums, axis=1).reshape(tasks, tasks)
    gram_weights = upper + upper.T - jnp.diag(jnp.diag(upper))
    gram_weights = lax.psum(gram_weights, ("dp", "tensor"))
    gram_heads = jnp.einsum("axy,bxy->ab", all_head, all_head, precision=highest)
    gram_heads = lax.psum(gram_heads, "tensor")
    gram = gram_weights + gram_heads + jnp.einsum(
        "axy,bxy->ab", all_row, all_row, precision=highest
    )
    task_weights = combine_weights(gram, task_order)
    tile = 64 if share_rows % 64 == 0 else share_rows
    param_update = pl.pallas_call(
        update_kernel,
        grid=(share_rows // tile,),
        out_shape=jax.ShapeDtypeStruct((share_rows, block_count, half), F32),
        in_specs=[
            pl.BlockSpec(memory_space=pltpu.SMEM),
            pl.BlockSpec((tasks, block_count, tile, half), lambda r: (0, 0, r, 0)),
        ],
        out_specs=pl.BlockSpec((tile, block_count, half), lambda r: (r, 0, 0)),
        compiler_params=params_for(),
        name="update",
    )(task_weights, all_shards)
    head_bias_update = jnp.einsum("a,axy->xy", task_weights, all_head, precision=highest)
    row_update = jnp.einsum("a,axy->xy", task_weights, all_row, precision=highest)
    return (
        block_out, query_grad, memory_grad, param_update, head_bias_update,
        row_update[:6].reshape(3, 2, width), row_update[6:9], gram,
    )


def solution(mesh):
    return jax.shard_map(
        body,
        mesh=mesh,
        in_specs=(
            P("task", "dp", None),
            P("task", "dp", None),
            P("task", "dp", None),
            P("task", "dp", None),
            P("task", "dp"),
            P(),
            P(None, None, "tensor"),
            P(None, "tensor"),
            P(),
            P(),
        ),
        out_specs=(
            P("task", "dp", None),
            P("task", ("dp", "tensor"), None),
            P("task", ("dp", "tensor"), None),
            P("dp", None, "tensor"),
            P(None, "tensor"),
            P(),
            P(),
            P(),
        ),
        check_vma=False,
    )
```

```python
import functools

import jax
import jax.numpy as jnp
from jax import lax
from jax.experimental import pallas as pl
from jax.experimental.pallas import tpu as pltpu
from jax.sharding import PartitionSpec as P

HD = 64
GROUP = 4
SLAB = GROUP * HD
BF = jnp.bfloat16
F32 = jnp.float32
MESH_ID = pl.DeviceIdType.MESH
highest = lax.Precision.HIGHEST
VMEM_LIMIT = 62 * 2**20


def combine_weights(gram_matrix, order_list):
    task_count = gram_matrix.shape[0]
    task_index = jnp.arange(task_count, dtype=jnp.int32)
    summed = jnp.zeros((task_count,), F32)
    for own_task in range(task_count):
        coeffs = (task_index == own_task).astype(F32)
        for position in range(task_count):
            chosen = (task_index == order_list[position]).astype(F32)
            column = jnp.sum(gram_matrix * chosen[None, :], axis=1)
            inner_dot = jnp.sum(coeffs * column)
            square = jnp.sum(chosen * column)
            others = (order_list[position] != own_task).astype(F32)
            coeffs = coeffs - others * jnp.minimum(inner_dot, 0.0) / (square + 1e-06) * chosen
        summed = summed + coeffs
    return summed


def mm(a, b):
    return jnp.dot(a, b, preferred_element_type=F32)


def mm_nt(a, b):
    return lax.dot_general(a, b, (((1,), (1,)), ((), ())), preferred_element_type=F32)


def mm_tn(a, b):
    return lax.dot_general(a, b, (((0,), (0,)), ((), ())), preferred_element_type=F32)


def norm_parts(residual):
    row_mean = jnp.mean(residual, axis=-1, keepdims=True)
    centred = residual - row_mean
    variance = jnp.mean(centred * centred, axis=-1, keepdims=True)
    scale = lax.rsqrt(variance + 1e-05)
    return centred * scale, scale


def norm_back(normed, scale, gain_row, grad):
    scaled = grad * gain_row
    first = jnp.mean(scaled, axis=-1, keepdims=True)
    second = jnp.mean(scaled * normed, axis=-1, keepdims=True)
    return scale * (scaled - first - normed * second)


def rows_sum(value):
    return jnp.sum(value, axis=0, keepdims=True)


def gelu_tanh(hidden):
    return (
        0.5
        * hidden
        * (1.0 + jnp.tanh(0.7978845608028654 * (hidden + 0.044715 * hidden * hidden * hidden)))
    )


def gelu_slope(hidden):
    square = hidden * hidden
    tanh = jnp.tanh(0.7978845608028654 * (hidden + 0.044715 * hidden * square))
    inner = 0.7978845608028654 * (1.0 + 3 * 0.044715 * square)
    return 0.5 * (1.0 + tanh) + 0.5 * hidden * (1.0 - tanh * tanh) * inner


def head_mask(head, rows, dtype):
    lane = lax.broadcasted_iota(jnp.int32, (rows, SLAB), 1)
    return (lane // HD == head).astype(F32).astype(dtype)


def stack_heads(slab):
    return jnp.concatenate(
        [slab * head_mask(head, slab.shape[0], slab.dtype) for head in range(GROUP)], axis=0
    )


def unstack_heads(stacked):
    rows = stacked.shape[0] // GROUP
    total = None
    for head in range(GROUP):
        part = stacked[head * rows : (head + 1) * rows] * head_mask(head, rows, stacked.dtype)
        total = part if total is None else total + part
    return total


def scores_of(query_stack, key_slab, valid):
    scores = mm_nt(key_slab, query_stack)
    if valid < key_slab.shape[0]:
        row = lax.broadcasted_iota(jnp.int32, scores.shape, 0)
        scores = jnp.where(row < valid, scores, -1e30)
    return scores


def attend(query_slab, key_slab, value_slab, valid):
    scores = scores_of(stack_heads(query_slab * HD ** (-0.5)), key_slab, valid)
    row_max = jnp.max(scores, axis=0, keepdims=True)
    exps = jnp.exp(scores - row_max)
    total = jnp.sum(exps, axis=0, keepdims=True)
    probs = (exps * (1.0 / total)).astype(BF)
    mixed = unstack_heads(mm_tn(value_slab, probs).T)
    return mixed, row_max + jnp.log(total)


def attend_back(query_slab, key_slab, value_slab, log_total, grad_slab, valid):
    query_stack = stack_heads(query_slab * HD ** (-0.5))
    grad_stack = stack_heads(grad_slab)
    probs = jnp.exp(scores_of(query_stack, key_slab, valid) - log_total)
    grad_value = mm(probs.astype(BF), grad_stack)
    grad_probs = mm_nt(value_slab, grad_stack)
    inner = jnp.sum(probs * grad_probs, axis=0, keepdims=True)
    grad_scores = (probs * (grad_probs - inner)).astype(BF)
    grad_key = mm(grad_scores, query_stack)
    grad_query = unstack_heads(mm_tn(key_slab, grad_scores).T) * HD ** (-0.5)
    return grad_query.astype(BF), grad_key.astype(BF), grad_value.astype(BF)


def gather_kernel(own_ref, bias_ref, full_ref, full_bias_ref, turned, bias_own, remote_send,
                  remote_recv, local_sem):
    step, steps = pl.program_id(0), pl.num_programs(0)
    other = 1 - lax.axis_index("tensor")
    rows, _, width = own_ref.shape
    near, far = pl.ds(0, width), pl.ds(width, width)

    def copies(chunk):
        at = pl.ds(pl.multiple_of(chunk * rows, rows), rows)
        source = turned.at[:, at]
        return (
            pltpu.make_async_remote_copy(
                source, full_ref.at[:, at, far], remote_send.at[chunk], remote_recv.at[chunk],
                device_id={"tensor": other}, device_id_type=MESH_ID,
            ),
            pltpu.make_async_copy(source, full_ref.at[:, at, near], local_sem.at[chunk]),
        )

    def bias_copies():
        return (
            pltpu.make_async_remote_copy(
                bias_own, full_bias_ref.at[:, far], remote_send.at[steps], remote_recv.at[steps],
                device_id={"tensor": other}, device_id_type=MESH_ID,
            ),
            pltpu.make_async_copy(bias_own, full_bias_ref.at[:, near], local_sem.at[steps]),
        )

    @pl.when(step == 0)
    def _():
        barrier = pltpu.get_barrier_semaphore()
        pl.semaphore_signal(barrier, inc=1, device_id={"tensor": other}, device_id_type=MESH_ID)
        pl.semaphore_wait(barrier, 1)
        bias_own[...] = bias_ref[...]
        for copy in bias_copies():
            copy.start()

    turned[:, pl.ds(pl.multiple_of(step * rows, rows), rows)] = jnp.swapaxes(own_ref[...], 0, 1)
    for copy in copies(step):
        copy.start()

    @pl.when(step == steps - 1)
    def _():
        for copy in bias_copies():
            copy.wait()

        def finish(chunk, carry):
            for copy in copies(chunk):
                copy.wait()
            return carry

        lax.fori_loop(0, steps, finish, 0)


def any_spec():
    return pl.BlockSpec(memory_space=pl.ANY)


def whole_spec():
    return pl.BlockSpec(memory_space=pltpu.VMEM)


def params_for(**keys):
    return pltpu.CompilerParams(vmem_limit_bytes=VMEM_LIMIT, **keys)


def self_kernel(images, valid, tokens_ref, weight_ref, head_ref, row_ref, gain_ref, qkv_ref,
                mixed_ref, total_ref, sum_ref, cross_query_ref):
    tokens = tokens_ref[...]
    rows = tokens.shape[0] // images
    width = tokens.shape[1]
    qkv_ref[0] = (mm(tokens, weight_ref[0]) + head_ref[0:1]).astype(BF)
    qkv_ref[1] = mm(tokens, weight_ref[1]).astype(BF)
    qkv_ref[2] = (mm(tokens, weight_ref[2]) + head_ref[1:2]).astype(BF)
    for image in range(images):
        at = slice(image * rows, (image + 1) * rows)
        for group in range(width // SLAB):
            lanes = slice(group * SLAB, (group + 1) * SLAB)
            mixed, log_total = attend(
                qkv_ref[0, at, lanes], qkv_ref[1, at, lanes], qkv_ref[2, at, lanes], valid
            )
            mixed_ref[at, lanes] = mixed.astype(BF)
            total_ref[image * (width // SLAB) + group] = jnp.broadcast_to(
                log_total, total_ref.shape[1:]
            )
    first_sum = tokens.astype(F32) + mm_nt(mixed_ref[...], weight_ref[3]) + row_ref[0:1]
    sum_ref[...] = first_sum
    first_low = (norm_parts(first_sum)[0] * gain_ref[0:1] + row_ref[1:2]).astype(BF)
    cross_query_ref[...] = (mm(first_low, weight_ref[4]) + head_ref[2:3]).astype(BF)


def cross_kernel(context_ref, query_ref, key_w_ref, value_w_ref, head_ref, key_ref, value_ref,
                 mixed_ref, total_ref):
    context = context_ref[...]
    key_ref[...] = mm(context, key_w_ref[0]).astype(BF)
    value_ref[...] = (mm(context, value_w_ref[0]) + head_ref[3:4]).astype(BF)
    mixed, log_total = attend(query_ref[...], key_ref[...], value_ref[...], key_ref.shape[0])
    mixed_ref[...] = mixed.astype(BF)
    total_ref[0] = jnp.broadcast_to(log_total, total_ref.shape[1:])


def ffn_kernel(
    images, blocks, sum_ref, mixed_ref, cotangent_ref, matches_ref, counts_ref, cross_w_ref, in_ref,
    out_ref, head_ref, row_ref, gain_ref,
    block_ref, grad_in_ref, grad_out_ref, cross_grad_ref, mixed_grad_ref, residual_ref, small_ref,
    second_sum, second_low_t, low_t, hidden, activated, branch, third_grad,
):
    step = pl.program_id(0)
    rows = sum_ref.shape[0] // images

    @pl.when(step == 0)
    def _():
        first_out = norm_parts(sum_ref[...])[0] * gain_ref[0:1] + row_ref[1:2]
        second_sum[...] = first_out + mm_nt(mixed_ref[...], cross_w_ref[0]) + row_ref[2:3]
        branch[...] = jnp.zeros_like(branch)
        small_ref[...] = jnp.zeros_like(small_ref)

    def second_out():
        return norm_parts(second_sum[...])[0] * gain_ref[1:2] + row_ref[3:4]

    @pl.when(step < blocks)
    def _():
        second_low = second_out().astype(BF)
        pre = mm(second_low, in_ref[0]) + head_ref[pl.ds(4 + step, 1)]
        hidden[step] = pre
        act = gelu_tanh(pre).astype(BF)
        activated[step] = act
        branch[...] += mm_nt(act, out_ref[0])

    @pl.when(step == blocks - 1)
    def _():
        second = second_out()
        second_low_t[...] = second.astype(BF).T
        third_sum = second + branch[...] + row_ref[4:5]
        normed, scale = norm_parts(third_sum)
        block_ref[...] = (normed * gain_ref[2:3] + row_ref[5:6]).astype(BF)
        count = matches_ref.shape[2]
        slot = lax.broadcasted_iota(jnp.int32, (rows, count), 0)
        box = lax.broadcasted_iota(jnp.int32, (rows, count), 1)
        grads = []
        for image in range(images):
            live = (matches_ref[image] == slot) & (box < counts_ref[image])
            mask = jnp.sum(jnp.where(live, 1.0, 0.0), axis=1, keepdims=True)
            cot = cotangent_ref[image * rows : (image + 1) * rows].astype(F32)
            grads.append(cot * mask)
        out_grad = jnp.concatenate(grads, axis=0)
        grad = norm_back(normed, scale, gain_ref[2:3], out_grad)
        third_grad[...] = grad
        low_t[...] = grad.astype(BF).T
        small_ref[12:13] = rows_sum(grad)
        small_ref[13:14] = rows_sum(out_grad)
        small_ref[16:17] = rows_sum(out_grad * normed)
        branch[...] = jnp.zeros_like(branch)

    @pl.when(step >= blocks)
    def _():
        block = step - blocks
        ffn_low = third_grad[...].astype(BF)
        grad_out_ref[0] = mm(low_t[...], activated[block]).astype(BF)
        grad_hidden = mm(ffn_low, out_ref[0]) * gelu_slope(hidden[block])
        grad_low = grad_hidden.astype(BF)
        small_ref[pl.ds(4 + block, 1)] = rows_sum(grad_low.astype(F32))
        grad_in_ref[0] = mm(second_low_t[...], grad_low).astype(BF)
        branch[...] += mm_nt(grad_low, in_ref[0])

    @pl.when(step == 2 * blocks - 1)
    def _():
        second_in = third_grad[...] + branch[...]
        normed, scale = norm_parts(second_sum[...])
        grad = norm_back(normed, scale, gain_ref[1:2], second_in)
        residual_ref[...] = grad
        small_ref[10:11] = rows_sum(grad)
        small_ref[11:12] = rows_sum(second_in)
        small_ref[15:16] = rows_sum(second_in * normed)
        cross_low = grad.astype(BF)
        cross_grad_ref[...] = mm(cross_low.T, mixed_ref[...]).astype(BF)
        mixed_grad_ref[...] = mm(cross_low, cross_w_ref[0]).astype(BF)


def cross_back_step(
    image, group, images, groups, context_ref, query_ref, key_ref, value_ref, total_ref,
    mixed_grad_ref, key_w_ref, value_w_ref, context_grad_ref, small_ref, context_t, acc, key_acc,
    value_acc, unit,
):
    @pl.when(group == 0)
    def _():
        context_t[...] = context_ref[...].T

    unit(0)
    grad_query, grad_key, grad_value = attend_back(
        query_ref[...], key_ref[...], value_ref[...], total_ref[0, 0:1], mixed_grad_ref[...],
        key_ref.shape[0],
    )
    lanes = pl.ds(pl.multiple_of(group * SLAB, SLAB), SLAB)
    small_ref[2:3, lanes] += rows_sum(grad_query.astype(F32))
    small_ref[3:4, lanes] += rows_sum(grad_value.astype(F32))
    unit(1)
    key_wg = mm(context_t[...], grad_key)
    unit(2)
    value_wg = mm(context_t[...], grad_value)
    unit(3)
    context_part = mm_nt(grad_key, key_w_ref[0]) + mm_nt(grad_value, value_w_ref[0])

    @pl.when(group == 0)
    def _():
        acc[...] = context_part

    @pl.when((group > 0) & (group < groups - 1))
    def _():
        acc[...] += context_part

    @pl.when(group == groups - 1)
    def _():
        context_grad_ref[...] = (acc[...] + context_part).astype(BF)

    @pl.when(image == 0)
    def _():
        key_acc[:, lanes] = key_wg
        value_acc[:, lanes] = value_wg

    @pl.when(image > 0)
    def _():
        key_acc[:, lanes] += key_wg
        value_acc[:, lanes] += value_wg

    return grad_query


def cross_back_kernel(
    context_ref, query_ref, key_ref, value_ref, total_ref, mixed_grad_ref, key_w_ref, value_w_ref,
    query_grad_ref, context_grad_ref, key_wg_ref, value_wg_ref, small_ref,
    context_t, acc, key_acc, value_acc,
):
    image, group = pl.program_id(0), pl.program_id(1)
    images, groups = pl.num_programs(0), pl.num_programs(1)

    @pl.when((image == 0) & (group == 0))
    def _():
        small_ref[...] = jnp.zeros_like(small_ref)

    query_grad_ref[...] = cross_back_step(
        image, group, images, groups, context_ref, query_ref, key_ref, value_ref, total_ref,
        mixed_grad_ref, key_w_ref, value_w_ref, context_grad_ref, small_ref, context_t, acc,
        key_acc, value_acc, lambda part: None,
    )

    @pl.when((image == images - 1) & (group == groups - 1))
    def _():
        key_wg_ref[...] = key_acc[...].astype(BF)
        value_wg_ref[...] = value_acc[...].astype(BF)


def self_back(
    images, valid, tokens_ref, weight_ref, row_ref, gain_ref, qkv_ref, mixed_ref, total_ref, sum_ref,
    residual_ref, cross_query_grad_ref, small_ref, qkv_grad, emit, unit,
):
    tokens = tokens_ref[...]
    rows = tokens.shape[0] // images
    width = tokens.shape[1]
    normed, scale = norm_parts(sum_ref[...])
    first_low = (normed * gain_ref[0:1] + row_ref[1:2]).astype(BF)
    cross_query_grad = cross_query_grad_ref[...]
    emit(4, mm(first_low.T, cross_query_grad))
    unit()
    first_in = residual_ref[...] + mm_nt(cross_query_grad, weight_ref[4])
    first_grad = norm_back(normed, scale, gain_ref[0:1], first_in)
    small_ref[8:9] = rows_sum(first_grad)
    small_ref[9:10] = rows_sum(first_in)
    small_ref[14:15] = rows_sum(first_in * normed)
    unit()
    self_low = first_grad.astype(BF)
    emit(3, mm(self_low.T, mixed_ref[...]))
    unit()
    mixed_grad = mm(self_low, weight_ref[3]).astype(BF)
    for image in range(images):
        at = slice(image * rows, (image + 1) * rows)
        for group in range(width // SLAB):
            lanes = slice(group * SLAB, (group + 1) * SLAB)
            grads = attend_back(
                qkv_ref[0, at, lanes], qkv_ref[1, at, lanes], qkv_ref[2, at, lanes],
                total_ref[image * (width // SLAB) + group, 0:1], mixed_grad[at, lanes], valid,
            )
            for which in range(3):
                qkv_grad[which, at, lanes] = grads[which]
            unit()
    tokens_t = tokens.T
    total = first_grad
    for which in range(3):
        grad = qkv_grad[which]
        emit(which, mm(tokens_t, grad))
        unit()
        total = total + mm_nt(grad, weight_ref[which])
    small_ref[0:1] = rows_sum(qkv_grad[0].astype(F32))
    small_ref[1:2] = rows_sum(qkv_grad[2].astype(F32))
    return total


def self_back_kernel(
    images, valid, tokens_ref, weight_ref, row_ref, gain_ref, qkv_ref, mixed_ref, total_ref, sum_ref,
    residual_ref, cross_query_grad_ref, query_grad_ref, wg_ref, small_ref, qkv_grad,
):
    small_ref[...] = jnp.zeros_like(small_ref)

    def emit(block, value):
        wg_ref[block] = value.astype(BF)

    query_grad_ref[...] = self_back(
        images, valid, tokens_ref, weight_ref, row_ref, gain_ref, qkv_ref, mixed_ref, total_ref,
        sum_ref, residual_ref, cross_query_grad_ref, small_ref, qkv_grad, emit, lambda: None,
    ).astype(BF)


def task_peers(tasks):
    me = lax.axis_index("task")
    return [lax.rem(me + shift, tasks) for shift in range(1, tasks)]


def task_senders(tasks):
    me = lax.axis_index("task")
    return [lax.rem(me + tasks - shift, tasks) for shift in range(1, tasks)]


def send(source, target, send_sem, recv_sem, **device):
    return pltpu.make_async_remote_copy(
        source, target, send_sem, recv_sem, device_id=device, device_id_type=MESH_ID
    )


def greet(depth, tasks):
    me = lax.axis_index("dp")
    barrier = pltpu.get_barrier_semaphore()
    for peer in task_peers(tasks):
        pl.semaphore_signal(barrier, inc=1, device_id={"task": peer}, device_id_type=MESH_ID)
    for shift in range(1, depth):
        pl.semaphore_signal(
            barrier, inc=1, device_id={"dp": lax.rem(me + shift, depth)}, device_id_type=MESH_ID
        )
    pl.semaphore_signal(
        barrier, inc=1, device_id={"tensor": 1 - lax.axis_index("tensor")}, device_id_type=MESH_ID
    )
    pl.semaphore_wait(barrier, tasks + depth - 1)


LAG = 3
AHEAD = 2
RING = 4


class Chain:
    def __init__(self, depth, tasks, sources, near, far, refs):
        self.depth, self.tasks = depth, tasks
        self.sources, self.near, self.far = sources, near, far
        (self.near_ring, self.far_ring, self.passed, self.parts,
         self.near_sem, self.far_sem, self.far_send, self.far_recv, self.pass_send, self.pass_recv,
         self.part_send, self.part_recv) = refs
        self.chunks = self.passed.shape[1]
        self.rows, self.half = self.passed.shape[2:]
        self.size = self.rows // 2
        self.me = lax.axis_index("dp")
        self.task = lax.axis_index("task")
        self.is_end = (self.me == 0) | (self.me == depth - 1)
        self.given = sum(source.shape[0] for source in sources)

    SCRATCH = 12

    @staticmethod
    def scratch(blocks, rows, half, tasks):
        chunks = 2 * blocks
        dma = pltpu.SemaphoreType.DMA
        return [
            pltpu.VMEM((RING, 2, rows // 2, half), BF),
            pltpu.VMEM((RING, 2, rows // 2, half), BF),
            pltpu.VMEM((2, chunks, rows, half), BF),
            pltpu.VMEM((tasks, chunks, rows // tasks, half), BF),
            dma((RING, 2)),
            dma((RING, 2)),
            dma((2, blocks)),
            dma((2, blocks)),
            dma((2, chunks, 2)),
            dma((2, chunks, 2)),
            dma((chunks, tasks - 1)),
            dma((chunks, tasks - 1)),
        ]

    def far_copy(self, source, way, block):
        rows = pl.ds(way * 2 * self.rows, 2 * self.rows)
        return send(
            source.at[rows], self.far.at[way, block], self.far_send.at[way, block],
            self.far_recv.at[way, block], tensor=1 - lax.axis_index("tensor"),
        )

    def far_arrival(self, way, block):
        landed = self.far.at[way, block]
        return send(
            landed, landed, self.far_send.at[way, block], self.far_recv.at[way, block],
            tensor=1 - lax.axis_index("tensor"),
        )

    def exchange(self):
        base = 0
        for source in self.sources:
            for block in range(source.shape[0]):
                for way in range(2):
                    columns = pl.ds(self.half, self.half)
                    self.far_copy(source.at[block, :, columns], way, base + block).start()
            base += source.shape[0]

    def pass_copy(self, way, chunk, sub):
        rows = pl.ds(pl.multiple_of(sub * self.size, self.size), self.size)
        piece = self.passed.at[way, chunk, rows]
        target = self.me - 1 if way == 0 else self.me + 1
        return send(
            piece, piece, self.pass_send.at[way, chunk, sub], self.pass_recv.at[way, chunk, sub],
            dp=target,
        )

    def part_rows(self, peer):
        size = self.rows // self.tasks
        return pl.ds(pl.multiple_of(peer * size, size), size)

    def part_copy(self, way, chunk, shift, peer):
        return send(
            self.passed.at[way, chunk, self.part_rows(peer)], self.parts.at[self.task, chunk],
            self.part_send.at[chunk, shift], self.part_recv.at[chunk, shift], task=peer,
        )

    def hops(self, way):
        return self.depth - 1 - self.me if way == 0 else self.me

    def units(self):
        return 2 * self.chunks + LAG * (self.depth - 1)

    def near_fetch(self, source, slot, way):
        return pltpu.make_async_copy(
            source, self.near_ring.at[slot, way], self.near_sem.at[slot, way]
        )

    def far_fetch(self, source, slot, way):
        return pltpu.make_async_copy(
            source, self.far_ring.at[slot, way], self.far_sem.at[slot, way]
        )

    def fetch(self, index):
        slot = lax.rem(index, RING)
        for way in range(2):
            at = index - LAG * self.hops(way)

            @pl.when((at >= 0) & (at < 2 * self.chunks))
            def _(way=way, at=at):
                block = at // 4
                place = at - 4 * block

                @pl.when(place == 0)
                def _():
                    self.far_arrival(way, block).wait_recv()

                start = pl.multiple_of(place * self.size, self.size)
                rows = pl.ds(way * 2 * self.rows + start, self.size)
                base = 0
                for source in self.sources:
                    count = source.shape[0]

                    @pl.when((block >= base) & (block < base + count))
                    def _(source=source, base=base):
                        columns = pl.ds(0, self.half)
                        self.near_fetch(source.at[block - base, rows, columns], slot, way).start()

                    base += count

                @pl.when(block >= base)
                def _():
                    self.near_fetch(self.near.at[block - base, rows], slot, way).start()

                self.far_fetch(
                    self.far.at[way, block, pl.ds(start, self.size)], slot, way
                ).start()

    def unit(self, index):
        self.fetch(index + AHEAD)
        slot = lax.rem(index, RING)
        for way in range(2):
            at = index - LAG * self.hops(way)

            @pl.when((at >= 0) & (at < 2 * self.chunks))
            def _(way=way, at=at):
                chunk = at // 2
                self.half_step(way, chunk, at - 2 * chunk, slot)

    def half_step(self, way, chunk, sub, slot):
        first, last = self.hops(way) == 0, self.hops(way) == self.depth - 1
        piece = self.near_ring.at[slot, way]
        self.near_fetch(piece, slot, way).wait()
        self.far_fetch(piece, slot, way).wait()
        rows = pl.ds(pl.multiple_of(sub * self.size, self.size), self.size)
        own = self.near_ring[slot, way].astype(F32) + self.far_ring[slot, way].astype(F32)

        @pl.when(first)
        def _():
            self.passed[way, chunk, rows] = own.astype(BF)

        @pl.when(jnp.logical_not(first))
        def _():
            self.pass_copy(way, chunk, sub).wait_recv()
            self.passed[way, chunk, rows] = (
                own + self.passed[way, chunk, rows].astype(F32)
            ).astype(BF)

        @pl.when(jnp.logical_not(last))
        def _():
            self.pass_copy(way, chunk, sub).start()

        @pl.when(last & (sub == 1))
        def _():
            for shift, peer in enumerate(task_peers(self.tasks)):
                self.part_copy(way, chunk, shift, peer).start()
            self.parts[self.task, chunk] = self.passed[way, chunk, self.part_rows(self.task)]

    def wait_parts(self, chunk):
        for shift, peer in enumerate(task_senders(self.tasks)):
            landed = self.parts.at[peer, chunk]
            send(
                landed, landed, self.part_send.at[chunk, shift], self.part_recv.at[chunk, shift],
                task=peer,
            ).wait_recv()

    def finish(self):
        def chunks(chunk, carry):
            for way in range(2):

                @pl.when(self.hops(way) != self.depth - 1)
                def _(way=way):
                    for sub in range(2):
                        self.pass_copy(way, chunk, sub).wait_send()

                @pl.when(self.hops(way) == self.depth - 1)
                def _(way=way):
                    for shift, peer in enumerate(task_peers(self.tasks)):
                        self.part_copy(way, chunk, shift, peer).wait_send()

            return carry

        lax.fori_loop(0, self.chunks, chunks, 0)


def pairs_of(tasks):
    return [(a, b) for a in range(tasks) for b in range(a, tasks)]


def weights_of(gram, order_ref, tasks):
    totals = [0.0] * tasks
    for own in range(tasks):
        coeffs = [jnp.full_like(gram[0, 0], 1.0 if t == own else 0.0) for t in range(tasks)]
        for position in range(tasks):
            chosen = [
                jnp.where(order_ref[position] == t, 1.0, 0.0).astype(F32) for t in range(tasks)
            ]
            column = [sum(gram[t, j] * chosen[j] for j in range(tasks)) for t in range(tasks)]
            inner = sum(coeffs[t] * column[t] for t in range(tasks))
            square = sum(chosen[t] * column[t] for t in range(tasks))
            others = 1.0 - chosen[own]
            share = others * jnp.minimum(inner, 0.0) / (square + 1e-06)
            coeffs = [coeffs[t] - share * chosen[t] for t in range(tasks)]
        totals = [total + coeff for total, coeff in zip(totals, coeffs)]
    return totals


GROUPS = 4
UNITS = 4


def back_kernel(
    depth, tasks, images, groups, valid, block_order, order_ref, context_ref, query_ref, key_ref,
    value_ref, total_ref, mixed_grad_ref, key_w_ref, value_w_ref, tokens_ref, weight_ref, row_ref,
    gain_ref, qkv_ref, mixed_ref, self_total_ref, sum_ref, residual_ref, small_in_ref, *refs
):
    sources, refs = refs[:3], refs[3:]
    (context_grad_ref, query_grad_ref, update_ref, small_out_ref, gram_ref, near, far), refs = (
        refs[:7], refs[7:],
    )
    (context_t, acc, key_acc, value_acc, cross_query_grad, qkv_grad, stage, stage_sem), refs = (
        refs[:8], refs[8:],
    )
    chain = Chain(depth, tasks, sources, near, far, refs[: Chain.SCRATCH])
    refs = refs[Chain.SCRATCH :]
    (
        small, small_own, small_other, small_far, small_pass, small_all, small_both, gram_acc,
        gram_task, gram_core, gram_end, hop, out,
        small_far_sem, small_pass_sem, small_task_sem, small_dp_sem, small_core_sem,
        gram_task_sem, gram_core_sem, gram_dp_sem, hop_sem, out_sem, update_sem,
    ) = refs
    step = pl.program_id(0)
    cross_steps = images * groups
    me, task, core = (lax.axis_index(axis) for axis in ("dp", "task", "tensor"))
    half = chain.half
    is_end = chain.is_end
    top = me == 0
    pairs = pairs_of(tasks)

    def add_products(shares):
        for index, (a, b) in enumerate(pairs):
            product = shares[a] * shares[b]
            total = product[0:8]
            for row in range(8, product.shape[0], 8):
                total = total + product[row : row + 8]
            gram_acc[index * 8 : index * 8 + 8] += total

    def unit(index):
        chain.unit(index)
        since = index - LAG * (depth - 1) - 4
        landed = since // 2

        @pl.when(is_end & (since >= 0) & (since == 2 * landed))
        def _():
            chain.wait_parts(landed)
            add_products([chain.parts[t, landed].astype(F32) for t in range(tasks)])

    @pl.when(step == 0)
    def _():
        greet(depth, tasks)
        chain.exchange()
        gram_acc[...] = jnp.zeros_like(gram_acc)
        small[...] = small_in_ref[...]
        for index in range(AHEAD):
            chain.fetch(index)

    given = chain.given
    slots = stage.shape[0]

    def stage_copies(position):
        slot = position % slots
        return [
            chain.far_copy(stage.at[slot, :, pl.ds(half, half)], way, given + position)
            for way in range(2)
        ]

    def emit(position, value):
        slot = position % slots
        if position >= slots:
            for copy in stage_copies(position - slots):
                copy.wait_send()
        stage[slot] = value.astype(BF)
        for copy in stage_copies(position):
            copy.start()
        copy = pltpu.make_async_copy(
            stage.at[slot, :, pl.ds(0, half)], near.at[position], stage_sem
        )
        copy.start()
        copy.wait()

    def finish_reduction(done):
        rest(
            chain, unit, done, order_ref, update_ref, small_out_ref, gram_ref, small, small_own,
            small_other, small_far, small_pass, small_all, small_both, gram_acc, gram_task,
            gram_core, gram_end, hop, out, small_far_sem, small_pass_sem, small_task_sem,
            small_dp_sem, small_core_sem, gram_task_sem, gram_core_sem, gram_dp_sem, hop_sem,
            out_sem, update_sem,
        )
        for position in range(len(block_order) - given - slots, len(block_order) - given):
            for copy in stage_copies(position):
                copy.wait_send()
        for block in range(given):
            for way in range(2):
                chain.far_arrival(way, block).wait_send()

    @pl.when(step < cross_steps)
    def _():
        image = step // groups
        group = step - image * groups

        def cross_unit(part):
            if part < 2:
                unit(step * UNITS + part)
            else:

                @pl.when(step < cross_steps - 1)
                def _():
                    unit(step * UNITS + part)

        grad_query = cross_back_step(
            image, group, images, groups, context_ref, query_ref, key_ref, value_ref, total_ref,
            mixed_grad_ref, key_w_ref, value_w_ref, context_grad_ref, small, context_t, acc,
            key_acc, value_acc, cross_unit,
        )
        rows = grad_query.shape[0]
        cross_query_grad[
            pl.ds(pl.multiple_of(image * rows, rows), rows),
            pl.ds(pl.multiple_of(group * SLAB, SLAB), SLAB),
        ] = grad_query

        @pl.when(step == cross_steps - 1)
        def _():
            emit(0, key_acc[...])
            emit(1, value_acc[...])

    @pl.when(step == cross_steps)
    def _():
        done = [cross_steps * UNITS - 2]

        def self_unit():
            unit(jnp.int32(done[0]))
            done[0] += 1

        positions = {4: 2, 3: 3, 0: 4, 1: 5, 2: 6}
        query_grad_ref[...] = self_back(
            images, valid, tokens_ref, weight_ref, row_ref, gain_ref, qkv_ref, mixed_ref,
            self_total_ref, sum_ref, residual_ref, cross_query_grad, small, qkv_grad,
            lambda block, value: emit(positions[block], value), self_unit,
        ).astype(BF)
        finish_reduction(done[0])


def rest(
    chain, unit, done, order_ref, update_ref, small_out_ref, gram_ref, small, small_own, small_other,
    small_far, small_pass, small_all, small_both, gram_acc, gram_task, gram_core, gram_end, hop, out,
    small_far_sem, small_pass_sem, small_task_sem, small_dp_sem, small_core_sem, gram_task_sem,
    gram_core_sem, gram_dp_sem, hop_sem, out_sem, update_sem,
):
    depth, tasks, half = chain.depth, chain.tasks, chain.half
    me, task, core = (lax.axis_index(axis) for axis in ("dp", "task", "tensor"))
    is_end = chain.is_end
    top = me == 0
    pairs = pairs_of(tasks)
    own_lanes = pl.ds(pl.multiple_of(core * half, half), half)
    other_lanes = pl.ds(pl.multiple_of((1 - core) * half, half), half)
    small_own[0:8] = small[0:8, 0:half]
    small_own[8:] = small[8:, own_lanes]
    small_other[0:8] = small[0:8, half:]
    small_other[8:] = small[8:, other_lanes]
    small_copy = send(
        small_other, small_far, small_far_sem.at[0], small_far_sem.at[1], tensor=1 - core
    )
    small_copy.start()

    def small_hop():
        return send(
            small_pass, small_pass, small_pass_sem.at[0], small_pass_sem.at[1], dp=me - 1
        )

    def small_task_copy(shift, peer):
        return send(
            small_pass, small_all.at[task], small_task_sem.at[0, shift],
            small_task_sem.at[1, shift], task=peer,
        )

    def step(index, carry):
        unit(index)

        @pl.when(index == done + 1 + LAG * chain.hops(0))
        def _():
            small_copy.wait_recv()
            total = small_own[...] + small_far[...]

            @pl.when(me == depth - 1)
            def _():
                small_pass[...] = total

            @pl.when(me < depth - 1)
            def _():
                small_hop().wait_recv()
                small_pass[...] += total

            @pl.when(me > 0)
            def _():
                small_hop().start()

            @pl.when(top)
            def _():
                for shift, peer in enumerate(task_peers(tasks)):
                    small_task_copy(shift, peer).start()
                small_all[task] = small_pass[...]

        return carry

    lax.fori_loop(done, chain.units() + 4, step, 0)

    @pl.when(top)
    def _():
        for shift, peer in enumerate(task_senders(tasks)):
            landed = small_all.at[peer]
            send(
                landed, landed, small_task_sem.at[0, shift], small_task_sem.at[1, shift], task=peer
            ).wait_recv()

    lanes = gram_task.shape[2]

    def gram_task_copy(shift, peer):
        return send(
            gram_task.at[task], gram_task.at[task], gram_task_sem.at[0, shift],
            gram_task_sem.at[1, shift], task=peer,
        )

    def gram_core_copy(which):
        return send(
            gram_core.at[which], gram_core.at[which], gram_core_sem.at[0], gram_core_sem.at[1],
            tensor=1 - core,
        )

    def gram_dp_copy(end, shift):
        return send(
            gram_end.at[end], gram_end.at[end], gram_dp_sem.at[0, end, shift],
            gram_dp_sem.at[1, end, shift], dp=lax.rem((depth - 1) * end + shift + 1, depth),
        )

    def one_number(values):
        return jnp.sum(jnp.sum(values, axis=0, keepdims=True), axis=1, keepdims=True)

    @pl.when(is_end)
    def _():
        gram_task[task] = jnp.zeros(gram_task.shape[1:], F32)
        for index in range(len(pairs)):
            gram_task[task, index : index + 1] = jnp.broadcast_to(
                one_number(gram_acc[index * 8 : index * 8 + 8]), (1, lanes)
            )
        for shift, peer in enumerate(task_peers(tasks)):
            gram_task_copy(shift, peer).start()

    @pl.when(top)
    def _():
        small_all_values = [small_all[t] for t in range(tasks)]
        for index, (a, b) in enumerate(pairs):
            gram_end[0, index : index + 1] = jnp.broadcast_to(
                one_number(small_all_values[a] * small_all_values[b]), (1, lanes)
            )

    @pl.when(is_end)
    def _():
        for shift, peer in enumerate(task_senders(tasks)):
            landed = gram_task.at[peer]
            send(
                landed, landed, gram_task_sem.at[0, shift], gram_task_sem.at[1, shift], task=peer
            ).wait_recv()
        total = gram_task[0]
        for t in range(1, tasks):
            total = total + gram_task[t]

        @pl.when(top)
        def _():
            gram_core[core] = total + gram_end[0]

        @pl.when(jnp.logical_not(top))
        def _():
            gram_core[core] = total

        gram_core_copy(core).start()
        gram_core_copy(1 - core).wait_recv()

    for end in range(2):

        @pl.when(me == (depth - 1) * end)
        def _(end=end):
            gram_end[end] = gram_core[0] + gram_core[1]
            for shift in range(depth - 1):
                gram_dp_copy(end, shift).start()

    for end in range(2):
        for shift in range(depth - 1):

            @pl.when(me == ((depth - 1) * end + shift + 1) % depth)
            def _(end=end, shift=shift):
                gram_dp_copy(end, shift).wait_recv()

    gram = {}
    for index, (a, b) in enumerate(pairs):
        row = slice(index, index + 1)
        gram[a, b] = gram[b, a] = gram_end[0, row] + gram_end[1, row]
    for a in range(tasks):
        for b in range(tasks):
            gram_ref[a * tasks + b : a * tasks + b + 1] = gram[a, b]
    weights = [
        jnp.concatenate([weight] * (half // lanes), axis=1)
        for weight in weights_of(gram, order_ref, tasks)
    ]

    blocks = out.shape[0]
    group = blocks // GROUPS
    share = chain.rows // tasks
    mine = pl.ds(pl.multiple_of(task * share, share), share)
    own_part = jnp.minimum(me, 1)

    def hop_copy(index):
        return send(
            hop.at[pl.ds(index * group, group)], out.at[pl.ds(index * group, group), mine],
            hop_sem.at[0, index], hop_sem.at[1, index],
            dp=jnp.where(top, 1, depth - 2),
        )

    def out_copy(index, shift, peer):
        piece = out.at[pl.ds(index * group, group), mine]
        return send(piece, piece, out_sem.at[0, index, shift], out_sem.at[1, index, shift], task=peer)

    def update_copy(index):
        at = pl.ds(index * group, group)
        return pltpu.make_async_copy(out.at[at], update_ref.at[at], update_sem.at[index])

    def weighted(chunk):
        total = weights[0] * chain.parts[0, chunk].astype(F32)
        for t in range(1, tasks):
            total = total + weights[t] * chain.parts[t, chunk].astype(F32)
        return total.astype(BF)

    def small_dp_copy(shift):
        return send(
            small_both.at[0], small_both.at[0], small_dp_sem.at[0, shift],
            small_dp_sem.at[1, shift], dp=shift + 1,
        )

    def small_core_copy():
        return send(
            small_both.at[0], small_both.at[1], small_core_sem.at[0], small_core_sem.at[1],
            tensor=1 - core,
        )

    @pl.when(top)
    def _():
        total = weights[0] * small_all[0]
        for t in range(1, tasks):
            total = total + weights[t] * small_all[t]
        small_both[0] = total
        for shift in range(depth - 1):
            small_dp_copy(shift).start()

    @pl.when(is_end)
    def _():
        for index in range(GROUPS):

            def other(block, carry):
                hop[block] = weighted(2 * block + 1 - own_part)
                return carry

            lax.fori_loop(index * group, (index + 1) * group, other, 0)
            hop_copy(index).start()

            def own(block, carry):
                out[block, mine] = weighted(2 * block + own_part)
                return carry

            lax.fori_loop(index * group, (index + 1) * group, own, 0)
            for shift, peer in enumerate(task_peers(tasks)):
                out_copy(index, shift, peer).start()

    @pl.when(jnp.logical_not(is_end))
    def _():
        for index in range(GROUPS):
            hop_copy(index).wait_recv()
            for shift, peer in enumerate(task_peers(tasks)):
                out_copy(index, shift, peer).start()

    for shift in range(depth - 1):

        @pl.when(me == shift + 1)
        def _(shift=shift):
            small_dp_copy(shift).wait_recv()

    small_core_copy().start()

    for index in range(GROUPS):
        for shift, peer in enumerate(task_senders(tasks)):
            piece = out.at[
                pl.ds(index * group, group), pl.ds(pl.multiple_of(peer * share, share), share)
            ]
            send(
                piece, piece, out_sem.at[0, index, shift], out_sem.at[1, index, shift], task=peer
            ).wait_recv()
        update_copy(index).start()

    small_core_copy().wait_recv()
    small_out_ref[0:8, 0:half] = small_both[0, 0:8]
    small_out_ref[0:8, half:] = small_both[1, 0:8]
    small_out_ref[8:, own_lanes] = small_both[0, 8:]
    small_out_ref[8:, other_lanes] = small_both[1, 8:]

    small_copy.wait_send()
    small_core_copy().wait_send()
    chain.finish()

    @pl.when(me > 0)
    def _():
        small_hop().wait_send()

    @pl.when(top)
    def _():
        for shift, peer in enumerate(task_peers(tasks)):
            small_task_copy(shift, peer).wait_send()
        for shift in range(depth - 1):
            small_dp_copy(shift).wait_send()

    for end in range(2):

        @pl.when(me == (depth - 1) * end)
        def _(end=end):
            for shift in range(depth - 1):
                gram_dp_copy(end, shift).wait_send()

    @pl.when(is_end)
    def _():
        gram_core_copy(core).wait_send()
        for shift, peer in enumerate(task_peers(tasks)):
            gram_task_copy(shift, peer).wait_send()
        for index in range(GROUPS):
            hop_copy(index).wait_send()

    for index in range(GROUPS):
        update_copy(index).wait()
        for shift, peer in enumerate(task_peers(tasks)):
            out_copy(index, shift, peer).wait_send()


def spread_kernel(block_order, parts_ref, update_ref):
    for index, block in enumerate(block_order):
        update_ref[:, block, :] = parts_ref[index].astype(F32)


def gram_kernel(parts_ref, gram_ref):
    tasks = parts_ref.shape[0]

    @pl.when(pl.program_id(0) == 0)
    def _():
        gram_ref[...] = jnp.zeros_like(gram_ref)

    shares = [parts_ref[task, 0].astype(F32) for task in range(tasks)]
    for a in range(tasks):
        for b in range(a, tasks):
            gram_ref[a * tasks + b : a * tasks + b + 1] += rows_sum(shares[a] * shares[b])


def update_kernel(weights_ref, parts_ref, update_ref):
    tasks, blocks = parts_ref.shape[:2]
    for block in range(blocks):
        total = weights_ref[0] * parts_ref[0, block].astype(F32)
        for task in range(1, tasks):
            total += weights_ref[task] * parts_ref[task, block].astype(F32)
        update_ref[:, block, :] = total


def body(
    queries, memory, cotangent, matches, counts, task_order, params, head_bias, row_bias, norm_gain
):
    all_images = matches.shape[1]
    valid = matches.shape[2]
    width = queries.shape[2]
    half = params.shape[2]
    block_count = params.shape[1]
    blocks = (block_count - 8) // 2
    cores = lax.axis_size("tensor")
    images = all_images // cores
    keys = memory.shape[1] // all_images
    padded = -(-valid // 16) * 16
    rows = images * padded
    groups = width // SLAB
    stack = GROUP * padded
    core = lax.axis_index("tensor")

    def own_rows(array):
        split = array[0].reshape(all_images, valid, width)
        mine = lax.dynamic_slice_in_dim(split, core * images, images, 0)
        return jnp.pad(mine, ((0, 0), (0, padded - valid), (0, 0))).reshape(rows, width)

    tokens = own_rows(queries)
    own_cotangent = own_rows(cotangent)
    own_matches = lax.dynamic_slice_in_dim(matches[0], core * images, images, 0)[:, None, :]
    own_counts = lax.dynamic_slice_in_dim(counts[0], core * images, images, 0)
    context = memory[0]
    row_f = jnp.pad(row_bias.astype(F32).reshape(6, width), ((0, 2), (0, 0)))
    gain_f = jnp.pad(norm_gain.astype(F32), ((0, 5), (0, 0)))
    own_bias = jnp.pad(head_bias, ((0, 8), (0, 0)))
    chunk = 96
    weights, full_bias = pl.pallas_call(
        gather_kernel,
        grid=(width // chunk,),
        out_shape=(
            jax.ShapeDtypeStruct((block_count, width, cores * half), BF),
            jax.ShapeDtypeStruct((16, cores * half), BF),
        ),
        in_specs=[
            pl.BlockSpec((chunk, block_count, half), lambda i: (i, 0, 0)),
            pl.BlockSpec((16, half), lambda i: (0, 0)),
        ],
        out_specs=(any_spec(), any_spec()),
        scratch_shapes=[
            pltpu.VMEM((block_count, width, half), BF),
            pltpu.VMEM((16, half), BF),
            pltpu.SemaphoreType.DMA((width // chunk + 1,)),
            pltpu.SemaphoreType.DMA((width // chunk + 1,)),
            pltpu.SemaphoreType.DMA((width // chunk + 1,)),
        ],
        compiler_params=params_for(collective_id=0, has_side_effects=True),
        name="gather_weights",
    )(params, own_bias)
    head_f = full_bias.astype(F32)

    def const(shape, *index):
        return pl.BlockSpec(shape, lambda *_: index)

    total_shape = jax.ShapeDtypeStruct((images * groups, 8, stack), F32)
    low_rows = jax.ShapeDtypeStruct((rows, width), BF)
    full_rows = jax.ShapeDtypeStruct((rows, width), F32)
    small_shape = jax.ShapeDtypeStruct((24, width), F32)
    one_block = jax.ShapeDtypeStruct((width, width), BF)
    small_spec = const((24, width), 0, 0)
    vec8 = const((8, width), 0, 0)
    head_spec = const((16, width), 0, 0)
    rows_spec = const((rows, width), 0, 0)

    qkv, self_mixed, self_total, first_sum, cross_query = pl.pallas_call(
        functools.partial(self_kernel, images, valid),
        grid=(1,),
        out_shape=(
            jax.ShapeDtypeStruct((3, rows, width), BF), low_rows, total_shape, full_rows, low_rows,
        ),
        in_specs=[rows_spec, const((5, width, width), 0, 0, 0), head_spec, vec8, vec8],
        out_specs=(
            const((3, rows, width), 0, 0, 0), rows_spec, const(total_shape.shape, 0, 0, 0),
            rows_spec, rows_spec,
        ),
        compiler_params=params_for(),
        name="self_forward",
    )(tokens, weights, head_f, row_f, gain_f)


    def own_image(i, g):
        return lax.axis_index("tensor") * images + i, 0

    context_all = pl.BlockSpec((keys, width), own_image)
    slab_q = pl.BlockSpec((padded, SLAB), lambda i, g: (i, g))
    slab_k = pl.BlockSpec((keys, SLAB), lambda i, g: (i, g))
    slab_t = pl.BlockSpec((1, 8, stack), lambda i, g: (i * groups + g, 0, 0))

    def slab_w(block):
        return pl.BlockSpec((1, width, SLAB), lambda i, g: (block, 0, g))

    key_rows = jax.ShapeDtypeStruct((images * keys, width), BF)
    keys_act, values_act, cross_mixed, cross_total = pl.pallas_call(
        cross_kernel,
        grid=(images, groups),
        in_specs=[
            context_all, slab_q, slab_w(5), slab_w(6),
            pl.BlockSpec((16, SLAB), lambda i, g: (0, g)),
        ],
        out_specs=(slab_k, slab_k, slab_q, slab_t),
        out_shape=(key_rows, key_rows, low_rows, total_shape),
        compiler_params=params_for(),
        name="cross_forward",
    )(context, cross_query, weights, weights, head_f)

    (
        block_rows, grad_in, grad_out, cross_out_wg, mixed_grad, second_grad, ffn_small,
    ) = pl.pallas_call(
        functools.partial(ffn_kernel, images, blocks),
        grid=(2 * blocks,),
        out_shape=(
            low_rows,
            jax.ShapeDtypeStruct((blocks, width, width), BF),
            jax.ShapeDtypeStruct((blocks, width, width), BF),
            one_block, low_rows, full_rows, small_shape,
        ),
        in_specs=[
            rows_spec, rows_spec, rows_spec,
            const(own_matches.shape, 0, 0, 0),
            pl.BlockSpec(memory_space=pltpu.SMEM),
            const((1, width, width), 7, 0, 0),
            pl.BlockSpec((1, width, width), lambda s: (8 + s % blocks, 0, 0)),
            pl.BlockSpec((1, width, width), lambda s: (8 + blocks + s % blocks, 0, 0)),
            head_spec, vec8, vec8,
        ],
        out_specs=(
            rows_spec,
            pl.BlockSpec((1, width, width), lambda s: (jnp.maximum(s - blocks, 0), 0, 0)),
            pl.BlockSpec((1, width, width), lambda s: (jnp.maximum(s - blocks, 0), 0, 0)),
            const((width, width), 0, 0), rows_spec, rows_spec, small_spec,
        ),
        scratch_shapes=[
            pltpu.VMEM((rows, width), F32),
            pltpu.VMEM((width, rows), BF),
            pltpu.VMEM((width, rows), BF),
            pltpu.VMEM((blocks, rows, width), F32),
            pltpu.VMEM((blocks, rows, width), BF),
            pltpu.VMEM((rows, width), F32),
            pltpu.VMEM((rows, width), F32),
        ],
        compiler_params=params_for(),
        name="ffn",
    )(
        first_sum, cross_mixed, own_cotangent, own_matches, own_counts, weights, weights, weights,
        head_f, row_f, gain_f,
    )

    depth, tasks = lax.axis_size("dp"), lax.axis_size("task")
    by_chain = depth == 4 and tasks == 4 and cores == 2

    def unpad(array):
        return array.reshape(images, padded, width)[:, :valid].reshape(1, images * valid, width)

    block_out = lax.all_gather(unpad(block_rows), "tensor", axis=1, tiled=True)
    if by_chain:
        block_order = [*range(8, block_count), 7, 5, 6, 4, 3, 0, 1, 2]
        chain_rows = width // depth
        pair_rows = 8 * len(pairs_of(tasks))
        dma = pltpu.SemaphoreType.DMA
        last = images * groups - 1

        def at_step(make):
            def index_map(step):
                now = jnp.minimum(step, last)
                return make(now // groups, now - groups * (now // groups))

            return index_map

        def once(shape):
            return pl.BlockSpec(
                shape, lambda step: (0,) * len(shape), pipeline_mode=pl.Buffered(1)
            )

        step_q = pl.BlockSpec((padded, SLAB), at_step(lambda i, g: (i, g)))
        step_k = pl.BlockSpec((keys, SLAB), at_step(lambda i, g: (i, g)))

        def step_w(block):
            return pl.BlockSpec((1, width, SLAB), at_step(lambda i, g: (block, 0, g)))

        small_half = pltpu.VMEM((24, half), F32)
        (
            context_grad, token_grad, update_parts, small_out, gram_rows, _, _,
        ) = pl.pallas_call(
            functools.partial(
                back_kernel, depth, tasks, images, groups, valid, block_order
            ),
            grid=(images * groups + 1,),
            out_shape=(
                key_rows, low_rows,
                jax.ShapeDtypeStruct((block_count, chain_rows, half), BF),
                small_shape,
                jax.ShapeDtypeStruct((16, 128), F32),
                jax.ShapeDtypeStruct((7, width, half), BF),
                jax.ShapeDtypeStruct((2, block_count, width // 2, half), BF),
            ),
            in_specs=[
                pl.BlockSpec(memory_space=pltpu.SMEM),
                pl.BlockSpec((keys, width), at_step(own_image)),
                step_q, step_k, step_k,
                pl.BlockSpec((1, 8, stack), at_step(lambda i, g: (i * groups + g, 0, 0))),
                step_q, step_w(5), step_w(6),
                once((rows, width)), once((5, width, width)), once((8, width)), once((8, width)),
                once((3, rows, width)), once((rows, width)), once(total_shape.shape),
                once((rows, width)), once((rows, width)), once((24, width)),
                any_spec(), any_spec(), any_spec(),
            ],
            out_specs=(
                pl.BlockSpec((keys, width), at_step(lambda i, g: (i, 0))),
                once((rows, width)), any_spec(), once((24, width)), once((16, 128)),
                any_spec(), any_spec(),
            ),
            scratch_shapes=[
                pltpu.VMEM((width, keys), BF),
                pltpu.VMEM((keys, width), F32),
                pltpu.VMEM((width, width), F32),
                pltpu.VMEM((width, width), F32),
                pltpu.VMEM((rows, width), BF),
                pltpu.VMEM((3, rows, width), BF),
                pltpu.VMEM((3, width, width), BF),
                dma(()),
                *Chain.scratch(block_count, chain_rows, half, tasks),
                pltpu.VMEM((24, width), F32),
                small_half, small_half, small_half, small_half,
                pltpu.VMEM((tasks, 24, half), F32),
                pltpu.VMEM((2, 24, half), F32),
                pltpu.VMEM((pair_rows, half), F32),
                pltpu.VMEM((tasks, 16, 128), F32),
                pltpu.VMEM((2, 16, 128), F32),
                pltpu.VMEM((2, 16, 128), F32),
                pltpu.VMEM((block_count, chain_rows // tasks, half), BF),
                pltpu.VMEM((block_count, chain_rows, half), BF),
                dma((2,)),
                dma((2,)),
                dma((2, tasks - 1)),
                dma((2, depth - 1)),
                dma((2,)),
                dma((2, tasks - 1)),
                dma((2,)),
                dma((2, 2, depth - 1)),
                dma((2, GROUPS)),
                dma((2, GROUPS, tasks - 1)),
                dma((GROUPS,)),
            ],
            compiler_params=params_for(collective_id=1, has_side_effects=True),
            name="backward",
        )(
            task_order, context, cross_query, keys_act, values_act, cross_total, mixed_grad, weights,
            weights, tokens, weights, row_f, gain_f, qkv, self_mixed, self_total, first_sum,
            second_grad, ffn_small, grad_in, grad_out, cross_out_wg[None],
        )
        tile = chain_rows // 4
        param_update = pl.pallas_call(
            functools.partial(spread_kernel, block_order),
            grid=(4,),
            out_shape=jax.ShapeDtypeStruct((chain_rows, block_count, half), F32),
            in_specs=[pl.BlockSpec((block_count, tile, half), lambda r: (0, r, 0))],
            out_specs=pl.BlockSpec((tile, block_count, half), lambda r: (r, 0, 0)),
            compiler_params=params_for(),
            name="spread",
        )(update_parts)
        return (
            block_out, unpad(token_grad), context_grad[None], param_update, small_out[:8, :half],
            small_out[8:14].reshape(3, 2, width), small_out[14:17],
            gram_rows[: tasks * tasks, 0].reshape(tasks, tasks),
        )

    cross_query_grad, context_grad, key_wg, value_wg, cross_small = pl.pallas_call(
        cross_back_kernel,
        grid=(images, groups),
        in_specs=[
            context_all, slab_q, slab_k, slab_k, slab_t, slab_q, slab_w(5), slab_w(6),
        ],
        out_specs=(
            slab_q,
            pl.BlockSpec((keys, width), lambda i, g: (i, 0)),
            const((width, width), 0, 0), const((width, width), 0, 0), small_spec,
        ),
        scratch_shapes=[
            pltpu.VMEM((width, keys), BF),
            pltpu.VMEM((keys, width), F32),
            pltpu.VMEM((width, width), F32),
            pltpu.VMEM((width, width), F32),
        ],
        out_shape=(low_rows, key_rows, one_block, one_block, small_shape),
        compiler_params=params_for(),
        name="cross_backward",
    )(context, cross_query, keys_act, values_act, cross_total, mixed_grad, weights, weights)

    token_grad, self_wg, self_small = pl.pallas_call(
        functools.partial(self_back_kernel, images, valid),
        grid=(1,),
        out_shape=(
            low_rows, jax.ShapeDtypeStruct((5, width, width), BF), small_shape,
        ),
        in_specs=[
            rows_spec, const((5, width, width), 0, 0, 0), vec8, vec8,
            const((3, rows, width), 0, 0, 0), rows_spec, const(total_shape.shape, 0, 0, 0),
            rows_spec, rows_spec, rows_spec,
        ],
        out_specs=(
            rows_spec, const((5, width, width), 0, 0, 0), small_spec,
        ),
        scratch_shapes=[pltpu.VMEM((3, rows, width), BF)],
        compiler_params=params_for(),
        name="self_backward",
    )(
        tokens, weights, row_f, gain_f, qkv, self_mixed, self_total, first_sum, second_grad,
        cross_query_grad,
    )

    query_grad = unpad(token_grad)
    memory_grad = context_grad[None]

    small = self_small + cross_small + ffn_small
    grads = jnp.concatenate(
        [self_wg, jnp.stack([key_wg, value_wg, cross_out_wg]), grad_in, grad_out], axis=0
    )
    swap = [(0, 1), (1, 0)]
    grads = (
        grads[:, :, :half].astype(F32) + lax.ppermute(grads[:, :, half:], "tensor", swap).astype(F32)
    ).astype(BF)
    head_small = small[:8, :half] + lax.ppermute(small[:8, half:], "tensor", swap)
    row_small = lax.psum(small[8:17], ("dp", "tensor"))
    head_small = lax.psum(head_small, "dp")
    shard = lax.psum_scatter(grads, "dp", scatter_dimension=1, tiled=True)
    all_shards = lax.all_gather(shard, "task", axis=0, tiled=False)
    all_head = lax.all_gather(head_small, "task", axis=0, tiled=False)
    all_row = lax.all_gather(row_small, "task", axis=0, tiled=False)
    tasks = all_shards.shape[0]
    share_rows = shard.shape[1]
    sums = pl.pallas_call(
        gram_kernel,
        grid=(block_count,),
        out_shape=jax.ShapeDtypeStruct((tasks * tasks, half), F32),
        in_specs=[pl.BlockSpec((tasks, 1, share_rows, half), lambda k: (0, k, 0, 0))],
        out_specs=const((tasks * tasks, half), 0, 0),
        compiler_params=params_for(),
        name="gram",
    )(all_shards)
    upper = jnp.sum(sums, axis=1).reshape(tasks, tasks)
    gram_weights = upper + upper.T - jnp.diag(jnp.diag(upper))
    gram_weights = lax.psum(gram_weights, ("dp", "tensor"))
    gram_heads = jnp.einsum("axy,bxy->ab", all_head, all_head, precision=highest)
    gram_heads = lax.psum(gram_heads, "tensor")
    gram = gram_weights + gram_heads + jnp.einsum(
        "axy,bxy->ab", all_row, all_row, precision=highest
    )
    task_weights = combine_weights(gram, task_order)
    tile = 64 if share_rows % 64 == 0 else share_rows
    param_update = pl.pallas_call(
        update_kernel,
        grid=(share_rows // tile,),
        out_shape=jax.ShapeDtypeStruct((share_rows, block_count, half), F32),
        in_specs=[
            pl.BlockSpec(memory_space=pltpu.SMEM),
            pl.BlockSpec((tasks, block_count, tile, half), lambda r: (0, 0, r, 0)),
        ],
        out_specs=pl.BlockSpec((tile, block_count, half), lambda r: (r, 0, 0)),
        compiler_params=params_for(),
        name="update",
    )(task_weights, all_shards)
    head_bias_update = jnp.einsum("a,axy->xy", task_weights, all_head, precision=highest)
    row_update = jnp.einsum("a,axy->xy", task_weights, all_row, precision=highest)
    return (
        block_out, query_grad, memory_grad, param_update, head_bias_update,
        row_update[:6].reshape(3, 2, width), row_update[6:9], gram,
    )


def solution(mesh):
    return jax.shard_map(
        body,
        mesh=mesh,
        in_specs=(
            P("task", "dp", None),
            P("task", "dp", None),
            P("task", "dp", None),
            P("task", "dp", None),
            P("task", "dp"),
            P(),
            P(None, None, "tensor"),
            P(None, "tensor"),
            P(),
            P(),
        ),
        out_specs=(
            P("task", "dp", None),
            P("task", ("dp", "tensor"), None),
            P("task", ("dp", "tensor"), None),
            P("dp", None, "tensor"),
            P(None, "tensor"),
            P(),
            P(),
            P(),
        ),
        check_vma=False,
    )
```

```python
import functools

import jax
import jax.numpy as jnp
from jax import lax
from jax.experimental import pallas as pl
from jax.experimental.pallas import tpu as pltpu
from jax.sharding import PartitionSpec as P

HD = 64
GROUP = 4
SLAB = GROUP * HD
BF = jnp.bfloat16
F32 = jnp.float32
MESH_ID = pl.DeviceIdType.MESH
highest = lax.Precision.HIGHEST
VMEM_LIMIT = 62 * 2**20


def combine_weights(gram_matrix, order_list):
    task_count = gram_matrix.shape[0]
    task_index = jnp.arange(task_count, dtype=jnp.int32)
    summed = jnp.zeros((task_count,), F32)
    for own_task in range(task_count):
        coeffs = (task_index == own_task).astype(F32)
        for position in range(task_count):
            chosen = (task_index == order_list[position]).astype(F32)
            column = jnp.sum(gram_matrix * chosen[None, :], axis=1)
            inner_dot = jnp.sum(coeffs * column)
            square = jnp.sum(chosen * column)
            others = (order_list[position] != own_task).astype(F32)
            coeffs = coeffs - others * jnp.minimum(inner_dot, 0.0) / (square + 1e-06) * chosen
        summed = summed + coeffs
    return summed


def mm(a, b):
    return jnp.dot(a, b, preferred_element_type=F32)


def mm_nt(a, b):
    return lax.dot_general(a, b, (((1,), (1,)), ((), ())), preferred_element_type=F32)


def mm_tn(a, b):
    return lax.dot_general(a, b, (((0,), (0,)), ((), ())), preferred_element_type=F32)


def row_of(row_ref, which):
    return row_ref[which // 2, which % 2 : which % 2 + 1].astype(F32)


def gain_of(gain_ref, which):
    return gain_ref[which : which + 1].astype(F32)


def norm_parts(residual):
    row_mean = jnp.mean(residual, axis=-1, keepdims=True)
    centred = residual - row_mean
    variance = jnp.mean(centred * centred, axis=-1, keepdims=True)
    scale = lax.rsqrt(variance + 1e-05)
    return centred * scale, scale


def norm_back(normed, scale, gain_row, grad):
    scaled = grad * gain_row
    first = jnp.mean(scaled, axis=-1, keepdims=True)
    second = jnp.mean(scaled * normed, axis=-1, keepdims=True)
    return scale * (scaled - first - normed * second)


def rows_sum(value):
    return jnp.sum(value, axis=0, keepdims=True)


def gelu_tanh(hidden):
    return (
        0.5
        * hidden
        * (1.0 + jnp.tanh(0.7978845608028654 * (hidden + 0.044715 * hidden * hidden * hidden)))
    )


def gelu_slope(hidden):
    square = hidden * hidden
    tanh = jnp.tanh(0.7978845608028654 * (hidden + 0.044715 * hidden * square))
    inner = 0.7978845608028654 * (1.0 + 3 * 0.044715 * square)
    return 0.5 * (1.0 + tanh) + 0.5 * hidden * (1.0 - tanh * tanh) * inner


def head_mask(head, rows, dtype):
    lane = lax.broadcasted_iota(jnp.int32, (rows, SLAB), 1)
    return (lane // HD == head).astype(F32).astype(dtype)


def stack_heads(slab):
    return jnp.concatenate(
        [slab * head_mask(head, slab.shape[0], slab.dtype) for head in range(GROUP)], axis=0
    )


def unstack_heads(stacked):
    rows = stacked.shape[0] // GROUP
    total = None
    for head in range(GROUP):
        part = stacked[head * rows : (head + 1) * rows] * head_mask(head, rows, stacked.dtype)
        total = part if total is None else total + part
    return total


def scores_of(query_stack, key_slab, valid):
    scores = mm_nt(key_slab, query_stack)
    if valid < key_slab.shape[0]:
        row = lax.broadcasted_iota(jnp.int32, scores.shape, 0)
        scores = jnp.where(row < valid, scores, -1e30)
    return scores


def attend(query_slab, key_slab, value_slab, valid):
    scores = scores_of(stack_heads(query_slab * HD ** (-0.5)), key_slab, valid)
    row_max = jnp.max(scores, axis=0, keepdims=True)
    exps = jnp.exp(scores - row_max)
    total = jnp.sum(exps, axis=0, keepdims=True)
    probs = (exps * (1.0 / total)).astype(BF)
    mixed = unstack_heads(mm_tn(value_slab, probs).T)
    return mixed, row_max + jnp.log(total)


def attend_back(query_slab, key_slab, value_slab, log_total, grad_slab, valid):
    query_stack = stack_heads(query_slab * HD ** (-0.5))
    grad_stack = stack_heads(grad_slab)
    probs = jnp.exp(scores_of(query_stack, key_slab, valid) - log_total)
    grad_value = mm(probs.astype(BF), grad_stack)
    grad_probs = mm_nt(value_slab, grad_stack)
    inner = jnp.sum(probs * grad_probs, axis=0, keepdims=True)
    grad_scores = (probs * (grad_probs - inner)).astype(BF)
    grad_key = mm(grad_scores, query_stack)
    grad_query = unstack_heads(mm_tn(key_slab, grad_scores).T) * HD ** (-0.5)
    return grad_query.astype(BF), grad_key.astype(BF), grad_value.astype(BF)


def pad_rows(source_ref, target_ref, images, valid):
    first = lax.axis_index("tensor") == 0
    padded = target_ref.shape[0] // images
    for image in range(images):
        here, there = (
            source_ref[(core * images + image) * valid : (core * images + image + 1) * valid]
            for core in range(2)
        )
        rows = jnp.where(first, here.astype(F32), there.astype(F32))
        fill = jnp.zeros((padded - valid, rows.shape[1]), F32)
        target_ref[image * padded : (image + 1) * padded] = jnp.concatenate(
            [rows, fill], axis=0
        ).astype(target_ref.dtype)


def gather_kernel(images, valid, own_ref, bias_ref, queries_ref, cotangent_ref, full_ref,
                  full_bias_ref, tokens_ref, own_cotangent_ref, turned, bias_own, remote_send,
                  remote_recv, local_sem):
    step, steps = pl.program_id(0), pl.num_programs(0)
    other = 1 - lax.axis_index("tensor")
    rows, _, width = own_ref.shape
    near, far = pl.ds(0, width), pl.ds(width, width)

    def copies(chunk):
        at = pl.ds(pl.multiple_of(chunk * rows, rows), rows)
        source = turned.at[:, at]
        return (
            pltpu.make_async_remote_copy(
                source, full_ref.at[:, at, far], remote_send.at[chunk], remote_recv.at[chunk],
                device_id={"tensor": other}, device_id_type=MESH_ID,
            ),
            pltpu.make_async_copy(source, full_ref.at[:, at, near], local_sem.at[chunk]),
        )

    def bias_copies():
        return (
            pltpu.make_async_remote_copy(
                bias_own, full_bias_ref.at[:, far], remote_send.at[steps], remote_recv.at[steps],
                device_id={"tensor": other}, device_id_type=MESH_ID,
            ),
            pltpu.make_async_copy(bias_own, full_bias_ref.at[:, near], local_sem.at[steps]),
        )

    @pl.when(step == 0)
    def _():
        barrier = pltpu.get_barrier_semaphore()
        pl.semaphore_signal(barrier, inc=1, device_id={"tensor": other}, device_id_type=MESH_ID)
        pl.semaphore_wait(barrier, 1)
        bias_own[...] = jnp.zeros_like(bias_own)
        bias_own[0 : bias_ref.shape[0]] = bias_ref[...]
        for copy in bias_copies():
            copy.start()

    turned[:, pl.ds(pl.multiple_of(step * rows, rows), rows)] = jnp.swapaxes(own_ref[...], 0, 1)
    for copy in copies(step):
        copy.start()

    @pl.when(step == steps - 1)
    def _():
        pad_rows(queries_ref, tokens_ref, images, valid)
        pad_rows(cotangent_ref, own_cotangent_ref, images, valid)
        for copy in bias_copies():
            copy.wait()

        def finish(chunk, carry):
            for copy in copies(chunk):
                copy.wait()
            return carry

        lax.fori_loop(0, steps, finish, 0)


def any_spec():
    return pl.BlockSpec(memory_space=pl.ANY)


def whole_spec():
    return pl.BlockSpec(memory_space=pltpu.VMEM)


def params_for(**keys):
    return pltpu.CompilerParams(vmem_limit_bytes=VMEM_LIMIT, **keys)


def self_kernel(images, valid, tokens_ref, weight_ref, head_ref, row_ref, gain_ref, qkv_ref,
                mixed_ref, total_ref, sum_ref, cross_query_ref):
    tokens = tokens_ref[...]
    rows = tokens.shape[0] // images
    width = tokens.shape[1]
    qkv_ref[0] = (mm(tokens, weight_ref[0]) + head_ref[0:1].astype(F32)).astype(BF)
    qkv_ref[1] = mm(tokens, weight_ref[1]).astype(BF)
    qkv_ref[2] = (mm(tokens, weight_ref[2]) + head_ref[1:2].astype(F32)).astype(BF)
    for image in range(images):
        at = slice(image * rows, (image + 1) * rows)
        for group in range(width // SLAB):
            lanes = slice(group * SLAB, (group + 1) * SLAB)
            mixed, log_total = attend(
                qkv_ref[0, at, lanes], qkv_ref[1, at, lanes], qkv_ref[2, at, lanes], valid
            )
            mixed_ref[at, lanes] = mixed.astype(BF)
            total_ref[image * (width // SLAB) + group] = jnp.broadcast_to(
                log_total, total_ref.shape[1:]
            )
    first_sum = tokens.astype(F32) + mm_nt(mixed_ref[...], weight_ref[3]) + row_of(row_ref, 0)
    sum_ref[...] = first_sum
    first_low = (norm_parts(first_sum)[0] * gain_of(gain_ref, 0) + row_of(row_ref, 1)).astype(BF)
    cross_query_ref[...] = (mm(first_low, weight_ref[4]) + head_ref[2:3].astype(F32)).astype(BF)


def cross_kernel(context_ref, query_ref, key_w_ref, value_w_ref, head_ref, key_ref, value_ref,
                 mixed_ref, total_ref):
    context = context_ref[...]
    key_ref[...] = mm(context, key_w_ref[0]).astype(BF)
    value_ref[...] = (mm(context, value_w_ref[0]) + head_ref[3:4].astype(F32)).astype(BF)
    mixed, log_total = attend(query_ref[...], key_ref[...], value_ref[...], key_ref.shape[0])
    mixed_ref[...] = mixed.astype(BF)
    total_ref[0] = jnp.broadcast_to(log_total, total_ref.shape[1:])


def ffn_kernel(
    images, blocks, sum_ref, mixed_ref, cotangent_ref, matches_ref, counts_ref, cross_w_ref, in_ref,
    out_ref, head_ref, row_ref, gain_ref,
    block_ref, grad_in_ref, grad_out_ref, cross_grad_ref, mixed_grad_ref, residual_ref, small_ref,
    second_sum, second_low_t, low_t, hidden, activated, branch, third_grad, hidden_bias,
):
    step = pl.program_id(0)
    rows = sum_ref.shape[0] // images

    @pl.when(step == 0)
    def _():
        first_out = norm_parts(sum_ref[...])[0] * gain_of(gain_ref, 0) + row_of(row_ref, 1)
        second_sum[...] = first_out + mm_nt(mixed_ref[...], cross_w_ref[0]) + row_of(row_ref, 2)
        branch[...] = jnp.zeros_like(branch)
        small_ref[...] = jnp.zeros_like(small_ref)
        hidden_bias[0:blocks] = head_ref[4 : 4 + blocks].astype(F32)

    def second_out():
        return norm_parts(second_sum[...])[0] * gain_of(gain_ref, 1) + row_of(row_ref, 3)

    @pl.when(step < blocks)
    def _():
        second_low = second_out().astype(BF)
        pre = mm(second_low, in_ref[0]) + hidden_bias[pl.ds(step, 1)]
        hidden[step] = pre
        act = gelu_tanh(pre).astype(BF)
        activated[step] = act
        branch[...] += mm_nt(act, out_ref[0])

    @pl.when(step == blocks - 1)
    def _():
        second = second_out()
        second_low_t[...] = second.astype(BF).T
        third_sum = second + branch[...] + row_of(row_ref, 4)
        normed, scale = norm_parts(third_sum)
        block_ref[...] = (normed * gain_of(gain_ref, 2) + row_of(row_ref, 5)).astype(BF)
        count = matches_ref.shape[2]
        slot = lax.broadcasted_iota(jnp.int32, (rows, count), 0)
        box = lax.broadcasted_iota(jnp.int32, (rows, count), 1)
        grads = []
        for image in range(images):
            own = lax.axis_index("tensor") * images + image
            live = (matches_ref[0, pl.ds(own, 1)] == slot) & (box < counts_ref[0, own])
            mask = jnp.sum(jnp.where(live, 1.0, 0.0), axis=1, keepdims=True)
            cot = cotangent_ref[image * rows : (image + 1) * rows].astype(F32)
            grads.append(cot * mask)
        out_grad = jnp.concatenate(grads, axis=0)
        grad = norm_back(normed, scale, gain_of(gain_ref, 2), out_grad)
        third_grad[...] = grad
        low_t[...] = grad.astype(BF).T
        small_ref[12:13] = rows_sum(grad)
        small_ref[13:14] = rows_sum(out_grad)
        small_ref[16:17] = rows_sum(out_grad * normed)
        branch[...] = jnp.zeros_like(branch)

    @pl.when(step >= blocks)
    def _():
        block = step - blocks
        ffn_low = third_grad[...].astype(BF)
        grad_out_ref[0] = mm(low_t[...], activated[block]).astype(BF)
        grad_hidden = mm(ffn_low, out_ref[0]) * gelu_slope(hidden[block])
        grad_low = grad_hidden.astype(BF)
        small_ref[pl.ds(4 + block, 1)] = rows_sum(grad_low.astype(F32))
        grad_in_ref[0] = mm(second_low_t[...], grad_low).astype(BF)
        branch[...] += mm_nt(grad_low, in_ref[0])

    @pl.when(step == 2 * blocks - 1)
    def _():
        second_in = third_grad[...] + branch[...]
        normed, scale = norm_parts(second_sum[...])
        grad = norm_back(normed, scale, gain_of(gain_ref, 1), second_in)
        residual_ref[...] = grad
        small_ref[10:11] = rows_sum(grad)
        small_ref[11:12] = rows_sum(second_in)
        small_ref[15:16] = rows_sum(second_in * normed)
        cross_low = grad.astype(BF)
        cross_grad_ref[...] = mm(cross_low.T, mixed_ref[...]).astype(BF)
        mixed_grad_ref[...] = mm(cross_low, cross_w_ref[0]).astype(BF)


def cross_back_step(
    image, group, context_ref, query_ref, key_ref, value_ref, total_ref, mixed_grad_ref, small_ref,
    context_t, key_acc, value_acc, unit,
):
    @pl.when(group == 0)
    def _():
        context_t[...] = context_ref[...].T

    unit(0)
    grad_query, grad_key, grad_value = attend_back(
        query_ref[...], key_ref[...], value_ref[...], total_ref[0, 0:1], mixed_grad_ref[...],
        key_ref.shape[0],
    )
    lanes = pl.ds(pl.multiple_of(group * SLAB, SLAB), SLAB)
    small_ref[2:3, lanes] += rows_sum(grad_query.astype(F32))
    small_ref[3:4, lanes] += rows_sum(grad_value.astype(F32))
    unit(1)
    key_wg = mm(context_t[...], grad_key)
    value_wg = mm(context_t[...], grad_value)

    @pl.when(image == 0)
    def _():
        key_acc[:, lanes] = key_wg
        value_acc[:, lanes] = value_wg

    @pl.when(image > 0)
    def _():
        key_acc[:, lanes] += key_wg
        value_acc[:, lanes] += value_wg

    return grad_query, grad_key, grad_value


def cross_back_kernel(
    context_ref, query_ref, key_ref, value_ref, total_ref, mixed_grad_ref, key_w_ref, value_w_ref,
    query_grad_ref, context_grad_ref, key_wg_ref, value_wg_ref, small_ref,
    context_t, acc, key_acc, value_acc,
):
    image, group = pl.program_id(0), pl.program_id(1)
    images, groups = pl.num_programs(0), pl.num_programs(1)

    @pl.when((image == 0) & (group == 0))
    def _():
        small_ref[...] = jnp.zeros_like(small_ref)

    query_grad_ref[...], grad_key, grad_value = cross_back_step(
        image, group, context_ref, query_ref, key_ref, value_ref, total_ref, mixed_grad_ref,
        small_ref, context_t, key_acc, value_acc, lambda part: None,
    )
    context_part = mm_nt(grad_key, key_w_ref[0]) + mm_nt(grad_value, value_w_ref[0])

    @pl.when(group == 0)
    def _():
        acc[...] = context_part

    @pl.when(group > 0)
    def _():
        acc[...] += context_part

    @pl.when(group == groups - 1)
    def _():
        context_grad_ref[...] = acc[...].astype(BF)

    @pl.when((image == images - 1) & (group == groups - 1))
    def _():
        key_wg_ref[...] = key_acc[...].astype(BF)
        value_wg_ref[...] = value_acc[...].astype(BF)


def self_back(
    images, valid, tokens_ref, weight_ref, row_ref, gain_ref, qkv_ref, mixed_ref, total_ref, sum_ref,
    residual_ref, cross_query_grad_ref, small_ref, qkv_grad, emit, unit,
):
    tokens = tokens_ref[...]
    rows = tokens.shape[0] // images
    width = tokens.shape[1]
    normed, scale = norm_parts(sum_ref[...])
    first_low = (normed * gain_of(gain_ref, 0) + row_of(row_ref, 1)).astype(BF)
    cross_query_grad = cross_query_grad_ref[...]
    emit(4, mm(first_low.T, cross_query_grad))
    unit()
    first_in = residual_ref[...] + mm_nt(cross_query_grad, weight_ref[4])
    first_grad = norm_back(normed, scale, gain_of(gain_ref, 0), first_in)
    small_ref[8:9] = rows_sum(first_grad)
    small_ref[9:10] = rows_sum(first_in)
    small_ref[14:15] = rows_sum(first_in * normed)
    unit()
    self_low = first_grad.astype(BF)
    emit(3, mm(self_low.T, mixed_ref[...]))
    unit()
    mixed_grad = mm(self_low, weight_ref[3]).astype(BF)
    for image in range(images):
        at = slice(image * rows, (image + 1) * rows)
        for group in range(width // SLAB):
            lanes = slice(group * SLAB, (group + 1) * SLAB)
            grads = attend_back(
                qkv_ref[0, at, lanes], qkv_ref[1, at, lanes], qkv_ref[2, at, lanes],
                total_ref[image * (width // SLAB) + group, 0:1], mixed_grad[at, lanes], valid,
            )
            for which in range(3):
                qkv_grad[which, at, lanes] = grads[which]
            unit()
    tokens_t = tokens.T
    total = first_grad
    for which in range(3):
        grad = qkv_grad[which]
        emit(which, mm(tokens_t, grad))
        unit()
        total = total + mm_nt(grad, weight_ref[which])
    small_ref[0:1] = rows_sum(qkv_grad[0].astype(F32))
    small_ref[1:2] = rows_sum(qkv_grad[2].astype(F32))
    return total


def self_back_kernel(
    images, valid, tokens_ref, weight_ref, row_ref, gain_ref, qkv_ref, mixed_ref, total_ref, sum_ref,
    residual_ref, cross_query_grad_ref, query_grad_ref, wg_ref, small_ref, qkv_grad,
):
    small_ref[...] = jnp.zeros_like(small_ref)

    def emit(block, value):
        wg_ref[block] = value.astype(BF)

    query_grad_ref[...] = self_back(
        images, valid, tokens_ref, weight_ref, row_ref, gain_ref, qkv_ref, mixed_ref, total_ref,
        sum_ref, residual_ref, cross_query_grad_ref, small_ref, qkv_grad, emit, lambda: None,
    ).astype(BF)


def task_peers(tasks):
    me = lax.axis_index("task")
    return [lax.rem(me + shift, tasks) for shift in range(1, tasks)]


def task_senders(tasks):
    me = lax.axis_index("task")
    return [lax.rem(me + tasks - shift, tasks) for shift in range(1, tasks)]


def send(source, target, send_sem, recv_sem, **device):
    return pltpu.make_async_remote_copy(
        source, target, send_sem, recv_sem, device_id=device, device_id_type=MESH_ID
    )


def greet(depth, tasks):
    me = lax.axis_index("dp")
    barrier = pltpu.get_barrier_semaphore()
    for peer in task_peers(tasks):
        pl.semaphore_signal(barrier, inc=1, device_id={"task": peer}, device_id_type=MESH_ID)
    for shift in range(1, depth):
        pl.semaphore_signal(
            barrier, inc=1, device_id={"dp": lax.rem(me + shift, depth)}, device_id_type=MESH_ID
        )
    pl.semaphore_signal(
        barrier, inc=1, device_id={"tensor": 1 - lax.axis_index("tensor")}, device_id_type=MESH_ID
    )
    pl.semaphore_wait(barrier, tasks + depth - 1)


LAG = 2
AHEAD = 1
RING = 2


class Chain:
    def __init__(self, depth, tasks, sources, near, far, refs):
        self.depth, self.tasks = depth, tasks
        self.sources, self.near, self.far = sources, near, far
        (self.near_ring, self.far_ring, self.passed, self.parts,
         self.near_sem, self.far_sem, self.far_send, self.far_recv, self.pass_send, self.pass_recv,
         self.part_send, self.part_recv) = refs
        self.chunks = self.passed.shape[1]
        self.rows, self.half = self.passed.shape[2:]
        self.me = lax.axis_index("dp")
        self.task = lax.axis_index("task")
        self.is_end = (self.me == 0) | (self.me == depth - 1)
        self.given = sum(source.shape[0] for source in sources)

    SCRATCH = 12

    @staticmethod
    def scratch(blocks, rows, half, tasks):
        chunks = 2 * blocks
        dma = pltpu.SemaphoreType.DMA
        return [
            pltpu.VMEM((RING, 2, rows, half), BF),
            pltpu.VMEM((RING, 2, rows, half), BF),
            pltpu.VMEM((2, chunks, rows, half), BF),
            pltpu.VMEM((tasks, chunks, rows // tasks, half), BF),
            dma((RING, 2)),
            dma((RING, 2)),
            dma((2, blocks)),
            dma((2, blocks)),
            dma((2, chunks)),
            dma((2, chunks)),
            dma((blocks, tasks - 1)),
            dma((blocks, tasks - 1)),
        ]

    def far_copy(self, source, way, block):
        rows = pl.ds(way * 2 * self.rows, 2 * self.rows)
        return send(
            source.at[rows], self.far.at[way, block], self.far_send.at[way, block],
            self.far_recv.at[way, block], tensor=1 - lax.axis_index("tensor"),
        )

    def far_arrival(self, way, block):
        landed = self.far.at[way, block]
        return send(
            landed, landed, self.far_send.at[way, block], self.far_recv.at[way, block],
            tensor=1 - lax.axis_index("tensor"),
        )

    def exchange(self):
        base = 0
        for source in self.sources:
            for block in range(source.shape[0]):
                for way in range(2):
                    columns = pl.ds(self.half, self.half)
                    self.far_copy(source.at[block, :, columns], way, base + block).start()
            base += source.shape[0]

    def pass_copy(self, way, chunk):
        piece = self.passed.at[way, chunk]
        target = self.me - 1 if way == 0 else self.me + 1
        return send(
            piece, piece, self.pass_send.at[way, chunk], self.pass_recv.at[way, chunk], dp=target
        )

    def part_rows(self, peer):
        size = self.rows // self.tasks
        return pl.ds(pl.multiple_of(peer * size, size), size)

    def part_copy(self, way, block, shift, peer):
        chunks = pl.ds(2 * block, 2)
        return send(
            self.passed.at[way, chunks, self.part_rows(peer)], self.parts.at[self.task, chunks],
            self.part_send.at[block, shift], self.part_recv.at[block, shift], task=peer,
        )

    def hops(self, way):
        return self.depth - 1 - self.me if way == 0 else self.me

    def units(self):
        return self.chunks + LAG * (self.depth - 1)

    def near_fetch(self, source, slot, way):
        return pltpu.make_async_copy(
            source, self.near_ring.at[slot, way], self.near_sem.at[slot, way]
        )

    def far_fetch(self, source, slot, way):
        return pltpu.make_async_copy(
            source, self.far_ring.at[slot, way], self.far_sem.at[slot, way]
        )

    def fetch(self, index):
        slot = lax.rem(index, RING)
        for way in range(2):
            chunk = index - LAG * self.hops(way)

            @pl.when((chunk >= 0) & (chunk < self.chunks))
            def _(way=way, chunk=chunk):
                block = chunk // 2
                place = chunk - 2 * block

                @pl.when(place == 0)
                def _():
                    self.far_arrival(way, block).wait_recv()

                start = pl.multiple_of(place * self.rows, self.rows)
                rows = pl.ds(way * 2 * self.rows + start, self.rows)
                base = 0
                for source in self.sources:
                    count = source.shape[0]

                    @pl.when((block >= base) & (block < base + count))
                    def _(source=source, base=base):
                        columns = pl.ds(0, self.half)
                        self.near_fetch(source.at[block - base, rows, columns], slot, way).start()

                    base += count

                @pl.when(block >= base)
                def _():
                    self.near_fetch(self.near.at[block - base, rows], slot, way).start()

                self.far_fetch(
                    self.far.at[way, block, pl.ds(start, self.rows)], slot, way
                ).start()

    def unit(self, index):
        self.fetch(index + AHEAD)
        slot = lax.rem(index, RING)
        for way in range(2):
            chunk = index - LAG * self.hops(way)

            @pl.when((chunk >= 0) & (chunk < self.chunks))
            def _(way=way, chunk=chunk):
                self.chunk_step(way, chunk, slot)

    def chunk_step(self, way, chunk, slot):
        first, last = self.hops(way) == 0, self.hops(way) == self.depth - 1
        piece = self.near_ring.at[slot, way]
        self.near_fetch(piece, slot, way).wait()
        self.far_fetch(piece, slot, way).wait()
        own = self.near_ring[slot, way].astype(F32) + self.far_ring[slot, way].astype(F32)

        @pl.when(first)
        def _():
            self.passed[way, chunk] = own.astype(BF)

        @pl.when(jnp.logical_not(first))
        def _():
            self.pass_copy(way, chunk).wait_recv()
            self.passed[way, chunk] = (own + self.passed[way, chunk].astype(F32)).astype(BF)

        @pl.when(jnp.logical_not(last))
        def _():
            self.pass_copy(way, chunk).start()

        block = chunk // 2

        @pl.when(last & (chunk == 2 * block + 1))
        def _():
            for shift, peer in enumerate(task_peers(self.tasks)):
                self.part_copy(way, block, shift, peer).start()
            own_rows = self.part_rows(self.task)
            self.parts[self.task, chunk - 1] = self.passed[way, chunk - 1, own_rows]
            self.parts[self.task, chunk] = self.passed[way, chunk, own_rows]

    def wait_parts(self, block):
        for shift, peer in enumerate(task_senders(self.tasks)):
            landed = self.parts.at[peer, pl.ds(2 * block, 2)]
            send(
                landed, landed, self.part_send.at[block, shift], self.part_recv.at[block, shift],
                task=peer,
            ).wait_recv()

    def finish(self):
        def blocks(block, carry):
            for way in range(2):

                @pl.when(self.hops(way) != self.depth - 1)
                def _(way=way):
                    for part in range(2):
                        self.pass_copy(way, 2 * block + part).wait_send()

                @pl.when(self.hops(way) == self.depth - 1)
                def _(way=way):
                    for shift, peer in enumerate(task_peers(self.tasks)):
                        self.part_copy(way, block, shift, peer).wait_send()

            return carry

        lax.fori_loop(0, self.chunks // 2, blocks, 0)


def pairs_of(tasks):
    return [(a, b) for a in range(tasks) for b in range(a, tasks)]


def weights_of(gram, order_ref, tasks):
    totals = [0.0] * tasks
    for own in range(tasks):
        coeffs = [jnp.full_like(gram[0, 0], 1.0 if t == own else 0.0) for t in range(tasks)]
        for position in range(tasks):
            chosen = [
                jnp.where(order_ref[position] == t, 1.0, 0.0).astype(F32) for t in range(tasks)
            ]
            column = [sum(gram[t, j] * chosen[j] for j in range(tasks)) for t in range(tasks)]
            inner = sum(coeffs[t] * column[t] for t in range(tasks))
            square = sum(chosen[t] * column[t] for t in range(tasks))
            others = 1.0 - chosen[own]
            share = others * jnp.minimum(inner, 0.0) / (square + 1e-06)
            coeffs = [coeffs[t] - share * chosen[t] for t in range(tasks)]
        totals = [total + coeff for total, coeff in zip(totals, coeffs)]
    return totals


GROUPS = 4
UNITS = 2
TILE = 240


class ContextGrad:
    def __init__(self, key_grad, value_grad, result, refs):
        self.grads, self.result = (key_grad, value_grad), result
        (self.weights, self.staged, self.ring, self.done, self.weight_sem, self.staged_sem,
         self.ring_sem, self.done_sem) = refs
        self.tile, width = self.done.shape[1:]
        self.lanes = [pl.ds(0, width), pl.ds(width, width)]
        self.tiles = result.shape[0] // self.tile

    SCRATCH = 8

    @staticmethod
    def scratch(keys, width):
        dma = pltpu.SemaphoreType.DMA
        return [
            pltpu.VMEM((width, 2 * width), BF),
            pltpu.VMEM((2, 2, keys, SLAB), BF),
            pltpu.VMEM((2, TILE, 2 * width), BF),
            pltpu.VMEM((2, TILE, width), BF),
            dma((2,)),
            dma((2, 2)),
            dma((2, 2)),
            dma((2,)),
        ]

    def weight_copies(self, sources):
        return [
            pltpu.make_async_copy(source, self.weights.at[:, lanes], self.weight_sem.at[which])
            for which, (source, lanes) in enumerate(zip(sources, self.lanes))
        ]

    def staged_copies(self, step, image, group):
        slot = lax.rem(step, 2)
        keys = self.staged.shape[2]
        rows = pl.ds(pl.multiple_of(image * keys, keys), keys)
        lanes = pl.ds(pl.multiple_of(group * SLAB, SLAB), SLAB)
        return [
            pltpu.make_async_copy(
                self.staged.at[slot, which], self.grads[which].at[rows, lanes],
                self.staged_sem.at[slot, which],
            )
            for which in range(2)
        ]

    def put(self, step, image, group, values):
        @pl.when(step >= 2)
        def _():
            for copy in self.staged_copies(step, image, group):
                copy.wait()

        for which, value in enumerate(values):
            self.staged[lax.rem(step, 2), which] = value
        for copy in self.staged_copies(step, image, group):
            copy.start()

    def settle(self):
        for step in range(2):
            for copy in self.staged_copies(step, 0, 0):
                copy.wait()

    def fetches(self, index):
        slot = lax.rem(index, 2)
        rows = pl.ds(pl.multiple_of(index * self.tile, self.tile), self.tile)
        return [
            pltpu.make_async_copy(
                self.grads[which].at[rows], self.ring.at[slot, :, self.lanes[which]],
                self.ring_sem.at[slot, which],
            )
            for which in range(2)
        ]

    def store(self, index):
        slot = lax.rem(index, 2)
        rows = pl.ds(pl.multiple_of(index * self.tile, self.tile), self.tile)
        return pltpu.make_async_copy(
            self.done.at[slot], self.result.at[rows], self.done_sem.at[slot]
        )

    def compute(self, index):
        @pl.when(index < self.tiles)
        def _():
            for copy in self.fetches(index):
                copy.wait()

            @pl.when(index + 1 < self.tiles)
            def _():
                for copy in self.fetches(index + 1):
                    copy.start()

            @pl.when(index >= 2)
            def _():
                self.store(index - 2).wait()

            slot = lax.rem(index, 2)
            self.done[slot] = mm_nt(self.ring[slot], self.weights[...]).astype(BF)
            self.store(index).start()

    def finish(self):
        for index in range(self.tiles - 2, self.tiles):
            self.store(jnp.int32(index)).wait()


def back_kernel(
    depth, tasks, images, groups, valid, block_order, order_ref, context_ref, query_ref, key_ref,
    value_ref, total_ref, mixed_grad_ref, tokens_ref, weight_ref, row_ref,
    gain_ref, qkv_ref, mixed_ref, self_total_ref, sum_ref, residual_ref, small_in_ref, all_w_ref,
    block_ref, *refs
):
    sources, refs = refs[:3], refs[3:]
    (
        context_grad_ref, query_grad_ref, update_ref, small_out_ref, gram_ref, block_far, near, far,
        key_grad, value_grad,
    ), refs = refs[:10], refs[10:]
    (
        context_t, key_acc, value_acc, cross_query_grad, qkv_grad, stage, stage_sem, block_sem,
    ), refs = refs[:8], refs[8:]
    context_back = ContextGrad(
        key_grad, value_grad, context_grad_ref, refs[: ContextGrad.SCRATCH]
    )
    refs = refs[ContextGrad.SCRATCH :]
    chain = Chain(depth, tasks, sources, near, far, refs[: Chain.SCRATCH])
    refs = refs[Chain.SCRATCH :]
    gram_acc = refs[7]
    step = pl.program_id(0)
    cross_steps = images * groups
    half = chain.half
    is_end = chain.is_end
    pairs = pairs_of(tasks)

    def add_products(shares):
        for index, (a, b) in enumerate(pairs):
            product = shares[a] * shares[b]
            total = product[0:8]
            for row in range(8, product.shape[0], 8):
                total = total + product[row : row + 8]
            gram_acc[index * 8 : index * 8 + 8] += total

    def unit(index):
        chain.unit(index)
        since = index - LAG * (depth - 1) - 3
        block = since // 2

        @pl.when(is_end & (since >= 0) & (since == 2 * block))
        def _():
            chain.wait_parts(block)
            for part in range(2):
                add_products(
                    [chain.parts[t, 2 * block + part].astype(F32) for t in range(tasks)]
                )

    block_copy = send(
        block_ref, block_far, block_sem.at[0], block_sem.at[1], tensor=1 - lax.axis_index("tensor")
    )
    weight_copies = context_back.weight_copies([all_w_ref.at[5], all_w_ref.at[6]])

    @pl.when(step == 0)
    def _():
        greet(depth, tasks)
        chain.exchange()
        block_copy.start()
        for copy in weight_copies:
            copy.start()
        gram_acc[...] = jnp.zeros_like(gram_acc)
        refs[0][...] = small_in_ref[...]
        for index in range(AHEAD):
            chain.fetch(index)

    given = chain.given
    slots = stage.shape[0]

    def stage_copies(position):
        slot = position % slots
        return [
            chain.far_copy(stage.at[slot, :, pl.ds(half, half)], way, given + position)
            for way in range(2)
        ]

    def emit(position, value):
        slot = position % slots
        if position >= slots:
            for copy in stage_copies(position - slots):
                copy.wait_send()
        stage[slot] = value.astype(BF)
        for copy in stage_copies(position):
            copy.start()
        copy = pltpu.make_async_copy(
            stage.at[slot, :, pl.ds(0, half)], near.at[position], stage_sem
        )
        copy.start()
        copy.wait()

    @pl.when(step < cross_steps)
    def _():
        image = step // groups
        group = step - image * groups

        def cross_unit(part):
            if part == 0:
                unit(step * UNITS)
            else:

                @pl.when(step < cross_steps - 1)
                def _():
                    unit(step * UNITS + part)

        grad_query, *grads = cross_back_step(
            image, group, context_ref, query_ref, key_ref, value_ref, total_ref, mixed_grad_ref,
            refs[0], context_t, key_acc, value_acc, cross_unit,
        )
        context_back.put(step, image, group, grads)
        rows = grad_query.shape[0]
        cross_query_grad[
            pl.ds(pl.multiple_of(image * rows, rows), rows),
            pl.ds(pl.multiple_of(group * SLAB, SLAB), SLAB),
        ] = grad_query

        @pl.when(step == cross_steps - 1)
        def _():
            emit(0, key_acc[...])
            emit(1, value_acc[...])

    @pl.when(step == cross_steps)
    def _():
        calls, done = [0], [cross_steps * UNITS - 1]

        def self_unit():
            if calls[0] % 2 == 0:
                unit(jnp.int32(done[0]))
                done[0] += 1
            calls[0] += 1

        context_back.settle()
        for copy in context_back.fetches(jnp.int32(0)):
            copy.start()
        for copy in weight_copies:
            copy.wait()
        positions = {4: 2, 3: 3, 0: 4, 1: 5, 2: 6}
        query_grad_ref[...] = self_back(
            images, valid, tokens_ref, weight_ref, row_ref, gain_ref, qkv_ref, mixed_ref,
            self_total_ref, sum_ref, residual_ref, cross_query_grad, refs[0], qkv_grad,
            lambda block, value: emit(positions[block], value), self_unit,
        ).astype(BF)
        rest(
            chain, unit, context_back, done[0], order_ref, update_ref, small_out_ref, gram_ref, refs
        )
        for position in range(len(block_order) - given - slots, len(block_order) - given):
            for copy in stage_copies(position):
                copy.wait_send()
        for block in range(given):
            for way in range(2):
                chain.far_arrival(way, block).wait_send()
        block_copy.wait()
        context_back.finish()


def rest(
    chain, unit, context_back, done, order_ref, update_ref, small_out_ref, gram_ref, refs
):
    (
        small, small_own, small_other, small_far, small_pass, small_all, small_both, gram_acc,
        gram_task, gram_core, gram_end, hop, out,
        small_far_sem, small_pass_sem, small_task_sem, small_dp_sem, small_core_sem,
        gram_task_sem, gram_core_sem, gram_dp_sem, hop_sem, out_sem, update_sem,
    ) = refs
    depth, tasks, half = chain.depth, chain.tasks, chain.half
    me, task, core = (lax.axis_index(axis) for axis in ("dp", "task", "tensor"))
    is_end = chain.is_end
    top = me == 0
    pairs = pairs_of(tasks)
    own_lanes = pl.ds(pl.multiple_of(core * half, half), half)
    other_lanes = pl.ds(pl.multiple_of((1 - core) * half, half), half)
    small_own[0:8] = small[0:8, 0:half]
    small_own[8:] = small[8:, own_lanes]
    small_other[0:8] = small[0:8, half:]
    small_other[8:] = small[8:, other_lanes]
    small_copy = send(
        small_other, small_far, small_far_sem.at[0], small_far_sem.at[1], tensor=1 - core
    )
    small_copy.start()

    def small_hop():
        return send(
            small_pass, small_pass, small_pass_sem.at[0], small_pass_sem.at[1], dp=me - 1
        )

    def small_task_copy(shift, peer):
        return send(
            small_pass, small_all.at[task], small_task_sem.at[0, shift],
            small_task_sem.at[1, shift], task=peer,
        )

    def step(index, carry):
        unit(index)
        context_back.compute(index - done)

        @pl.when(index == done + 1 + LAG * chain.hops(0))
        def _():
            small_copy.wait_recv()
            total = small_own[...] + small_far[...]

            @pl.when(me == depth - 1)
            def _():
                small_pass[...] = total

            @pl.when(me < depth - 1)
            def _():
                small_hop().wait_recv()
                small_pass[...] += total

            @pl.when(me > 0)
            def _():
                small_hop().start()

            @pl.when(top)
            def _():
                for shift, peer in enumerate(task_peers(tasks)):
                    small_task_copy(shift, peer).start()
                small_all[task] = small_pass[...]

        return carry

    lax.fori_loop(done, max(chain.units() + 2, done + context_back.tiles), step, 0)

    @pl.when(top)
    def _():
        for shift, peer in enumerate(task_senders(tasks)):
            landed = small_all.at[peer]
            send(
                landed, landed, small_task_sem.at[0, shift], small_task_sem.at[1, shift], task=peer
            ).wait_recv()

    lanes = gram_task.shape[2]

    def gram_task_copy(shift, peer):
        return send(
            gram_task.at[task], gram_task.at[task], gram_task_sem.at[0, shift],
            gram_task_sem.at[1, shift], task=peer,
        )

    def gram_core_copy(which):
        return send(
            gram_core.at[which], gram_core.at[which], gram_core_sem.at[0], gram_core_sem.at[1],
            tensor=1 - core,
        )

    def gram_dp_copy(end, shift):
        return send(
            gram_end.at[end], gram_end.at[end], gram_dp_sem.at[0, end, shift],
            gram_dp_sem.at[1, end, shift], dp=lax.rem((depth - 1) * end + shift + 1, depth),
        )

    def one_number(values):
        return jnp.sum(jnp.sum(values, axis=0, keepdims=True), axis=1, keepdims=True)

    @pl.when(is_end)
    def _():
        gram_task[task] = jnp.zeros(gram_task.shape[1:], F32)
        for index in range(len(pairs)):
            gram_task[task, index : index + 1] = jnp.broadcast_to(
                one_number(gram_acc[index * 8 : index * 8 + 8]), (1, lanes)
            )
        for shift, peer in enumerate(task_peers(tasks)):
            gram_task_copy(shift, peer).start()

    @pl.when(top)
    def _():
        small_all_values = [small_all[t] for t in range(tasks)]
        for index, (a, b) in enumerate(pairs):
            gram_end[0, index : index + 1] = jnp.broadcast_to(
                one_number(small_all_values[a] * small_all_values[b]), (1, lanes)
            )

    @pl.when(is_end)
    def _():
        for shift, peer in enumerate(task_senders(tasks)):
            landed = gram_task.at[peer]
            send(
                landed, landed, gram_task_sem.at[0, shift], gram_task_sem.at[1, shift], task=peer
            ).wait_recv()
        total = gram_task[0]
        for t in range(1, tasks):
            total = total + gram_task[t]

        @pl.when(top)
        def _():
            gram_core[core] = total + gram_end[0]

        @pl.when(jnp.logical_not(top))
        def _():
            gram_core[core] = total

        gram_core_copy(core).start()
        gram_core_copy(1 - core).wait_recv()

    for end in range(2):

        @pl.when(me == (depth - 1) * end)
        def _(end=end):
            gram_end[end] = gram_core[0] + gram_core[1]
            for shift in range(depth - 1):
                gram_dp_copy(end, shift).start()

    for end in range(2):
        for shift in range(depth - 1):

            @pl.when(me == ((depth - 1) * end + shift + 1) % depth)
            def _(end=end, shift=shift):
                gram_dp_copy(end, shift).wait_recv()

    gram = {}
    for index, (a, b) in enumerate(pairs):
        row = slice(index, index + 1)
        gram[a, b] = gram[b, a] = gram_end[0, row] + gram_end[1, row]
    for a in range(tasks):
        for b in range(tasks):
            gram_ref[a * tasks + b : a * tasks + b + 1] = gram[a, b]
    weights = [
        jnp.concatenate([weight] * (half // lanes), axis=1)
        for weight in weights_of(gram, order_ref, tasks)
    ]

    blocks = out.shape[0]
    group = blocks // GROUPS
    share = chain.rows // tasks
    mine = pl.ds(pl.multiple_of(task * share, share), share)
    own_part = jnp.minimum(me, 1)

    def hop_copy(index):
        return send(
            hop.at[pl.ds(index * group, group)], out.at[pl.ds(index * group, group), mine],
            hop_sem.at[0, index], hop_sem.at[1, index],
            dp=jnp.where(top, 1, depth - 2),
        )

    def out_copy(index, shift, peer):
        piece = out.at[pl.ds(index * group, group), mine]
        return send(piece, piece, out_sem.at[0, index, shift], out_sem.at[1, index, shift], task=peer)

    def update_copy(index):
        at = pl.ds(index * group, group)
        return pltpu.make_async_copy(out.at[at], update_ref.at[at], update_sem.at[index])

    def weighted(chunk):
        total = weights[0] * chain.parts[0, chunk].astype(F32)
        for t in range(1, tasks):
            total = total + weights[t] * chain.parts[t, chunk].astype(F32)
        return total.astype(BF)

    def small_dp_copy(shift):
        return send(
            small_both.at[0], small_both.at[0], small_dp_sem.at[0, shift],
            small_dp_sem.at[1, shift], dp=shift + 1,
        )

    def small_core_copy():
        return send(
            small_both.at[0], small_both.at[1], small_core_sem.at[0], small_core_sem.at[1],
            tensor=1 - core,
        )

    @pl.when(top)
    def _():
        total = weights[0] * small_all[0]
        for t in range(1, tasks):
            total = total + weights[t] * small_all[t]
        small_both[0] = total
        for shift in range(depth - 1):
            small_dp_copy(shift).start()

    @pl.when(is_end)
    def _():
        for index in range(GROUPS):

            def other(block, carry):
                hop[block] = weighted(2 * block + 1 - own_part)
                return carry

            lax.fori_loop(index * group, (index + 1) * group, other, 0)
            hop_copy(index).start()

            def own(block, carry):
                out[block, mine] = weighted(2 * block + own_part)
                return carry

            lax.fori_loop(index * group, (index + 1) * group, own, 0)
            for shift, peer in enumerate(task_peers(tasks)):
                out_copy(index, shift, peer).start()

    @pl.when(jnp.logical_not(is_end))
    def _():
        for index in range(GROUPS):
            hop_copy(index).wait_recv()
            for shift, peer in enumerate(task_peers(tasks)):
                out_copy(index, shift, peer).start()

    for shift in range(depth - 1):

        @pl.when(me == shift + 1)
        def _(shift=shift):
            small_dp_copy(shift).wait_recv()

    small_core_copy().start()

    for index in range(GROUPS):
        for shift, peer in enumerate(task_senders(tasks)):
            piece = out.at[
                pl.ds(index * group, group), pl.ds(pl.multiple_of(peer * share, share), share)
            ]
            send(
                piece, piece, out_sem.at[0, index, shift], out_sem.at[1, index, shift], task=peer
            ).wait_recv()
        update_copy(index).start()

    small_core_copy().wait_recv()
    small_out_ref[0:8, 0:half] = small_both[0, 0:8]
    small_out_ref[0:8, half:] = small_both[1, 0:8]
    small_out_ref[8:, own_lanes] = small_both[0, 8:]
    small_out_ref[8:, other_lanes] = small_both[1, 8:]

    small_copy.wait_send()
    small_core_copy().wait_send()
    chain.finish()

    @pl.when(me > 0)
    def _():
        small_hop().wait_send()

    @pl.when(top)
    def _():
        for shift, peer in enumerate(task_peers(tasks)):
            small_task_copy(shift, peer).wait_send()
        for shift in range(depth - 1):
            small_dp_copy(shift).wait_send()

    for end in range(2):

        @pl.when(me == (depth - 1) * end)
        def _(end=end):
            for shift in range(depth - 1):
                gram_dp_copy(end, shift).wait_send()

    @pl.when(is_end)
    def _():
        gram_core_copy(core).wait_send()
        for shift, peer in enumerate(task_peers(tasks)):
            gram_task_copy(shift, peer).wait_send()
        for index in range(GROUPS):
            hop_copy(index).wait_send()

    for index in range(GROUPS):
        update_copy(index).wait()
        for shift, peer in enumerate(task_peers(tasks)):
            out_copy(index, shift, peer).wait_send()


def spread_kernel(
    images, valid, tasks, block_order, parts_ref, context_grad_ref, query_grad_ref, block_ref,
    block_far_ref, small_ref, gram_in_ref,
    update_ref, context_out_ref, query_out_ref, block_out_ref, head_ref, row_ref, gain_ref, gram_ref,
):
    for index, block in enumerate(block_order):
        update_ref[:, block, :] = parts_ref[index].astype(F32)
    context_out_ref[...] = context_grad_ref[...]

    @pl.when(pl.program_id(0) == 0)
    def _():
        padded = query_grad_ref.shape[0] // images
        first = lax.axis_index("tensor") == 0

        def rows(ref, image):
            return ref[image * padded : (image + 1) * padded].astype(F32)[:valid]

        for image in range(images):
            at = slice(image * valid, (image + 1) * valid)
            after = slice((images + image) * valid, (images + image + 1) * valid)
            query_out_ref[at] = rows(query_grad_ref, image).astype(BF)
            near, far = rows(block_ref, image), rows(block_far_ref, image)
            block_out_ref[at] = jnp.where(first, near, far).astype(BF)
            block_out_ref[after] = jnp.where(first, far, near).astype(BF)
        head_ref[...] = small_ref[0:8, 0 : head_ref.shape[1]]
        for which in range(6):
            row_ref[which // 2, which % 2 : which % 2 + 1] = small_ref[8 + which : 9 + which]
        gain_ref[...] = small_ref[14:17]
        for a in range(tasks):
            for b in range(tasks):
                at = a * tasks + b
                gram_ref[a : a + 1, b : b + 1] = gram_in_ref[at : at + 1, 0:1]


def gram_kernel(parts_ref, gram_ref):
    tasks = parts_ref.shape[0]

    @pl.when(pl.program_id(0) == 0)
    def _():
        gram_ref[...] = jnp.zeros_like(gram_ref)

    shares = [parts_ref[task, 0].astype(F32) for task in range(tasks)]
    for a in range(tasks):
        for b in range(a, tasks):
            gram_ref[a * tasks + b : a * tasks + b + 1] += rows_sum(shares[a] * shares[b])


def update_kernel(weights_ref, parts_ref, update_ref):
    tasks, blocks = parts_ref.shape[:2]
    for block in range(blocks):
        total = weights_ref[0] * parts_ref[0, block].astype(F32)
        for task in range(1, tasks):
            total += weights_ref[task] * parts_ref[task, block].astype(F32)
        update_ref[:, block, :] = total


def body(
    queries, memory, cotangent, matches, counts, task_order, params, head_bias, row_bias, norm_gain
):
    all_images = matches.shape[1]
    valid = matches.shape[2]
    width = queries.shape[2]
    half = params.shape[2]
    block_count = params.shape[1]
    blocks = (block_count - 8) // 2
    cores = lax.axis_size("tensor")
    images = all_images // cores
    keys = memory.shape[1] // all_images
    padded = -(-valid // 16) * 16
    rows = images * padded
    groups = width // SLAB
    stack = GROUP * padded
    core = lax.axis_index("tensor")

    chunk = 96
    weights, head_rows, tokens, own_cotangent = pl.pallas_call(
        functools.partial(gather_kernel, images, valid),
        grid=(width // chunk,),
        out_shape=(
            jax.ShapeDtypeStruct((block_count, width, cores * half), BF),
            jax.ShapeDtypeStruct((16, cores * half), BF),
            jax.ShapeDtypeStruct((rows, width), BF),
            jax.ShapeDtypeStruct((rows, width), BF),
        ),
        in_specs=[
            pl.BlockSpec((chunk, block_count, half), lambda i: (i, 0, 0)),
            pl.BlockSpec((8, half), lambda i: (0, 0)),
            pl.BlockSpec((None, *queries.shape[1:]), lambda i: (0, 0, 0)),
            pl.BlockSpec((None, *queries.shape[1:]), lambda i: (0, 0, 0)),
        ],
        out_specs=(
            any_spec(), any_spec(),
            pl.BlockSpec((rows, width), lambda i: (0, 0)),
            pl.BlockSpec((rows, width), lambda i: (0, 0)),
        ),
        scratch_shapes=[
            pltpu.VMEM((block_count, width, half), BF),
            pltpu.VMEM((16, half), BF),
            pltpu.SemaphoreType.DMA((width // chunk + 1,)),
            pltpu.SemaphoreType.DMA((width // chunk + 1,)),
            pltpu.SemaphoreType.DMA((width // chunk + 1,)),
        ],
        compiler_params=params_for(collective_id=0, has_side_effects=True),
        name="gather_weights",
    )(params, head_bias, queries, cotangent)

    def const(shape, *index):
        return pl.BlockSpec(shape, lambda *_: index)

    total_shape = jax.ShapeDtypeStruct((images * groups, 8, stack), F32)
    low_rows = jax.ShapeDtypeStruct((rows, width), BF)
    full_rows = jax.ShapeDtypeStruct((rows, width), F32)
    small_shape = jax.ShapeDtypeStruct((24, width), F32)
    one_block = jax.ShapeDtypeStruct((width, width), BF)
    small_spec = const((24, width), 0, 0)
    row_spec = const(row_bias.shape, 0, 0, 0)
    gain_spec = const(norm_gain.shape, 0, 0)
    head_spec = const((16, width), 0, 0)
    rows_spec = const((rows, width), 0, 0)

    qkv, self_mixed, self_total, first_sum, cross_query = pl.pallas_call(
        functools.partial(self_kernel, images, valid),
        grid=(1,),
        out_shape=(
            jax.ShapeDtypeStruct((3, rows, width), BF), low_rows, total_shape, full_rows, low_rows,
        ),
        in_specs=[rows_spec, const((5, width, width), 0, 0, 0), head_spec, row_spec, gain_spec],
        out_specs=(
            const((3, rows, width), 0, 0, 0), rows_spec, const(total_shape.shape, 0, 0, 0),
            rows_spec, rows_spec,
        ),
        compiler_params=params_for(),
        name="self_forward",
    )(tokens, weights, head_rows, row_bias, norm_gain)


    def own_image(i, g):
        return 0, lax.axis_index("tensor") * images + i, 0

    context_all = pl.BlockSpec((None, keys, width), own_image)
    slab_q = pl.BlockSpec((padded, SLAB), lambda i, g: (i, g))
    slab_k = pl.BlockSpec((keys, SLAB), lambda i, g: (i, g))
    slab_t = pl.BlockSpec((1, 8, stack), lambda i, g: (i * groups + g, 0, 0))

    def slab_w(block):
        return pl.BlockSpec((1, width, SLAB), lambda i, g: (block, 0, g))

    key_rows = jax.ShapeDtypeStruct((images * keys, width), BF)
    keys_act, values_act, cross_mixed, cross_total = pl.pallas_call(
        cross_kernel,
        grid=(images, groups),
        in_specs=[
            context_all, slab_q, slab_w(5), slab_w(6),
            pl.BlockSpec((16, SLAB), lambda i, g: (0, g)),
        ],
        out_specs=(slab_k, slab_k, slab_q, slab_t),
        out_shape=(key_rows, key_rows, low_rows, total_shape),
        compiler_params=params_for(),
        name="cross_forward",
    )(memory, cross_query, weights, weights, head_rows)

    (
        block_rows, grad_in, grad_out, cross_out_wg, mixed_grad, second_grad, ffn_small,
    ) = pl.pallas_call(
        functools.partial(ffn_kernel, images, blocks),
        grid=(2 * blocks,),
        out_shape=(
            low_rows,
            jax.ShapeDtypeStruct((blocks, width, width), BF),
            jax.ShapeDtypeStruct((blocks, width, width), BF),
            one_block, low_rows, full_rows, small_shape,
        ),
        in_specs=[
            rows_spec, rows_spec, rows_spec,
            const(matches.shape, 0, 0, 0),
            pl.BlockSpec(memory_space=pltpu.SMEM),
            const((1, width, width), 7, 0, 0),
            pl.BlockSpec((1, width, width), lambda s: (8 + s % blocks, 0, 0)),
            pl.BlockSpec((1, width, width), lambda s: (8 + blocks + s % blocks, 0, 0)),
            head_spec, row_spec, gain_spec,
        ],
        out_specs=(
            rows_spec,
            pl.BlockSpec((1, width, width), lambda s: (jnp.maximum(s - blocks, 0), 0, 0)),
            pl.BlockSpec((1, width, width), lambda s: (jnp.maximum(s - blocks, 0), 0, 0)),
            const((width, width), 0, 0), rows_spec, rows_spec, small_spec,
        ),
        scratch_shapes=[
            pltpu.VMEM((rows, width), F32),
            pltpu.VMEM((width, rows), BF),
            pltpu.VMEM((width, rows), BF),
            pltpu.VMEM((blocks, rows, width), F32),
            pltpu.VMEM((blocks, rows, width), BF),
            pltpu.VMEM((rows, width), F32),
            pltpu.VMEM((rows, width), F32),
            pltpu.VMEM((8, width), F32),
        ],
        compiler_params=params_for(),
        name="ffn",
    )(
        first_sum, cross_mixed, own_cotangent, matches, counts, weights, weights, weights,
        head_rows, row_bias, norm_gain,
    )

    depth, tasks = lax.axis_size("dp"), lax.axis_size("task")
    by_chain = depth == 4 and tasks == 4 and cores == 2

    if by_chain:
        block_order = [*range(8, block_count), 7, 5, 6, 4, 3, 0, 1, 2]
        chain_rows = width // depth
        pair_rows = 8 * len(pairs_of(tasks))
        dma = pltpu.SemaphoreType.DMA
        last = images * groups - 1

        def at_step(make):
            def index_map(step):
                now = jnp.minimum(step, last)
                return make(now // groups, now - groups * (now // groups))

            return index_map

        def once(shape):
            return pl.BlockSpec(
                shape, lambda step: (0,) * len(shape), pipeline_mode=pl.Buffered(1)
            )

        step_q = pl.BlockSpec((padded, SLAB), at_step(lambda i, g: (i, g)))
        step_k = pl.BlockSpec((keys, SLAB), at_step(lambda i, g: (i, g)))

        small_half = pltpu.VMEM((24, half), F32)
        (
            context_grad, token_grad, update_parts, small_out, gram_rows, block_far, *_,
        ) = pl.pallas_call(
            functools.partial(
                back_kernel, depth, tasks, images, groups, valid, block_order
            ),
            grid=(images * groups + 1,),
            out_shape=(
                key_rows, low_rows,
                jax.ShapeDtypeStruct((block_count, chain_rows, half), BF),
                small_shape,
                jax.ShapeDtypeStruct((16, 128), F32),
                low_rows,
                jax.ShapeDtypeStruct((7, width, half), BF),
                jax.ShapeDtypeStruct((2, block_count, width // 2, half), BF),
                key_rows, key_rows,
            ),
            in_specs=[
                pl.BlockSpec(memory_space=pltpu.SMEM),
                pl.BlockSpec((None, keys, width), at_step(own_image)),
                step_q, step_k, step_k,
                pl.BlockSpec((1, 8, stack), at_step(lambda i, g: (i * groups + g, 0, 0))),
                step_q,
                once((rows, width)), once((5, width, width)), once(row_bias.shape),
                once(norm_gain.shape),
                once((3, rows, width)), once((rows, width)), once(total_shape.shape),
                once((rows, width)), once((rows, width)), once((24, width)),
                any_spec(), any_spec(), any_spec(), any_spec(), any_spec(),
            ],
            out_specs=(
                any_spec(), once((rows, width)), any_spec(), once((24, width)), once((16, 128)),
                *[any_spec()] * 5,
            ),
            scratch_shapes=[
                pltpu.VMEM((width, keys), BF),
                pltpu.VMEM((width, width), F32),
                pltpu.VMEM((width, width), F32),
                pltpu.VMEM((rows, width), BF),
                pltpu.VMEM((3, rows, width), BF),
                pltpu.VMEM((3, width, width), BF),
                dma(()),
                dma((2,)),
                *ContextGrad.scratch(keys, width),
                *Chain.scratch(block_count, chain_rows, half, tasks),
                pltpu.VMEM((24, width), F32),
                small_half, small_half, small_half, small_half,
                pltpu.VMEM((tasks, 24, half), F32),
                pltpu.VMEM((2, 24, half), F32),
                pltpu.VMEM((pair_rows, half), F32),
                pltpu.VMEM((tasks, 16, 128), F32),
                pltpu.VMEM((2, 16, 128), F32),
                pltpu.VMEM((2, 16, 128), F32),
                pltpu.VMEM((block_count, chain_rows // tasks, half), BF),
                pltpu.VMEM((block_count, chain_rows, half), BF),
                dma((2,)),
                dma((2,)),
                dma((2, tasks - 1)),
                dma((2, depth - 1)),
                dma((2,)),
                dma((2, tasks - 1)),
                dma((2,)),
                dma((2, 2, depth - 1)),
                dma((2, GROUPS)),
                dma((2, GROUPS, tasks - 1)),
                dma((GROUPS,)),
            ],
            compiler_params=params_for(collective_id=1, has_side_effects=True),
            name="backward",
        )(
            task_order, memory, cross_query, keys_act, values_act, cross_total, mixed_grad,
            tokens, weights, row_bias, norm_gain, qkv, self_mixed, self_total, first_sum,
            second_grad, ffn_small, weights, block_rows, grad_in, grad_out, cross_out_wg[None],
        )
        tile = chain_rows // images
        (
            param_update, memory_grad, query_grad, block_out, head_update, row_update, gain_update,
            gram,
        ) = pl.pallas_call(
            functools.partial(spread_kernel, images, valid, tasks, block_order),
            grid=(images,),
            out_shape=(
                jax.ShapeDtypeStruct((chain_rows, block_count, half), F32),
                key_rows,
                jax.ShapeDtypeStruct((images * valid, width), BF),
                jax.ShapeDtypeStruct((all_images * valid, width), BF),
                jax.ShapeDtypeStruct((8, half), F32),
                jax.ShapeDtypeStruct((3, 2, width), F32),
                jax.ShapeDtypeStruct((3, width), F32),
                jax.ShapeDtypeStruct((tasks, tasks), F32),
            ),
            in_specs=[
                pl.BlockSpec((block_count, tile, half), lambda r: (0, r, 0)),
                pl.BlockSpec((keys, width), lambda r: (r, 0)),
                rows_spec, rows_spec, rows_spec, small_spec, const((16, 128), 0, 0),
            ],
            out_specs=(
                pl.BlockSpec((tile, block_count, half), lambda r: (r, 0, 0)),
                pl.BlockSpec((keys, width), lambda r: (r, 0)),
                const((images * valid, width), 0, 0),
                const((all_images * valid, width), 0, 0),
                const((8, half), 0, 0), const((3, 2, width), 0, 0, 0),
                const((3, width), 0, 0), const((tasks, tasks), 0, 0),
            ),
            compiler_params=params_for(),
            name="spread",
        )(update_parts, context_grad, token_grad, block_rows, block_far, small_out, gram_rows)
        return (
            block_out[None], query_grad[None], memory_grad[None], param_update, head_update,
            row_update, gain_update, gram,
        )

    def unpad(array):
        return array.reshape(images, padded, width)[:, :valid].reshape(1, images * valid, width)

    block_out = lax.all_gather(unpad(block_rows), "tensor", axis=1, tiled=True)
    cross_query_grad, context_grad, key_wg, value_wg, cross_small = pl.pallas_call(
        cross_back_kernel,
        grid=(images, groups),
        in_specs=[
            context_all, slab_q, slab_k, slab_k, slab_t, slab_q, slab_w(5), slab_w(6),
        ],
        out_specs=(
            slab_q,
            pl.BlockSpec((keys, width), lambda i, g: (i, 0)),
            const((width, width), 0, 0), const((width, width), 0, 0), small_spec,
        ),
        scratch_shapes=[
            pltpu.VMEM((width, keys), BF),
            pltpu.VMEM((keys, width), F32),
            pltpu.VMEM((width, width), F32),
            pltpu.VMEM((width, width), F32),
        ],
        out_shape=(low_rows, key_rows, one_block, one_block, small_shape),
        compiler_params=params_for(),
        name="cross_backward",
    )(memory, cross_query, keys_act, values_act, cross_total, mixed_grad, weights, weights)

    token_grad, self_wg, self_small = pl.pallas_call(
        functools.partial(self_back_kernel, images, valid),
        grid=(1,),
        out_shape=(
            low_rows, jax.ShapeDtypeStruct((5, width, width), BF), small_shape,
        ),
        in_specs=[
            rows_spec, const((5, width, width), 0, 0, 0), row_spec, gain_spec,
            const((3, rows, width), 0, 0, 0), rows_spec, const(total_shape.shape, 0, 0, 0),
            rows_spec, rows_spec, rows_spec,
        ],
        out_specs=(
            rows_spec, const((5, width, width), 0, 0, 0), small_spec,
        ),
        scratch_shapes=[pltpu.VMEM((3, rows, width), BF)],
        compiler_params=params_for(),
        name="self_backward",
    )(
        tokens, weights, row_bias, norm_gain, qkv, self_mixed, self_total, first_sum, second_grad,
        cross_query_grad,
    )

    query_grad = unpad(token_grad)
    memory_grad = context_grad[None]

    small = self_small + cross_small + ffn_small
    grads = jnp.concatenate(
        [self_wg, jnp.stack([key_wg, value_wg, cross_out_wg]), grad_in, grad_out], axis=0
    )
    swap = [(0, 1), (1, 0)]
    grads = (
        grads[:, :, :half].astype(F32) + lax.ppermute(grads[:, :, half:], "tensor", swap).astype(F32)
    ).astype(BF)
    head_small = small[:8, :half] + lax.ppermute(small[:8, half:], "tensor", swap)
    row_small = lax.psum(small[8:17], ("dp", "tensor"))
    head_small = lax.psum(head_small, "dp")
    shard = lax.psum_scatter(grads, "dp", scatter_dimension=1, tiled=True)
    all_shards = lax.all_gather(shard, "task", axis=0, tiled=False)
    all_head = lax.all_gather(head_small, "task", axis=0, tiled=False)
    all_row = lax.all_gather(row_small, "task", axis=0, tiled=False)
    tasks = all_shards.shape[0]
    share_rows = shard.shape[1]
    sums = pl.pallas_call(
        gram_kernel,
        grid=(block_count,),
        out_shape=jax.ShapeDtypeStruct((tasks * tasks, half), F32),
        in_specs=[pl.BlockSpec((tasks, 1, share_rows, half), lambda k: (0, k, 0, 0))],
        out_specs=const((tasks * tasks, half), 0, 0),
        compiler_params=params_for(),
        name="gram",
    )(all_shards)
    upper = jnp.sum(sums, axis=1).reshape(tasks, tasks)
    gram_weights = upper + upper.T - jnp.diag(jnp.diag(upper))
    gram_weights = lax.psum(gram_weights, ("dp", "tensor"))
    gram_heads = jnp.einsum("axy,bxy->ab", all_head, all_head, precision=highest)
    gram_heads = lax.psum(gram_heads, "tensor")
    gram = gram_weights + gram_heads + jnp.einsum(
        "axy,bxy->ab", all_row, all_row, precision=highest
    )
    task_weights = combine_weights(gram, task_order)
    tile = 64 if share_rows % 64 == 0 else share_rows
    param_update = pl.pallas_call(
        update_kernel,
        grid=(share_rows // tile,),
        out_shape=jax.ShapeDtypeStruct((share_rows, block_count, half), F32),
        in_specs=[
            pl.BlockSpec(memory_space=pltpu.SMEM),
            pl.BlockSpec((tasks, block_count, tile, half), lambda r: (0, 0, r, 0)),
        ],
        out_specs=pl.BlockSpec((tile, block_count, half), lambda r: (r, 0, 0)),
        compiler_params=params_for(),
        name="update",
    )(task_weights, all_shards)
    head_bias_update = jnp.einsum("a,axy->xy", task_weights, all_head, precision=highest)
    row_update = jnp.einsum("a,axy->xy", task_weights, all_row, precision=highest)
    return (
        block_out, query_grad, memory_grad, param_update, head_bias_update,
        row_update[:6].reshape(3, 2, width), row_update[6:9], gram,
    )


def solution(mesh):
    return jax.shard_map(
        body,
        mesh=mesh,
        in_specs=(
            P("task", "dp", None),
            P("task", "dp", None),
            P("task", "dp", None),
            P("task", "dp", None),
            P("task", "dp"),
            P(),
            P(None, None, "tensor"),
            P(None, "tensor"),
            P(),
            P(),
        ),
        out_specs=(
            P("task", "dp", None),
            P("task", ("dp", "tensor"), None),
            P("task", ("dp", "tensor"), None),
            P("dp", None, "tensor"),
            P(None, "tensor"),
            P(),
            P(),
            P(),
        ),
        check_vma=False,
    )
```

```python
import functools

import jax
import jax.numpy as jnp
from jax import lax
from jax.experimental import pallas as pl
from jax.experimental.pallas import tpu as pltpu
from jax.sharding import PartitionSpec as P

HD = 64
GROUP = 4
SLAB = GROUP * HD
BF = jnp.bfloat16
F32 = jnp.float32
MESH_ID = pl.DeviceIdType.MESH
highest = lax.Precision.HIGHEST
VMEM_LIMIT = 62 * 2**20


def combine_weights(gram_matrix, order_list):
    task_count = gram_matrix.shape[0]
    task_index = jnp.arange(task_count, dtype=jnp.int32)
    summed = jnp.zeros((task_count,), F32)
    for own_task in range(task_count):
        coeffs = (task_index == own_task).astype(F32)
        for position in range(task_count):
            chosen = (task_index == order_list[position]).astype(F32)
            column = jnp.sum(gram_matrix * chosen[None, :], axis=1)
            inner_dot = jnp.sum(coeffs * column)
            square = jnp.sum(chosen * column)
            others = (order_list[position] != own_task).astype(F32)
            coeffs = coeffs - others * jnp.minimum(inner_dot, 0.0) / (square + 1e-06) * chosen
        summed = summed + coeffs
    return summed


def mm(a, b):
    return jnp.dot(a, b, preferred_element_type=F32)


def mm_nt(a, b):
    return lax.dot_general(a, b, (((1,), (1,)), ((), ())), preferred_element_type=F32)


def mm_tn(a, b):
    return lax.dot_general(a, b, (((0,), (0,)), ((), ())), preferred_element_type=F32)


def row_of(row_ref, which):
    return row_ref[which // 2, which % 2 : which % 2 + 1].astype(F32)


def gain_of(gain_ref, which):
    return gain_ref[which : which + 1].astype(F32)


def norm_parts(residual):
    row_mean = jnp.mean(residual, axis=-1, keepdims=True)
    centred = residual - row_mean
    variance = jnp.mean(centred * centred, axis=-1, keepdims=True)
    scale = lax.rsqrt(variance + 1e-05)
    return centred * scale, scale


def norm_back(normed, scale, gain_row, grad):
    scaled = grad * gain_row
    first = jnp.mean(scaled, axis=-1, keepdims=True)
    second = jnp.mean(scaled * normed, axis=-1, keepdims=True)
    return scale * (scaled - first - normed * second)


def rows_sum(value):
    return jnp.sum(value, axis=0, keepdims=True)


def gelu_tanh(hidden):
    square = hidden * hidden
    tanh = jnp.tanh(hidden * (0.7978845608028654 + 0.7978845608028654 * 0.044715 * square))
    half = 0.5 * (1.0 + tanh)
    inner = 0.7978845608028654 + 0.7978845608028654 * 3 * 0.044715 * square
    return hidden * half, half + 0.5 * hidden * (1.0 - tanh * tanh) * inner


def head_mask(head, rows, dtype):
    lane = lax.broadcasted_iota(jnp.int32, (rows, SLAB), 1)
    return (lane // HD == head).astype(F32).astype(dtype)


def stack_heads(slab):
    return jnp.concatenate(
        [slab * head_mask(head, slab.shape[0], slab.dtype) for head in range(GROUP)], axis=0
    )


def unstack_heads(stacked):
    rows = stacked.shape[0] // GROUP
    total = None
    for head in range(GROUP):
        part = stacked[head * rows : (head + 1) * rows] * head_mask(head, rows, stacked.dtype)
        total = part if total is None else total + part
    return total


def scores_of(query_stack, key_slab, valid):
    scores = mm_nt(key_slab, query_stack)
    if valid < key_slab.shape[0]:
        row = lax.broadcasted_iota(jnp.int32, scores.shape, 0)
        scores = jnp.where(row < valid, scores, -1e30)
    return scores


def attend(query_slab, key_slab, value_slab, valid):
    scores = scores_of(stack_heads(query_slab * HD ** (-0.5)), key_slab, valid)
    row_max = jnp.max(scores, axis=0, keepdims=True)
    exps = jnp.exp(scores - row_max)
    total = jnp.sum(exps, axis=0, keepdims=True)
    probs = (exps * (1.0 / total)).astype(BF)
    mixed = unstack_heads(mm_tn(value_slab, probs).T)
    return mixed, row_max + jnp.log(total)


def attend_back(query_slab, key_slab, value_slab, log_total, grad_slab, valid):
    query_stack = stack_heads(query_slab * HD ** (-0.5))
    grad_stack = stack_heads(grad_slab)
    probs = jnp.exp(scores_of(query_stack, key_slab, valid) - log_total)
    grad_value = mm(probs.astype(BF), grad_stack)
    grad_probs = mm_nt(value_slab, grad_stack)
    inner = jnp.sum(probs * grad_probs, axis=0, keepdims=True)
    grad_scores = (probs * (grad_probs - inner)).astype(BF)
    grad_key = mm(grad_scores, query_stack)
    grad_query = unstack_heads(mm_tn(key_slab, grad_scores).T) * HD ** (-0.5)
    return grad_query.astype(BF), grad_key.astype(BF), grad_value.astype(BF)


def pad_rows(source_ref, target_ref, images, valid):
    first = lax.axis_index("tensor") == 0
    padded = target_ref.shape[0] // images
    for image in range(images):
        here, there = (
            source_ref[(core * images + image) * valid : (core * images + image + 1) * valid]
            for core in range(2)
        )
        rows = jnp.where(first, here.astype(F32), there.astype(F32))
        fill = jnp.zeros((padded - valid, rows.shape[1]), F32)
        target_ref[image * padded : (image + 1) * padded] = jnp.concatenate(
            [rows, fill], axis=0
        ).astype(target_ref.dtype)


def gather_kernel(images, valid, own_ref, bias_ref, queries_ref, cotangent_ref, full_ref,
                  full_bias_ref, tokens_ref, own_cotangent_ref, turned, bias_own, remote_send,
                  remote_recv, local_sem):
    step, steps = pl.program_id(0), pl.num_programs(0)
    other = 1 - lax.axis_index("tensor")
    rows, _, width = own_ref.shape
    near, far = pl.ds(0, width), pl.ds(width, width)

    def copies(chunk):
        at = pl.ds(pl.multiple_of(chunk * rows, rows), rows)
        source = turned.at[:, at]
        return (
            pltpu.make_async_remote_copy(
                source, full_ref.at[:, at, far], remote_send.at[chunk], remote_recv.at[chunk],
                device_id={"tensor": other}, device_id_type=MESH_ID,
            ),
            pltpu.make_async_copy(source, full_ref.at[:, at, near], local_sem.at[chunk]),
        )

    def bias_copies():
        return (
            pltpu.make_async_remote_copy(
                bias_own, full_bias_ref.at[:, far], remote_send.at[steps], remote_recv.at[steps],
                device_id={"tensor": other}, device_id_type=MESH_ID,
            ),
            pltpu.make_async_copy(bias_own, full_bias_ref.at[:, near], local_sem.at[steps]),
        )

    @pl.when(step == 0)
    def _():
        barrier = pltpu.get_barrier_semaphore()
        pl.semaphore_signal(barrier, inc=1, device_id={"tensor": other}, device_id_type=MESH_ID)
        pl.semaphore_wait(barrier, 1)
        bias_own[...] = jnp.zeros_like(bias_own)
        bias_own[0 : bias_ref.shape[0]] = bias_ref[...]
        for copy in bias_copies():
            copy.start()

    turned[:, pl.ds(pl.multiple_of(step * rows, rows), rows)] = jnp.swapaxes(own_ref[...], 0, 1)
    for copy in copies(step):
        copy.start()

    @pl.when(step == steps - 1)
    def _():
        pad_rows(queries_ref, tokens_ref, images, valid)
        pad_rows(cotangent_ref, own_cotangent_ref, images, valid)
        for copy in bias_copies():
            copy.wait()

        def finish(chunk, carry):
            for copy in copies(chunk):
                copy.wait()
            return carry

        lax.fori_loop(0, steps, finish, 0)


def any_spec():
    return pl.BlockSpec(memory_space=pl.ANY)


def whole_spec():
    return pl.BlockSpec(memory_space=pltpu.VMEM)


def params_for(**keys):
    return pltpu.CompilerParams(vmem_limit_bytes=VMEM_LIMIT, **keys)


def self_kernel(images, valid, tokens_ref, weight_ref, head_ref, row_ref, gain_ref, qkv_ref,
                mixed_ref, total_ref, sum_ref, cross_query_ref):
    tokens = tokens_ref[...]
    rows = tokens.shape[0] // images
    width = tokens.shape[1]
    qkv_ref[0] = (mm(tokens, weight_ref[0]) + head_ref[0:1].astype(F32)).astype(BF)
    qkv_ref[1] = mm(tokens, weight_ref[1]).astype(BF)
    qkv_ref[2] = (mm(tokens, weight_ref[2]) + head_ref[1:2].astype(F32)).astype(BF)
    for image in range(images):
        at = slice(image * rows, (image + 1) * rows)
        for group in range(width // SLAB):
            lanes = slice(group * SLAB, (group + 1) * SLAB)
            mixed, log_total = attend(
                qkv_ref[0, at, lanes], qkv_ref[1, at, lanes], qkv_ref[2, at, lanes], valid
            )
            mixed_ref[at, lanes] = mixed.astype(BF)
            total_ref[image * (width // SLAB) + group] = jnp.broadcast_to(
                log_total, total_ref.shape[1:]
            )
    first_sum = tokens.astype(F32) + mm_nt(mixed_ref[...], weight_ref[3]) + row_of(row_ref, 0)
    sum_ref[...] = first_sum
    first_low = (norm_parts(first_sum)[0] * gain_of(gain_ref, 0) + row_of(row_ref, 1)).astype(BF)
    cross_query_ref[...] = (mm(first_low, weight_ref[4]) + head_ref[2:3].astype(F32)).astype(BF)


def cross_kernel(context_ref, query_ref, key_w_ref, value_w_ref, head_ref, key_ref, value_ref,
                 mixed_ref, total_ref):
    context = context_ref[...]
    key_ref[...] = mm(context, key_w_ref[0]).astype(BF)
    value_ref[...] = (mm(context, value_w_ref[0]) + head_ref[3:4].astype(F32)).astype(BF)
    mixed, log_total = attend(query_ref[...], key_ref[...], value_ref[...], key_ref.shape[0])
    mixed_ref[...] = mixed.astype(BF)
    total_ref[0] = jnp.broadcast_to(log_total, total_ref.shape[1:])


def ffn_kernel(
    images, blocks, sum_ref, mixed_ref, cotangent_ref, matches_ref, counts_ref, cross_w_ref, in_ref,
    out_ref, head_ref, row_ref, gain_ref,
    block_ref, left_ref, right_ref, mixed_grad_ref, residual_ref, small_ref,
    second_sum, second_low, left, right, slope, branch, third_grad, hidden_bias, left_sem, right_sem,
):
    step = pl.program_id(0)
    per = in_ref.shape[0]
    half_steps = blocks // per
    rows = sum_ref.shape[0] // images

    def left_copy(which):
        return pltpu.make_async_copy(left.at[which], left_ref.at[which], left_sem.at[which])

    def right_copy(which):
        return pltpu.make_async_copy(right.at[which], right_ref.at[which], right_sem.at[which])

    mixed_copy = pltpu.make_async_copy(
        mixed_ref, right_ref.at[2 * blocks], right_sem.at[2 * blocks]
    )

    @pl.when(step == 0)
    def _():
        mixed_copy.start()
        first_out = norm_parts(sum_ref[...])[0] * gain_of(gain_ref, 0) + row_of(row_ref, 1)
        second = first_out + mm_nt(mixed_ref[...], cross_w_ref[0]) + row_of(row_ref, 2)
        second_sum[...] = second
        second_low[...] = (
            norm_parts(second)[0] * gain_of(gain_ref, 1) + row_of(row_ref, 3)
        ).astype(BF)
        branch[...] = jnp.zeros_like(branch)
        small_ref[...] = jnp.zeros_like(small_ref)
        hidden_bias[0:blocks] = head_ref[4 : 4 + blocks].astype(F32)
        left[0] = second_low[...].T
        left_copy(0).start()

    @pl.when(step < half_steps)
    def _():
        low = second_low[...]
        pres = [
            mm(low, in_ref[k]) + hidden_bias[pl.ds(step * per + k, 1)] for k in range(per)
        ]
        total = branch[...]
        for k in range(per):
            act, grad = gelu_tanh(pres[k])
            act = act.astype(BF)
            slope[step * per + k] = grad
            right[blocks + step * per + k] = act
            right_copy(blocks + step * per + k).start()
            total = total + mm_nt(act, out_ref[k])
        branch[...] = total

    @pl.when(step == half_steps - 1)
    def _():
        second = norm_parts(second_sum[...])[0] * gain_of(gain_ref, 1) + row_of(row_ref, 3)
        third_sum = second + branch[...] + row_of(row_ref, 4)
        normed, scale = norm_parts(third_sum)
        block_ref[...] = (normed * gain_of(gain_ref, 2) + row_of(row_ref, 5)).astype(BF)
        count = matches_ref.shape[2]
        slot = lax.broadcasted_iota(jnp.int32, (rows, count), 0)
        box = lax.broadcasted_iota(jnp.int32, (rows, count), 1)
        grads = []
        for image in range(images):
            own = lax.axis_index("tensor") * images + image
            live = (matches_ref[0, pl.ds(own, 1)] == slot) & (box < counts_ref[0, own])
            mask = jnp.sum(jnp.where(live, 1.0, 0.0), axis=1, keepdims=True)
            cot = cotangent_ref[image * rows : (image + 1) * rows].astype(F32)
            grads.append(cot * mask)
        out_grad = jnp.concatenate(grads, axis=0)
        grad = norm_back(normed, scale, gain_of(gain_ref, 2), out_grad)
        third_grad[...] = grad
        left[1] = grad.astype(BF).T
        left_copy(1).start()
        small_ref[12:13] = rows_sum(grad)
        small_ref[13:14] = rows_sum(out_grad)
        small_ref[16:17] = rows_sum(out_grad * normed)
        branch[...] = jnp.zeros_like(branch)

    @pl.when(step >= half_steps)
    def _():
        ffn_low = third_grad[...].astype(BF)
        first = (step - half_steps) * per
        grads = [mm(ffn_low, out_ref[k]) for k in range(per)]
        total = branch[...]
        for k in range(per):
            grad_low = (grads[k] * slope[first + k]).astype(BF)
            right[first + k] = grad_low
            right_copy(first + k).start()
            small_ref[pl.ds(4 + first + k, 1)] = rows_sum(grad_low.astype(F32))
            total = total + mm_nt(grad_low, in_ref[k])
        branch[...] = total

    @pl.when(step == 2 * half_steps - 1)
    def _():
        second_in = third_grad[...] + branch[...]
        normed, scale = norm_parts(second_sum[...])
        grad = norm_back(normed, scale, gain_of(gain_ref, 1), second_in)
        residual_ref[...] = grad
        small_ref[10:11] = rows_sum(grad)
        small_ref[11:12] = rows_sum(second_in)
        small_ref[15:16] = rows_sum(second_in * normed)
        cross_low = grad.astype(BF)
        left[2] = cross_low.T
        left_copy(2).start()
        mixed_grad_ref[...] = mm(cross_low, cross_w_ref[0]).astype(BF)
        mixed_copy.wait()
        for which in range(3):
            left_copy(which).wait()
        for which in range(2 * blocks):
            right_copy(which).wait()


def cross_back_step(
    image, group, context_ref, query_ref, key_ref, value_ref, total_ref, mixed_grad_ref, small_ref,
    context_t, key_acc, value_acc, unit,
):
    @pl.when(group == 0)
    def _():
        context_t[...] = context_ref[...].T

    unit(0)
    grad_query, grad_key, grad_value = attend_back(
        query_ref[...], key_ref[...], value_ref[...], total_ref[0, 0:1], mixed_grad_ref[...],
        key_ref.shape[0],
    )
    lanes = pl.ds(pl.multiple_of(group * SLAB, SLAB), SLAB)
    small_ref[2:3, lanes] += rows_sum(grad_query.astype(F32))
    small_ref[3:4, lanes] += rows_sum(grad_value.astype(F32))
    unit(1)
    key_wg = mm(context_t[...], grad_key)
    value_wg = mm(context_t[...], grad_value)

    @pl.when(image == 0)
    def _():
        key_acc[:, lanes] = key_wg
        value_acc[:, lanes] = value_wg

    @pl.when(image > 0)
    def _():
        key_acc[:, lanes] += key_wg
        value_acc[:, lanes] += value_wg

    return grad_query, grad_key, grad_value


def cross_back_kernel(
    context_ref, query_ref, key_ref, value_ref, total_ref, mixed_grad_ref, key_w_ref, value_w_ref,
    query_grad_ref, context_grad_ref, key_wg_ref, value_wg_ref, small_ref,
    context_t, acc, key_acc, value_acc,
):
    image, group = pl.program_id(0), pl.program_id(1)
    images, groups = pl.num_programs(0), pl.num_programs(1)

    @pl.when((image == 0) & (group == 0))
    def _():
        small_ref[...] = jnp.zeros_like(small_ref)

    query_grad_ref[...], grad_key, grad_value = cross_back_step(
        image, group, context_ref, query_ref, key_ref, value_ref, total_ref, mixed_grad_ref,
        small_ref, context_t, key_acc, value_acc, lambda part: None,
    )
    context_part = mm_nt(grad_key, key_w_ref[0]) + mm_nt(grad_value, value_w_ref[0])

    @pl.when(group == 0)
    def _():
        acc[...] = context_part

    @pl.when(group > 0)
    def _():
        acc[...] += context_part

    @pl.when(group == groups - 1)
    def _():
        context_grad_ref[...] = acc[...].astype(BF)

    @pl.when((image == images - 1) & (group == groups - 1))
    def _():
        key_wg_ref[...] = key_acc[...].astype(BF)
        value_wg_ref[...] = value_acc[...].astype(BF)


def self_back(
    images, valid, tokens_ref, weight_ref, row_ref, gain_ref, qkv_ref, mixed_ref, total_ref, sum_ref,
    residual_ref, cross_query_grad_ref, small_ref, qkv_grad, emit, unit,
):
    tokens = tokens_ref[...]
    rows = tokens.shape[0] // images
    width = tokens.shape[1]
    normed, scale = norm_parts(sum_ref[...])
    first_low = (normed * gain_of(gain_ref, 0) + row_of(row_ref, 1)).astype(BF)
    cross_query_grad = cross_query_grad_ref[...]
    first_low_t = first_low.T
    emit(4, lambda lanes: mm(first_low_t, cross_query_grad_ref[:, lanes]))
    unit()
    first_in = residual_ref[...] + mm_nt(cross_query_grad, weight_ref[4])
    first_grad = norm_back(normed, scale, gain_of(gain_ref, 0), first_in)
    small_ref[8:9] = rows_sum(first_grad)
    small_ref[9:10] = rows_sum(first_in)
    small_ref[14:15] = rows_sum(first_in * normed)
    unit()
    self_low = first_grad.astype(BF)
    self_low_t = self_low.T
    emit(3, lambda lanes: mm(self_low_t, mixed_ref[:, lanes]))
    unit()
    mixed_grad = mm(self_low, weight_ref[3]).astype(BF)
    for image in range(images):
        at = slice(image * rows, (image + 1) * rows)
        for group in range(width // SLAB):
            lanes = slice(group * SLAB, (group + 1) * SLAB)
            grads = attend_back(
                qkv_ref[0, at, lanes], qkv_ref[1, at, lanes], qkv_ref[2, at, lanes],
                total_ref[image * (width // SLAB) + group, 0:1], mixed_grad[at, lanes], valid,
            )
            for which in range(3):
                qkv_grad[which, at, lanes] = grads[which]
            unit()
    tokens_t = tokens.T
    total = first_grad
    for which in range(3):
        grad = qkv_grad[which]
        emit(which, lambda lanes, which=which: mm(tokens_t, qkv_grad[which, :, lanes]))
        unit()
        total = total + mm_nt(grad, weight_ref[which])
    small_ref[0:1] = rows_sum(qkv_grad[0].astype(F32))
    small_ref[1:2] = rows_sum(qkv_grad[2].astype(F32))
    return total


def self_back_kernel(
    images, valid, tokens_ref, weight_ref, row_ref, gain_ref, qkv_ref, mixed_ref, total_ref, sum_ref,
    residual_ref, cross_query_grad_ref, query_grad_ref, wg_ref, small_ref, qkv_grad,
):
    small_ref[...] = jnp.zeros_like(small_ref)

    def emit(block, value):
        for lane in range(0, wg_ref.shape[2], SLAB):
            lanes = slice(lane, lane + SLAB)
            wg_ref[block, :, lanes] = value(lanes).astype(BF)

    query_grad_ref[...] = self_back(
        images, valid, tokens_ref, weight_ref, row_ref, gain_ref, qkv_ref, mixed_ref, total_ref,
        sum_ref, residual_ref, cross_query_grad_ref, small_ref, qkv_grad, emit, lambda: None,
    ).astype(BF)


def task_peers(tasks):
    me = lax.axis_index("task")
    return [lax.rem(me + shift, tasks) for shift in range(1, tasks)]


def task_senders(tasks):
    me = lax.axis_index("task")
    return [lax.rem(me + tasks - shift, tasks) for shift in range(1, tasks)]


def send(source, target, send_sem, recv_sem, **device):
    return pltpu.make_async_remote_copy(
        source, target, send_sem, recv_sem, device_id=device, device_id_type=MESH_ID
    )


def greet(depth, tasks):
    me = lax.axis_index("dp")
    barrier = pltpu.get_barrier_semaphore()
    other = 1 - lax.axis_index("tensor")
    for peer in task_peers(tasks):
        pl.semaphore_signal(barrier, inc=1, device_id={"task": peer}, device_id_type=MESH_ID)
        pl.semaphore_signal(
            barrier, inc=1, device_id={"task": peer, "tensor": other}, device_id_type=MESH_ID
        )
    for shift in range(1, depth):
        pl.semaphore_signal(
            barrier, inc=1, device_id={"dp": lax.rem(me + shift, depth)}, device_id_type=MESH_ID
        )
    pl.semaphore_signal(barrier, inc=1, device_id={"tensor": other}, device_id_type=MESH_ID)
    pl.semaphore_wait(barrier, 2 * (tasks - 1) + depth)


LAG = 2
AHEAD = 1
RING = 2


class Chain:
    def __init__(self, depth, tasks, near, far, refs):
        self.depth, self.tasks = depth, tasks
        self.near, self.far = near, far
        (self.near_ring, self.far_ring, self.passed, self.parts,
         self.near_sem, self.far_sem, self.far_send, self.far_recv, self.pass_send, self.pass_recv,
         self.part_send, self.part_recv) = refs
        self.chunks = self.passed.shape[1]
        self.rows, self.half = self.passed.shape[2:]
        self.me = lax.axis_index("dp")
        self.task = lax.axis_index("task")
        self.is_end = (self.me == 0) | (self.me == depth - 1)

    SCRATCH = 12

    @staticmethod
    def scratch(blocks, rows, half, tasks):
        chunks = 2 * blocks
        dma = pltpu.SemaphoreType.DMA
        return [
            pltpu.VMEM((RING, 2, rows, half), BF),
            pltpu.VMEM((RING, 2, rows, half), BF),
            pltpu.VMEM((2, chunks, rows, half), BF),
            pltpu.VMEM((tasks, chunks, rows // tasks, half), BF),
            dma((RING, 2)),
            dma((RING, 2)),
            dma((2, blocks)),
            dma((2, blocks)),
            dma((2, chunks)),
            dma((2, chunks)),
            dma((blocks, tasks - 1)),
            dma((blocks, tasks - 1)),
        ]

    def far_copy(self, source, way, block):
        rows = pl.ds(way * 2 * self.rows, 2 * self.rows)
        return send(
            source.at[rows], self.far.at[way, block], self.far_send.at[way, block],
            self.far_recv.at[way, block], tensor=1 - lax.axis_index("tensor"),
        )

    def far_arrival(self, way, block):
        landed = self.far.at[way, block]
        return send(
            landed, landed, self.far_send.at[way, block], self.far_recv.at[way, block],
            tensor=1 - lax.axis_index("tensor"),
        )

    def pass_copy(self, way, chunk):
        piece = self.passed.at[way, chunk]
        target = self.me - 1 if way == 0 else self.me + 1
        return send(
            piece, piece, self.pass_send.at[way, chunk], self.pass_recv.at[way, chunk], dp=target
        )

    def part_rows(self, peer):
        size = self.rows // self.tasks
        return pl.ds(pl.multiple_of(peer * size, size), size)

    def part_copy(self, way, block, shift, peer):
        chunks = pl.ds(2 * block, 2)
        return send(
            self.passed.at[way, chunks, self.part_rows(peer)], self.parts.at[self.task, chunks],
            self.part_send.at[block, shift], self.part_recv.at[block, shift], task=peer,
        )

    def hops(self, way):
        return self.depth - 1 - self.me if way == 0 else self.me

    def units(self):
        return self.chunks + LAG * (self.depth - 1)

    def near_fetch(self, source, slot, way):
        return pltpu.make_async_copy(
            source, self.near_ring.at[slot, way], self.near_sem.at[slot, way]
        )

    def far_fetch(self, source, slot, way):
        return pltpu.make_async_copy(
            source, self.far_ring.at[slot, way], self.far_sem.at[slot, way]
        )

    def fetch(self, index):
        slot = lax.rem(index, RING)
        for way in range(2):
            chunk = index - LAG * self.hops(way)

            @pl.when((chunk >= 0) & (chunk < self.chunks))
            def _(way=way, chunk=chunk):
                block = chunk // 2
                place = chunk - 2 * block

                @pl.when(place == 0)
                def _():
                    self.far_arrival(way, block).wait_recv()

                start = pl.multiple_of(place * self.rows, self.rows)
                rows = pl.ds(way * 2 * self.rows + start, self.rows)
                self.near_fetch(self.near.at[block, rows], slot, way).start()
                self.far_fetch(
                    self.far.at[way, block, pl.ds(start, self.rows)], slot, way
                ).start()

    def unit(self, index):
        self.fetch(index + AHEAD)
        slot = lax.rem(index, RING)
        for way in range(2):
            chunk = index - LAG * self.hops(way)

            @pl.when((chunk >= 0) & (chunk < self.chunks))
            def _(way=way, chunk=chunk):
                self.chunk_step(way, chunk, slot)

    def chunk_step(self, way, chunk, slot):
        first, last = self.hops(way) == 0, self.hops(way) == self.depth - 1
        piece = self.near_ring.at[slot, way]
        self.near_fetch(piece, slot, way).wait()
        self.far_fetch(piece, slot, way).wait()
        own = self.near_ring[slot, way].astype(F32) + self.far_ring[slot, way].astype(F32)

        @pl.when(first)
        def _():
            self.passed[way, chunk] = own.astype(BF)

        @pl.when(jnp.logical_not(first))
        def _():
            self.pass_copy(way, chunk).wait_recv()
            self.passed[way, chunk] = (own + self.passed[way, chunk].astype(F32)).astype(BF)

        @pl.when(jnp.logical_not(last))
        def _():
            self.pass_copy(way, chunk).start()

        block = chunk // 2

        @pl.when(last & (chunk == 2 * block + 1))
        def _():
            for shift, peer in enumerate(task_peers(self.tasks)):
                self.part_copy(way, block, shift, peer).start()
            own_rows = self.part_rows(self.task)
            self.parts[self.task, chunk - 1] = self.passed[way, chunk - 1, own_rows]
            self.parts[self.task, chunk] = self.passed[way, chunk, own_rows]

    def wait_parts(self, block):
        for shift, peer in enumerate(task_senders(self.tasks)):
            landed = self.parts.at[peer, pl.ds(2 * block, 2)]
            send(
                landed, landed, self.part_send.at[block, shift], self.part_recv.at[block, shift],
                task=peer,
            ).wait_recv()

    def finish(self):
        def blocks(block, carry):
            for way in range(2):

                @pl.when(self.hops(way) != self.depth - 1)
                def _(way=way):
                    for part in range(2):
                        self.pass_copy(way, 2 * block + part).wait_send()

                @pl.when(self.hops(way) == self.depth - 1)
                def _(way=way):
                    for shift, peer in enumerate(task_peers(self.tasks)):
                        self.part_copy(way, block, shift, peer).wait_send()

            return carry

        lax.fori_loop(0, self.chunks // 2, blocks, 0)


def pairs_of(tasks):
    return [(a, b) for a in range(tasks) for b in range(a, tasks)]


def weights_of(gram, order_ref, tasks):
    totals = [0.0] * tasks
    for own in range(tasks):
        coeffs = [jnp.full_like(gram[0, 0], 1.0 if t == own else 0.0) for t in range(tasks)]
        for position in range(tasks):
            chosen = [
                jnp.where(order_ref[position] == t, 1.0, 0.0).astype(F32) for t in range(tasks)
            ]
            column = [sum(gram[t, j] * chosen[j] for j in range(tasks)) for t in range(tasks)]
            inner = sum(coeffs[t] * column[t] for t in range(tasks))
            square = sum(chosen[t] * column[t] for t in range(tasks))
            others = 1.0 - chosen[own]
            share = others * jnp.minimum(inner, 0.0) / (square + 1e-06)
            coeffs = [coeffs[t] - share * chosen[t] for t in range(tasks)]
        totals = [total + coeff for total, coeff in zip(totals, coeffs)]
    return totals


GROUPS = 4
UNITS = 2
TILE = 240


class ContextGrad:
    def __init__(self, key_grad, value_grad, result, refs):
        self.grads, self.result = (key_grad, value_grad), result
        (self.weights, self.staged, self.ring, self.done, self.weight_sem, self.staged_sem,
         self.ring_sem, self.done_sem) = refs
        self.tile, width = self.done.shape[1:]
        self.lanes = [pl.ds(0, width), pl.ds(width, width)]
        self.tiles = result.shape[0] // self.tile

    SCRATCH = 8

    @staticmethod
    def scratch(keys, width):
        dma = pltpu.SemaphoreType.DMA
        return [
            pltpu.VMEM((width, 2 * width), BF),
            pltpu.VMEM((2, 2, keys, SLAB), BF),
            pltpu.VMEM((2, TILE, 2 * width), BF),
            pltpu.VMEM((2, TILE, width), BF),
            dma((2,)),
            dma((2, 2)),
            dma((2, 2)),
            dma((2,)),
        ]

    def weight_copies(self, sources):
        return [
            pltpu.make_async_copy(source, self.weights.at[:, lanes], self.weight_sem.at[which])
            for which, (source, lanes) in enumerate(zip(sources, self.lanes))
        ]

    def staged_copies(self, step, image, group):
        slot = lax.rem(step, 2)
        keys = self.staged.shape[2]
        rows = pl.ds(pl.multiple_of(image * keys, keys), keys)
        lanes = pl.ds(pl.multiple_of(group * SLAB, SLAB), SLAB)
        return [
            pltpu.make_async_copy(
                self.staged.at[slot, which], self.grads[which].at[rows, lanes],
                self.staged_sem.at[slot, which],
            )
            for which in range(2)
        ]

    def put(self, step, image, group, values):
        @pl.when(step >= 2)
        def _():
            for copy in self.staged_copies(step, image, group):
                copy.wait()

        for which, value in enumerate(values):
            self.staged[lax.rem(step, 2), which] = value
        for copy in self.staged_copies(step, image, group):
            copy.start()

    def settle(self):
        for step in range(2):
            for copy in self.staged_copies(step, 0, 0):
                copy.wait()

    def fetches(self, index):
        slot = lax.rem(index, 2)
        rows = pl.ds(pl.multiple_of(index * self.tile, self.tile), self.tile)
        return [
            pltpu.make_async_copy(
                self.grads[which].at[rows], self.ring.at[slot, :, self.lanes[which]],
                self.ring_sem.at[slot, which],
            )
            for which in range(2)
        ]

    def store(self, index):
        slot = lax.rem(index, 2)
        rows = pl.ds(pl.multiple_of(index * self.tile, self.tile), self.tile)
        return pltpu.make_async_copy(
            self.done.at[slot], self.result.at[rows], self.done_sem.at[slot]
        )

    def compute(self, index):
        @pl.when(index < self.tiles)
        def _():
            for copy in self.fetches(index):
                copy.wait()

            @pl.when(index + 1 < self.tiles)
            def _():
                for copy in self.fetches(index + 1):
                    copy.start()

            @pl.when(index >= 2)
            def _():
                self.store(index - 2).wait()

            slot = lax.rem(index, 2)
            self.done[slot] = mm_nt(self.ring[slot], self.weights[...]).astype(BF)
            self.store(index).start()

    def finish(self):
        for index in range(self.tiles - 2, self.tiles):
            self.store(jnp.int32(index)).wait()


def back_kernel(
    depth, tasks, images, groups, valid, block_order, order_ref, context_ref, query_ref, key_ref,
    value_ref, total_ref, mixed_grad_ref, tokens_ref, weight_ref, row_ref,
    gain_ref, qkv_ref, mixed_ref, self_total_ref, sum_ref, residual_ref, small_in_ref, all_w_ref,
    block_ref, left_first_ref, right_first_ref, left_ref, right_ref, *refs
):
    (
        context_grad_ref, query_grad_ref, update_ref, small_out_ref, gram_ref, block_far, near, far,
        key_grad, value_grad,
    ), refs = refs[:10], refs[10:]
    (
        context_t, key_acc, value_acc, cross_query_grad, qkv_grad, stage, stage_sem, block_sem,
    ), refs = refs[:8], refs[8:]
    context_back = ContextGrad(
        key_grad, value_grad, context_grad_ref, refs[: ContextGrad.SCRATCH]
    )
    refs = refs[ContextGrad.SCRATCH :]
    chain = Chain(depth, tasks, near, far, refs[: Chain.SCRATCH])
    refs = refs[Chain.SCRATCH :]
    gram_acc = refs[7]
    step = pl.program_id(0)
    cross_steps = images * groups
    half = chain.half
    is_end = chain.is_end
    pairs = pairs_of(tasks)

    def add_products(shares):
        for index, (a, b) in enumerate(pairs):
            product = shares[a] * shares[b]
            total = product[0:8]
            for row in range(8, product.shape[0], 8):
                total = total + product[row : row + 8]
            gram_acc[index * 8 : index * 8 + 8] += total

    def unit(index):
        chain.unit(index)
        since = index - LAG * (depth - 1) - 3
        block = since // 2

        @pl.when(is_end & (since >= 0) & (since == 2 * block))
        def _():
            chain.wait_parts(block)
            for part in range(2):
                add_products(
                    [chain.parts[t, 2 * block + part].astype(F32) for t in range(tasks)]
                )

    block_copy = send(
        block_ref, block_far, block_sem.at[0], block_sem.at[1], tensor=1 - lax.axis_index("tensor")
    )
    weight_copies = context_back.weight_copies([all_w_ref.at[5], all_w_ref.at[6]])

    slots = stage.shape[0]

    def far_copies(position):
        slot = lax.rem(position, slots)
        return [
            chain.far_copy(stage.at[slot, :, pl.ds(half, half)], way, position) for way in range(2)
        ]

    def near_copy(position):
        slot = lax.rem(position, slots)
        return pltpu.make_async_copy(
            stage.at[slot, :, pl.ds(0, half)], near.at[position], stage_sem.at[slot]
        )

    def emit(position, value):
        position = jnp.int32(position)

        @pl.when(position >= slots)
        def _():
            for copy in far_copies(position - slots):
                copy.wait_send()

        for lane in range(0, 2 * half, SLAB):
            stage[lax.rem(position, slots), :, lane : lane + SLAB] = value(
                slice(lane, lane + SLAB)
            ).astype(BF)
        for copy in far_copies(position):
            copy.start()
        near_copy(position).start()

    @pl.when(step == 0)
    def _():
        greet(depth, tasks)
        emit(0, lambda lanes: mm(left_first_ref[0], right_first_ref[0, :, lanes]))
        block_copy.start()
        for copy in weight_copies:
            copy.start()
        gram_acc[...] = jnp.zeros_like(gram_acc)
        refs[0][...] = small_in_ref[...]

    @pl.when(step < cross_steps)
    def _():
        image = step // groups
        group = step - image * groups

        emitted = step < cross_steps - 1

        @pl.when(emitted)
        def _():
            emit(step + 1, lambda lanes: mm(left_ref[0], right_ref[0, :, lanes]))

        @pl.when(step == 0)
        def _():
            near_copy(jnp.int32(0)).wait()
            for index in range(AHEAD):
                chain.fetch(jnp.int32(index))

        def cross_unit(part):
            if part == 0:
                unit(step * UNITS)
            else:

                @pl.when(emitted)
                def _():
                    near_copy(step + 1).wait()
                    unit(step * UNITS + part)

        grad_query, *grads = cross_back_step(
            image, group, context_ref, query_ref, key_ref, value_ref, total_ref, mixed_grad_ref,
            refs[0], context_t, key_acc, value_acc, cross_unit,
        )
        context_back.put(step, image, group, grads)
        rows = grad_query.shape[0]
        cross_query_grad[
            pl.ds(pl.multiple_of(image * rows, rows), rows),
            pl.ds(pl.multiple_of(group * SLAB, SLAB), SLAB),
        ] = grad_query

        @pl.when(step == cross_steps - 1)
        def _():
            emit(cross_steps, lambda lanes: key_acc[:, lanes])
            emit(cross_steps + 1, lambda lanes: value_acc[:, lanes])
            near_copy(jnp.int32(cross_steps)).wait()
            near_copy(jnp.int32(cross_steps + 1)).wait()

    @pl.when(step == cross_steps)
    def _():
        calls, done = [0], [cross_steps * UNITS - 1]

        def self_unit():
            if calls[0] % 2 == 0:
                unit(jnp.int32(done[0]))
                done[0] += 1
            calls[0] += 1

        context_back.settle()
        for copy in context_back.fetches(jnp.int32(0)):
            copy.start()
        for copy in weight_copies:
            copy.wait()
        pending = []

        def self_emit(block, value):
            for position in pending:
                near_copy(jnp.int32(position)).wait()
            pending[:] = [block_order.index(block)]
            emit(pending[0], value)

        query_grad_ref[...] = self_back(
            images, valid, tokens_ref, weight_ref, row_ref, gain_ref, qkv_ref, mixed_ref,
            self_total_ref, sum_ref, residual_ref, cross_query_grad, refs[0], qkv_grad,
            self_emit, self_unit,
        ).astype(BF)
        for position in pending:
            near_copy(jnp.int32(position)).wait()
        rest(
            chain, unit, context_back, done[0], order_ref, update_ref, small_out_ref, gram_ref, refs
        )
        for position in range(len(block_order) - slots, len(block_order)):
            for copy in far_copies(jnp.int32(position)):
                copy.wait_send()
        block_copy.wait()
        context_back.finish()


def rest(
    chain, unit, context_back, done, order_ref, update_ref, small_out_ref, gram_ref, refs
):
    (
        small, small_own, small_other, small_far, small_pass, small_all, small_both, gram_acc,
        gram_plane, gram_end, hop, out,
        small_far_sem, small_pass_sem, small_task_sem, small_dp_sem, small_core_sem,
        gram_plane_sem, gram_dp_sem, hop_sem, out_sem, update_sem,
    ) = refs
    depth, tasks, half = chain.depth, chain.tasks, chain.half
    me, task, core = (lax.axis_index(axis) for axis in ("dp", "task", "tensor"))
    is_end = chain.is_end
    top = me == 0
    pairs = pairs_of(tasks)
    own_lanes = pl.ds(pl.multiple_of(core * half, half), half)
    other_lanes = pl.ds(pl.multiple_of((1 - core) * half, half), half)
    small_own[0:8] = small[0:8, 0:half]
    small_own[8:] = small[8:, own_lanes]
    small_other[0:8] = small[0:8, half:]
    small_other[8:] = small[8:, other_lanes]
    small_copy = send(
        small_other, small_far, small_far_sem.at[0], small_far_sem.at[1], tensor=1 - core
    )
    small_copy.start()

    def small_hop():
        return send(
            small_pass, small_pass, small_pass_sem.at[0], small_pass_sem.at[1], dp=me - 1
        )

    def small_task_copy(shift, peer):
        return send(
            small_pass, small_all.at[task], small_task_sem.at[0, shift],
            small_task_sem.at[1, shift], task=peer,
        )

    def step(index, carry):
        unit(index)
        context_back.compute(index - done)

        @pl.when(index == done + 1 + LAG * chain.hops(0))
        def _():
            small_copy.wait_recv()
            total = small_own[...] + small_far[...]

            @pl.when(me == depth - 1)
            def _():
                small_pass[...] = total

            @pl.when(me < depth - 1)
            def _():
                small_hop().wait_recv()
                small_pass[...] += total

            @pl.when(me > 0)
            def _():
                small_hop().start()

            @pl.when(top)
            def _():
                for shift, peer in enumerate(task_peers(tasks)):
                    small_task_copy(shift, peer).start()
                small_all[task] = small_pass[...]

        return carry

    lax.fori_loop(done, max(chain.units() + 2, done + context_back.tiles), step, 0)

    @pl.when(top)
    def _():
        for shift, peer in enumerate(task_senders(tasks)):
            landed = small_all.at[peer]
            send(
                landed, landed, small_task_sem.at[0, shift], small_task_sem.at[1, shift], task=peer
            ).wait_recv()

    lanes = gram_plane.shape[2]
    plane = 2 * tasks
    mine = 2 * task + core

    def gram_copy(shift):
        to = lax.rem(mine + shift, plane)
        return send(
            gram_plane.at[mine], gram_plane.at[mine], gram_plane_sem.at[0, shift - 1],
            gram_plane_sem.at[1, shift - 1], task=to // 2, tensor=lax.rem(to, 2),
        )

    def gram_arrival(shift):
        place = lax.rem(mine + plane - shift, plane)
        return send(
            gram_plane.at[place], gram_plane.at[place], gram_plane_sem.at[0, shift - 1],
            gram_plane_sem.at[1, shift - 1], task=place // 2, tensor=lax.rem(place, 2),
        )

    def gram_dp_copy(end, shift):
        return send(
            gram_end.at[end], gram_end.at[end], gram_dp_sem.at[0, end, shift],
            gram_dp_sem.at[1, end, shift], dp=lax.rem((depth - 1) * end + shift + 1, depth),
        )

    def one_number(values):
        return jnp.sum(jnp.sum(values, axis=0, keepdims=True), axis=1, keepdims=True)

    @pl.when(top & (task == 0))
    def _():
        small_values = [small_all[t] for t in range(tasks)]
        for index, (a, b) in enumerate(pairs):
            product = small_values[a] * small_values[b]
            gram_acc[index * 8 : index * 8 + 8] += product[0:8] + product[8:16] + product[16:24]

    @pl.when(is_end)
    def _():
        gram_plane[mine] = jnp.zeros(gram_plane.shape[1:], F32)
        for index in range(len(pairs)):
            gram_plane[mine, index : index + 1] = jnp.broadcast_to(
                one_number(gram_acc[index * 8 : index * 8 + 8]), (1, lanes)
            )
        for shift in range(1, plane):
            gram_copy(shift).start()
        for shift in range(1, plane):
            gram_arrival(shift).wait_recv()

    for end in range(2):

        @pl.when(me == (depth - 1) * end)
        def _(end=end):
            total = gram_plane[0]
            for place in range(1, plane):
                total = total + gram_plane[place]
            gram_end[end] = total
            for shift in range(depth - 1):
                gram_dp_copy(end, shift).start()

    for end in range(2):
        for shift in range(depth - 1):

            @pl.when(me == ((depth - 1) * end + shift + 1) % depth)
            def _(end=end, shift=shift):
                gram_dp_copy(end, shift).wait_recv()

    gram = {}
    for index, (a, b) in enumerate(pairs):
        row = slice(index, index + 1)
        gram[a, b] = gram[b, a] = gram_end[0, row] + gram_end[1, row]
    for a in range(tasks):
        for b in range(tasks):
            gram_ref[a * tasks + b : a * tasks + b + 1] = gram[a, b]
    weights = [
        jnp.concatenate([weight] * (half // lanes), axis=1)
        for weight in weights_of(gram, order_ref, tasks)
    ]

    blocks = out.shape[0]
    group = blocks // GROUPS
    share = chain.rows // tasks
    own_share = pl.ds(pl.multiple_of(task * share, share), share)
    own_part = jnp.minimum(me, 1)

    def hop_copy(index):
        return send(
            hop.at[pl.ds(index * group, group)], out.at[pl.ds(index * group, group), own_share],
            hop_sem.at[0, index], hop_sem.at[1, index],
            dp=jnp.where(top, 1, depth - 2),
        )

    beside = [task + 1 - 2 * lax.rem(task, 2), task + 2 - 4 * (task // 2)]
    across = tasks - 1 - task

    def out_piece(index, owner):
        rows = pl.ds(pl.multiple_of(owner * share, share), share)
        return out.at[pl.ds(index * group, group), rows]

    def out_copy(index, which, owner):
        piece = out_piece(index, owner)
        peer = beside[which] if which < 2 else beside[1 if index < GROUPS // 2 else 0]
        return send(
            piece, piece, out_sem.at[0, index, which], out_sem.at[1, index, which], task=peer
        )

    def update_copy(index):
        at = pl.ds(index * group, group)
        return pltpu.make_async_copy(out.at[at], update_ref.at[at], update_sem.at[index])

    def weighted(chunk):
        total = weights[0] * chain.parts[0, chunk].astype(F32)
        for t in range(1, tasks):
            total = total + weights[t] * chain.parts[t, chunk].astype(F32)
        return total.astype(BF)

    def small_dp_copy(shift):
        return send(
            small_both.at[0], small_both.at[0], small_dp_sem.at[0, shift],
            small_dp_sem.at[1, shift], dp=shift + 1,
        )

    def small_core_copy():
        return send(
            small_both.at[0], small_both.at[1], small_core_sem.at[0], small_core_sem.at[1],
            tensor=1 - core,
        )

    @pl.when(top)
    def _():
        total = weights[0] * small_all[0]
        for t in range(1, tasks):
            total = total + weights[t] * small_all[t]
        small_both[0] = total
        for shift in range(depth - 1):
            small_dp_copy(shift).start()

    @pl.when(is_end)
    def _():
        for index in range(GROUPS):

            def other(block, carry):
                hop[block] = weighted(2 * block + 1 - own_part)
                return carry

            lax.fori_loop(index * group, (index + 1) * group, other, 0)
            hop_copy(index).start()

            def own(block, carry):
                out[block, own_share] = weighted(2 * block + own_part)
                return carry

            lax.fori_loop(index * group, (index + 1) * group, own, 0)
            for which in range(2):
                out_copy(index, which, task).start()

    @pl.when(jnp.logical_not(is_end))
    def _():
        for index in range(GROUPS):
            hop_copy(index).wait_recv()
            for which in range(2):
                out_copy(index, which, task).start()

    for shift in range(depth - 1):

        @pl.when(me == shift + 1)
        def _(shift=shift):
            small_dp_copy(shift).wait_recv()

    small_core_copy().start()

    for index in range(GROUPS):
        for which in range(2):
            out_copy(index, which, beside[which]).wait_recv()
        out_copy(index, 2, beside[0 if index < GROUPS // 2 else 1]).start()
    for index in range(GROUPS):
        out_copy(index, 2, across).wait_recv()
        update_copy(index).start()

    small_core_copy().wait_recv()
    small_out_ref[0:8, 0:half] = small_both[0, 0:8]
    small_out_ref[0:8, half:] = small_both[1, 0:8]
    small_out_ref[8:, own_lanes] = small_both[0, 8:]
    small_out_ref[8:, other_lanes] = small_both[1, 8:]

    small_copy.wait_send()
    small_core_copy().wait_send()
    chain.finish()

    @pl.when(me > 0)
    def _():
        small_hop().wait_send()

    @pl.when(top)
    def _():
        for shift, peer in enumerate(task_peers(tasks)):
            small_task_copy(shift, peer).wait_send()
        for shift in range(depth - 1):
            small_dp_copy(shift).wait_send()

    for end in range(2):

        @pl.when(me == (depth - 1) * end)
        def _(end=end):
            for shift in range(depth - 1):
                gram_dp_copy(end, shift).wait_send()

    @pl.when(is_end)
    def _():
        for shift in range(1, plane):
            gram_copy(shift).wait_send()
        for index in range(GROUPS):
            hop_copy(index).wait_send()

    for index in range(GROUPS):
        update_copy(index).wait()
        for which in range(3):
            out_copy(index, which, task).wait_send()


def spread_kernel(
    images, valid, tasks, block_order, parts_ref, context_grad_ref, query_grad_ref, block_ref,
    block_far_ref, small_ref, gram_in_ref,
    update_ref, context_out_ref, query_out_ref, block_out_ref, head_ref, row_ref, gain_ref, gram_ref,
):
    ordered = [parts_ref[block_order.index(block)] for block in range(len(block_order))]
    update_ref[...] = jnp.swapaxes(jnp.stack(ordered), 0, 1).astype(F32)
    context_out_ref[...] = context_grad_ref[...]

    @pl.when(pl.program_id(0) == 0)
    def _():
        padded = query_grad_ref.shape[0] // images
        first = lax.axis_index("tensor") == 0

        def rows(ref, image):
            return ref[image * padded : (image + 1) * padded].astype(F32)[:valid]

        for image in range(images):
            at = slice(image * valid, (image + 1) * valid)
            after = slice((images + image) * valid, (images + image + 1) * valid)
            query_out_ref[at] = rows(query_grad_ref, image).astype(BF)
            near, far = rows(block_ref, image), rows(block_far_ref, image)
            block_out_ref[at] = jnp.where(first, near, far).astype(BF)
            block_out_ref[after] = jnp.where(first, far, near).astype(BF)
        head_ref[...] = small_ref[0:8, 0 : head_ref.shape[1]]
        for which in range(6):
            row_ref[which // 2, which % 2 : which % 2 + 1] = small_ref[8 + which : 9 + which]
        gain_ref[...] = small_ref[14:17]
        for a in range(tasks):
            for b in range(tasks):
                at = a * tasks + b
                gram_ref[a : a + 1, b : b + 1] = gram_in_ref[at : at + 1, 0:1]


def gram_kernel(parts_ref, gram_ref):
    tasks = parts_ref.shape[0]

    @pl.when(pl.program_id(0) == 0)
    def _():
        gram_ref[...] = jnp.zeros_like(gram_ref)

    shares = [parts_ref[task, 0].astype(F32) for task in range(tasks)]
    for a in range(tasks):
        for b in range(a, tasks):
            gram_ref[a * tasks + b : a * tasks + b + 1] += rows_sum(shares[a] * shares[b])


def update_kernel(weights_ref, parts_ref, update_ref):
    tasks, blocks = parts_ref.shape[:2]
    for block in range(blocks):
        total = weights_ref[0] * parts_ref[0, block].astype(F32)
        for task in range(1, tasks):
            total += weights_ref[task] * parts_ref[task, block].astype(F32)
        update_ref[:, block, :] = total


def body(
    queries, memory, cotangent, matches, counts, task_order, params, head_bias, row_bias, norm_gain
):
    all_images = matches.shape[1]
    valid = matches.shape[2]
    width = queries.shape[2]
    half = params.shape[2]
    block_count = params.shape[1]
    blocks = (block_count - 8) // 2
    cores = lax.axis_size("tensor")
    images = all_images // cores
    keys = memory.shape[1] // all_images
    padded = -(-valid // 16) * 16
    rows = images * padded
    groups = width // SLAB
    stack = GROUP * padded
    core = lax.axis_index("tensor")

    chunk = 96
    weights, head_rows, tokens, own_cotangent = pl.pallas_call(
        functools.partial(gather_kernel, images, valid),
        grid=(width // chunk,),
        out_shape=(
            jax.ShapeDtypeStruct((block_count, width, cores * half), BF),
            jax.ShapeDtypeStruct((16, cores * half), BF),
            jax.ShapeDtypeStruct((rows, width), BF),
            jax.ShapeDtypeStruct((rows, width), BF),
        ),
        in_specs=[
            pl.BlockSpec((chunk, block_count, half), lambda i: (i, 0, 0)),
            pl.BlockSpec((8, half), lambda i: (0, 0)),
            pl.BlockSpec((None, *queries.shape[1:]), lambda i: (0, 0, 0)),
            pl.BlockSpec((None, *queries.shape[1:]), lambda i: (0, 0, 0)),
        ],
        out_specs=(
            any_spec(), any_spec(),
            pl.BlockSpec((rows, width), lambda i: (0, 0)),
            pl.BlockSpec((rows, width), lambda i: (0, 0)),
        ),
        scratch_shapes=[
            pltpu.VMEM((block_count, width, half), BF),
            pltpu.VMEM((16, half), BF),
            pltpu.SemaphoreType.DMA((width // chunk + 1,)),
            pltpu.SemaphoreType.DMA((width // chunk + 1,)),
            pltpu.SemaphoreType.DMA((width // chunk + 1,)),
        ],
        compiler_params=params_for(collective_id=0, has_side_effects=True),
        name="gather_weights",
    )(params, head_bias, queries, cotangent)

    def const(shape, *index):
        return pl.BlockSpec(shape, lambda *_: index)

    total_shape = jax.ShapeDtypeStruct((images * groups, 8, stack), F32)
    low_rows = jax.ShapeDtypeStruct((rows, width), BF)
    full_rows = jax.ShapeDtypeStruct((rows, width), F32)
    small_shape = jax.ShapeDtypeStruct((24, width), F32)
    one_block = jax.ShapeDtypeStruct((width, width), BF)
    small_spec = const((24, width), 0, 0)
    row_spec = const(row_bias.shape, 0, 0, 0)
    gain_spec = const(norm_gain.shape, 0, 0)
    head_spec = const((16, width), 0, 0)
    rows_spec = const((rows, width), 0, 0)

    qkv, self_mixed, self_total, first_sum, cross_query = pl.pallas_call(
        functools.partial(self_kernel, images, valid),
        grid=(1,),
        out_shape=(
            jax.ShapeDtypeStruct((3, rows, width), BF), low_rows, total_shape, full_rows, low_rows,
        ),
        in_specs=[rows_spec, const((5, width, width), 0, 0, 0), head_spec, row_spec, gain_spec],
        out_specs=(
            const((3, rows, width), 0, 0, 0), rows_spec, const(total_shape.shape, 0, 0, 0),
            rows_spec, rows_spec,
        ),
        compiler_params=params_for(),
        name="self_forward",
    )(tokens, weights, head_rows, row_bias, norm_gain)


    def own_image(i, g):
        return 0, lax.axis_index("tensor") * images + i, 0

    context_all = pl.BlockSpec((None, keys, width), own_image)
    slab_q = pl.BlockSpec((padded, SLAB), lambda i, g: (i, g))
    slab_k = pl.BlockSpec((keys, SLAB), lambda i, g: (i, g))
    slab_t = pl.BlockSpec((1, 8, stack), lambda i, g: (i * groups + g, 0, 0))

    def slab_w(block):
        return pl.BlockSpec((1, width, SLAB), lambda i, g: (block, 0, g))

    key_rows = jax.ShapeDtypeStruct((images * keys, width), BF)
    keys_act, values_act, cross_mixed, cross_total = pl.pallas_call(
        cross_kernel,
        grid=(images, groups),
        in_specs=[
            context_all, slab_q, slab_w(5), slab_w(6),
            pl.BlockSpec((16, SLAB), lambda i, g: (0, g)),
        ],
        out_specs=(slab_k, slab_k, slab_q, slab_t),
        out_shape=(key_rows, key_rows, low_rows, total_shape),
        compiler_params=params_for(),
        name="cross_forward",
    )(memory, cross_query, weights, weights, head_rows)

    per = 2 if blocks % 2 == 0 else 1
    block_rows, left, right, mixed_grad, second_grad, ffn_small = pl.pallas_call(
        functools.partial(ffn_kernel, images, blocks),
        grid=(2 * blocks // per,),
        out_shape=(
            low_rows,
            jax.ShapeDtypeStruct((3, width, rows), BF),
            jax.ShapeDtypeStruct((2 * blocks + 1, rows, width), BF),
            low_rows, full_rows, small_shape,
        ),
        in_specs=[
            rows_spec, rows_spec, rows_spec,
            const(matches.shape, 0, 0, 0),
            pl.BlockSpec(memory_space=pltpu.SMEM),
            const((1, width, width), 7, 0, 0),
            pl.BlockSpec((per, width, width), lambda s: (8 // per + s % (blocks // per), 0, 0)),
            pl.BlockSpec(
                (per, width, width), lambda s: ((8 + blocks) // per + s % (blocks // per), 0, 0)
            ),
            head_spec, row_spec, gain_spec,
        ],
        out_specs=(rows_spec, any_spec(), any_spec(), rows_spec, rows_spec, small_spec),
        scratch_shapes=[
            pltpu.VMEM((rows, width), F32),
            pltpu.VMEM((rows, width), BF),
            pltpu.VMEM((3, width, rows), BF),
            pltpu.VMEM((2 * blocks, rows, width), BF),
            pltpu.VMEM((blocks, rows, width), F32),
            pltpu.VMEM((rows, width), F32),
            pltpu.VMEM((rows, width), F32),
            pltpu.VMEM((8, width), F32),
            pltpu.SemaphoreType.DMA((3,)),
            pltpu.SemaphoreType.DMA((2 * blocks + 1,)),
        ],
        compiler_params=params_for(),
        name="ffn",
    )(
        first_sum, cross_mixed, own_cotangent, matches, counts, weights, weights, weights,
        head_rows, row_bias, norm_gain,
    )

    depth, tasks = lax.axis_size("dp"), lax.axis_size("task")
    by_chain = depth == 4 and tasks == 4 and cores == 2

    if by_chain:
        block_order = [*range(8, block_count), 7, 5, 6, 4, 3, 0, 1, 2]
        chain_rows = width // depth
        pair_rows = 8 * len(pairs_of(tasks))
        dma = pltpu.SemaphoreType.DMA
        last = images * groups - 1

        def at_step(make):
            def index_map(step):
                now = jnp.minimum(step, last)
                return make(now // groups, now - groups * (now // groups))

            return index_map

        def ahead(step):
            return jnp.minimum(step + 1, 2 * blocks)

        def once(shape):
            return pl.BlockSpec(
                shape, lambda step: (0,) * len(shape), pipeline_mode=pl.Buffered(1)
            )

        step_q = pl.BlockSpec((padded, SLAB), at_step(lambda i, g: (i, g)))
        step_k = pl.BlockSpec((keys, SLAB), at_step(lambda i, g: (i, g)))

        small_half = pltpu.VMEM((24, half), F32)
        (
            context_grad, token_grad, update_parts, small_out, gram_rows, block_far, *_,
        ) = pl.pallas_call(
            functools.partial(
                back_kernel, depth, tasks, images, groups, valid, block_order
            ),
            grid=(images * groups + 1,),
            out_shape=(
                key_rows, low_rows,
                jax.ShapeDtypeStruct((block_count, chain_rows, half), BF),
                small_shape,
                jax.ShapeDtypeStruct((16, 128), F32),
                low_rows,
                jax.ShapeDtypeStruct((block_count, width, half), BF),
                jax.ShapeDtypeStruct((2, block_count, width // 2, half), BF),
                key_rows, key_rows,
            ),
            in_specs=[
                pl.BlockSpec(memory_space=pltpu.SMEM),
                pl.BlockSpec((None, keys, width), at_step(own_image)),
                step_q, step_k, step_k,
                pl.BlockSpec((1, 8, stack), at_step(lambda i, g: (i * groups + g, 0, 0))),
                step_q,
                once((rows, width)), once((5, width, width)), once(row_bias.shape),
                once(norm_gain.shape),
                once((3, rows, width)), once((rows, width)), once(total_shape.shape),
                once((rows, width)), once((rows, width)), once((24, width)),
                any_spec(), any_spec(),
                once((1, width, rows)), once((1, rows, width)),
                pl.BlockSpec((1, width, rows), lambda step: (ahead(step) // blocks, 0, 0)),
                pl.BlockSpec((1, rows, width), lambda step: (ahead(step), 0, 0)),
            ],
            out_specs=(
                any_spec(), once((rows, width)), any_spec(), once((24, width)), once((16, 128)),
                *[any_spec()] * 5,
            ),
            scratch_shapes=[
                pltpu.VMEM((width, keys), BF),
                pltpu.VMEM((width, width), F32),
                pltpu.VMEM((width, width), F32),
                pltpu.VMEM((rows, width), BF),
                pltpu.VMEM((3, rows, width), BF),
                pltpu.VMEM((3, width, width), BF),
                dma((3,)),
                dma((2,)),
                *ContextGrad.scratch(keys, width),
                *Chain.scratch(block_count, chain_rows, half, tasks),
                pltpu.VMEM((24, width), F32),
                small_half, small_half, small_half, small_half,
                pltpu.VMEM((tasks, 24, half), F32),
                pltpu.VMEM((2, 24, half), F32),
                pltpu.VMEM((pair_rows, half), F32),
                pltpu.VMEM((2 * tasks, 16, 128), F32),
                pltpu.VMEM((2, 16, 128), F32),
                pltpu.VMEM((block_count, chain_rows // tasks, half), BF),
                pltpu.VMEM((block_count, chain_rows, half), BF),
                dma((2,)),
                dma((2,)),
                dma((2, tasks - 1)),
                dma((2, depth - 1)),
                dma((2,)),
                dma((2, 2 * tasks - 1)),
                dma((2, 2, depth - 1)),
                dma((2, GROUPS)),
                dma((2, GROUPS, tasks - 1)),
                dma((GROUPS,)),
            ],
            compiler_params=params_for(collective_id=1, has_side_effects=True),
            name="backward",
        )(
            task_order, memory, cross_query, keys_act, values_act, cross_total, mixed_grad,
            tokens, weights, row_bias, norm_gain, qkv, self_mixed, self_total, first_sum,
            second_grad, ffn_small, weights, block_rows, left, right, left, right,
        )
        tile = chain_rows // images
        (
            param_update, memory_grad, query_grad, block_out, head_update, row_update, gain_update,
            gram,
        ) = pl.pallas_call(
            functools.partial(spread_kernel, images, valid, tasks, block_order),
            grid=(images,),
            out_shape=(
                jax.ShapeDtypeStruct((chain_rows, block_count, half), F32),
                key_rows,
                jax.ShapeDtypeStruct((images * valid, width), BF),
                jax.ShapeDtypeStruct((all_images * valid, width), BF),
                jax.ShapeDtypeStruct((8, half), F32),
                jax.ShapeDtypeStruct((3, 2, width), F32),
                jax.ShapeDtypeStruct((3, width), F32),
                jax.ShapeDtypeStruct((tasks, tasks), F32),
            ),
            in_specs=[
                pl.BlockSpec((block_count, tile, half), lambda r: (0, r, 0)),
                pl.BlockSpec((keys, width), lambda r: (r, 0)),
                rows_spec, rows_spec, rows_spec, small_spec, const((16, 128), 0, 0),
            ],
            out_specs=(
                pl.BlockSpec((tile, block_count, half), lambda r: (r, 0, 0)),
                pl.BlockSpec((keys, width), lambda r: (r, 0)),
                const((images * valid, width), 0, 0),
                const((all_images * valid, width), 0, 0),
                const((8, half), 0, 0), const((3, 2, width), 0, 0, 0),
                const((3, width), 0, 0), const((tasks, tasks), 0, 0),
            ),
            compiler_params=params_for(),
            name="spread",
        )(update_parts, context_grad, token_grad, block_rows, block_far, small_out, gram_rows)
        return (
            block_out[None], query_grad[None], memory_grad[None], param_update, head_update,
            row_update, gain_update, gram,
        )

    def unpad(array):
        return array.reshape(images, padded, width)[:, :valid].reshape(1, images * valid, width)

    block_out = lax.all_gather(unpad(block_rows), "tensor", axis=1, tiled=True)
    cross_query_grad, context_grad, key_wg, value_wg, cross_small = pl.pallas_call(
        cross_back_kernel,
        grid=(images, groups),
        in_specs=[
            context_all, slab_q, slab_k, slab_k, slab_t, slab_q, slab_w(5), slab_w(6),
        ],
        out_specs=(
            slab_q,
            pl.BlockSpec((keys, width), lambda i, g: (i, 0)),
            const((width, width), 0, 0), const((width, width), 0, 0), small_spec,
        ),
        scratch_shapes=[
            pltpu.VMEM((width, keys), BF),
            pltpu.VMEM((keys, width), F32),
            pltpu.VMEM((width, width), F32),
            pltpu.VMEM((width, width), F32),
        ],
        out_shape=(low_rows, key_rows, one_block, one_block, small_shape),
        compiler_params=params_for(),
        name="cross_backward",
    )(memory, cross_query, keys_act, values_act, cross_total, mixed_grad, weights, weights)

    token_grad, self_wg, self_small = pl.pallas_call(
        functools.partial(self_back_kernel, images, valid),
        grid=(1,),
        out_shape=(
            low_rows, jax.ShapeDtypeStruct((5, width, width), BF), small_shape,
        ),
        in_specs=[
            rows_spec, const((5, width, width), 0, 0, 0), row_spec, gain_spec,
            const((3, rows, width), 0, 0, 0), rows_spec, const(total_shape.shape, 0, 0, 0),
            rows_spec, rows_spec, rows_spec,
        ],
        out_specs=(
            rows_spec, const((5, width, width), 0, 0, 0), small_spec,
        ),
        scratch_shapes=[pltpu.VMEM((3, rows, width), BF)],
        compiler_params=params_for(),
        name="self_backward",
    )(
        tokens, weights, row_bias, norm_gain, qkv, self_mixed, self_total, first_sum, second_grad,
        cross_query_grad,
    )

    query_grad = unpad(token_grad)
    memory_grad = context_grad[None]

    small = self_small + cross_small + ffn_small
    product = functools.partial(jnp.einsum, "dr,jre->jde", preferred_element_type=F32)
    grad_in = product(left[0], right[:blocks]).astype(BF)
    grad_out = product(left[1], right[blocks : 2 * blocks]).astype(BF)
    cross_out_wg = product(left[2], right[2 * blocks :])[0].astype(BF)
    grads = jnp.concatenate(
        [self_wg, jnp.stack([key_wg, value_wg, cross_out_wg]), grad_in, grad_out], axis=0
    )
    swap = [(0, 1), (1, 0)]
    grads = (
        grads[:, :, :half].astype(F32) + lax.ppermute(grads[:, :, half:], "tensor", swap).astype(F32)
    ).astype(BF)
    head_small = small[:8, :half] + lax.ppermute(small[:8, half:], "tensor", swap)
    row_small = lax.psum(small[8:17], ("dp", "tensor"))
    head_small = lax.psum(head_small, "dp")
    shard = lax.psum_scatter(grads, "dp", scatter_dimension=1, tiled=True)
    all_shards = lax.all_gather(shard, "task", axis=0, tiled=False)
    all_head = lax.all_gather(head_small, "task", axis=0, tiled=False)
    all_row = lax.all_gather(row_small, "task", axis=0, tiled=False)
    tasks = all_shards.shape[0]
    share_rows = shard.shape[1]
    sums = pl.pallas_call(
        gram_kernel,
        grid=(block_count,),
        out_shape=jax.ShapeDtypeStruct((tasks * tasks, half), F32),
        in_specs=[pl.BlockSpec((tasks, 1, share_rows, half), lambda k: (0, k, 0, 0))],
        out_specs=const((tasks * tasks, half), 0, 0),
        compiler_params=params_for(),
        name="gram",
    )(all_shards)
    upper = jnp.sum(sums, axis=1).reshape(tasks, tasks)
    gram_weights = upper + upper.T - jnp.diag(jnp.diag(upper))
    gram_weights = lax.psum(gram_weights, ("dp", "tensor"))
    gram_heads = jnp.einsum("axy,bxy->ab", all_head, all_head, precision=highest)
    gram_heads = lax.psum(gram_heads, "tensor")
    gram = gram_weights + gram_heads + jnp.einsum(
        "axy,bxy->ab", all_row, all_row, precision=highest
    )
    task_weights = combine_weights(gram, task_order)
    tile = 64 if share_rows % 64 == 0 else share_rows
    param_update = pl.pallas_call(
        update_kernel,
        grid=(share_rows // tile,),
        out_shape=jax.ShapeDtypeStruct((share_rows, block_count, half), F32),
        in_specs=[
            pl.BlockSpec(memory_space=pltpu.SMEM),
            pl.BlockSpec((tasks, block_count, tile, half), lambda r: (0, 0, r, 0)),
        ],
        out_specs=pl.BlockSpec((tile, block_count, half), lambda r: (r, 0, 0)),
        compiler_params=params_for(),
        name="update",
    )(task_weights, all_shards)
    head_bias_update = jnp.einsum("a,axy->xy", task_weights, all_head, precision=highest)
    row_update = jnp.einsum("a,axy->xy", task_weights, all_row, precision=highest)
    return (
        block_out, query_grad, memory_grad, param_update, head_bias_update,
        row_update[:6].reshape(3, 2, width), row_update[6:9], gram,
    )


def solution(mesh):
    return jax.shard_map(
        body,
        mesh=mesh,
        in_specs=(
            P("task", "dp", None),
            P("task", "dp", None),
            P("task", "dp", None),
            P("task", "dp", None),
            P("task", "dp"),
            P(),
            P(None, None, "tensor"),
            P(None, "tensor"),
            P(),
            P(),
        ),
        out_specs=(
            P("task", "dp", None),
            P("task", ("dp", "tensor"), None),
            P("task", ("dp", "tensor"), None),
            P("dp", None, "tensor"),
            P(None, "tensor"),
            P(),
            P(),
            P(),
        ),
        check_vma=False,
    )
```

```python
import functools

import jax
import jax.numpy as jnp
from jax import lax
from jax.experimental import pallas as pl
from jax.experimental.pallas import tpu as pltpu
from jax.sharding import PartitionSpec as P

HD = 64
GROUP = 4
SLAB = GROUP * HD
BF = jnp.bfloat16
F32 = jnp.float32
MESH_ID = pl.DeviceIdType.MESH
highest = lax.Precision.HIGHEST
VMEM_LIMIT = 63 * 2**20


def combine_weights(gram_matrix, order_list):
    task_count = gram_matrix.shape[0]
    task_index = jnp.arange(task_count, dtype=jnp.int32)
    summed = jnp.zeros((task_count,), F32)
    for own_task in range(task_count):
        coeffs = (task_index == own_task).astype(F32)
        for position in range(task_count):
            chosen = (task_index == order_list[position]).astype(F32)
            column = jnp.sum(gram_matrix * chosen[None, :], axis=1)
            inner_dot = jnp.sum(coeffs * column)
            square = jnp.sum(chosen * column)
            others = (order_list[position] != own_task).astype(F32)
            coeffs = coeffs - others * jnp.minimum(inner_dot, 0.0) / (square + 1e-06) * chosen
        summed = summed + coeffs
    return summed


def mm(a, b):
    return jnp.dot(a, b, preferred_element_type=F32)


def mm_nt(a, b):
    return lax.dot_general(a, b, (((1,), (1,)), ((), ())), preferred_element_type=F32)


def mm_tn(a, b):
    return lax.dot_general(a, b, (((0,), (0,)), ((), ())), preferred_element_type=F32)


def row_of(row_ref, which):
    return row_ref[which // 2, which % 2 : which % 2 + 1].astype(F32)


def gain_of(gain_ref, which):
    return gain_ref[which : which + 1].astype(F32)


def norm_parts(residual):
    row_mean = jnp.mean(residual, axis=-1, keepdims=True)
    centred = residual - row_mean
    variance = jnp.mean(centred * centred, axis=-1, keepdims=True)
    scale = lax.rsqrt(variance + 1e-05)
    return centred * scale, scale


def norm_back(normed, scale, gain_row, grad):
    scaled = grad * gain_row
    first = jnp.mean(scaled, axis=-1, keepdims=True)
    second = jnp.mean(scaled * normed, axis=-1, keepdims=True)
    return scale * (scaled - first - normed * second)


def rows_sum(value):
    return jnp.sum(value, axis=0, keepdims=True)


def gelu_tanh(hidden):
    square = hidden * hidden
    tanh = jnp.tanh(hidden * (0.7978845608028654 + 0.7978845608028654 * 0.044715 * square))
    half = 0.5 * (1.0 + tanh)
    inner = 0.7978845608028654 + 0.7978845608028654 * 3 * 0.044715 * square
    return hidden * half, half + 0.5 * hidden * (1.0 - tanh * tanh) * inner


def head_mask(head, rows, dtype):
    lane = lax.broadcasted_iota(jnp.int32, (rows, SLAB), 1)
    return (lane // HD == head).astype(F32).astype(dtype)


def stack_heads(slab):
    return jnp.concatenate(
        [slab * head_mask(head, slab.shape[0], slab.dtype) for head in range(GROUP)], axis=0
    )


def unstack_heads(stacked):
    rows = stacked.shape[0] // GROUP
    total = None
    for head in range(GROUP):
        part = stacked[head * rows : (head + 1) * rows] * head_mask(head, rows, stacked.dtype)
        total = part if total is None else total + part
    return total


def scores_of(query_stack, key_slab, valid):
    scores = mm_nt(key_slab, query_stack)
    if valid < key_slab.shape[0]:
        row = lax.broadcasted_iota(jnp.int32, scores.shape, 0)
        scores = jnp.where(row < valid, scores, -1e30)
    return scores


def attend(query_slab, key_slab, value_slab, valid):
    scores = scores_of(stack_heads(query_slab * HD ** (-0.5)), key_slab, valid)
    row_max = jnp.max(scores, axis=0, keepdims=True)
    exps = jnp.exp(scores - row_max)
    total = jnp.sum(exps, axis=0, keepdims=True)
    probs = (exps * (1.0 / total)).astype(BF)
    mixed = unstack_heads(mm_tn(value_slab, probs).T)
    return mixed, row_max + jnp.log(total)


def attend_back(query_slab, key_slab, value_slab, log_total, grad_slab, valid):
    query_stack = stack_heads(query_slab * HD ** (-0.5))
    grad_stack = stack_heads(grad_slab)
    probs = jnp.exp(scores_of(query_stack, key_slab, valid) - log_total)
    grad_value = mm(probs.astype(BF), grad_stack)
    grad_probs = mm_nt(value_slab, grad_stack)
    inner = jnp.sum(probs * grad_probs, axis=0, keepdims=True)
    grad_scores = (probs * (grad_probs - inner)).astype(BF)
    grad_key = mm(grad_scores, query_stack)
    grad_query = unstack_heads(mm_tn(key_slab, grad_scores).T) * HD ** (-0.5)
    return grad_query.astype(BF), grad_key.astype(BF), grad_value.astype(BF)


def pad_rows(source_ref, target_ref, images, valid):
    first = lax.axis_index("tensor") == 0
    padded = target_ref.shape[0] // images
    for image in range(images):
        here, there = (
            source_ref[(core * images + image) * valid : (core * images + image + 1) * valid]
            for core in range(2)
        )
        rows = jnp.where(first, here.astype(F32), there.astype(F32))
        fill = jnp.zeros((padded - valid, rows.shape[1]), F32)
        target_ref[image * padded : (image + 1) * padded] = jnp.concatenate(
            [rows, fill], axis=0
        ).astype(target_ref.dtype)


def gather_kernel(images, valid, own_ref, bias_ref, queries_ref, cotangent_ref, full_ref,
                  full_bias_ref, tokens_ref, own_cotangent_ref, turned, bias_own, remote_send,
                  remote_recv, local_sem):
    step, steps = pl.program_id(0), pl.num_programs(0)
    other = 1 - lax.axis_index("tensor")
    rows, _, width = own_ref.shape
    near, far = pl.ds(0, width), pl.ds(width, width)

    def copies(chunk):
        at = pl.ds(pl.multiple_of(chunk * rows, rows), rows)
        source = turned.at[:, at]
        return (
            pltpu.make_async_remote_copy(
                source, full_ref.at[:, at, far], remote_send.at[chunk], remote_recv.at[chunk],
                device_id={"tensor": other}, device_id_type=MESH_ID,
            ),
            pltpu.make_async_copy(source, full_ref.at[:, at, near], local_sem.at[chunk]),
        )

    def bias_copies():
        return (
            pltpu.make_async_remote_copy(
                bias_own, full_bias_ref.at[:, far], remote_send.at[steps], remote_recv.at[steps],
                device_id={"tensor": other}, device_id_type=MESH_ID,
            ),
            pltpu.make_async_copy(bias_own, full_bias_ref.at[:, near], local_sem.at[steps]),
        )

    @pl.when(step == 0)
    def _():
        barrier = pltpu.get_barrier_semaphore()
        pl.semaphore_signal(barrier, inc=1, device_id={"tensor": other}, device_id_type=MESH_ID)
        pl.semaphore_wait(barrier, 1)
        bias_own[...] = jnp.zeros_like(bias_own)
        bias_own[0 : bias_ref.shape[0]] = bias_ref[...]
        for copy in bias_copies():
            copy.start()

    turned[:, pl.ds(pl.multiple_of(step * rows, rows), rows)] = jnp.swapaxes(own_ref[...], 0, 1)
    for copy in copies(step):
        copy.start()

    @pl.when(step == steps - 1)
    def _():
        pad_rows(queries_ref, tokens_ref, images, valid)
        pad_rows(cotangent_ref, own_cotangent_ref, images, valid)
        for copy in bias_copies():
            copy.wait()

        def finish(chunk, carry):
            for copy in copies(chunk):
                copy.wait()
            return carry

        lax.fori_loop(0, steps, finish, 0)


def any_spec():
    return pl.BlockSpec(memory_space=pl.ANY)


def whole_spec():
    return pl.BlockSpec(memory_space=pltpu.VMEM)


def params_for(**keys):
    return pltpu.CompilerParams(vmem_limit_bytes=VMEM_LIMIT, **keys)


def self_kernel(images, valid, tokens_ref, weight_ref, head_ref, row_ref, gain_ref, qkv_ref,
                mixed_ref, total_ref, sum_ref, cross_query_ref):
    tokens = tokens_ref[...]
    rows = tokens.shape[0] // images
    width = tokens.shape[1]
    qkv_ref[0] = (mm(tokens, weight_ref[0]) + head_ref[0:1].astype(F32)).astype(BF)
    qkv_ref[1] = mm(tokens, weight_ref[1]).astype(BF)
    qkv_ref[2] = (mm(tokens, weight_ref[2]) + head_ref[1:2].astype(F32)).astype(BF)
    for image in range(images):
        at = slice(image * rows, (image + 1) * rows)
        for group in range(width // SLAB):
            lanes = slice(group * SLAB, (group + 1) * SLAB)
            mixed, log_total = attend(
                qkv_ref[0, at, lanes], qkv_ref[1, at, lanes], qkv_ref[2, at, lanes], valid
            )
            mixed_ref[at, lanes] = mixed.astype(BF)
            total_ref[image * (width // SLAB) + group] = jnp.broadcast_to(
                log_total, total_ref.shape[1:]
            )
    first_sum = tokens.astype(F32) + mm_nt(mixed_ref[...], weight_ref[3]) + row_of(row_ref, 0)
    sum_ref[...] = first_sum
    first_low = (norm_parts(first_sum)[0] * gain_of(gain_ref, 0) + row_of(row_ref, 1)).astype(BF)
    cross_query_ref[...] = (mm(first_low, weight_ref[4]) + head_ref[2:3].astype(F32)).astype(BF)


def cross_kernel(context_ref, query_ref, key_w_ref, value_w_ref, head_ref, key_ref, value_ref,
                 mixed_ref, total_ref):
    context = context_ref[...]
    key_ref[...] = mm(context, key_w_ref[0]).astype(BF)
    value_ref[...] = (mm(context, value_w_ref[0]) + head_ref[3:4].astype(F32)).astype(BF)
    mixed, log_total = attend(query_ref[...], key_ref[...], value_ref[...], key_ref.shape[0])
    mixed_ref[...] = mixed.astype(BF)
    total_ref[0] = jnp.broadcast_to(log_total, total_ref.shape[1:])


def ffn_kernel(
    images, blocks, sum_ref, mixed_ref, cotangent_ref, matches_ref, counts_ref, cross_w_ref, in_ref,
    out_ref, head_ref, row_ref, gain_ref,
    block_ref, left_ref, right_ref, mixed_grad_ref, residual_ref, small_ref,
    second_sum, second_low, left, right, slope, branch, third_grad, hidden_bias, left_sem, right_sem,
):
    step = pl.program_id(0)
    per = in_ref.shape[0]
    half_steps = blocks // per
    rows = sum_ref.shape[0] // images

    def left_copy(which):
        return pltpu.make_async_copy(left.at[which], left_ref.at[which], left_sem.at[which])

    def right_copy(which):
        return pltpu.make_async_copy(right.at[which], right_ref.at[which], right_sem.at[which])

    mixed_copy = pltpu.make_async_copy(
        mixed_ref, right_ref.at[2 * blocks], right_sem.at[2 * blocks]
    )

    @pl.when(step == 0)
    def _():
        mixed_copy.start()
        first_out = norm_parts(sum_ref[...])[0] * gain_of(gain_ref, 0) + row_of(row_ref, 1)
        second = first_out + mm_nt(mixed_ref[...], cross_w_ref[0]) + row_of(row_ref, 2)
        second_sum[...] = second
        second_low[...] = (
            norm_parts(second)[0] * gain_of(gain_ref, 1) + row_of(row_ref, 3)
        ).astype(BF)
        branch[...] = jnp.zeros_like(branch)
        small_ref[...] = jnp.zeros_like(small_ref)
        hidden_bias[0:blocks] = head_ref[4 : 4 + blocks].astype(F32)
        left[0] = second_low[...].T
        left_copy(0).start()

    @pl.when(step < half_steps)
    def _():
        low = second_low[...]
        pres = [
            mm(low, in_ref[k]) + hidden_bias[pl.ds(step * per + k, 1)] for k in range(per)
        ]
        total = branch[...]
        for k in range(per):
            act, grad = gelu_tanh(pres[k])
            act = act.astype(BF)
            slope[step * per + k] = grad
            right[blocks + step * per + k] = act
            right_copy(blocks + step * per + k).start()
            total = total + mm_nt(act, out_ref[k])
        branch[...] = total

    @pl.when(step == half_steps - 1)
    def _():
        second = norm_parts(second_sum[...])[0] * gain_of(gain_ref, 1) + row_of(row_ref, 3)
        third_sum = second + branch[...] + row_of(row_ref, 4)
        normed, scale = norm_parts(third_sum)
        block_ref[...] = (normed * gain_of(gain_ref, 2) + row_of(row_ref, 5)).astype(BF)
        count = matches_ref.shape[2]
        slot = lax.broadcasted_iota(jnp.int32, (rows, count), 0)
        box = lax.broadcasted_iota(jnp.int32, (rows, count), 1)
        grads = []
        for image in range(images):
            own = lax.axis_index("tensor") * images + image
            live = (matches_ref[0, pl.ds(own, 1)] == slot) & (box < counts_ref[0, own])
            mask = jnp.sum(jnp.where(live, 1.0, 0.0), axis=1, keepdims=True)
            cot = cotangent_ref[image * rows : (image + 1) * rows].astype(F32)
            grads.append(cot * mask)
        out_grad = jnp.concatenate(grads, axis=0)
        grad = norm_back(normed, scale, gain_of(gain_ref, 2), out_grad)
        third_grad[...] = grad
        left[1] = grad.astype(BF).T
        left_copy(1).start()
        small_ref[12:13] = rows_sum(grad)
        small_ref[13:14] = rows_sum(out_grad)
        small_ref[16:17] = rows_sum(out_grad * normed)
        branch[...] = jnp.zeros_like(branch)

    @pl.when(step >= half_steps)
    def _():
        ffn_low = third_grad[...].astype(BF)
        first = (step - half_steps) * per
        grads = [mm(ffn_low, out_ref[k]) for k in range(per)]
        total = branch[...]
        for k in range(per):
            grad_low = (grads[k] * slope[first + k]).astype(BF)
            right[first + k] = grad_low
            right_copy(first + k).start()
            small_ref[pl.ds(4 + first + k, 1)] = rows_sum(grad_low.astype(F32))
            total = total + mm_nt(grad_low, in_ref[k])
        branch[...] = total

    @pl.when(step == 2 * half_steps - 1)
    def _():
        second_in = third_grad[...] + branch[...]
        normed, scale = norm_parts(second_sum[...])
        grad = norm_back(normed, scale, gain_of(gain_ref, 1), second_in)
        residual_ref[...] = grad
        small_ref[10:11] = rows_sum(grad)
        small_ref[11:12] = rows_sum(second_in)
        small_ref[15:16] = rows_sum(second_in * normed)
        cross_low = grad.astype(BF)
        left[2] = cross_low.T
        left_copy(2).start()
        mixed_grad_ref[...] = mm(cross_low, cross_w_ref[0]).astype(BF)
        mixed_copy.wait()
        for which in range(3):
            left_copy(which).wait()
        for which in range(2 * blocks):
            right_copy(which).wait()


def cross_back_step(
    image, group, query_ref, key_ref, value_ref, total_ref, mixed_grad_ref, small_ref, context_t,
    key_acc, value_acc, unit,
):
    grad_query, grad_key, grad_value = attend_back(
        query_ref[...], key_ref[...], value_ref[...], total_ref[0, 0:1], mixed_grad_ref[...],
        key_ref.shape[0],
    )
    lanes = pl.ds(pl.multiple_of(group * SLAB, SLAB), SLAB)
    small_ref[2:3, lanes] += rows_sum(grad_query.astype(F32))
    small_ref[3:4, lanes] += rows_sum(grad_value.astype(F32))
    unit(0)
    key_wg = mm(context_t[...], grad_key)
    value_wg = mm(context_t[...], grad_value)

    @pl.when(image == 0)
    def _():
        key_acc[:, lanes] = key_wg
        value_acc[:, lanes] = value_wg

    @pl.when(image > 0)
    def _():
        key_acc[:, lanes] += key_wg
        value_acc[:, lanes] += value_wg

    unit(1)
    return grad_query, grad_key, grad_value


def cross_back_kernel(
    context_ref, query_ref, key_ref, value_ref, total_ref, mixed_grad_ref, key_w_ref, value_w_ref,
    query_grad_ref, context_grad_ref, key_wg_ref, value_wg_ref, small_ref,
    context_t, acc, key_acc, value_acc,
):
    image, group = pl.program_id(0), pl.program_id(1)
    images, groups = pl.num_programs(0), pl.num_programs(1)

    @pl.when((image == 0) & (group == 0))
    def _():
        small_ref[...] = jnp.zeros_like(small_ref)

    @pl.when(group == 0)
    def _():
        context_t[...] = context_ref[...].T

    query_grad_ref[...], grad_key, grad_value = cross_back_step(
        image, group, query_ref, key_ref, value_ref, total_ref, mixed_grad_ref,
        small_ref, context_t, key_acc, value_acc, lambda part: None,
    )
    context_part = mm_nt(grad_key, key_w_ref[0]) + mm_nt(grad_value, value_w_ref[0])

    @pl.when(group == 0)
    def _():
        acc[...] = context_part

    @pl.when(group > 0)
    def _():
        acc[...] += context_part

    @pl.when(group == groups - 1)
    def _():
        context_grad_ref[...] = acc[...].astype(BF)

    @pl.when((image == images - 1) & (group == groups - 1))
    def _():
        key_wg_ref[...] = key_acc[...].astype(BF)
        value_wg_ref[...] = value_acc[...].astype(BF)


def self_back(
    images, valid, tokens_ref, weight_ref, row_ref, gain_ref, qkv_ref, mixed_ref, total_ref, sum_ref,
    residual_ref, cross_query_grad_ref, small_ref, qkv_grad, emit, unit, used=lambda: None,
):
    tokens = tokens_ref[...]
    rows = tokens.shape[0] // images
    width = tokens.shape[1]
    normed, scale = norm_parts(sum_ref[...])
    first_low = (normed * gain_of(gain_ref, 0) + row_of(row_ref, 1)).astype(BF)
    cross_query_grad = cross_query_grad_ref[...]
    first_low_t = first_low.T
    emit(4, lambda lanes: mm(first_low_t, cross_query_grad_ref[:, lanes]))
    unit()
    first_in = residual_ref[...] + mm_nt(cross_query_grad, weight_ref[4])
    first_grad = norm_back(normed, scale, gain_of(gain_ref, 0), first_in)
    small_ref[8:9] = rows_sum(first_grad)
    small_ref[9:10] = rows_sum(first_in)
    small_ref[14:15] = rows_sum(first_in * normed)
    unit()
    self_low = first_grad.astype(BF)
    self_low_t = self_low.T
    emit(3, lambda lanes: mm(self_low_t, mixed_ref[:, lanes]))
    unit()
    mixed_grad = mm(self_low, weight_ref[3]).astype(BF)
    used()
    for image in range(images):
        at = slice(image * rows, (image + 1) * rows)
        for group in range(width // SLAB):
            lanes = slice(group * SLAB, (group + 1) * SLAB)
            grads = attend_back(
                qkv_ref[0, at, lanes], qkv_ref[1, at, lanes], qkv_ref[2, at, lanes],
                total_ref[image * (width // SLAB) + group, 0:1], mixed_grad[at, lanes], valid,
            )
            for which in range(3):
                qkv_grad[which, at, lanes] = grads[which]
            unit()
    tokens_t = tokens.T
    total = first_grad
    for which in range(3):
        grad = qkv_grad[which]
        emit(which, lambda lanes, which=which: mm(tokens_t, qkv_grad[which, :, lanes]))
        unit()
        total = total + mm_nt(grad, weight_ref[which])
    small_ref[0:1] = rows_sum(qkv_grad[0].astype(F32))
    small_ref[1:2] = rows_sum(qkv_grad[2].astype(F32))
    return total


def self_back_kernel(
    images, valid, tokens_ref, weight_ref, row_ref, gain_ref, qkv_ref, mixed_ref, total_ref, sum_ref,
    residual_ref, cross_query_grad_ref, query_grad_ref, wg_ref, small_ref, qkv_grad,
):
    small_ref[...] = jnp.zeros_like(small_ref)

    def emit(block, value):
        for lane in range(0, wg_ref.shape[2], SLAB):
            lanes = slice(lane, lane + SLAB)
            wg_ref[block, :, lanes] = value(lanes).astype(BF)

    query_grad_ref[...] = self_back(
        images, valid, tokens_ref, weight_ref, row_ref, gain_ref, qkv_ref, mixed_ref, total_ref,
        sum_ref, residual_ref, cross_query_grad_ref, small_ref, qkv_grad, emit, lambda: None,
    ).astype(BF)


def task_peers(tasks):
    me = lax.axis_index("task")
    return [lax.rem(me + shift, tasks) for shift in range(1, tasks)]


def task_senders(tasks):
    me = lax.axis_index("task")
    return [lax.rem(me + tasks - shift, tasks) for shift in range(1, tasks)]


def send(source, target, send_sem, recv_sem, **device):
    return pltpu.make_async_remote_copy(
        source, target, send_sem, recv_sem, device_id=device, device_id_type=MESH_ID
    )


def greet(depth, tasks):
    me = lax.axis_index("dp")
    barrier = pltpu.get_barrier_semaphore()
    other = 1 - lax.axis_index("tensor")
    for peer in task_peers(tasks):
        pl.semaphore_signal(barrier, inc=1, device_id={"task": peer}, device_id_type=MESH_ID)
        pl.semaphore_signal(
            barrier, inc=1, device_id={"task": peer, "tensor": other}, device_id_type=MESH_ID
        )
    for shift in range(1, depth):
        pl.semaphore_signal(
            barrier, inc=1, device_id={"dp": lax.rem(me + shift, depth)}, device_id_type=MESH_ID
        )
    pl.semaphore_signal(barrier, inc=1, device_id={"tensor": other}, device_id_type=MESH_ID)
    pl.semaphore_wait(barrier, 2 * (tasks - 1) + depth)


LAG = 2
SLOTS = 3
STAGES = 2


class Chain:
    def __init__(self, depth, tasks, refs):
        self.depth, self.tasks = depth, tasks
        (self.near, self.far, self.stage, self.passed, self.parts,
         self.far_send, self.far_recv, self.far_free, self.pass_send, self.pass_recv,
         self.part_send, self.part_recv) = refs
        self.chunks = self.passed.shape[1]
        self.rows, self.half = self.passed.shape[2:]
        self.me = lax.axis_index("dp")
        self.task = lax.axis_index("task")
        self.is_end = (self.me == 0) | (self.me == depth - 1)

    SCRATCH = 12

    @staticmethod
    def scratch(blocks, rows, half, tasks):
        chunks = 2 * blocks
        dma = pltpu.SemaphoreType.DMA
        return [
            pltpu.VMEM((2, chunks, rows, half), BF),
            pltpu.VMEM((SLOTS, 2, 2, rows, half), BF),
            pltpu.VMEM((STAGES, 2, 2, rows, half), BF),
            pltpu.VMEM((2, chunks, rows, half), BF),
            pltpu.VMEM((tasks, chunks, rows // tasks, half), BF),
            dma((STAGES,)),
            dma((SLOTS,)),
            pltpu.SemaphoreType.REGULAR,
            dma((2, chunks)),
            dma((2, chunks)),
            dma((blocks, tasks - 1)),
            dma((blocks, tasks - 1)),
        ]

    def far_copy(self, block):
        slot, stage = lax.rem(block, SLOTS), lax.rem(block, STAGES)
        return send(
            self.stage.at[stage], self.far.at[slot], self.far_send.at[stage], self.far_recv.at[slot],
            tensor=1 - lax.axis_index("tensor"),
        )

    def emit(self, block, value):
        block = jnp.int32(block)
        stage = lax.rem(block, STAGES)

        @pl.when(block >= STAGES)
        def _():
            self.far_copy(block).wait_send()

        @pl.when(block >= SLOTS)
        def _():
            pl.semaphore_wait(self.far_free, 1)

        size = self.half // 3
        for lane in range(0, self.half, size):
            lanes = slice(lane, lane + size)
            low = value(slice(self.half + lane, self.half + lane + size)).astype(BF)
            for way in range(2):
                for part in range(2):
                    row = (2 * way + part) * self.rows
                    self.stage[stage, way, part, :, lanes] = low[row : row + self.rows]
        self.far_copy(block).start()
        for lane in range(0, self.half, size):
            lanes = slice(lane, lane + size)
            low = value(lanes).astype(BF)
            for way in range(2):
                for part in range(2):
                    row = (2 * way + part) * self.rows
                    self.near[way, 2 * block + part, :, lanes] = low[row : row + self.rows]

    def absorb(self, block):
        block = jnp.int32(block)
        slot = lax.rem(block, SLOTS)
        self.far_copy(block).wait_recv()
        for way in range(2):
            chunks = pl.ds(2 * block, 2)
            self.near[way, chunks] = (
                self.near[way, chunks].astype(F32) + self.far[slot, way].astype(F32)
            ).astype(BF)

        @pl.when(block < self.chunks // 2 - SLOTS)
        def _():
            pl.semaphore_signal(
                self.far_free, inc=1, device_id={"tensor": 1 - lax.axis_index("tensor")},
                device_id_type=MESH_ID,
            )

    def pass_copy(self, way, chunk):
        piece = self.passed.at[way, chunk]
        target = self.me - 1 if way == 0 else self.me + 1
        return send(
            piece, piece, self.pass_send.at[way, chunk], self.pass_recv.at[way, chunk], dp=target
        )

    def part_rows(self, peer):
        size = self.rows // self.tasks
        return pl.ds(pl.multiple_of(peer * size, size), size)

    def part_copy(self, way, block, shift, peer):
        chunks = pl.ds(2 * block, 2)
        return send(
            self.passed.at[way, chunks, self.part_rows(peer)], self.parts.at[self.task, chunks],
            self.part_send.at[block, shift], self.part_recv.at[block, shift], task=peer,
        )

    def hops(self, way):
        return self.depth - 1 - self.me if way == 0 else self.me

    def units(self):
        return self.chunks + LAG * (self.depth - 1)

    def unit(self, index):
        for way in range(2):
            chunk = index - LAG * self.hops(way)

            @pl.when((chunk >= 0) & (chunk < self.chunks))
            def _(way=way, chunk=chunk):
                self.chunk_step(way, chunk)

    def chunk_step(self, way, chunk):
        first, last = self.hops(way) == 0, self.hops(way) == self.depth - 1
        block = chunk // 2
        own = self.near[way, chunk]

        @pl.when(first)
        def _():
            self.passed[way, chunk] = own

        @pl.when(jnp.logical_not(first))
        def _():
            self.pass_copy(way, chunk).wait_recv()
            self.passed[way, chunk] = (
                own.astype(F32) + self.passed[way, chunk].astype(F32)
            ).astype(BF)

        @pl.when(jnp.logical_not(last))
        def _():
            self.pass_copy(way, chunk).start()

        @pl.when(last & (chunk == 2 * block + 1))
        def _():
            for shift, peer in enumerate(task_peers(self.tasks)):
                self.part_copy(way, block, shift, peer).start()
            own_rows = self.part_rows(self.task)
            self.parts[self.task, chunk - 1] = self.passed[way, chunk - 1, own_rows]
            self.parts[self.task, chunk] = self.passed[way, chunk, own_rows]

    def wait_parts(self, block):
        for shift, peer in enumerate(task_senders(self.tasks)):
            landed = self.parts.at[peer, pl.ds(2 * block, 2)]
            send(
                landed, landed, self.part_send.at[block, shift], self.part_recv.at[block, shift],
                task=peer,
            ).wait_recv()

    def finish(self):
        def blocks(block, carry):
            for way in range(2):

                @pl.when(self.hops(way) != self.depth - 1)
                def _(way=way):
                    for part in range(2):
                        self.pass_copy(way, 2 * block + part).wait_send()

                @pl.when(self.hops(way) == self.depth - 1)
                def _(way=way):
                    for shift, peer in enumerate(task_peers(self.tasks)):
                        self.part_copy(way, block, shift, peer).wait_send()

            return carry

        lax.fori_loop(0, self.chunks // 2, blocks, 0)


def pairs_of(tasks):
    return [(a, b) for a in range(tasks) for b in range(a, tasks)]


def weights_of(gram, order_ref, tasks):
    totals = [0.0] * tasks
    for own in range(tasks):
        coeffs = [jnp.full_like(gram[0, 0], 1.0 if t == own else 0.0) for t in range(tasks)]
        for position in range(tasks):
            chosen = [
                jnp.where(order_ref[position] == t, 1.0, 0.0).astype(F32) for t in range(tasks)
            ]
            column = [sum(gram[t, j] * chosen[j] for j in range(tasks)) for t in range(tasks)]
            inner = sum(coeffs[t] * column[t] for t in range(tasks))
            square = sum(chosen[t] * column[t] for t in range(tasks))
            others = 1.0 - chosen[own]
            share = others * jnp.minimum(inner, 0.0) / (square + 1e-06)
            coeffs = [coeffs[t] - share * chosen[t] for t in range(tasks)]
        totals = [total + coeff for total, coeff in zip(totals, coeffs)]
    return totals


GROUPS = 4
UNITS = 2
TILE = 240


class ContextGrad:
    def __init__(self, key_grad, value_grad, weights, result, refs):
        self.grads, self.weights, self.result = (key_grad, value_grad), weights, result
        (self.staged, self.ring, self.done, self.staged_sem, self.ring_sem, self.done_sem) = refs
        self.tile, width = self.done.shape[1:]
        self.lanes = [pl.ds(0, width), pl.ds(width, width)]
        self.tiles = result.shape[0] // self.tile

    SCRATCH = 6

    @staticmethod
    def scratch(keys, width):
        dma = pltpu.SemaphoreType.DMA
        return [
            pltpu.VMEM((2, keys, SLAB), BF),
            pltpu.VMEM((2, TILE, 2 * width), BF),
            pltpu.VMEM((2, TILE, width), BF),
            dma((2,)),
            dma((2, 2)),
            dma((2,)),
        ]

    def staged_copies(self, image, group):
        keys = self.staged.shape[1]
        rows = pl.ds(pl.multiple_of(image * keys, keys), keys)
        lanes = pl.ds(pl.multiple_of(group * SLAB, SLAB), SLAB)
        return [
            pltpu.make_async_copy(
                self.staged.at[which], self.grads[which].at[rows, lanes], self.staged_sem.at[which]
            )
            for which in range(2)
        ]

    def put(self, step, image, group, values):
        @pl.when(step > 0)
        def _():
            self.settle()

        for which, value in enumerate(values):
            self.staged[which] = value
        for copy in self.staged_copies(image, group):
            copy.start()

    def settle(self):
        for copy in self.staged_copies(0, 0):
            copy.wait()

    def fetches(self, index):
        slot = lax.rem(index, 2)
        rows = pl.ds(pl.multiple_of(index * self.tile, self.tile), self.tile)
        return [
            pltpu.make_async_copy(
                self.grads[which].at[rows], self.ring.at[slot, :, self.lanes[which]],
                self.ring_sem.at[slot, which],
            )
            for which in range(2)
        ]

    def store(self, index):
        slot = lax.rem(index, 2)
        rows = pl.ds(pl.multiple_of(index * self.tile, self.tile), self.tile)
        return pltpu.make_async_copy(
            self.done.at[slot], self.result.at[rows], self.done_sem.at[slot]
        )

    def compute(self, index):
        @pl.when(index < self.tiles)
        def _():
            for copy in self.fetches(index):
                copy.wait()

            @pl.when(index + 1 < self.tiles)
            def _():
                for copy in self.fetches(index + 1):
                    copy.start()

            @pl.when(index >= 2)
            def _():
                self.store(index - 2).wait()

            slot = lax.rem(index, 2)
            total = mm_nt(self.ring[slot, :, self.lanes[0]], self.weights[0])
            total = total + mm_nt(self.ring[slot, :, self.lanes[1]], self.weights[1])
            self.done[slot] = total.astype(BF)
            self.store(index).start()

    def finish(self):
        for index in range(self.tiles - 2, self.tiles):
            self.store(jnp.int32(index)).wait()


def back_kernel(
    depth, tasks, images, groups, valid, block_order, order_ref, context_ref, query_ref, key_ref,
    value_ref, total_ref, mixed_grad_ref, tokens_ref, row_ref, gain_ref, qkv_ref, mixed_ref,
    self_total_ref, sum_ref, residual_ref, small_in_ref, all_w_ref, block_ref, left_ref, right_ref,
    *refs
):
    (
        context_grad_ref, query_grad_ref, update_ref, small_out_ref, gram_ref, block_far,
        key_grad, value_grad,
    ), refs = refs[:8], refs[8:]
    (
        context, context_t, key_acc, value_acc, cross_query_grad, qkv_grad, weights, block_sem,
        weight_sem, context_sem,
    ), refs = refs[:10], refs[10:]
    context_back = ContextGrad(
        key_grad, value_grad, weights.at[pl.ds(3, 2)], context_grad_ref,
        refs[: ContextGrad.SCRATCH],
    )
    refs = refs[ContextGrad.SCRATCH :]
    chain = Chain(depth, tasks, refs[: Chain.SCRATCH])
    refs = refs[Chain.SCRATCH :]
    gram_acc = refs[7]
    step = pl.program_id(0)
    cross_steps = images * groups
    half = chain.half
    is_end = chain.is_end
    pairs = pairs_of(tasks)

    def add_products(shares):
        for index, (a, b) in enumerate(pairs):
            product = shares[a] * shares[b]
            total = product[0:8]
            for row in range(8, product.shape[0], 8):
                total = total + product[row : row + 8]
            gram_acc[index * 8 : index * 8 + 8] += total

    def unit(index):
        chain.unit(index)
        since = index - LAG * (depth - 1) - 3
        block = since // 2

        @pl.when(is_end & (since >= 0) & (since == 2 * block))
        def _():
            chain.wait_parts(block)
            for part in range(2):
                add_products(
                    [chain.parts[t, 2 * block + part].astype(F32) for t in range(tasks)]
                )

    block_copy = send(
        block_ref, block_far, block_sem.at[0], block_sem.at[1], tensor=1 - lax.axis_index("tensor")
    )
    weight_copies = [
        pltpu.make_async_copy(all_w_ref.at[source], weights.at[target], weight_sem.at[index])
        for index, (source, target) in enumerate(
            [(pl.ds(0, 5), pl.ds(0, 5)), (pl.ds(5, 2), pl.ds(3, 2))]
        )
    ]

    def context_copy(image):
        keys = context.shape[0]
        own = lax.axis_index("tensor") * images + image
        rows = pl.ds(pl.multiple_of(own * keys, keys), keys)
        return pltpu.make_async_copy(context_ref.at[0, rows], context, context_sem)

    @pl.when(step == 0)
    def _():
        context_copy(0).start()
        weight_copies[0].start()
        greet(depth, tasks)
        block_copy.start()
        gram_acc[...] = jnp.zeros_like(gram_acc)
        refs[0][...] = small_in_ref[...]

    @pl.when(step < cross_steps)
    def _():
        image = step // groups
        group = step - image * groups

        chain.emit(step, lambda lanes: mm(left_ref[0], right_ref[0, :, lanes]))

        @pl.when(group == 0)
        def _():
            context_copy(image).wait()
            context_t[...] = context[...].T

            @pl.when(image + 1 < images)
            def _():
                context_copy(image + 1).start()

        def cross_unit(part):
            if part == 0:
                chain.absorb(step)
            unit(step * UNITS + part)

        grad_query, *grads = cross_back_step(
            image, group, query_ref, key_ref, value_ref, total_ref, mixed_grad_ref, refs[0],
            context_t, key_acc, value_acc, cross_unit,
        )
        context_back.put(step, image, group, grads)
        rows = grad_query.shape[0]
        cross_query_grad[
            pl.ds(pl.multiple_of(image * rows, rows), rows),
            pl.ds(pl.multiple_of(group * SLAB, SLAB), SLAB),
        ] = grad_query

        @pl.when(step == cross_steps - 1)
        def _():
            chain.emit(cross_steps, lambda lanes: key_acc[:, lanes])
            chain.emit(cross_steps + 1, lambda lanes: value_acc[:, lanes])

    @pl.when(step == cross_steps)
    def _():
        calls, done = [0], [cross_steps * UNITS]
        blocks = len(block_order)

        def self_unit():
            if calls[0] % 2 == 0:
                if done[0] % 2 == 0:
                    chain.absorb(done[0] // 2)
                unit(jnp.int32(done[0]))
                done[0] += 1
            calls[0] += 1

        context_back.settle()
        for copy in context_back.fetches(jnp.int32(0)):
            copy.start()
        weight_copies[0].wait()
        query_grad_ref[...] = self_back(
            images, valid, tokens_ref, weights, row_ref, gain_ref, qkv_ref, mixed_ref,
            self_total_ref, sum_ref, residual_ref, cross_query_grad, refs[0], qkv_grad,
            lambda block, value: chain.emit(block_order.index(block), value), self_unit,
            weight_copies[1].start,
        ).astype(BF)
        for block in range(-(-done[0] // 2), blocks):
            chain.absorb(block)
        weight_copies[1].wait()
        rest(
            chain, unit, context_back, done[0], order_ref, update_ref, small_out_ref, gram_ref, refs
        )
        for block in range(blocks - STAGES, blocks):
            chain.far_copy(jnp.int32(block)).wait_send()
        block_copy.wait()
        context_back.finish()


def rest(
    chain, unit, context_back, done, order_ref, update_ref, small_out_ref, gram_ref, refs
):
    (
        small, small_own, small_other, small_far, small_pass, small_all, small_both, gram_acc,
        gram_plane, gram_end, hop, out,
        small_far_sem, small_pass_sem, small_task_sem, small_dp_sem, small_core_sem,
        gram_plane_sem, gram_dp_sem, hop_sem, out_sem, update_sem,
    ) = refs
    depth, tasks, half = chain.depth, chain.tasks, chain.half
    me, task, core = (lax.axis_index(axis) for axis in ("dp", "task", "tensor"))
    is_end = chain.is_end
    top = me == 0
    pairs = pairs_of(tasks)
    own_lanes = pl.ds(pl.multiple_of(core * half, half), half)
    other_lanes = pl.ds(pl.multiple_of((1 - core) * half, half), half)
    small_own[0:8] = small[0:8, 0:half]
    small_own[8:] = small[8:, own_lanes]
    small_other[0:8] = small[0:8, half:]
    small_other[8:] = small[8:, other_lanes]
    small_copy = send(
        small_other, small_far, small_far_sem.at[0], small_far_sem.at[1], tensor=1 - core
    )
    small_copy.start()

    def small_hop():
        return send(
            small_pass, small_pass, small_pass_sem.at[0], small_pass_sem.at[1], dp=me - 1
        )

    def small_task_copy(shift, peer):
        return send(
            small_pass, small_all.at[task], small_task_sem.at[0, shift],
            small_task_sem.at[1, shift], task=peer,
        )

    def step(index, carry):
        unit(index)
        context_back.compute(index - done)

        @pl.when(index == done + 1 + LAG * chain.hops(0))
        def _():
            small_copy.wait_recv()
            total = small_own[...] + small_far[...]

            @pl.when(me == depth - 1)
            def _():
                small_pass[...] = total

            @pl.when(me < depth - 1)
            def _():
                small_hop().wait_recv()
                small_pass[...] += total

            @pl.when(me > 0)
            def _():
                small_hop().start()

            @pl.when(top)
            def _():
                for shift, peer in enumerate(task_peers(tasks)):
                    small_task_copy(shift, peer).start()
                small_all[task] = small_pass[...]

        return carry

    lax.fori_loop(done, max(chain.units() + 2, done + context_back.tiles), step, 0)

    @pl.when(top)
    def _():
        for shift, peer in enumerate(task_senders(tasks)):
            landed = small_all.at[peer]
            send(
                landed, landed, small_task_sem.at[0, shift], small_task_sem.at[1, shift], task=peer
            ).wait_recv()

    lanes = gram_plane.shape[2]
    plane = 2 * tasks
    mine = 2 * task + core

    def gram_copy(shift):
        to = lax.rem(mine + shift, plane)
        return send(
            gram_plane.at[mine], gram_plane.at[mine], gram_plane_sem.at[0, shift - 1],
            gram_plane_sem.at[1, shift - 1], task=to // 2, tensor=lax.rem(to, 2),
        )

    def gram_arrival(shift):
        place = lax.rem(mine + plane - shift, plane)
        return send(
            gram_plane.at[place], gram_plane.at[place], gram_plane_sem.at[0, shift - 1],
            gram_plane_sem.at[1, shift - 1], task=place // 2, tensor=lax.rem(place, 2),
        )

    def gram_dp_copy(end, shift):
        return send(
            gram_end.at[end], gram_end.at[end], gram_dp_sem.at[0, end, shift],
            gram_dp_sem.at[1, end, shift], dp=lax.rem((depth - 1) * end + shift + 1, depth),
        )

    def one_number(values):
        return jnp.sum(jnp.sum(values, axis=0, keepdims=True), axis=1, keepdims=True)

    @pl.when(top & (task == 0))
    def _():
        small_values = [small_all[t] for t in range(tasks)]
        for index, (a, b) in enumerate(pairs):
            product = small_values[a] * small_values[b]
            gram_acc[index * 8 : index * 8 + 8] += product[0:8] + product[8:16] + product[16:24]

    @pl.when(is_end)
    def _():
        gram_plane[mine] = jnp.zeros(gram_plane.shape[1:], F32)
        for index in range(len(pairs)):
            gram_plane[mine, index : index + 1] = jnp.broadcast_to(
                one_number(gram_acc[index * 8 : index * 8 + 8]), (1, lanes)
            )
        for shift in range(1, plane):
            gram_copy(shift).start()
        for shift in range(1, plane):
            gram_arrival(shift).wait_recv()

    for end in range(2):

        @pl.when(me == (depth - 1) * end)
        def _(end=end):
            total = gram_plane[0]
            for place in range(1, plane):
                total = total + gram_plane[place]
            gram_end[end] = total
            for shift in range(depth - 1):
                gram_dp_copy(end, shift).start()

    for end in range(2):
        for shift in range(depth - 1):

            @pl.when(me == ((depth - 1) * end + shift + 1) % depth)
            def _(end=end, shift=shift):
                gram_dp_copy(end, shift).wait_recv()

    gram = {}
    for index, (a, b) in enumerate(pairs):
        row = slice(index, index + 1)
        gram[a, b] = gram[b, a] = gram_end[0, row] + gram_end[1, row]
    for a in range(tasks):
        for b in range(tasks):
            gram_ref[a * tasks + b : a * tasks + b + 1] = gram[a, b]
    weights = [
        jnp.concatenate([weight] * (half // lanes), axis=1)
        for weight in weights_of(gram, order_ref, tasks)
    ]

    blocks = out.shape[0]
    group = blocks // GROUPS
    share = chain.rows // tasks
    own_share = pl.ds(pl.multiple_of(task * share, share), share)
    own_part = jnp.minimum(me, 1)

    def hop_copy(index):
        return send(
            hop.at[pl.ds(index * group, group)], out.at[pl.ds(index * group, group), own_share],
            hop_sem.at[0, index], hop_sem.at[1, index],
            dp=jnp.where(top, 1, depth - 2),
        )

    beside = [task + 1 - 2 * lax.rem(task, 2), task + 2 - 4 * (task // 2)]
    across = tasks - 1 - task

    def out_piece(index, owner):
        rows = pl.ds(pl.multiple_of(owner * share, share), share)
        return out.at[pl.ds(index * group, group), rows]

    def out_copy(index, which, owner):
        piece = out_piece(index, owner)
        peer = beside[which] if which < 2 else beside[1 if index < GROUPS // 2 else 0]
        return send(
            piece, piece, out_sem.at[0, index, which], out_sem.at[1, index, which], task=peer
        )

    def update_copy(index):
        at = pl.ds(index * group, group)
        return pltpu.make_async_copy(out.at[at], update_ref.at[at], update_sem.at[index])

    def weighted(chunk):
        total = weights[0] * chain.parts[0, chunk].astype(F32)
        for t in range(1, tasks):
            total = total + weights[t] * chain.parts[t, chunk].astype(F32)
        return total.astype(BF)

    def small_dp_copy(shift):
        return send(
            small_both.at[0], small_both.at[0], small_dp_sem.at[0, shift],
            small_dp_sem.at[1, shift], dp=shift + 1,
        )

    def small_core_copy():
        return send(
            small_both.at[0], small_both.at[1], small_core_sem.at[0], small_core_sem.at[1],
            tensor=1 - core,
        )

    @pl.when(top)
    def _():
        total = weights[0] * small_all[0]
        for t in range(1, tasks):
            total = total + weights[t] * small_all[t]
        small_both[0] = total
        for shift in range(depth - 1):
            small_dp_copy(shift).start()

    @pl.when(is_end)
    def _():
        for index in range(GROUPS):

            def other(block, carry):
                hop[block] = weighted(2 * block + 1 - own_part)
                return carry

            lax.fori_loop(index * group, (index + 1) * group, other, 0)
            hop_copy(index).start()

            def own(block, carry):
                out[block, own_share] = weighted(2 * block + own_part)
                return carry

            lax.fori_loop(index * group, (index + 1) * group, own, 0)
            for which in range(2):
                out_copy(index, which, task).start()

    @pl.when(jnp.logical_not(is_end))
    def _():
        for index in range(GROUPS):
            hop_copy(index).wait_recv()
            for which in range(2):
                out_copy(index, which, task).start()

    for shift in range(depth - 1):

        @pl.when(me == shift + 1)
        def _(shift=shift):
            small_dp_copy(shift).wait_recv()

    small_core_copy().start()

    for index in range(GROUPS):
        for which in range(2):
            out_copy(index, which, beside[which]).wait_recv()
        out_copy(index, 2, beside[0 if index < GROUPS // 2 else 1]).start()
    for index in range(GROUPS):
        out_copy(index, 2, across).wait_recv()
        update_copy(index).start()

    small_core_copy().wait_recv()
    small_out_ref[0:8, 0:half] = small_both[0, 0:8]
    small_out_ref[0:8, half:] = small_both[1, 0:8]
    small_out_ref[8:, own_lanes] = small_both[0, 8:]
    small_out_ref[8:, other_lanes] = small_both[1, 8:]

    small_copy.wait_send()
    small_core_copy().wait_send()
    chain.finish()

    @pl.when(me > 0)
    def _():
        small_hop().wait_send()

    @pl.when(top)
    def _():
        for shift, peer in enumerate(task_peers(tasks)):
            small_task_copy(shift, peer).wait_send()
        for shift in range(depth - 1):
            small_dp_copy(shift).wait_send()

    for end in range(2):

        @pl.when(me == (depth - 1) * end)
        def _(end=end):
            for shift in range(depth - 1):
                gram_dp_copy(end, shift).wait_send()

    @pl.when(is_end)
    def _():
        for shift in range(1, plane):
            gram_copy(shift).wait_send()
        for index in range(GROUPS):
            hop_copy(index).wait_send()

    for index in range(GROUPS):
        update_copy(index).wait()
        for which in range(3):
            out_copy(index, which, task).wait_send()


def spread_kernel(
    images, valid, tasks, block_order, parts_ref, context_grad_ref, query_grad_ref, block_ref,
    block_far_ref, small_ref, gram_in_ref,
    update_ref, context_out_ref, query_out_ref, block_out_ref, head_ref, row_ref, gain_ref, gram_ref,
):
    ordered = [parts_ref[block_order.index(block)] for block in range(len(block_order))]
    update_ref[...] = jnp.swapaxes(jnp.stack(ordered), 0, 1).astype(F32)
    context_out_ref[...] = context_grad_ref[...]

    @pl.when(pl.program_id(0) == 0)
    def _():
        padded = query_grad_ref.shape[0] // images
        first = lax.axis_index("tensor") == 0

        def rows(ref, image):
            return ref[image * padded : (image + 1) * padded].astype(F32)[:valid]

        for image in range(images):
            at = slice(image * valid, (image + 1) * valid)
            after = slice((images + image) * valid, (images + image + 1) * valid)
            query_out_ref[at] = rows(query_grad_ref, image).astype(BF)
            near, far = rows(block_ref, image), rows(block_far_ref, image)
            block_out_ref[at] = jnp.where(first, near, far).astype(BF)
            block_out_ref[after] = jnp.where(first, far, near).astype(BF)
        head_ref[...] = small_ref[0:8, 0 : head_ref.shape[1]]
        for which in range(6):
            row_ref[which // 2, which % 2 : which % 2 + 1] = small_ref[8 + which : 9 + which]
        gain_ref[...] = small_ref[14:17]
        for a in range(tasks):
            for b in range(tasks):
                at = a * tasks + b
                gram_ref[a : a + 1, b : b + 1] = gram_in_ref[at : at + 1, 0:1]


def gram_kernel(parts_ref, gram_ref):
    tasks = parts_ref.shape[0]

    @pl.when(pl.program_id(0) == 0)
    def _():
        gram_ref[...] = jnp.zeros_like(gram_ref)

    shares = [parts_ref[task, 0].astype(F32) for task in range(tasks)]
    for a in range(tasks):
        for b in range(a, tasks):
            gram_ref[a * tasks + b : a * tasks + b + 1] += rows_sum(shares[a] * shares[b])


def update_kernel(weights_ref, parts_ref, update_ref):
    tasks, blocks = parts_ref.shape[:2]
    for block in range(blocks):
        total = weights_ref[0] * parts_ref[0, block].astype(F32)
        for task in range(1, tasks):
            total += weights_ref[task] * parts_ref[task, block].astype(F32)
        update_ref[:, block, :] = total


def body(
    queries, memory, cotangent, matches, counts, task_order, params, head_bias, row_bias, norm_gain
):
    all_images = matches.shape[1]
    valid = matches.shape[2]
    width = queries.shape[2]
    half = params.shape[2]
    block_count = params.shape[1]
    blocks = (block_count - 8) // 2
    cores = lax.axis_size("tensor")
    images = all_images // cores
    keys = memory.shape[1] // all_images
    padded = -(-valid // 16) * 16
    rows = images * padded
    groups = width // SLAB
    stack = GROUP * padded
    core = lax.axis_index("tensor")

    chunk = 96
    weights, head_rows, tokens, own_cotangent = pl.pallas_call(
        functools.partial(gather_kernel, images, valid),
        grid=(width // chunk,),
        out_shape=(
            jax.ShapeDtypeStruct((block_count, width, cores * half), BF),
            jax.ShapeDtypeStruct((16, cores * half), BF),
            jax.ShapeDtypeStruct((rows, width), BF),
            jax.ShapeDtypeStruct((rows, width), BF),
        ),
        in_specs=[
            pl.BlockSpec((chunk, block_count, half), lambda i: (i, 0, 0)),
            pl.BlockSpec((8, half), lambda i: (0, 0)),
            pl.BlockSpec((None, *queries.shape[1:]), lambda i: (0, 0, 0)),
            pl.BlockSpec((None, *queries.shape[1:]), lambda i: (0, 0, 0)),
        ],
        out_specs=(
            any_spec(), any_spec(),
            pl.BlockSpec((rows, width), lambda i: (0, 0)),
            pl.BlockSpec((rows, width), lambda i: (0, 0)),
        ),
        scratch_shapes=[
            pltpu.VMEM((block_count, width, half), BF),
            pltpu.VMEM((16, half), BF),
            pltpu.SemaphoreType.DMA((width // chunk + 1,)),
            pltpu.SemaphoreType.DMA((width // chunk + 1,)),
            pltpu.SemaphoreType.DMA((width // chunk + 1,)),
        ],
        compiler_params=params_for(collective_id=0, has_side_effects=True),
        name="gather_weights",
    )(params, head_bias, queries, cotangent)

    def const(shape, *index):
        return pl.BlockSpec(shape, lambda *_: index)

    total_shape = jax.ShapeDtypeStruct((images * groups, 8, stack), F32)
    low_rows = jax.ShapeDtypeStruct((rows, width), BF)
    full_rows = jax.ShapeDtypeStruct((rows, width), F32)
    small_shape = jax.ShapeDtypeStruct((24, width), F32)
    one_block = jax.ShapeDtypeStruct((width, width), BF)
    small_spec = const((24, width), 0, 0)
    row_spec = const(row_bias.shape, 0, 0, 0)
    gain_spec = const(norm_gain.shape, 0, 0)
    head_spec = const((16, width), 0, 0)
    rows_spec = const((rows, width), 0, 0)

    qkv, self_mixed, self_total, first_sum, cross_query = pl.pallas_call(
        functools.partial(self_kernel, images, valid),
        grid=(1,),
        out_shape=(
            jax.ShapeDtypeStruct((3, rows, width), BF), low_rows, total_shape, full_rows, low_rows,
        ),
        in_specs=[rows_spec, const((5, width, width), 0, 0, 0), head_spec, row_spec, gain_spec],
        out_specs=(
            const((3, rows, width), 0, 0, 0), rows_spec, const(total_shape.shape, 0, 0, 0),
            rows_spec, rows_spec,
        ),
        compiler_params=params_for(),
        name="self_forward",
    )(tokens, weights, head_rows, row_bias, norm_gain)


    def own_image(i, g):
        return 0, lax.axis_index("tensor") * images + i, 0

    context_all = pl.BlockSpec((None, keys, width), own_image)
    slab_q = pl.BlockSpec((padded, SLAB), lambda i, g: (i, g))
    slab_k = pl.BlockSpec((keys, SLAB), lambda i, g: (i, g))
    slab_t = pl.BlockSpec((1, 8, stack), lambda i, g: (i * groups + g, 0, 0))

    def slab_w(block):
        return pl.BlockSpec((1, width, SLAB), lambda i, g: (block, 0, g))

    key_rows = jax.ShapeDtypeStruct((images * keys, width), BF)
    keys_act, values_act, cross_mixed, cross_total = pl.pallas_call(
        cross_kernel,
        grid=(images, groups),
        in_specs=[
            context_all, slab_q, slab_w(5), slab_w(6),
            pl.BlockSpec((16, SLAB), lambda i, g: (0, g)),
        ],
        out_specs=(slab_k, slab_k, slab_q, slab_t),
        out_shape=(key_rows, key_rows, low_rows, total_shape),
        compiler_params=params_for(),
        name="cross_forward",
    )(memory, cross_query, weights, weights, head_rows)

    per = 2 if blocks % 2 == 0 else 1
    block_rows, left, right, mixed_grad, second_grad, ffn_small = pl.pallas_call(
        functools.partial(ffn_kernel, images, blocks),
        grid=(2 * blocks // per,),
        out_shape=(
            low_rows,
            jax.ShapeDtypeStruct((3, width, rows), BF),
            jax.ShapeDtypeStruct((2 * blocks + 1, rows, width), BF),
            low_rows, full_rows, small_shape,
        ),
        in_specs=[
            rows_spec, rows_spec, rows_spec,
            const(matches.shape, 0, 0, 0),
            pl.BlockSpec(memory_space=pltpu.SMEM),
            const((1, width, width), 7, 0, 0),
            pl.BlockSpec((per, width, width), lambda s: (8 // per + s % (blocks // per), 0, 0)),
            pl.BlockSpec(
                (per, width, width), lambda s: ((8 + blocks) // per + s % (blocks // per), 0, 0)
            ),
            head_spec, row_spec, gain_spec,
        ],
        out_specs=(rows_spec, any_spec(), any_spec(), rows_spec, rows_spec, small_spec),
        scratch_shapes=[
            pltpu.VMEM((rows, width), F32),
            pltpu.VMEM((rows, width), BF),
            pltpu.VMEM((3, width, rows), BF),
            pltpu.VMEM((2 * blocks, rows, width), BF),
            pltpu.VMEM((blocks, rows, width), F32),
            pltpu.VMEM((rows, width), F32),
            pltpu.VMEM((rows, width), F32),
            pltpu.VMEM((8, width), F32),
            pltpu.SemaphoreType.DMA((3,)),
            pltpu.SemaphoreType.DMA((2 * blocks + 1,)),
        ],
        compiler_params=params_for(),
        name="ffn",
    )(
        first_sum, cross_mixed, own_cotangent, matches, counts, weights, weights, weights,
        head_rows, row_bias, norm_gain,
    )

    depth, tasks = lax.axis_size("dp"), lax.axis_size("task")
    by_chain = depth == 4 and tasks == 4 and cores == 2

    if by_chain:
        block_order = [*range(8, block_count), 7, 5, 6, 4, 3, 0, 1, 2]
        chain_rows = width // depth
        pair_rows = 8 * len(pairs_of(tasks))
        dma = pltpu.SemaphoreType.DMA
        last = images * groups - 1

        def at_step(make):
            def index_map(step):
                now = jnp.minimum(step, last)
                return make(now // groups, now - groups * (now // groups))

            return index_map

        def product(step):
            return jnp.minimum(step, 2 * blocks)

        def once(shape):
            return pl.BlockSpec(
                shape, lambda step: (0,) * len(shape), pipeline_mode=pl.Buffered(1)
            )

        step_q = pl.BlockSpec((padded, SLAB), at_step(lambda i, g: (i, g)))
        step_k = pl.BlockSpec((keys, SLAB), at_step(lambda i, g: (i, g)))

        small_half = pltpu.VMEM((24, half), F32)
        (
            context_grad, token_grad, update_parts, small_out, gram_rows, block_far, *_,
        ) = pl.pallas_call(
            functools.partial(
                back_kernel, depth, tasks, images, groups, valid, block_order
            ),
            grid=(images * groups + 1,),
            out_shape=(
                key_rows, low_rows,
                jax.ShapeDtypeStruct((block_count, chain_rows, half), BF),
                small_shape,
                jax.ShapeDtypeStruct((16, 128), F32),
                low_rows,
                key_rows, key_rows,
            ),
            in_specs=[
                pl.BlockSpec(memory_space=pltpu.SMEM),
                any_spec(), step_q, step_k, step_k,
                pl.BlockSpec((1, 8, stack), at_step(lambda i, g: (i * groups + g, 0, 0))),
                step_q,
                once((rows, width)), once(row_bias.shape), once(norm_gain.shape),
                once((3, rows, width)), once((rows, width)), once(total_shape.shape),
                once((rows, width)), once((rows, width)), once((24, width)),
                any_spec(), any_spec(),
                pl.BlockSpec((1, width, rows), lambda step: (product(step) // blocks, 0, 0)),
                pl.BlockSpec((1, rows, width), lambda step: (product(step), 0, 0)),
            ],
            out_specs=(
                any_spec(), once((rows, width)), any_spec(), once((24, width)), once((16, 128)),
                *[any_spec()] * 3,
            ),
            scratch_shapes=[
                pltpu.VMEM((keys, width), BF),
                pltpu.VMEM((width, keys), BF),
                pltpu.VMEM((width, width), F32),
                pltpu.VMEM((width, width), F32),
                pltpu.VMEM((rows, width), BF),
                pltpu.VMEM((3, rows, width), BF),
                pltpu.VMEM((5, width, width), BF),
                dma((2,)),
                dma((2,)),
                dma(()),
                *ContextGrad.scratch(keys, width),
                *Chain.scratch(block_count, chain_rows, half, tasks),
                pltpu.VMEM((24, width), F32),
                small_half, small_half, small_half, small_half,
                pltpu.VMEM((tasks, 24, half), F32),
                pltpu.VMEM((2, 24, half), F32),
                pltpu.VMEM((pair_rows, half), F32),
                pltpu.VMEM((2 * tasks, 16, 128), F32),
                pltpu.VMEM((2, 16, 128), F32),
                pltpu.VMEM((block_count, chain_rows // tasks, half), BF),
                pltpu.VMEM((block_count, chain_rows, half), BF),
                dma((2,)),
                dma((2,)),
                dma((2, tasks - 1)),
                dma((2, depth - 1)),
                dma((2,)),
                dma((2, 2 * tasks - 1)),
                dma((2, 2, depth - 1)),
                dma((2, GROUPS)),
                dma((2, GROUPS, tasks - 1)),
                dma((GROUPS,)),
            ],
            compiler_params=params_for(collective_id=1, has_side_effects=True),
            name="backward",
        )(
            task_order, memory, cross_query, keys_act, values_act, cross_total, mixed_grad,
            tokens, row_bias, norm_gain, qkv, self_mixed, self_total, first_sum,
            second_grad, ffn_small, weights, block_rows, left, right,
        )
        tile = chain_rows // images
        (
            param_update, memory_grad, query_grad, block_out, head_update, row_update, gain_update,
            gram,
        ) = pl.pallas_call(
            functools.partial(spread_kernel, images, valid, tasks, block_order),
            grid=(images,),
            out_shape=(
                jax.ShapeDtypeStruct((chain_rows, block_count, half), F32),
                key_rows,
                jax.ShapeDtypeStruct((images * valid, width), BF),
                jax.ShapeDtypeStruct((all_images * valid, width), BF),
                jax.ShapeDtypeStruct((8, half), F32),
                jax.ShapeDtypeStruct((3, 2, width), F32),
                jax.ShapeDtypeStruct((3, width), F32),
                jax.ShapeDtypeStruct((tasks, tasks), F32),
            ),
            in_specs=[
                pl.BlockSpec((block_count, tile, half), lambda r: (0, r, 0)),
                pl.BlockSpec((keys, width), lambda r: (r, 0)),
                rows_spec, rows_spec, rows_spec, small_spec, const((16, 128), 0, 0),
            ],
            out_specs=(
                pl.BlockSpec((tile, block_count, half), lambda r: (r, 0, 0)),
                pl.BlockSpec((keys, width), lambda r: (r, 0)),
                const((images * valid, width), 0, 0),
                const((all_images * valid, width), 0, 0),
                const((8, half), 0, 0), const((3, 2, width), 0, 0, 0),
                const((3, width), 0, 0), const((tasks, tasks), 0, 0),
            ),
            compiler_params=params_for(),
            name="spread",
        )(update_parts, context_grad, token_grad, block_rows, block_far, small_out, gram_rows)
        return (
            block_out[None], query_grad[None], memory_grad[None], param_update, head_update,
            row_update, gain_update, gram,
        )

    def unpad(array):
        return array.reshape(images, padded, width)[:, :valid].reshape(1, images * valid, width)

    block_out = lax.all_gather(unpad(block_rows), "tensor", axis=1, tiled=True)
    cross_query_grad, context_grad, key_wg, value_wg, cross_small = pl.pallas_call(
        cross_back_kernel,
        grid=(images, groups),
        in_specs=[
            context_all, slab_q, slab_k, slab_k, slab_t, slab_q, slab_w(5), slab_w(6),
        ],
        out_specs=(
            slab_q,
            pl.BlockSpec((keys, width), lambda i, g: (i, 0)),
            const((width, width), 0, 0), const((width, width), 0, 0), small_spec,
        ),
        scratch_shapes=[
            pltpu.VMEM((width, keys), BF),
            pltpu.VMEM((keys, width), F32),
            pltpu.VMEM((width, width), F32),
            pltpu.VMEM((width, width), F32),
        ],
        out_shape=(low_rows, key_rows, one_block, one_block, small_shape),
        compiler_params=params_for(),
        name="cross_backward",
    )(memory, cross_query, keys_act, values_act, cross_total, mixed_grad, weights, weights)

    token_grad, self_wg, self_small = pl.pallas_call(
        functools.partial(self_back_kernel, images, valid),
        grid=(1,),
        out_shape=(
            low_rows, jax.ShapeDtypeStruct((5, width, width), BF), small_shape,
        ),
        in_specs=[
            rows_spec, const((5, width, width), 0, 0, 0), row_spec, gain_spec,
            const((3, rows, width), 0, 0, 0), rows_spec, const(total_shape.shape, 0, 0, 0),
            rows_spec, rows_spec, rows_spec,
        ],
        out_specs=(
            rows_spec, const((5, width, width), 0, 0, 0), small_spec,
        ),
        scratch_shapes=[pltpu.VMEM((3, rows, width), BF)],
        compiler_params=params_for(),
        name="self_backward",
    )(
        tokens, weights, row_bias, norm_gain, qkv, self_mixed, self_total, first_sum, second_grad,
        cross_query_grad,
    )

    query_grad = unpad(token_grad)
    memory_grad = context_grad[None]

    small = self_small + cross_small + ffn_small
    product = functools.partial(jnp.einsum, "dr,jre->jde", preferred_element_type=F32)
    grad_in = product(left[0], right[:blocks]).astype(BF)
    grad_out = product(left[1], right[blocks : 2 * blocks]).astype(BF)
    cross_out_wg = product(left[2], right[2 * blocks :])[0].astype(BF)
    grads = jnp.concatenate(
        [self_wg, jnp.stack([key_wg, value_wg, cross_out_wg]), grad_in, grad_out], axis=0
    )
    swap = [(0, 1), (1, 0)]
    grads = (
        grads[:, :, :half].astype(F32) + lax.ppermute(grads[:, :, half:], "tensor", swap).astype(F32)
    ).astype(BF)
    head_small = small[:8, :half] + lax.ppermute(small[:8, half:], "tensor", swap)
    row_small = lax.psum(small[8:17], ("dp", "tensor"))
    head_small = lax.psum(head_small, "dp")
    shard = lax.psum_scatter(grads, "dp", scatter_dimension=1, tiled=True)
    all_shards = lax.all_gather(shard, "task", axis=0, tiled=False)
    all_head = lax.all_gather(head_small, "task", axis=0, tiled=False)
    all_row = lax.all_gather(row_small, "task", axis=0, tiled=False)
    tasks = all_shards.shape[0]
    share_rows = shard.shape[1]
    sums = pl.pallas_call(
        gram_kernel,
        grid=(block_count,),
        out_shape=jax.ShapeDtypeStruct((tasks * tasks, half), F32),
        in_specs=[pl.BlockSpec((tasks, 1, share_rows, half), lambda k: (0, k, 0, 0))],
        out_specs=const((tasks * tasks, half), 0, 0),
        compiler_params=params_for(),
        name="gram",
    )(all_shards)
    upper = jnp.sum(sums, axis=1).reshape(tasks, tasks)
    gram_weights = upper + upper.T - jnp.diag(jnp.diag(upper))
    gram_weights = lax.psum(gram_weights, ("dp", "tensor"))
    gram_heads = jnp.einsum("axy,bxy->ab", all_head, all_head, precision=highest)
    gram_heads = lax.psum(gram_heads, "tensor")
    gram = gram_weights + gram_heads + jnp.einsum(
        "axy,bxy->ab", all_row, all_row, precision=highest
    )
    task_weights = combine_weights(gram, task_order)
    tile = 64 if share_rows % 64 == 0 else share_rows
    param_update = pl.pallas_call(
        update_kernel,
        grid=(share_rows // tile,),
        out_shape=jax.ShapeDtypeStruct((share_rows, block_count, half), F32),
        in_specs=[
            pl.BlockSpec(memory_space=pltpu.SMEM),
            pl.BlockSpec((tasks, block_count, tile, half), lambda r: (0, 0, r, 0)),
        ],
        out_specs=pl.BlockSpec((tile, block_count, half), lambda r: (r, 0, 0)),
        compiler_params=params_for(),
        name="update",
    )(task_weights, all_shards)
    head_bias_update = jnp.einsum("a,axy->xy", task_weights, all_head, precision=highest)
    row_update = jnp.einsum("a,axy->xy", task_weights, all_row, precision=highest)
    return (
        block_out, query_grad, memory_grad, param_update, head_bias_update,
        row_update[:6].reshape(3, 2, width), row_update[6:9], gram,
    )


def solution(mesh):
    return jax.shard_map(
        body,
        mesh=mesh,
        in_specs=(
            P("task", "dp", None),
            P("task", "dp", None),
            P("task", "dp", None),
            P("task", "dp", None),
            P("task", "dp"),
            P(),
            P(None, None, "tensor"),
            P(None, "tensor"),
            P(),
            P(),
        ),
        out_specs=(
            P("task", "dp", None),
            P("task", ("dp", "tensor"), None),
            P("task", ("dp", "tensor"), None),
            P("dp", None, "tensor"),
            P(None, "tensor"),
            P(),
            P(),
            P(),
        ),
        check_vma=False,
    )
```

```python
import functools

import jax
import jax.numpy as jnp
from jax import lax
from jax.experimental import pallas as pl
from jax.experimental.pallas import tpu as pltpu
from jax.sharding import PartitionSpec as P

HD = 64
GROUP = 4
SLAB = GROUP * HD
BF = jnp.bfloat16
F32 = jnp.float32
MESH_ID = pl.DeviceIdType.MESH
highest = lax.Precision.HIGHEST
VMEM_LIMIT = 63 * 2**20


def combine_weights(gram_matrix, order_list):
    task_count = gram_matrix.shape[0]
    task_index = jnp.arange(task_count, dtype=jnp.int32)
    summed = jnp.zeros((task_count,), F32)
    for own_task in range(task_count):
        coeffs = (task_index == own_task).astype(F32)
        for position in range(task_count):
            chosen = (task_index == order_list[position]).astype(F32)
            column = jnp.sum(gram_matrix * chosen[None, :], axis=1)
            inner_dot = jnp.sum(coeffs * column)
            square = jnp.sum(chosen * column)
            others = (order_list[position] != own_task).astype(F32)
            coeffs = coeffs - others * jnp.minimum(inner_dot, 0.0) / (square + 1e-06) * chosen
        summed = summed + coeffs
    return summed


def mm(a, b):
    return jnp.dot(a, b, preferred_element_type=F32)


def mm_nt(a, b):
    return lax.dot_general(a, b, (((1,), (1,)), ((), ())), preferred_element_type=F32)


def mm_tn(a, b):
    return lax.dot_general(a, b, (((0,), (0,)), ((), ())), preferred_element_type=F32)


def row_of(row_ref, which):
    return row_ref[which // 2, which % 2 : which % 2 + 1].astype(F32)


def gain_of(gain_ref, which):
    return gain_ref[which : which + 1].astype(F32)


def norm_parts(residual):
    row_mean = jnp.mean(residual, axis=-1, keepdims=True)
    centred = residual - row_mean
    variance = jnp.mean(centred * centred, axis=-1, keepdims=True)
    scale = lax.rsqrt(variance + 1e-05)
    return centred * scale, scale


def norm_back(normed, scale, gain_row, grad):
    scaled = grad * gain_row
    first = jnp.mean(scaled, axis=-1, keepdims=True)
    second = jnp.mean(scaled * normed, axis=-1, keepdims=True)
    return scale * (scaled - first - normed * second)


def rows_sum(value):
    return jnp.sum(value, axis=0, keepdims=True)


def gelu_tanh(hidden):
    square = hidden * hidden
    tanh = jnp.tanh(hidden * (0.7978845608028654 + 0.7978845608028654 * 0.044715 * square))
    half = 0.5 * (1.0 + tanh)
    inner = 0.7978845608028654 + 0.7978845608028654 * 3 * 0.044715 * square
    return hidden * half, half + 0.5 * hidden * (1.0 - tanh * tanh) * inner


def head_mask(head, rows, dtype):
    lane = lax.broadcasted_iota(jnp.int32, (rows, SLAB), 1)
    return (lane // HD == head).astype(F32).astype(dtype)


def stack_heads(slab):
    return jnp.concatenate(
        [slab * head_mask(head, slab.shape[0], slab.dtype) for head in range(GROUP)], axis=0
    )


def unstack_heads(stacked):
    rows = stacked.shape[0] // GROUP
    total = None
    for head in range(GROUP):
        part = stacked[head * rows : (head + 1) * rows] * head_mask(head, rows, stacked.dtype)
        total = part if total is None else total + part
    return total


def scores_of(query_stack, key_slab, valid):
    scores = mm_nt(key_slab, query_stack)
    if valid < key_slab.shape[0]:
        row = lax.broadcasted_iota(jnp.int32, scores.shape, 0)
        scores = jnp.where(row < valid, scores, -1e30)
    return scores


def attend(query_slab, key_slab, value_slab, valid):
    scores = scores_of(stack_heads(query_slab * HD ** (-0.5)), key_slab, valid)
    row_max = jnp.max(scores, axis=0, keepdims=True)
    exps = jnp.exp(scores - row_max)
    total = jnp.sum(exps, axis=0, keepdims=True)
    probs = (exps * (1.0 / total)).astype(BF)
    mixed = unstack_heads(mm_tn(value_slab, probs).T)
    return mixed, row_max + jnp.log(total)


def attend_back(query_slab, key_slab, value_slab, log_total, grad_slab, valid):
    query_stack = stack_heads(query_slab * HD ** (-0.5))
    grad_stack = stack_heads(grad_slab)
    probs = jnp.exp(scores_of(query_stack, key_slab, valid) - log_total)
    grad_value = mm(probs.astype(BF), grad_stack)
    grad_probs = mm_nt(value_slab, grad_stack)
    inner = jnp.sum(probs * grad_probs, axis=0, keepdims=True)
    grad_scores = (probs * (grad_probs - inner)).astype(BF)
    grad_key = mm(grad_scores, query_stack)
    grad_query = unstack_heads(mm_tn(key_slab, grad_scores).T) * HD ** (-0.5)
    return grad_query.astype(BF), grad_key.astype(BF), grad_value.astype(BF)


def pad_rows(source_ref, target_ref, images, valid):
    first = lax.axis_index("tensor") == 0
    padded = target_ref.shape[0] // images
    for image in range(images):
        here, there = (
            source_ref[(core * images + image) * valid : (core * images + image + 1) * valid]
            for core in range(2)
        )
        rows = jnp.where(first, here.astype(F32), there.astype(F32))
        fill = jnp.zeros((padded - valid, rows.shape[1]), F32)
        target_ref[image * padded : (image + 1) * padded] = jnp.concatenate(
            [rows, fill], axis=0
        ).astype(target_ref.dtype)


def send(source, target, send_sem, recv_sem, **device):
    return pltpu.make_async_remote_copy(
        source, target, send_sem, recv_sem, device_id=device, device_id_type=MESH_ID
    )


def start_kernel(
    images, valid, own_ref, bias_ref, queries_ref, cotangent_ref, row_ref, gain_ref,
    full_ref, head_ref, tokens_ref, own_cotangent_ref, qkv_ref, mixed_ref, total_ref, sum_ref,
    cross_query_ref, first, second, bias_own, bias_all, remote_send, remote_recv, local_sem, far_sem,
):
    step, steps = pl.program_id(0), pl.num_programs(0)
    other = 1 - lax.axis_index("tensor")
    rows, blocks, width = own_ref.shape
    parts = steps // 2
    near, far = pl.ds(0, width), pl.ds(width, width)
    lower, upper = pl.ds(0, blocks), pl.ds(blocks, blocks)

    def rows_of(part):
        return pl.ds(pl.multiple_of(part * rows, rows), rows)

    def first_copies(part):
        at = rows_of(part)
        return (
            send(
                first.at[:, at, near], first.at[:, at, far], remote_send.at[part],
                remote_recv.at[part], tensor=other,
            ),
            pltpu.make_async_copy(
                first.at[:, at, near], full_ref.at[lower, at, near], local_sem.at[part]
            ),
        )

    def second_copies(part):
        at = rows_of(part)
        return (
            send(
                second.at[:, at], full_ref.at[upper, at, far], remote_send.at[parts + part],
                remote_recv.at[parts + part], tensor=other,
            ),
            pltpu.make_async_copy(
                second.at[:, at], full_ref.at[upper, at, near], local_sem.at[parts + part]
            ),
        )

    bias_copy = send(
        bias_own, bias_all.at[:, far], remote_send.at[steps], remote_recv.at[steps], tensor=other
    )
    far_copy = pltpu.make_async_copy(first.at[:, :, far], full_ref.at[lower, :, far], far_sem)

    @pl.when(step == 0)
    def _():
        barrier = pltpu.get_barrier_semaphore()
        pl.semaphore_signal(barrier, inc=1, device_id={"tensor": other}, device_id_type=MESH_ID)
        pl.semaphore_wait(barrier, 1)
        bias_own[...] = jnp.zeros_like(bias_own)
        bias_own[0 : bias_ref.shape[0]] = bias_ref[...]
        bias_copy.start()
        bias_all[:, near] = bias_own[...]

    @pl.when(step < parts)
    def _():
        first[:, rows_of(step), near] = jnp.swapaxes(own_ref[...], 0, 1)
        for copy in first_copies(step):
            copy.start()

    @pl.when(step >= parts)
    def _():
        second[:, rows_of(step - parts)] = jnp.swapaxes(own_ref[...], 0, 1)
        for copy in second_copies(step - parts):
            copy.start()

    @pl.when(step == steps - 1)
    def _():
        pad_rows(queries_ref, tokens_ref, images, valid)
        pad_rows(cotangent_ref, own_cotangent_ref, images, valid)
        bias_copy.wait()
        head_ref[...] = bias_all[...]
        for part in range(parts):
            first_copies(part)[0].wait_recv()
        far_copy.start()
        self_forward(
            images, valid, tokens_ref, first, head_ref, row_ref, gain_ref, qkv_ref, mixed_ref,
            total_ref, sum_ref, cross_query_ref,
        )
        far_copy.wait()
        for part in range(parts):
            remote, local = first_copies(part)
            remote.wait_send()
            local.wait()
            for copy in second_copies(part):
                copy.wait()


def any_spec():
    return pl.BlockSpec(memory_space=pl.ANY)


def whole_spec():
    return pl.BlockSpec(memory_space=pltpu.VMEM)


def params_for(**keys):
    return pltpu.CompilerParams(vmem_limit_bytes=VMEM_LIMIT, **keys)


def self_forward(images, valid, tokens_ref, weight_ref, head_ref, row_ref, gain_ref, qkv_ref,
                 mixed_ref, total_ref, sum_ref, cross_query_ref):
    tokens = tokens_ref[...]
    rows = tokens.shape[0] // images
    width = tokens.shape[1]
    qkv_ref[0] = (mm(tokens, weight_ref[0]) + head_ref[0:1].astype(F32)).astype(BF)
    qkv_ref[1] = mm(tokens, weight_ref[1]).astype(BF)
    qkv_ref[2] = (mm(tokens, weight_ref[2]) + head_ref[1:2].astype(F32)).astype(BF)
    for image in range(images):
        at = slice(image * rows, (image + 1) * rows)
        for group in range(width // SLAB):
            lanes = slice(group * SLAB, (group + 1) * SLAB)
            mixed, log_total = attend(
                qkv_ref[0, at, lanes], qkv_ref[1, at, lanes], qkv_ref[2, at, lanes], valid
            )
            mixed_ref[at, lanes] = mixed.astype(BF)
            total_ref[image * (width // SLAB) + group] = jnp.broadcast_to(
                log_total, total_ref.shape[1:]
            )
    first_sum = tokens.astype(F32) + mm_nt(mixed_ref[...], weight_ref[3]) + row_of(row_ref, 0)
    sum_ref[...] = first_sum
    first_low = (norm_parts(first_sum)[0] * gain_of(gain_ref, 0) + row_of(row_ref, 1)).astype(BF)
    cross_query_ref[...] = (mm(first_low, weight_ref[4]) + head_ref[2:3].astype(F32)).astype(BF)


def cross_kernel(context_ref, query_ref, key_w_ref, value_w_ref, head_ref, key_ref, value_ref,
                 mixed_ref, total_ref):
    context = context_ref[...]
    for group in range(key_ref.shape[1] // SLAB):
        lanes = slice(group * SLAB, (group + 1) * SLAB)
        key_ref[:, lanes] = mm(context, key_w_ref[0, :, lanes]).astype(BF)
        value_ref[:, lanes] = (
            mm(context, value_w_ref[0, :, lanes]) + head_ref[3:4, lanes].astype(F32)
        ).astype(BF)
        mixed, log_total = attend(
            query_ref[:, lanes], key_ref[:, lanes], value_ref[:, lanes], key_ref.shape[0]
        )
        mixed_ref[:, lanes] = mixed.astype(BF)
        total_ref[group] = jnp.broadcast_to(log_total, total_ref.shape[1:])


def ffn_kernel(
    images, blocks, per, sum_ref, mixed_ref, cotangent_ref, matches_ref, counts_ref, cross_w_ref,
    weight_ref, head_ref, row_ref, gain_ref,
    block_ref, left_ref, right_ref, mixed_grad_ref, residual_ref, small_ref,
    second_sum, second_low, left, right, slope, branch, third_grad, hidden_bias, weights, left_sem,
    right_sem, weight_sem,
):
    step = pl.program_id(0)
    half_steps = blocks // per

    def weight_copies(first):
        at = pl.ds(first, per)
        return [
            pltpu.make_async_copy(
                weight_ref.at[pl.ds(8 + which * blocks + first, per)], weights.at[which, at],
                weight_sem.at[which, first // per],
            )
            for which in range(2)
        ]
    rows = sum_ref.shape[0] // images

    def left_copy(which):
        return pltpu.make_async_copy(left.at[which], left_ref.at[which], left_sem.at[which])

    def right_copy(which):
        return pltpu.make_async_copy(right.at[which], right_ref.at[which], right_sem.at[which])

    mixed_copy = pltpu.make_async_copy(
        mixed_ref, right_ref.at[2 * blocks], right_sem.at[2 * blocks]
    )

    @pl.when(step == 0)
    def _():
        for copy in weight_copies(0):
            copy.start()
        mixed_copy.start()
        first_out = norm_parts(sum_ref[...])[0] * gain_of(gain_ref, 0) + row_of(row_ref, 1)
        second = first_out + mm_nt(mixed_ref[...], cross_w_ref[0]) + row_of(row_ref, 2)
        second_sum[...] = second
        second_low[...] = (
            norm_parts(second)[0] * gain_of(gain_ref, 1) + row_of(row_ref, 3)
        ).astype(BF)
        branch[...] = jnp.zeros_like(branch)
        small_ref[...] = jnp.zeros_like(small_ref)
        hidden_bias[0:blocks] = head_ref[4 : 4 + blocks].astype(F32)
        left[0] = second_low[...].T
        left_copy(0).start()

    @pl.when(step < half_steps)
    def _():
        low = second_low[...]
        first = step * per
        copies = weight_copies(first)
        copies[0].wait()
        copies[1].wait()

        @pl.when(step + 1 < half_steps)
        def _():
            for copy in weight_copies(first + per):
                copy.start()

        pres = [
            mm(low, weights[0, first + k]) + hidden_bias[pl.ds(first + k, 1)] for k in range(per)
        ]
        total = branch[...]
        for k in range(per):
            act, grad = gelu_tanh(pres[k])
            act = act.astype(BF)
            slope[first + k] = grad
            right[blocks + first + k] = act
            right_copy(blocks + first + k).start()
            total = total + mm_nt(act, weights[1, first + k])
        branch[...] = total

    @pl.when(step == half_steps - 1)
    def _():
        second = norm_parts(second_sum[...])[0] * gain_of(gain_ref, 1) + row_of(row_ref, 3)
        third_sum = second + branch[...] + row_of(row_ref, 4)
        normed, scale = norm_parts(third_sum)
        block_ref[...] = (normed * gain_of(gain_ref, 2) + row_of(row_ref, 5)).astype(BF)
        count = matches_ref.shape[2]
        slot = lax.broadcasted_iota(jnp.int32, (rows, count), 0)
        box = lax.broadcasted_iota(jnp.int32, (rows, count), 1)
        grads = []
        for image in range(images):
            own = lax.axis_index("tensor") * images + image
            live = (matches_ref[0, pl.ds(own, 1)] == slot) & (box < counts_ref[0, own])
            mask = jnp.sum(jnp.where(live, 1.0, 0.0), axis=1, keepdims=True)
            cot = cotangent_ref[image * rows : (image + 1) * rows].astype(F32)
            grads.append(cot * mask)
        out_grad = jnp.concatenate(grads, axis=0)
        grad = norm_back(normed, scale, gain_of(gain_ref, 2), out_grad)
        third_grad[...] = grad
        left[1] = grad.astype(BF).T
        left_copy(1).start()
        small_ref[12:13] = rows_sum(grad)
        small_ref[13:14] = rows_sum(out_grad)
        small_ref[16:17] = rows_sum(out_grad * normed)
        branch[...] = jnp.zeros_like(branch)

    @pl.when(step >= half_steps)
    def _():
        ffn_low = third_grad[...].astype(BF)
        first = (step - half_steps) * per
        grads = [mm(ffn_low, weights[1, first + k]) for k in range(per)]
        total = branch[...]
        for k in range(per):
            grad_low = (grads[k] * slope[first + k]).astype(BF)
            right[first + k] = grad_low
            right_copy(first + k).start()
            small_ref[pl.ds(4 + first + k, 1)] = rows_sum(grad_low.astype(F32))
            total = total + mm_nt(grad_low, weights[0, first + k])
        branch[...] = total

    @pl.when(step == 2 * half_steps - 1)
    def _():
        second_in = third_grad[...] + branch[...]
        normed, scale = norm_parts(second_sum[...])
        grad = norm_back(normed, scale, gain_of(gain_ref, 1), second_in)
        residual_ref[...] = grad
        small_ref[10:11] = rows_sum(grad)
        small_ref[11:12] = rows_sum(second_in)
        small_ref[15:16] = rows_sum(second_in * normed)
        cross_low = grad.astype(BF)
        left[2] = cross_low.T
        left_copy(2).start()
        mixed_grad_ref[...] = mm(cross_low, cross_w_ref[0]).astype(BF)
        mixed_copy.wait()
        for which in range(3):
            left_copy(which).wait()
        for which in range(2 * blocks):
            right_copy(which).wait()


def cross_back_step(
    image, group, query_ref, key_ref, value_ref, total_ref, mixed_grad_ref, small_ref, context_t,
    key_acc, value_acc, unit,
):
    grad_query, grad_key, grad_value = attend_back(
        query_ref[...], key_ref[...], value_ref[...], total_ref[0, 0:1], mixed_grad_ref[...],
        key_ref.shape[0],
    )
    lanes = pl.ds(pl.multiple_of(group * SLAB, SLAB), SLAB)
    small_ref[2:3, lanes] += rows_sum(grad_query.astype(F32))
    small_ref[3:4, lanes] += rows_sum(grad_value.astype(F32))
    unit(0)
    key_wg = mm(context_t[...], grad_key)
    value_wg = mm(context_t[...], grad_value)

    @pl.when(image == 0)
    def _():
        key_acc[:, lanes] = key_wg
        value_acc[:, lanes] = value_wg

    @pl.when(image > 0)
    def _():
        key_acc[:, lanes] += key_wg
        value_acc[:, lanes] += value_wg

    unit(1)
    return grad_query, grad_key, grad_value


def cross_back_kernel(
    context_ref, query_ref, key_ref, value_ref, total_ref, mixed_grad_ref, key_w_ref, value_w_ref,
    query_grad_ref, context_grad_ref, key_wg_ref, value_wg_ref, small_ref,
    context_t, acc, key_acc, value_acc,
):
    image, group = pl.program_id(0), pl.program_id(1)
    images, groups = pl.num_programs(0), pl.num_programs(1)

    @pl.when((image == 0) & (group == 0))
    def _():
        small_ref[...] = jnp.zeros_like(small_ref)

    @pl.when(group == 0)
    def _():
        context_t[...] = context_ref[...].T

    query_grad_ref[...], grad_key, grad_value = cross_back_step(
        image, group, query_ref, key_ref, value_ref, total_ref, mixed_grad_ref,
        small_ref, context_t, key_acc, value_acc, lambda part: None,
    )
    context_part = mm_nt(grad_key, key_w_ref[0]) + mm_nt(grad_value, value_w_ref[0])

    @pl.when(group == 0)
    def _():
        acc[...] = context_part

    @pl.when(group > 0)
    def _():
        acc[...] += context_part

    @pl.when(group == groups - 1)
    def _():
        context_grad_ref[...] = acc[...].astype(BF)

    @pl.when((image == images - 1) & (group == groups - 1))
    def _():
        key_wg_ref[...] = key_acc[...].astype(BF)
        value_wg_ref[...] = value_acc[...].astype(BF)


def self_back(
    images, valid, tokens_ref, weight_ref, row_ref, gain_ref, qkv_ref, mixed_ref, total_ref, sum_ref,
    residual_ref, cross_query_grad_ref, small_ref, qkv_grad, emit, unit, used=lambda: None,
):
    tokens = tokens_ref[...]
    rows = tokens.shape[0] // images
    width = tokens.shape[1]
    normed, scale = norm_parts(sum_ref[...])
    first_low = (normed * gain_of(gain_ref, 0) + row_of(row_ref, 1)).astype(BF)
    cross_query_grad = cross_query_grad_ref[...]
    first_low_t = first_low.T
    emit(4, lambda lanes: mm(first_low_t, cross_query_grad_ref[:, lanes]))
    unit()
    first_in = residual_ref[...] + mm_nt(cross_query_grad, weight_ref[4])
    first_grad = norm_back(normed, scale, gain_of(gain_ref, 0), first_in)
    small_ref[8:9] = rows_sum(first_grad)
    small_ref[9:10] = rows_sum(first_in)
    small_ref[14:15] = rows_sum(first_in * normed)
    unit()
    self_low = first_grad.astype(BF)
    self_low_t = self_low.T
    emit(3, lambda lanes: mm(self_low_t, mixed_ref[:, lanes]))
    unit()
    mixed_grad = mm(self_low, weight_ref[3]).astype(BF)
    used()
    for image in range(images):
        at = slice(image * rows, (image + 1) * rows)
        for group in range(width // SLAB):
            lanes = slice(group * SLAB, (group + 1) * SLAB)
            grads = attend_back(
                qkv_ref[0, at, lanes], qkv_ref[1, at, lanes], qkv_ref[2, at, lanes],
                total_ref[image * (width // SLAB) + group, 0:1], mixed_grad[at, lanes], valid,
            )
            for which in range(3):
                qkv_grad[which, at, lanes] = grads[which]
            unit()
    tokens_t = tokens.T
    total = first_grad
    for which in range(3):
        grad = qkv_grad[which]
        emit(which, lambda lanes, which=which: mm(tokens_t, qkv_grad[which, :, lanes]))
        unit()
        total = total + mm_nt(grad, weight_ref[which])
    small_ref[0:1] = rows_sum(qkv_grad[0].astype(F32))
    small_ref[1:2] = rows_sum(qkv_grad[2].astype(F32))
    return total


def self_back_kernel(
    images, valid, tokens_ref, weight_ref, row_ref, gain_ref, qkv_ref, mixed_ref, total_ref, sum_ref,
    residual_ref, cross_query_grad_ref, query_grad_ref, wg_ref, small_ref, qkv_grad,
):
    small_ref[...] = jnp.zeros_like(small_ref)

    def emit(block, value):
        for lane in range(0, wg_ref.shape[2], SLAB):
            lanes = slice(lane, lane + SLAB)
            wg_ref[block, :, lanes] = value(lanes).astype(BF)

    query_grad_ref[...] = self_back(
        images, valid, tokens_ref, weight_ref, row_ref, gain_ref, qkv_ref, mixed_ref, total_ref,
        sum_ref, residual_ref, cross_query_grad_ref, small_ref, qkv_grad, emit, lambda: None,
    ).astype(BF)


def task_peers(tasks):
    me = lax.axis_index("task")
    return [lax.rem(me + shift, tasks) for shift in range(1, tasks)]


def task_senders(tasks):
    me = lax.axis_index("task")
    return [lax.rem(me + tasks - shift, tasks) for shift in range(1, tasks)]


def greet(depth, tasks):
    me = lax.axis_index("dp")
    barrier = pltpu.get_barrier_semaphore()
    other = 1 - lax.axis_index("tensor")
    for peer in task_peers(tasks):
        pl.semaphore_signal(barrier, inc=1, device_id={"task": peer}, device_id_type=MESH_ID)
        pl.semaphore_signal(
            barrier, inc=1, device_id={"task": peer, "tensor": other}, device_id_type=MESH_ID
        )
    for shift in range(1, depth):
        pl.semaphore_signal(
            barrier, inc=1, device_id={"dp": lax.rem(me + shift, depth)}, device_id_type=MESH_ID
        )
    pl.semaphore_signal(barrier, inc=1, device_id={"tensor": other}, device_id_type=MESH_ID)
    pl.semaphore_wait(barrier, 2 * (tasks - 1) + depth)


LAG = 2
SLOTS = 3
STAGES = 2


class Chain:
    def __init__(self, depth, tasks, refs):
        self.depth, self.tasks = depth, tasks
        (self.near, self.far, self.stage, self.passed, self.parts,
         self.far_send, self.far_recv, self.far_free, self.pass_send, self.pass_recv,
         self.part_send, self.part_recv) = refs
        self.chunks = self.passed.shape[1]
        self.rows, self.half = self.passed.shape[2:]
        self.me = lax.axis_index("dp")
        self.task = lax.axis_index("task")
        self.is_end = (self.me == 0) | (self.me == depth - 1)

    SCRATCH = 12

    @staticmethod
    def scratch(blocks, rows, half, tasks):
        chunks = 2 * blocks
        dma = pltpu.SemaphoreType.DMA
        return [
            pltpu.VMEM((2, chunks, rows, half), BF),
            pltpu.VMEM((SLOTS, 2, 2, rows, half), BF),
            pltpu.VMEM((STAGES, 2, 2, rows, half), BF),
            pltpu.VMEM((2, chunks, rows, half), BF),
            pltpu.VMEM((tasks, chunks, rows // tasks, half), BF),
            dma((STAGES,)),
            dma((SLOTS,)),
            pltpu.SemaphoreType.REGULAR,
            dma((2, chunks)),
            dma((2, chunks)),
            dma((blocks, tasks - 1)),
            dma((blocks, tasks - 1)),
        ]

    def far_copy(self, block):
        slot, stage = lax.rem(block, SLOTS), lax.rem(block, STAGES)
        return send(
            self.stage.at[stage], self.far.at[slot], self.far_send.at[stage], self.far_recv.at[slot],
            tensor=1 - lax.axis_index("tensor"),
        )

    def emit(self, block, value):
        block = jnp.int32(block)
        stage = lax.rem(block, STAGES)

        @pl.when(block >= STAGES)
        def _():
            self.far_copy(block).wait_send()

        @pl.when(block >= SLOTS)
        def _():
            pl.semaphore_wait(self.far_free, 1)

        size = self.half // 3
        for lane in range(0, self.half, size):
            lanes = slice(lane, lane + size)
            low = value(slice(self.half + lane, self.half + lane + size)).astype(BF)
            for way in range(2):
                for part in range(2):
                    row = (2 * way + part) * self.rows
                    self.stage[stage, way, part, :, lanes] = low[row : row + self.rows]
        self.far_copy(block).start()
        for lane in range(0, self.half, size):
            lanes = slice(lane, lane + size)
            low = value(lanes).astype(BF)
            for way in range(2):
                for part in range(2):
                    row = (2 * way + part) * self.rows
                    self.near[way, 2 * block + part, :, lanes] = low[row : row + self.rows]

    def absorb(self, block):
        block = jnp.int32(block)
        slot = lax.rem(block, SLOTS)
        self.far_copy(block).wait_recv()
        for way in range(2):
            chunks = pl.ds(2 * block, 2)
            self.near[way, chunks] = (
                self.near[way, chunks].astype(F32) + self.far[slot, way].astype(F32)
            ).astype(BF)

        @pl.when(block < self.chunks // 2 - SLOTS)
        def _():
            pl.semaphore_signal(
                self.far_free, inc=1, device_id={"tensor": 1 - lax.axis_index("tensor")},
                device_id_type=MESH_ID,
            )

    def pass_copy(self, way, chunk):
        piece = self.passed.at[way, chunk]
        target = self.me - 1 if way == 0 else self.me + 1
        return send(
            piece, piece, self.pass_send.at[way, chunk], self.pass_recv.at[way, chunk], dp=target
        )

    def part_rows(self, peer):
        size = self.rows // self.tasks
        return pl.ds(pl.multiple_of(peer * size, size), size)

    def part_copy(self, way, block, shift, peer):
        chunks = pl.ds(2 * block, 2)
        return send(
            self.passed.at[way, chunks, self.part_rows(peer)], self.parts.at[self.task, chunks],
            self.part_send.at[block, shift], self.part_recv.at[block, shift], task=peer,
        )

    def hops(self, way):
        return self.depth - 1 - self.me if way == 0 else self.me

    def units(self):
        return self.chunks + LAG * (self.depth - 1)

    def unit(self, index):
        for way in range(2):
            chunk = index - LAG * self.hops(way)

            @pl.when((chunk >= 0) & (chunk < self.chunks))
            def _(way=way, chunk=chunk):
                self.chunk_step(way, chunk)

    def chunk_step(self, way, chunk):
        first, last = self.hops(way) == 0, self.hops(way) == self.depth - 1
        block = chunk // 2
        own = self.near[way, chunk]

        @pl.when(first)
        def _():
            self.passed[way, chunk] = own

        @pl.when(jnp.logical_not(first))
        def _():
            self.pass_copy(way, chunk).wait_recv()
            self.passed[way, chunk] = (
                own.astype(F32) + self.passed[way, chunk].astype(F32)
            ).astype(BF)

        @pl.when(jnp.logical_not(last))
        def _():
            self.pass_copy(way, chunk).start()

        @pl.when(last & (chunk == 2 * block + 1))
        def _():
            for shift, peer in enumerate(task_peers(self.tasks)):
                self.part_copy(way, block, shift, peer).start()
            own_rows = self.part_rows(self.task)
            self.parts[self.task, chunk - 1] = self.passed[way, chunk - 1, own_rows]
            self.parts[self.task, chunk] = self.passed[way, chunk, own_rows]

    def wait_parts(self, block):
        for shift, peer in enumerate(task_senders(self.tasks)):
            landed = self.parts.at[peer, pl.ds(2 * block, 2)]
            send(
                landed, landed, self.part_send.at[block, shift], self.part_recv.at[block, shift],
                task=peer,
            ).wait_recv()

    def finish(self):
        def blocks(block, carry):
            for way in range(2):

                @pl.when(self.hops(way) != self.depth - 1)
                def _(way=way):
                    for part in range(2):
                        self.pass_copy(way, 2 * block + part).wait_send()

                @pl.when(self.hops(way) == self.depth - 1)
                def _(way=way):
                    for shift, peer in enumerate(task_peers(self.tasks)):
                        self.part_copy(way, block, shift, peer).wait_send()

            return carry

        lax.fori_loop(0, self.chunks // 2, blocks, 0)


def pairs_of(tasks):
    return [(a, b) for a in range(tasks) for b in range(a, tasks)]


def weights_of(gram, order_ref, tasks):
    totals = [0.0] * tasks
    for own in range(tasks):
        coeffs = [jnp.full_like(gram[0, 0], 1.0 if t == own else 0.0) for t in range(tasks)]
        for position in range(tasks):
            chosen = [
                jnp.where(order_ref[position] == t, 1.0, 0.0).astype(F32) for t in range(tasks)
            ]
            column = [sum(gram[t, j] * chosen[j] for j in range(tasks)) for t in range(tasks)]
            inner = sum(coeffs[t] * column[t] for t in range(tasks))
            square = sum(chosen[t] * column[t] for t in range(tasks))
            others = 1.0 - chosen[own]
            share = others * jnp.minimum(inner, 0.0) / (square + 1e-06)
            coeffs = [coeffs[t] - share * chosen[t] for t in range(tasks)]
        totals = [total + coeff for total, coeff in zip(totals, coeffs)]
    return totals


GROUPS = 4
UNITS = 2
TILE = 240


class ContextGrad:
    def __init__(self, key_grad, value_grad, weights, result, refs):
        self.grads, self.weights, self.result = (key_grad, value_grad), weights, result
        (self.staged, self.ring, self.done, self.staged_sem, self.ring_sem, self.done_sem) = refs
        self.tile, width = self.done.shape[1:]
        self.lanes = [pl.ds(0, width), pl.ds(width, width)]
        self.tiles = result.shape[0] // self.tile

    SCRATCH = 6

    @staticmethod
    def scratch(keys, width):
        dma = pltpu.SemaphoreType.DMA
        return [
            pltpu.VMEM((2, keys, SLAB), BF),
            pltpu.VMEM((2, TILE, 2 * width), BF),
            pltpu.VMEM((2, TILE, width), BF),
            dma((2,)),
            dma((2, 2)),
            dma((2,)),
        ]

    def staged_copies(self, image, group):
        keys = self.staged.shape[1]
        rows = pl.ds(pl.multiple_of(image * keys, keys), keys)
        lanes = pl.ds(pl.multiple_of(group * SLAB, SLAB), SLAB)
        return [
            pltpu.make_async_copy(
                self.staged.at[which], self.grads[which].at[rows, lanes], self.staged_sem.at[which]
            )
            for which in range(2)
        ]

    def put(self, step, image, group, values):
        @pl.when(step > 0)
        def _():
            self.settle()

        for which, value in enumerate(values):
            self.staged[which] = value
        for copy in self.staged_copies(image, group):
            copy.start()

    def settle(self):
        for copy in self.staged_copies(0, 0):
            copy.wait()

    def fetches(self, index):
        slot = lax.rem(index, 2)
        rows = pl.ds(pl.multiple_of(index * self.tile, self.tile), self.tile)
        return [
            pltpu.make_async_copy(
                self.grads[which].at[rows], self.ring.at[slot, :, self.lanes[which]],
                self.ring_sem.at[slot, which],
            )
            for which in range(2)
        ]

    def store(self, index):
        slot = lax.rem(index, 2)
        rows = pl.ds(pl.multiple_of(index * self.tile, self.tile), self.tile)
        return pltpu.make_async_copy(
            self.done.at[slot], self.result.at[rows], self.done_sem.at[slot]
        )

    def compute(self, index):
        @pl.when(index < self.tiles)
        def _():
            for copy in self.fetches(index):
                copy.wait()

            @pl.when(index + 1 < self.tiles)
            def _():
                for copy in self.fetches(index + 1):
                    copy.start()

            @pl.when(index >= 2)
            def _():
                self.store(index - 2).wait()

            slot = lax.rem(index, 2)
            total = mm_nt(self.ring[slot, :, self.lanes[0]], self.weights[0])
            total = total + mm_nt(self.ring[slot, :, self.lanes[1]], self.weights[1])
            self.done[slot] = total.astype(BF)
            self.store(index).start()

    def finish(self):
        for index in range(self.tiles - 2, self.tiles):
            self.store(jnp.int32(index)).wait()


def back_kernel(
    depth, tasks, images, groups, valid, block_order, order_ref, context_ref, query_ref, key_ref,
    value_ref, total_ref, mixed_grad_ref, tokens_ref, row_ref, gain_ref, qkv_ref, mixed_ref,
    self_total_ref, sum_ref, residual_ref, small_in_ref, all_w_ref, block_ref, left_ref, right_ref,
    *refs
):
    (
        context_grad_ref, query_grad_ref, update_ref, small_out_ref, gram_ref, block_far,
        key_grad, value_grad,
    ), refs = refs[:8], refs[8:]
    (
        context, context_t, key_acc, value_acc, cross_query_grad, qkv_grad, weights, block_sem,
        weight_sem, context_sem,
    ), refs = refs[:10], refs[10:]
    context_back = ContextGrad(
        key_grad, value_grad, weights.at[pl.ds(3, 2)], context_grad_ref,
        refs[: ContextGrad.SCRATCH],
    )
    refs = refs[ContextGrad.SCRATCH :]
    chain = Chain(depth, tasks, refs[: Chain.SCRATCH])
    refs = refs[Chain.SCRATCH :]
    gram_acc = refs[7]
    step = pl.program_id(0)
    cross_steps = images * groups
    half = chain.half
    is_end = chain.is_end
    pairs = pairs_of(tasks)

    def add_products(shares):
        for index, (a, b) in enumerate(pairs):
            product = shares[a] * shares[b]
            total = product[0:8]
            for row in range(8, product.shape[0], 8):
                total = total + product[row : row + 8]
            gram_acc[index * 8 : index * 8 + 8] += total

    def unit(index):
        chain.unit(index)
        since = index - LAG * (depth - 1) - 3
        block = since // 2

        @pl.when(is_end & (since >= 0) & (since == 2 * block))
        def _():
            chain.wait_parts(block)
            for part in range(2):
                add_products(
                    [chain.parts[t, 2 * block + part].astype(F32) for t in range(tasks)]
                )

    block_copy = send(
        block_ref, block_far, block_sem.at[0], block_sem.at[1], tensor=1 - lax.axis_index("tensor")
    )
    weight_copies = [
        pltpu.make_async_copy(all_w_ref.at[source], weights.at[target], weight_sem.at[index])
        for index, (source, target) in enumerate(
            [(pl.ds(0, 5), pl.ds(0, 5)), (pl.ds(5, 2), pl.ds(3, 2))]
        )
    ]

    def context_copy(image):
        keys = context.shape[0]
        own = lax.axis_index("tensor") * images + image
        rows = pl.ds(pl.multiple_of(own * keys, keys), keys)
        return pltpu.make_async_copy(context_ref.at[0, rows], context, context_sem)

    @pl.when(step == 0)
    def _():
        context_copy(0).start()
        weight_copies[0].start()
        greet(depth, tasks)
        block_copy.start()
        gram_acc[...] = jnp.zeros_like(gram_acc)
        refs[0][...] = small_in_ref[...]

    @pl.when(step < cross_steps)
    def _():
        image = step // groups
        group = step - image * groups

        chain.emit(step, lambda lanes: mm(left_ref[0], right_ref[0, :, lanes]))

        @pl.when(group == 0)
        def _():
            context_copy(image).wait()
            context_t[...] = context[...].T

            @pl.when(image + 1 < images)
            def _():
                context_copy(image + 1).start()

        def cross_unit(part):
            if part == 0:
                chain.absorb(step)
            unit(step * UNITS + part)

        grad_query, *grads = cross_back_step(
            image, group, query_ref, key_ref, value_ref, total_ref, mixed_grad_ref, refs[0],
            context_t, key_acc, value_acc, cross_unit,
        )
        context_back.put(step, image, group, grads)
        rows = grad_query.shape[0]
        cross_query_grad[
            pl.ds(pl.multiple_of(image * rows, rows), rows),
            pl.ds(pl.multiple_of(group * SLAB, SLAB), SLAB),
        ] = grad_query

        @pl.when(step == cross_steps - 1)
        def _():
            chain.emit(cross_steps, lambda lanes: key_acc[:, lanes])
            chain.emit(cross_steps + 1, lambda lanes: value_acc[:, lanes])

    @pl.when(step == cross_steps)
    def _():
        calls, done = [0], [cross_steps * UNITS]
        blocks = len(block_order)

        def self_unit():
            if calls[0] % 2 == 0:
                if done[0] % 2 == 0:
                    chain.absorb(done[0] // 2)
                unit(jnp.int32(done[0]))
                done[0] += 1
            calls[0] += 1

        context_back.settle()
        for copy in context_back.fetches(jnp.int32(0)):
            copy.start()
        weight_copies[0].wait()
        query_grad_ref[...] = self_back(
            images, valid, tokens_ref, weights, row_ref, gain_ref, qkv_ref, mixed_ref,
            self_total_ref, sum_ref, residual_ref, cross_query_grad, refs[0], qkv_grad,
            lambda block, value: chain.emit(block_order.index(block), value), self_unit,
            weight_copies[1].start,
        ).astype(BF)
        for block in range(-(-done[0] // 2), blocks):
            chain.absorb(block)
        weight_copies[1].wait()
        rest(
            chain, unit, context_back, done[0], order_ref, update_ref, small_out_ref, gram_ref, refs
        )
        for block in range(blocks - STAGES, blocks):
            chain.far_copy(jnp.int32(block)).wait_send()
        block_copy.wait()
        context_back.finish()


def rest(
    chain, unit, context_back, done, order_ref, update_ref, small_out_ref, gram_ref, refs
):
    (
        small, small_own, small_other, small_far, small_pass, small_all, small_both, gram_acc,
        gram_plane, gram_end, hop, out,
        small_far_sem, small_pass_sem, small_task_sem, small_dp_sem, small_core_sem,
        gram_plane_sem, gram_dp_sem, hop_sem, out_sem, update_sem,
    ) = refs
    depth, tasks, half = chain.depth, chain.tasks, chain.half
    me, task, core = (lax.axis_index(axis) for axis in ("dp", "task", "tensor"))
    is_end = chain.is_end
    top = me == 0
    pairs = pairs_of(tasks)
    own_lanes = pl.ds(pl.multiple_of(core * half, half), half)
    other_lanes = pl.ds(pl.multiple_of((1 - core) * half, half), half)
    small_own[0:8] = small[0:8, 0:half]
    small_own[8:] = small[8:, own_lanes]
    small_other[0:8] = small[0:8, half:]
    small_other[8:] = small[8:, other_lanes]
    small_copy = send(
        small_other, small_far, small_far_sem.at[0], small_far_sem.at[1], tensor=1 - core
    )
    small_copy.start()

    def small_hop():
        return send(
            small_pass, small_pass, small_pass_sem.at[0], small_pass_sem.at[1], dp=me - 1
        )

    def small_task_copy(shift, peer):
        return send(
            small_pass, small_all.at[task], small_task_sem.at[0, shift],
            small_task_sem.at[1, shift], task=peer,
        )

    def step(index, carry):
        unit(index)
        context_back.compute(index - done)

        @pl.when(index == done + 1 + LAG * chain.hops(0))
        def _():
            small_copy.wait_recv()
            total = small_own[...] + small_far[...]

            @pl.when(me == depth - 1)
            def _():
                small_pass[...] = total

            @pl.when(me < depth - 1)
            def _():
                small_hop().wait_recv()
                small_pass[...] += total

            @pl.when(me > 0)
            def _():
                small_hop().start()

            @pl.when(top)
            def _():
                for shift, peer in enumerate(task_peers(tasks)):
                    small_task_copy(shift, peer).start()
                small_all[task] = small_pass[...]

        return carry

    lax.fori_loop(done, max(chain.units() + 2, done + context_back.tiles), step, 0)

    @pl.when(top)
    def _():
        for shift, peer in enumerate(task_senders(tasks)):
            landed = small_all.at[peer]
            send(
                landed, landed, small_task_sem.at[0, shift], small_task_sem.at[1, shift], task=peer
            ).wait_recv()

    lanes = gram_plane.shape[2]
    plane = 2 * tasks
    mine = 2 * task + core

    def gram_copy(shift):
        to = lax.rem(mine + shift, plane)
        return send(
            gram_plane.at[mine], gram_plane.at[mine], gram_plane_sem.at[0, shift - 1],
            gram_plane_sem.at[1, shift - 1], task=to // 2, tensor=lax.rem(to, 2),
        )

    def gram_arrival(shift):
        place = lax.rem(mine + plane - shift, plane)
        return send(
            gram_plane.at[place], gram_plane.at[place], gram_plane_sem.at[0, shift - 1],
            gram_plane_sem.at[1, shift - 1], task=place // 2, tensor=lax.rem(place, 2),
        )

    def gram_dp_copy(end, shift):
        return send(
            gram_end.at[end], gram_end.at[end], gram_dp_sem.at[0, end, shift],
            gram_dp_sem.at[1, end, shift], dp=lax.rem((depth - 1) * end + shift + 1, depth),
        )

    def one_number(values):
        return jnp.sum(jnp.sum(values, axis=0, keepdims=True), axis=1, keepdims=True)

    @pl.when(top & (task == 0))
    def _():
        small_values = [small_all[t] for t in range(tasks)]
        for index, (a, b) in enumerate(pairs):
            product = small_values[a] * small_values[b]
            gram_acc[index * 8 : index * 8 + 8] += product[0:8] + product[8:16] + product[16:24]

    @pl.when(is_end)
    def _():
        gram_plane[mine] = jnp.zeros(gram_plane.shape[1:], F32)
        for index in range(len(pairs)):
            gram_plane[mine, index : index + 1] = jnp.broadcast_to(
                one_number(gram_acc[index * 8 : index * 8 + 8]), (1, lanes)
            )
        for shift in range(1, plane):
            gram_copy(shift).start()
        for shift in range(1, plane):
            gram_arrival(shift).wait_recv()

    for end in range(2):

        @pl.when(me == (depth - 1) * end)
        def _(end=end):
            total = gram_plane[0]
            for place in range(1, plane):
                total = total + gram_plane[place]
            gram_end[end] = total
            for shift in range(depth - 1):
                gram_dp_copy(end, shift).start()

    for end in range(2):
        for shift in range(depth - 1):

            @pl.when(me == ((depth - 1) * end + shift + 1) % depth)
            def _(end=end, shift=shift):
                gram_dp_copy(end, shift).wait_recv()

    gram = {}
    for index, (a, b) in enumerate(pairs):
        row = slice(index, index + 1)
        gram[a, b] = gram[b, a] = gram_end[0, row] + gram_end[1, row]
    for a in range(tasks):
        for b in range(tasks):
            gram_ref[a * tasks + b : a * tasks + b + 1] = gram[a, b]
    weights = [
        jnp.concatenate([weight] * (half // lanes), axis=1)
        for weight in weights_of(gram, order_ref, tasks)
    ]

    blocks = out.shape[0]
    group = blocks // GROUPS
    share = chain.rows // tasks
    own_share = pl.ds(pl.multiple_of(task * share, share), share)
    own_part = jnp.minimum(me, 1)

    def hop_copy(index):
        return send(
            hop.at[pl.ds(index * group, group)], out.at[pl.ds(index * group, group), own_share],
            hop_sem.at[0, index], hop_sem.at[1, index],
            dp=jnp.where(top, 1, depth - 2),
        )

    beside = [task + 1 - 2 * lax.rem(task, 2), task + 2 - 4 * (task // 2)]
    across = tasks - 1 - task

    def out_piece(index, owner):
        rows = pl.ds(pl.multiple_of(owner * share, share), share)
        return out.at[pl.ds(index * group, group), rows]

    def out_copy(index, which, owner):
        piece = out_piece(index, owner)
        peer = beside[which] if which < 2 else beside[1 if index < GROUPS // 2 else 0]
        return send(
            piece, piece, out_sem.at[0, index, which], out_sem.at[1, index, which], task=peer
        )

    def update_copy(index):
        at = pl.ds(index * group, group)
        return pltpu.make_async_copy(out.at[at], update_ref.at[at], update_sem.at[index])

    def weighted(chunk):
        total = weights[0] * chain.parts[0, chunk].astype(F32)
        for t in range(1, tasks):
            total = total + weights[t] * chain.parts[t, chunk].astype(F32)
        return total.astype(BF)

    def small_dp_copy(shift):
        return send(
            small_both.at[0], small_both.at[0], small_dp_sem.at[0, shift],
            small_dp_sem.at[1, shift], dp=shift + 1,
        )

    def small_core_copy():
        return send(
            small_both.at[0], small_both.at[1], small_core_sem.at[0], small_core_sem.at[1],
            tensor=1 - core,
        )

    @pl.when(top)
    def _():
        total = weights[0] * small_all[0]
        for t in range(1, tasks):
            total = total + weights[t] * small_all[t]
        small_both[0] = total
        for shift in range(depth - 1):
            small_dp_copy(shift).start()

    @pl.when(is_end)
    def _():
        for index in range(GROUPS):

            def other(block, carry):
                hop[block] = weighted(2 * block + 1 - own_part)
                return carry

            lax.fori_loop(index * group, (index + 1) * group, other, 0)
            hop_copy(index).start()

            def own(block, carry):
                out[block, own_share] = weighted(2 * block + own_part)
                return carry

            lax.fori_loop(index * group, (index + 1) * group, own, 0)
            for which in range(2):
                out_copy(index, which, task).start()

    @pl.when(jnp.logical_not(is_end))
    def _():
        for index in range(GROUPS):
            hop_copy(index).wait_recv()
            for which in range(2):
                out_copy(index, which, task).start()

    for shift in range(depth - 1):

        @pl.when(me == shift + 1)
        def _(shift=shift):
            small_dp_copy(shift).wait_recv()

    small_core_copy().start()

    for index in range(GROUPS):
        for which in range(2):
            out_copy(index, which, beside[which]).wait_recv()
        out_copy(index, 2, beside[0 if index < GROUPS // 2 else 1]).start()
    for index in range(GROUPS):
        out_copy(index, 2, across).wait_recv()
        update_copy(index).start()

    small_core_copy().wait_recv()
    small_out_ref[0:8, 0:half] = small_both[0, 0:8]
    small_out_ref[0:8, half:] = small_both[1, 0:8]
    small_out_ref[8:, own_lanes] = small_both[0, 8:]
    small_out_ref[8:, other_lanes] = small_both[1, 8:]

    small_copy.wait_send()
    small_core_copy().wait_send()
    chain.finish()

    @pl.when(me > 0)
    def _():
        small_hop().wait_send()

    @pl.when(top)
    def _():
        for shift, peer in enumerate(task_peers(tasks)):
            small_task_copy(shift, peer).wait_send()
        for shift in range(depth - 1):
            small_dp_copy(shift).wait_send()

    for end in range(2):

        @pl.when(me == (depth - 1) * end)
        def _(end=end):
            for shift in range(depth - 1):
                gram_dp_copy(end, shift).wait_send()

    @pl.when(is_end)
    def _():
        for shift in range(1, plane):
            gram_copy(shift).wait_send()
        for index in range(GROUPS):
            hop_copy(index).wait_send()

    for index in range(GROUPS):
        update_copy(index).wait()
        for which in range(3):
            out_copy(index, which, task).wait_send()


def spread_kernel(
    images, valid, tasks, block_order, parts_ref, context_grad_ref, query_grad_ref, block_ref,
    block_far_ref, small_ref, gram_in_ref,
    update_ref, context_out_ref, query_out_ref, block_out_ref, head_ref, row_ref, gain_ref, gram_ref,
):
    ordered = [parts_ref[block_order.index(block)] for block in range(len(block_order))]
    update_ref[...] = jnp.swapaxes(jnp.stack(ordered), 0, 1).astype(F32)
    context_out_ref[...] = context_grad_ref[...]

    @pl.when(pl.program_id(0) == 0)
    def _():
        padded = query_grad_ref.shape[0] // images
        first = lax.axis_index("tensor") == 0

        def rows(ref, image):
            return ref[image * padded : (image + 1) * padded].astype(F32)[:valid]

        for image in range(images):
            at = slice(image * valid, (image + 1) * valid)
            after = slice((images + image) * valid, (images + image + 1) * valid)
            query_out_ref[at] = rows(query_grad_ref, image).astype(BF)
            near, far = rows(block_ref, image), rows(block_far_ref, image)
            block_out_ref[at] = jnp.where(first, near, far).astype(BF)
            block_out_ref[after] = jnp.where(first, far, near).astype(BF)
        head_ref[...] = small_ref[0:8, 0 : head_ref.shape[1]]
        for which in range(6):
            row_ref[which // 2, which % 2 : which % 2 + 1] = small_ref[8 + which : 9 + which]
        gain_ref[...] = small_ref[14:17]
        for a in range(tasks):
            for b in range(tasks):
                at = a * tasks + b
                gram_ref[a : a + 1, b : b + 1] = gram_in_ref[at : at + 1, 0:1]


def gram_kernel(parts_ref, gram_ref):
    tasks = parts_ref.shape[0]

    @pl.when(pl.program_id(0) == 0)
    def _():
        gram_ref[...] = jnp.zeros_like(gram_ref)

    shares = [parts_ref[task, 0].astype(F32) for task in range(tasks)]
    for a in range(tasks):
        for b in range(a, tasks):
            gram_ref[a * tasks + b : a * tasks + b + 1] += rows_sum(shares[a] * shares[b])


def update_kernel(weights_ref, parts_ref, update_ref):
    tasks, blocks = parts_ref.shape[:2]
    for block in range(blocks):
        total = weights_ref[0] * parts_ref[0, block].astype(F32)
        for task in range(1, tasks):
            total += weights_ref[task] * parts_ref[task, block].astype(F32)
        update_ref[:, block, :] = total


def body(
    queries, memory, cotangent, matches, counts, task_order, params, head_bias, row_bias, norm_gain
):
    all_images = matches.shape[1]
    valid = matches.shape[2]
    width = queries.shape[2]
    half = params.shape[2]
    block_count = params.shape[1]
    blocks = (block_count - 8) // 2
    cores = lax.axis_size("tensor")
    images = all_images // cores
    keys = memory.shape[1] // all_images
    padded = -(-valid // 16) * 16
    rows = images * padded
    groups = width // SLAB
    stack = GROUP * padded
    core = lax.axis_index("tensor")

    def const(shape, *index):
        return pl.BlockSpec(shape, lambda *_: index)

    total_shape = jax.ShapeDtypeStruct((images * groups, 8, stack), F32)
    low_rows = jax.ShapeDtypeStruct((rows, width), BF)
    full_rows = jax.ShapeDtypeStruct((rows, width), F32)
    small_shape = jax.ShapeDtypeStruct((24, width), F32)
    one_block = jax.ShapeDtypeStruct((width, width), BF)
    small_spec = const((24, width), 0, 0)
    row_spec = const(row_bias.shape, 0, 0, 0)
    gain_spec = const(norm_gain.shape, 0, 0)
    head_spec = const((16, width), 0, 0)
    rows_spec = const((rows, width), 0, 0)

    parts = 4
    part_blocks = block_count // 2
    raw_spec = const((None, *queries.shape[1:]), 0, 0, 0)
    (
        weights, head_rows, tokens, own_cotangent, qkv, self_mixed, self_total, first_sum,
        cross_query,
    ) = pl.pallas_call(
        functools.partial(start_kernel, images, valid),
        grid=(2 * parts,),
        out_shape=(
            jax.ShapeDtypeStruct((block_count, width, cores * half), BF),
            jax.ShapeDtypeStruct((16, cores * half), BF),
            low_rows, low_rows,
            jax.ShapeDtypeStruct((3, rows, width), BF), low_rows, total_shape, full_rows, low_rows,
        ),
        in_specs=[
            pl.BlockSpec((width // parts, part_blocks, half), lambda s: (s % parts, s // parts, 0)),
            const((8, half), 0, 0), raw_spec, raw_spec, row_spec, gain_spec,
        ],
        out_specs=(
            any_spec(), head_spec, rows_spec, rows_spec,
            const((3, rows, width), 0, 0, 0), rows_spec, const(total_shape.shape, 0, 0, 0),
            rows_spec, rows_spec,
        ),
        scratch_shapes=[
            pltpu.VMEM((part_blocks, width, cores * half), BF),
            pltpu.VMEM((part_blocks, width, half), BF),
            pltpu.VMEM((16, half), BF),
            pltpu.VMEM((16, cores * half), BF),
            pltpu.SemaphoreType.DMA((2 * parts + 1,)),
            pltpu.SemaphoreType.DMA((2 * parts + 1,)),
            pltpu.SemaphoreType.DMA((2 * parts,)),
            pltpu.SemaphoreType.DMA(()),
        ],
        compiler_params=params_for(collective_id=0, has_side_effects=True),
        name="start",
    )(params, head_bias, queries, cotangent, row_bias, norm_gain)

    def own_image(i, g):
        return 0, lax.axis_index("tensor") * images + i, 0

    context_all = pl.BlockSpec((None, keys, width), own_image)
    slab_q = pl.BlockSpec((padded, SLAB), lambda i, g: (i, g))
    slab_k = pl.BlockSpec((keys, SLAB), lambda i, g: (i, g))
    slab_t = pl.BlockSpec((1, 8, stack), lambda i, g: (i * groups + g, 0, 0))
    image_q = pl.BlockSpec((padded, width), lambda i: (i, 0))
    image_k = pl.BlockSpec((keys, width), lambda i: (i, 0))

    def slab_w(block):
        return pl.BlockSpec((1, width, SLAB), lambda i, g: (block, 0, g))

    key_rows = jax.ShapeDtypeStruct((images * keys, width), BF)
    keys_act, values_act, cross_mixed, cross_total = pl.pallas_call(
        cross_kernel,
        grid=(images,),
        in_specs=[
            pl.BlockSpec((None, keys, width), lambda i: own_image(i, 0)),
            image_q, const((1, width, width), 5, 0, 0), const((1, width, width), 6, 0, 0), head_spec,
        ],
        out_specs=(
            image_k, image_k, image_q, pl.BlockSpec((groups, 8, stack), lambda i: (i, 0, 0)),
        ),
        out_shape=(key_rows, key_rows, low_rows, total_shape),
        compiler_params=params_for(),
        name="cross_forward",
    )(memory, cross_query, weights, weights, head_rows)

    per = 2 if blocks % 2 == 0 else 1
    block_rows, left, right, mixed_grad, second_grad, ffn_small = pl.pallas_call(
        functools.partial(ffn_kernel, images, blocks, per),
        grid=(2 * blocks // per,),
        out_shape=(
            low_rows,
            jax.ShapeDtypeStruct((3, width, rows), BF),
            jax.ShapeDtypeStruct((2 * blocks + 1, rows, width), BF),
            low_rows, full_rows, small_shape,
        ),
        in_specs=[
            rows_spec, rows_spec, rows_spec,
            const(matches.shape, 0, 0, 0),
            pl.BlockSpec(memory_space=pltpu.SMEM),
            const((1, width, width), 7, 0, 0),
            any_spec(), head_spec, row_spec, gain_spec,
        ],
        out_specs=(rows_spec, any_spec(), any_spec(), rows_spec, rows_spec, small_spec),
        scratch_shapes=[
            pltpu.VMEM((rows, width), F32),
            pltpu.VMEM((rows, width), BF),
            pltpu.VMEM((3, width, rows), BF),
            pltpu.VMEM((2 * blocks, rows, width), BF),
            pltpu.VMEM((blocks, rows, width), F32),
            pltpu.VMEM((rows, width), F32),
            pltpu.VMEM((rows, width), F32),
            pltpu.VMEM((8, width), F32),
            pltpu.VMEM((2, blocks, width, width), BF),
            pltpu.SemaphoreType.DMA((3,)),
            pltpu.SemaphoreType.DMA((2 * blocks + 1,)),
            pltpu.SemaphoreType.DMA((2, blocks // per)),
        ],
        compiler_params=params_for(),
        name="ffn",
    )(
        first_sum, cross_mixed, own_cotangent, matches, counts, weights, weights, head_rows, row_bias,
        norm_gain,
    )

    depth, tasks = lax.axis_size("dp"), lax.axis_size("task")
    by_chain = depth == 4 and tasks == 4 and cores == 2

    if by_chain:
        block_order = [*range(8, block_count), 7, 5, 6, 4, 3, 0, 1, 2]
        chain_rows = width // depth
        pair_rows = 8 * len(pairs_of(tasks))
        dma = pltpu.SemaphoreType.DMA
        last = images * groups - 1

        def at_step(make):
            def index_map(step):
                now = jnp.minimum(step, last)
                return make(now // groups, now - groups * (now // groups))

            return index_map

        def product(step):
            return jnp.minimum(step, 2 * blocks)

        def once(shape):
            return pl.BlockSpec(
                shape, lambda step: (0,) * len(shape), pipeline_mode=pl.Buffered(1)
            )

        step_q = pl.BlockSpec((padded, SLAB), at_step(lambda i, g: (i, g)))
        step_k = pl.BlockSpec((keys, SLAB), at_step(lambda i, g: (i, g)))

        small_half = pltpu.VMEM((24, half), F32)
        (
            context_grad, token_grad, update_parts, small_out, gram_rows, block_far, *_,
        ) = pl.pallas_call(
            functools.partial(
                back_kernel, depth, tasks, images, groups, valid, block_order
            ),
            grid=(images * groups + 1,),
            out_shape=(
                key_rows, low_rows,
                jax.ShapeDtypeStruct((block_count, chain_rows, half), BF),
                small_shape,
                jax.ShapeDtypeStruct((16, 128), F32),
                low_rows,
                key_rows, key_rows,
            ),
            in_specs=[
                pl.BlockSpec(memory_space=pltpu.SMEM),
                any_spec(), step_q, step_k, step_k,
                pl.BlockSpec((1, 8, stack), at_step(lambda i, g: (i * groups + g, 0, 0))),
                step_q,
                once((rows, width)), once(row_bias.shape), once(norm_gain.shape),
                once((3, rows, width)), once((rows, width)), once(total_shape.shape),
                once((rows, width)), once((rows, width)), once((24, width)),
                any_spec(), any_spec(),
                pl.BlockSpec((1, width, rows), lambda step: (product(step) // blocks, 0, 0)),
                pl.BlockSpec((1, rows, width), lambda step: (product(step), 0, 0)),
            ],
            out_specs=(
                any_spec(), once((rows, width)), any_spec(), once((24, width)), once((16, 128)),
                *[any_spec()] * 3,
            ),
            scratch_shapes=[
                pltpu.VMEM((keys, width), BF),
                pltpu.VMEM((width, keys), BF),
                pltpu.VMEM((width, width), F32),
                pltpu.VMEM((width, width), F32),
                pltpu.VMEM((rows, width), BF),
                pltpu.VMEM((3, rows, width), BF),
                pltpu.VMEM((5, width, width), BF),
                dma((2,)),
                dma((2,)),
                dma(()),
                *ContextGrad.scratch(keys, width),
                *Chain.scratch(block_count, chain_rows, half, tasks),
                pltpu.VMEM((24, width), F32),
                small_half, small_half, small_half, small_half,
                pltpu.VMEM((tasks, 24, half), F32),
                pltpu.VMEM((2, 24, half), F32),
                pltpu.VMEM((pair_rows, half), F32),
                pltpu.VMEM((2 * tasks, 16, 128), F32),
                pltpu.VMEM((2, 16, 128), F32),
                pltpu.VMEM((block_count, chain_rows // tasks, half), BF),
                pltpu.VMEM((block_count, chain_rows, half), BF),
                dma((2,)),
                dma((2,)),
                dma((2, tasks - 1)),
                dma((2, depth - 1)),
                dma((2,)),
                dma((2, 2 * tasks - 1)),
                dma((2, 2, depth - 1)),
                dma((2, GROUPS)),
                dma((2, GROUPS, tasks - 1)),
                dma((GROUPS,)),
            ],
            compiler_params=params_for(collective_id=1, has_side_effects=True),
            name="backward",
        )(
            task_order, memory, cross_query, keys_act, values_act, cross_total, mixed_grad,
            tokens, row_bias, norm_gain, qkv, self_mixed, self_total, first_sum,
            second_grad, ffn_small, weights, block_rows, left, right,
        )
        tile = chain_rows // images
        (
            param_update, memory_grad, query_grad, block_out, head_update, row_update, gain_update,
            gram,
        ) = pl.pallas_call(
            functools.partial(spread_kernel, images, valid, tasks, block_order),
            grid=(images,),
            out_shape=(
                jax.ShapeDtypeStruct((chain_rows, block_count, half), F32),
                key_rows,
                jax.ShapeDtypeStruct((images * valid, width), BF),
                jax.ShapeDtypeStruct((all_images * valid, width), BF),
                jax.ShapeDtypeStruct((8, half), F32),
                jax.ShapeDtypeStruct((3, 2, width), F32),
                jax.ShapeDtypeStruct((3, width), F32),
                jax.ShapeDtypeStruct((tasks, tasks), F32),
            ),
            in_specs=[
                pl.BlockSpec((block_count, tile, half), lambda r: (0, r, 0)),
                pl.BlockSpec((keys, width), lambda r: (r, 0)),
                rows_spec, rows_spec, rows_spec, small_spec, const((16, 128), 0, 0),
            ],
            out_specs=(
                pl.BlockSpec((tile, block_count, half), lambda r: (r, 0, 0)),
                pl.BlockSpec((keys, width), lambda r: (r, 0)),
                const((images * valid, width), 0, 0),
                const((all_images * valid, width), 0, 0),
                const((8, half), 0, 0), const((3, 2, width), 0, 0, 0),
                const((3, width), 0, 0), const((tasks, tasks), 0, 0),
            ),
            compiler_params=params_for(),
            name="spread",
        )(update_parts, context_grad, token_grad, block_rows, block_far, small_out, gram_rows)
        return (
            block_out[None], query_grad[None], memory_grad[None], param_update, head_update,
            row_update, gain_update, gram,
        )

    def unpad(array):
        return array.reshape(images, padded, width)[:, :valid].reshape(1, images * valid, width)

    block_out = lax.all_gather(unpad(block_rows), "tensor", axis=1, tiled=True)
    cross_query_grad, context_grad, key_wg, value_wg, cross_small = pl.pallas_call(
        cross_back_kernel,
        grid=(images, groups),
        in_specs=[
            context_all, slab_q, slab_k, slab_k, slab_t, slab_q, slab_w(5), slab_w(6),
        ],
        out_specs=(
            slab_q,
            pl.BlockSpec((keys, width), lambda i, g: (i, 0)),
            const((width, width), 0, 0), const((width, width), 0, 0), small_spec,
        ),
        scratch_shapes=[
            pltpu.VMEM((width, keys), BF),
            pltpu.VMEM((keys, width), F32),
            pltpu.VMEM((width, width), F32),
            pltpu.VMEM((width, width), F32),
        ],
        out_shape=(low_rows, key_rows, one_block, one_block, small_shape),
        compiler_params=params_for(),
        name="cross_backward",
    )(memory, cross_query, keys_act, values_act, cross_total, mixed_grad, weights, weights)

    token_grad, self_wg, self_small = pl.pallas_call(
        functools.partial(self_back_kernel, images, valid),
        grid=(1,),
        out_shape=(
            low_rows, jax.ShapeDtypeStruct((5, width, width), BF), small_shape,
        ),
        in_specs=[
            rows_spec, const((5, width, width), 0, 0, 0), row_spec, gain_spec,
            const((3, rows, width), 0, 0, 0), rows_spec, const(total_shape.shape, 0, 0, 0),
            rows_spec, rows_spec, rows_spec,
        ],
        out_specs=(
            rows_spec, const((5, width, width), 0, 0, 0), small_spec,
        ),
        scratch_shapes=[pltpu.VMEM((3, rows, width), BF)],
        compiler_params=params_for(),
        name="self_backward",
    )(
        tokens, weights, row_bias, norm_gain, qkv, self_mixed, self_total, first_sum, second_grad,
        cross_query_grad,
    )

    query_grad = unpad(token_grad)
    memory_grad = context_grad[None]

    small = self_small + cross_small + ffn_small
    product = functools.partial(jnp.einsum, "dr,jre->jde", preferred_element_type=F32)
    grad_in = product(left[0], right[:blocks]).astype(BF)
    grad_out = product(left[1], right[blocks : 2 * blocks]).astype(BF)
    cross_out_wg = product(left[2], right[2 * blocks :])[0].astype(BF)
    grads = jnp.concatenate(
        [self_wg, jnp.stack([key_wg, value_wg, cross_out_wg]), grad_in, grad_out], axis=0
    )
    swap = [(0, 1), (1, 0)]
    grads = (
        grads[:, :, :half].astype(F32) + lax.ppermute(grads[:, :, half:], "tensor", swap).astype(F32)
    ).astype(BF)
    head_small = small[:8, :half] + lax.ppermute(small[:8, half:], "tensor", swap)
    row_small = lax.psum(small[8:17], ("dp", "tensor"))
    head_small = lax.psum(head_small, "dp")
    shard = lax.psum_scatter(grads, "dp", scatter_dimension=1, tiled=True)
    all_shards = lax.all_gather(shard, "task", axis=0, tiled=False)
    all_head = lax.all_gather(head_small, "task", axis=0, tiled=False)
    all_row = lax.all_gather(row_small, "task", axis=0, tiled=False)
    tasks = all_shards.shape[0]
    share_rows = shard.shape[1]
    sums = pl.pallas_call(
        gram_kernel,
        grid=(block_count,),
        out_shape=jax.ShapeDtypeStruct((tasks * tasks, half), F32),
        in_specs=[pl.BlockSpec((tasks, 1, share_rows, half), lambda k: (0, k, 0, 0))],
        out_specs=const((tasks * tasks, half), 0, 0),
        compiler_params=params_for(),
        name="gram",
    )(all_shards)
    upper = jnp.sum(sums, axis=1).reshape(tasks, tasks)
    gram_weights = upper + upper.T - jnp.diag(jnp.diag(upper))
    gram_weights = lax.psum(gram_weights, ("dp", "tensor"))
    gram_heads = jnp.einsum("axy,bxy->ab", all_head, all_head, precision=highest)
    gram_heads = lax.psum(gram_heads, "tensor")
    gram = gram_weights + gram_heads + jnp.einsum(
        "axy,bxy->ab", all_row, all_row, precision=highest
    )
    task_weights = combine_weights(gram, task_order)
    tile = 64 if share_rows % 64 == 0 else share_rows
    param_update = pl.pallas_call(
        update_kernel,
        grid=(share_rows // tile,),
        out_shape=jax.ShapeDtypeStruct((share_rows, block_count, half), F32),
        in_specs=[
            pl.BlockSpec(memory_space=pltpu.SMEM),
            pl.BlockSpec((tasks, block_count, tile, half), lambda r: (0, 0, r, 0)),
        ],
        out_specs=pl.BlockSpec((tile, block_count, half), lambda r: (r, 0, 0)),
        compiler_params=params_for(),
        name="update",
    )(task_weights, all_shards)
    head_bias_update = jnp.einsum("a,axy->xy", task_weights, all_head, precision=highest)
    row_update = jnp.einsum("a,axy->xy", task_weights, all_row, precision=highest)
    return (
        block_out, query_grad, memory_grad, param_update, head_bias_update,
        row_update[:6].reshape(3, 2, width), row_update[6:9], gram,
    )


def solution(mesh):
    return jax.shard_map(
        body,
        mesh=mesh,
        in_specs=(
            P("task", "dp", None),
            P("task", "dp", None),
            P("task", "dp", None),
            P("task", "dp", None),
            P("task", "dp"),
            P(),
            P(None, None, "tensor"),
            P(None, "tensor"),
            P(),
            P(),
        ),
        out_specs=(
            P("task", "dp", None),
            P("task", ("dp", "tensor"), None),
            P("task", ("dp", "tensor"), None),
            P("dp", None, "tensor"),
            P(None, "tensor"),
            P(),
            P(),
            P(),
        ),
        check_vma=False,
    )
```

```python
import functools

import jax
import jax.numpy as jnp
from jax import lax
from jax.experimental import pallas as pl
from jax.experimental.pallas import tpu as pltpu
from jax.sharding import PartitionSpec as P

HD = 64
GROUP = 4
SLAB = GROUP * HD
BF = jnp.bfloat16
F32 = jnp.float32
MESH_ID = pl.DeviceIdType.MESH
highest = lax.Precision.HIGHEST
VMEM_LIMIT = 63 * 2**20


def combine_weights(gram_matrix, order_list):
    task_count = gram_matrix.shape[0]
    task_index = jnp.arange(task_count, dtype=jnp.int32)
    summed = jnp.zeros((task_count,), F32)
    for own_task in range(task_count):
        coeffs = (task_index == own_task).astype(F32)
        for position in range(task_count):
            chosen = (task_index == order_list[position]).astype(F32)
            column = jnp.sum(gram_matrix * chosen[None, :], axis=1)
            inner_dot = jnp.sum(coeffs * column)
            square = jnp.sum(chosen * column)
            others = (order_list[position] != own_task).astype(F32)
            coeffs = coeffs - others * jnp.minimum(inner_dot, 0.0) / (square + 1e-06) * chosen
        summed = summed + coeffs
    return summed


def mm(a, b):
    return jnp.dot(a, b, preferred_element_type=F32)


def mm_nt(a, b):
    return lax.dot_general(a, b, (((1,), (1,)), ((), ())), preferred_element_type=F32)


def mm_tn(a, b):
    return lax.dot_general(a, b, (((0,), (0,)), ((), ())), preferred_element_type=F32)


def row_of(row_ref, which):
    return row_ref[which // 2, which % 2 : which % 2 + 1].astype(F32)


def gain_of(gain_ref, which):
    return gain_ref[which : which + 1].astype(F32)


def norm_parts(residual):
    row_mean = jnp.mean(residual, axis=-1, keepdims=True)
    centred = residual - row_mean
    variance = jnp.mean(centred * centred, axis=-1, keepdims=True)
    scale = lax.rsqrt(variance + 1e-05)
    return centred * scale, scale


def norm_back(normed, scale, gain_row, grad):
    scaled = grad * gain_row
    first = jnp.mean(scaled, axis=-1, keepdims=True)
    second = jnp.mean(scaled * normed, axis=-1, keepdims=True)
    return scale * (scaled - first - normed * second)


def rows_sum(value):
    return jnp.sum(value, axis=0, keepdims=True)


def gelu_tanh(hidden):
    square = hidden * hidden
    tanh = jnp.tanh(hidden * (0.7978845608028654 + 0.7978845608028654 * 0.044715 * square))
    half = 0.5 * (1.0 + tanh)
    inner = 0.7978845608028654 + 0.7978845608028654 * 3 * 0.044715 * square
    return hidden * half, half + 0.5 * hidden * (1.0 - tanh * tanh) * inner


def head_mask(head, rows, dtype):
    lane = lax.broadcasted_iota(jnp.int32, (rows, SLAB), 1)
    return (lane // HD == head).astype(F32).astype(dtype)


def stack_heads(slab):
    return jnp.concatenate(
        [slab * head_mask(head, slab.shape[0], slab.dtype) for head in range(GROUP)], axis=0
    )


def unstack_heads(stacked):
    rows = stacked.shape[0] // GROUP
    total = None
    for head in range(GROUP):
        part = stacked[head * rows : (head + 1) * rows] * head_mask(head, rows, stacked.dtype)
        total = part if total is None else total + part
    return total


def scores_of(query_stack, key_slab, valid):
    scores = mm_nt(key_slab, query_stack)
    if valid < key_slab.shape[0]:
        row = lax.broadcasted_iota(jnp.int32, scores.shape, 0)
        scores = jnp.where(row < valid, scores, -1e30)
    return scores


def attend(query_slab, key_slab, value_slab, valid):
    scores = scores_of(stack_heads(query_slab * HD ** (-0.5)), key_slab, valid)
    row_max = jnp.max(scores, axis=0, keepdims=True)
    exps = jnp.exp(scores - row_max)
    total = jnp.sum(exps, axis=0, keepdims=True)
    probs = (exps * (1.0 / total)).astype(BF)
    mixed = unstack_heads(mm_tn(value_slab, probs).T)
    return mixed, row_max + jnp.log(total)


def attend_back(query_slab, key_slab, value_slab, log_total, grad_slab, valid):
    query_stack = stack_heads(query_slab * HD ** (-0.5))
    grad_stack = stack_heads(grad_slab)
    probs = jnp.exp(scores_of(query_stack, key_slab, valid) - log_total)
    grad_value = mm(probs.astype(BF), grad_stack)
    grad_probs = mm_nt(value_slab, grad_stack)
    inner = jnp.sum(probs * grad_probs, axis=0, keepdims=True)
    grad_scores = (probs * (grad_probs - inner)).astype(BF)
    grad_key = mm(grad_scores, query_stack)
    grad_query = unstack_heads(mm_tn(key_slab, grad_scores).T) * HD ** (-0.5)
    return grad_query.astype(BF), grad_key.astype(BF), grad_value.astype(BF)


KEY_TILE = 400


def attend_back_tiles(
    query_slab, key_ref, value_ref, log_total, grad_slab, mixed_slab, key_grad_ref, value_grad_ref
):
    query_stack = stack_heads(query_slab * HD ** (-0.5))
    grad_stack = stack_heads(grad_slab)
    product = stack_heads(grad_slab.astype(F32) * mixed_slab.astype(F32))
    high = product.astype(BF)
    low = (product - high.astype(F32)).astype(BF)
    ones = jnp.ones((8, SLAB), BF)
    inner = (mm_nt(ones, high) + mm_nt(ones, low))[0:1]
    keys = key_ref.shape[0]
    size = KEY_TILE if keys % KEY_TILE == 0 else keys

    def tile(index, grad_query):
        rows = pl.ds(pl.multiple_of(index * size, size), size)
        key, value = key_ref[rows], value_ref[rows]
        probs = jnp.exp(mm_nt(key, query_stack) - log_total)
        grad_scores = (probs * (mm_nt(value, grad_stack) - inner)).astype(BF)
        value_grad_ref[rows] = mm(probs.astype(BF), grad_stack).astype(BF)
        key_grad_ref[rows] = mm(grad_scores, query_stack).astype(BF)
        return grad_query + mm_tn(key, grad_scores)

    grad_query = lax.fori_loop(
        0, keys // size, tile, jnp.zeros((SLAB, query_stack.shape[0]), F32)
    )
    return (unstack_heads(grad_query.T) * HD ** (-0.5)).astype(BF)


def pad_rows(source_ref, target_ref, images, valid):
    first = lax.axis_index("tensor") == 0
    padded = target_ref.shape[0] // images
    for image in range(images):
        here, there = (
            source_ref[(core * images + image) * valid : (core * images + image + 1) * valid]
            for core in range(2)
        )
        rows = jnp.where(first, here.astype(F32), there.astype(F32))
        fill = jnp.zeros((padded - valid, rows.shape[1]), F32)
        target_ref[image * padded : (image + 1) * padded] = jnp.concatenate(
            [rows, fill], axis=0
        ).astype(target_ref.dtype)


def send(source, target, send_sem, recv_sem, **device):
    return pltpu.make_async_remote_copy(
        source, target, send_sem, recv_sem, device_id=device, device_id_type=MESH_ID
    )


def start_kernel(
    images, valid, own_ref, bias_ref, queries_ref, cotangent_ref, row_ref, gain_ref,
    full_ref, head_ref, tokens_ref, own_cotangent_ref, qkv_ref, mixed_ref, total_ref, sum_ref,
    cross_query_ref, first, second, bias_own, bias_all, remote_send, remote_recv, local_sem, far_sem,
):
    step, steps = pl.program_id(0), pl.num_programs(0)
    other = 1 - lax.axis_index("tensor")
    rows, blocks, width = own_ref.shape
    parts = steps // 2
    near, far = pl.ds(0, width), pl.ds(width, width)
    lower, upper = pl.ds(0, blocks), pl.ds(blocks, blocks)

    def rows_of(part):
        return pl.ds(pl.multiple_of(part * rows, rows), rows)

    def first_copies(part):
        at = rows_of(part)
        return (
            send(
                first.at[:, at, near], first.at[:, at, far], remote_send.at[part],
                remote_recv.at[part], tensor=other,
            ),
            pltpu.make_async_copy(
                first.at[:, at, near], full_ref.at[lower, at, near], local_sem.at[part]
            ),
        )

    def second_copies(part):
        at = rows_of(part)
        return (
            send(
                second.at[:, at], full_ref.at[upper, at, far], remote_send.at[parts + part],
                remote_recv.at[parts + part], tensor=other,
            ),
            pltpu.make_async_copy(
                second.at[:, at], full_ref.at[upper, at, near], local_sem.at[parts + part]
            ),
        )

    bias_copy = send(
        bias_own, bias_all.at[:, far], remote_send.at[steps], remote_recv.at[steps], tensor=other
    )
    far_copy = pltpu.make_async_copy(first.at[:, :, far], full_ref.at[lower, :, far], far_sem)

    @pl.when(step == 0)
    def _():
        barrier = pltpu.get_barrier_semaphore()
        pl.semaphore_signal(barrier, inc=1, device_id={"tensor": other}, device_id_type=MESH_ID)
        pl.semaphore_wait(barrier, 1)
        bias_own[...] = jnp.zeros_like(bias_own)
        bias_own[0 : bias_ref.shape[0]] = bias_ref[...]
        bias_copy.start()
        bias_all[:, near] = bias_own[...]

    @pl.when(step < parts)
    def _():
        first[:, rows_of(step), near] = jnp.swapaxes(own_ref[...], 0, 1)
        for copy in first_copies(step):
            copy.start()

    @pl.when(step >= parts)
    def _():
        second[:, rows_of(step - parts)] = jnp.swapaxes(own_ref[...], 0, 1)
        for copy in second_copies(step - parts):
            copy.start()

    @pl.when(step == steps - 1)
    def _():
        pad_rows(queries_ref, tokens_ref, images, valid)
        pad_rows(cotangent_ref, own_cotangent_ref, images, valid)
        bias_copy.wait()
        head_ref[...] = bias_all[...]
        for part in range(parts):
            first_copies(part)[0].wait_recv()
        far_copy.start()
        self_forward(
            images, valid, tokens_ref, first, head_ref, row_ref, gain_ref, qkv_ref, mixed_ref,
            total_ref, sum_ref, cross_query_ref,
        )
        far_copy.wait()
        for part in range(parts):
            remote, local = first_copies(part)
            remote.wait_send()
            local.wait()
            for copy in second_copies(part):
                copy.wait()


def any_spec():
    return pl.BlockSpec(memory_space=pl.ANY)


def whole_spec():
    return pl.BlockSpec(memory_space=pltpu.VMEM)


def params_for(**keys):
    return pltpu.CompilerParams(vmem_limit_bytes=VMEM_LIMIT, **keys)


def place_of(index, groups, rows):
    image = index // groups
    group = index - image * groups
    if isinstance(index, int):
        return pl.ds(image * rows, rows), pl.ds(group * SLAB, SLAB)
    return (
        pl.ds(pl.multiple_of(image * rows, rows), rows),
        pl.ds(pl.multiple_of(group * SLAB, SLAB), SLAB),
    )


def self_forward(images, valid, tokens_ref, weight_ref, head_ref, row_ref, gain_ref, qkv_ref,
                 mixed_ref, total_ref, sum_ref, cross_query_ref):
    tokens = tokens_ref[...]
    rows = tokens.shape[0] // images
    width = tokens.shape[1]
    qkv_ref[0] = (mm(tokens, weight_ref[0]) + head_ref[0:1].astype(F32)).astype(BF)
    qkv_ref[1] = mm(tokens, weight_ref[1]).astype(BF)
    qkv_ref[2] = (mm(tokens, weight_ref[2]) + head_ref[1:2].astype(F32)).astype(BF)
    groups = width // SLAB

    for index in range(images * groups):
        at, lanes = place_of(index, groups, rows)
        mixed, log_total = attend(
            qkv_ref[0, at, lanes], qkv_ref[1, at, lanes], qkv_ref[2, at, lanes], valid
        )
        mixed_ref[at, lanes] = mixed.astype(BF)
        total_ref[index] = jnp.broadcast_to(log_total, total_ref.shape[1:])
    first_sum = tokens.astype(F32) + mm_nt(mixed_ref[...], weight_ref[3]) + row_of(row_ref, 0)
    sum_ref[...] = first_sum
    first_low = (norm_parts(first_sum)[0] * gain_of(gain_ref, 0) + row_of(row_ref, 1)).astype(BF)
    cross_query_ref[...] = (mm(first_low, weight_ref[4]) + head_ref[2:3].astype(F32)).astype(BF)


def cross_kernel(context_ref, query_ref, key_w_ref, value_w_ref, head_ref, key_ref, value_ref,
                 mixed_ref, total_ref):
    context = context_ref[...]
    for group in range(key_ref.shape[1] // SLAB):
        lanes = slice(group * SLAB, (group + 1) * SLAB)
        key_ref[:, lanes] = mm(context, key_w_ref[0, :, lanes]).astype(BF)
        value_ref[:, lanes] = (
            mm(context, value_w_ref[0, :, lanes]) + head_ref[3:4, lanes].astype(F32)
        ).astype(BF)
        mixed, log_total = attend(
            query_ref[:, lanes], key_ref[:, lanes], value_ref[:, lanes], key_ref.shape[0]
        )
        mixed_ref[:, lanes] = mixed.astype(BF)
        total_ref[group] = jnp.broadcast_to(log_total, total_ref.shape[1:])


def ffn_kernel(
    images, blocks, per, sum_ref, mixed_ref, cotangent_ref, matches_ref, counts_ref, cross_w_ref,
    weight_ref, head_ref, row_ref, gain_ref,
    block_ref, left_ref, right_ref, mixed_grad_ref, residual_ref, small_ref,
    second_sum, second_low, left, right, slope, branch, third_grad, hidden_bias, weights, left_sem,
    right_sem, weight_sem,
):
    step = pl.program_id(0)
    half_steps = blocks // per

    def weight_copies(first):
        at = pl.ds(first, per)
        return [
            pltpu.make_async_copy(
                weight_ref.at[pl.ds(8 + which * blocks + first, per)], weights.at[which, at],
                weight_sem.at[which, first // per],
            )
            for which in range(2)
        ]
    rows = sum_ref.shape[0] // images

    def left_copy(which):
        return pltpu.make_async_copy(left.at[which], left_ref.at[which], left_sem.at[which])

    def right_copy(which):
        return pltpu.make_async_copy(right.at[which], right_ref.at[which], right_sem.at[which])

    mixed_copy = pltpu.make_async_copy(
        mixed_ref, right_ref.at[2 * blocks], right_sem.at[2 * blocks]
    )

    @pl.when(step == 0)
    def _():
        for copy in weight_copies(0):
            copy.start()
        mixed_copy.start()
        first_out = norm_parts(sum_ref[...])[0] * gain_of(gain_ref, 0) + row_of(row_ref, 1)
        second = first_out + mm_nt(mixed_ref[...], cross_w_ref[0]) + row_of(row_ref, 2)
        second_sum[...] = second
        second_low[...] = (
            norm_parts(second)[0] * gain_of(gain_ref, 1) + row_of(row_ref, 3)
        ).astype(BF)
        branch[...] = jnp.zeros_like(branch)
        small_ref[...] = jnp.zeros_like(small_ref)
        hidden_bias[0:blocks] = head_ref[4 : 4 + blocks].astype(F32)
        left[0] = second_low[...].T
        left_copy(0).start()

    @pl.when(step < half_steps)
    def _():
        low = second_low[...]
        first = step * per
        copies = weight_copies(first)
        copies[0].wait()
        copies[1].wait()

        @pl.when(step + 1 < half_steps)
        def _():
            for copy in weight_copies(first + per):
                copy.start()

        pres = [
            mm(low, weights[0, first + k]) + hidden_bias[pl.ds(first + k, 1)] for k in range(per)
        ]
        total = branch[...]
        for k in range(per):
            act, grad = gelu_tanh(pres[k])
            act = act.astype(BF)
            slope[first + k] = grad
            right[blocks + first + k] = act
            right_copy(blocks + first + k).start()
            total = total + mm_nt(act, weights[1, first + k])
        branch[...] = total

    @pl.when(step == half_steps - 1)
    def _():
        second = norm_parts(second_sum[...])[0] * gain_of(gain_ref, 1) + row_of(row_ref, 3)
        third_sum = second + branch[...] + row_of(row_ref, 4)
        normed, scale = norm_parts(third_sum)
        block_ref[...] = (normed * gain_of(gain_ref, 2) + row_of(row_ref, 5)).astype(BF)
        count = matches_ref.shape[2]
        slot = lax.broadcasted_iota(jnp.int32, (rows, count), 0)
        box = lax.broadcasted_iota(jnp.int32, (rows, count), 1)
        grads = []
        for image in range(images):
            own = lax.axis_index("tensor") * images + image
            live = (matches_ref[0, pl.ds(own, 1)] == slot) & (box < counts_ref[0, own])
            mask = jnp.sum(jnp.where(live, 1.0, 0.0), axis=1, keepdims=True)
            cot = cotangent_ref[image * rows : (image + 1) * rows].astype(F32)
            grads.append(cot * mask)
        out_grad = jnp.concatenate(grads, axis=0)
        grad = norm_back(normed, scale, gain_of(gain_ref, 2), out_grad)
        third_grad[...] = grad
        left[1] = grad.astype(BF).T
        left_copy(1).start()
        small_ref[12:13] = rows_sum(grad)
        small_ref[13:14] = rows_sum(out_grad)
        small_ref[16:17] = rows_sum(out_grad * normed)
        branch[...] = jnp.zeros_like(branch)

    @pl.when(step >= half_steps)
    def _():
        ffn_low = third_grad[...].astype(BF)
        first = (step - half_steps) * per
        grads = [mm(ffn_low, weights[1, first + k]) for k in range(per)]
        total = branch[...]
        for k in range(per):
            grad_low = (grads[k] * slope[first + k]).astype(BF)
            right[first + k] = grad_low
            right_copy(first + k).start()
            small_ref[pl.ds(4 + first + k, 1)] = rows_sum(grad_low.astype(F32))
            total = total + mm_nt(grad_low, weights[0, first + k])
        branch[...] = total

    @pl.when(step == 2 * half_steps - 1)
    def _():
        second_in = third_grad[...] + branch[...]
        normed, scale = norm_parts(second_sum[...])
        grad = norm_back(normed, scale, gain_of(gain_ref, 1), second_in)
        residual_ref[...] = grad
        small_ref[10:11] = rows_sum(grad)
        small_ref[11:12] = rows_sum(second_in)
        small_ref[15:16] = rows_sum(second_in * normed)
        cross_low = grad.astype(BF)
        left[2] = cross_low.T
        left_copy(2).start()
        mixed_grad_ref[...] = mm(cross_low, cross_w_ref[0]).astype(BF)
        mixed_copy.wait()
        for which in range(3):
            left_copy(which).wait()
        for which in range(2 * blocks):
            right_copy(which).wait()


def cross_back_step(
    image, group, query_ref, key_ref, value_ref, total_ref, mixed_grad_ref, mixed_ref, small_ref,
    context_t, key_acc, value_acc, key_grad_ref, value_grad_ref, unit,
):
    grad_query = attend_back_tiles(
        query_ref[...], key_ref, value_ref, total_ref[0, 0:1], mixed_grad_ref[...], mixed_ref[...],
        key_grad_ref, value_grad_ref,
    )
    grad_key, grad_value = key_grad_ref[...], value_grad_ref[...]
    lanes = pl.ds(pl.multiple_of(group * SLAB, SLAB), SLAB)
    small_ref[2:3, lanes] += rows_sum(grad_query.astype(F32))
    small_ref[3:4, lanes] += rows_sum(grad_value.astype(F32))
    unit(0)
    key_wg = mm(context_t[...], grad_key)
    value_wg = mm(context_t[...], grad_value)

    @pl.when(image == 0)
    def _():
        key_acc[:, lanes] = key_wg
        value_acc[:, lanes] = value_wg

    @pl.when(image > 0)
    def _():
        key_acc[:, lanes] += key_wg
        value_acc[:, lanes] += value_wg

    unit(1)
    return grad_query


def cross_back_kernel(
    context_ref, query_ref, key_ref, value_ref, total_ref, mixed_grad_ref, mixed_ref, key_w_ref,
    value_w_ref, query_grad_ref, context_grad_ref, key_wg_ref, value_wg_ref, small_ref,
    context_t, acc, key_acc, value_acc, key_grad, value_grad,
):
    image, group = pl.program_id(0), pl.program_id(1)
    images, groups = pl.num_programs(0), pl.num_programs(1)

    @pl.when((image == 0) & (group == 0))
    def _():
        small_ref[...] = jnp.zeros_like(small_ref)

    @pl.when(group == 0)
    def _():
        context_t[...] = context_ref[...].T

    query_grad_ref[...] = cross_back_step(
        image, group, query_ref, key_ref, value_ref, total_ref, mixed_grad_ref, mixed_ref,
        small_ref, context_t, key_acc, value_acc, key_grad, value_grad, lambda part: None,
    )
    context_part = mm_nt(key_grad[...], key_w_ref[0]) + mm_nt(value_grad[...], value_w_ref[0])

    @pl.when(group == 0)
    def _():
        acc[...] = context_part

    @pl.when(group > 0)
    def _():
        acc[...] += context_part

    @pl.when(group == groups - 1)
    def _():
        context_grad_ref[...] = acc[...].astype(BF)

    @pl.when((image == images - 1) & (group == groups - 1))
    def _():
        key_wg_ref[...] = key_acc[...].astype(BF)
        value_wg_ref[...] = value_acc[...].astype(BF)


def self_back(
    images, valid, tokens_ref, weight_ref, row_ref, gain_ref, qkv_ref, mixed_ref, total_ref, sum_ref,
    residual_ref, cross_query_grad_ref, mixed_grad_ref, small_ref, qkv_grad, emit, unit, loop_unit,
    used,
):
    tokens = tokens_ref[...]
    rows = tokens.shape[0] // images
    width = tokens.shape[1]
    normed, scale = norm_parts(sum_ref[...])
    first_low = (normed * gain_of(gain_ref, 0) + row_of(row_ref, 1)).astype(BF)
    cross_query_grad = cross_query_grad_ref[...]
    first_low_t = first_low.T
    emit(4, lambda lanes: mm(first_low_t, cross_query_grad_ref[:, lanes]))
    unit()
    first_in = residual_ref[...] + mm_nt(cross_query_grad, weight_ref[4])
    first_grad = norm_back(normed, scale, gain_of(gain_ref, 0), first_in)
    small_ref[8:9] = rows_sum(first_grad)
    small_ref[9:10] = rows_sum(first_in)
    small_ref[14:15] = rows_sum(first_in * normed)
    self_low = first_grad.astype(BF)
    self_low_t = self_low.T
    emit(3, lambda lanes: mm(self_low_t, mixed_ref[:, lanes]))
    unit()
    mixed_grad_ref[...] = mm(self_low, weight_ref[3]).astype(BF)
    used()
    groups = width // SLAB

    def one(index, carry):
        at, lanes = place_of(index, groups, rows)
        grads = attend_back(
            qkv_ref[0, at, lanes], qkv_ref[1, at, lanes], qkv_ref[2, at, lanes],
            total_ref[index, 0:1], mixed_grad_ref[at, lanes], valid,
        )
        for which in range(3):
            qkv_grad[which, at, lanes] = grads[which]
        loop_unit(index)
        return carry

    lax.fori_loop(0, images * groups, one, 0)
    tokens_t = tokens.T
    total = first_grad
    for which in range(3):
        grad = qkv_grad[which]
        emit(which, lambda lanes, which=which: mm(tokens_t, qkv_grad[which, :, lanes]))
        if which != 1:
            unit()
        total = total + mm_nt(grad, weight_ref[which])
    small_ref[0:1] = rows_sum(qkv_grad[0].astype(F32))
    small_ref[1:2] = rows_sum(qkv_grad[2].astype(F32))
    return total


def self_back_kernel(
    images, valid, tokens_ref, weight_ref, row_ref, gain_ref, qkv_ref, mixed_ref, total_ref, sum_ref,
    residual_ref, cross_query_grad_ref, query_grad_ref, wg_ref, small_ref, qkv_grad, mixed_grad,
):
    small_ref[...] = jnp.zeros_like(small_ref)

    def emit(block, value):
        for lane in range(0, wg_ref.shape[2], SLAB):
            lanes = slice(lane, lane + SLAB)
            wg_ref[block, :, lanes] = value(lanes).astype(BF)

    query_grad_ref[...] = self_back(
        images, valid, tokens_ref, weight_ref, row_ref, gain_ref, qkv_ref, mixed_ref, total_ref,
        sum_ref, residual_ref, cross_query_grad_ref, mixed_grad, small_ref, qkv_grad, emit,
        lambda: None, lambda index: None, lambda: None,
    ).astype(BF)


def task_peers(tasks):
    me = lax.axis_index("task")
    return [lax.rem(me + shift, tasks) for shift in range(1, tasks)]


def task_senders(tasks):
    me = lax.axis_index("task")
    return [lax.rem(me + tasks - shift, tasks) for shift in range(1, tasks)]


def greet(depth, tasks):
    me = lax.axis_index("dp")
    barrier = pltpu.get_barrier_semaphore()
    other = 1 - lax.axis_index("tensor")
    for peer in task_peers(tasks):
        pl.semaphore_signal(barrier, inc=1, device_id={"task": peer}, device_id_type=MESH_ID)
        pl.semaphore_signal(
            barrier, inc=1, device_id={"task": peer, "tensor": other}, device_id_type=MESH_ID
        )
    for shift in range(1, depth):
        pl.semaphore_signal(
            barrier, inc=1, device_id={"dp": lax.rem(me + shift, depth)}, device_id_type=MESH_ID
        )
    pl.semaphore_signal(barrier, inc=1, device_id={"tensor": other}, device_id_type=MESH_ID)
    pl.semaphore_wait(barrier, 2 * (tasks - 1) + depth)


LAG = 2
SLOTS = 3
STAGES = 2


class Chain:
    def __init__(self, depth, tasks, refs):
        self.depth, self.tasks = depth, tasks
        (self.near, self.far, self.stage, self.passed, self.parts,
         self.far_send, self.far_recv, self.far_free, self.pass_send, self.pass_recv,
         self.part_send, self.part_recv) = refs
        self.chunks = self.passed.shape[1]
        self.rows, self.half = self.passed.shape[2:]
        self.me = lax.axis_index("dp")
        self.task = lax.axis_index("task")
        self.is_end = (self.me == 0) | (self.me == depth - 1)

    SCRATCH = 12

    @staticmethod
    def scratch(blocks, rows, half, tasks):
        chunks = 2 * blocks
        dma = pltpu.SemaphoreType.DMA
        return [
            pltpu.VMEM((2, chunks, rows, half), BF),
            pltpu.VMEM((SLOTS, 2, 2, rows, half), BF),
            pltpu.VMEM((STAGES, 2, 2, rows, half), BF),
            pltpu.VMEM((2, chunks, rows, half), BF),
            pltpu.VMEM((tasks, chunks, rows // tasks, half), BF),
            dma((STAGES,)),
            dma((SLOTS,)),
            pltpu.SemaphoreType.REGULAR,
            dma((2, chunks)),
            dma((2, chunks)),
            dma((blocks, tasks - 1)),
            dma((blocks, tasks - 1)),
        ]

    def far_copy(self, block):
        slot, stage = lax.rem(block, SLOTS), lax.rem(block, STAGES)
        return send(
            self.stage.at[stage], self.far.at[slot], self.far_send.at[stage], self.far_recv.at[slot],
            tensor=1 - lax.axis_index("tensor"),
        )

    def emit(self, block, value):
        block = jnp.int32(block)
        stage = lax.rem(block, STAGES)

        @pl.when(block >= STAGES)
        def _():
            self.far_copy(block).wait_send()

        @pl.when(block >= SLOTS)
        def _():
            pl.semaphore_wait(self.far_free, 1)

        def place(low, target):
            for way in range(2):
                for part in range(2):
                    row = (2 * way + part) * self.rows
                    target(way, part, low[row : row + self.rows])

        def slab(start):
            low = value(slice(start, start + SLAB)).astype(BF)
            own = max(min(self.half - start, SLAB), 0)
            if own:

                def keep(way, part, rows):
                    self.near[way, 2 * block + part, :, start : start + own] = rows

                place(low[:, :own], keep)
            if own < SLAB:
                first = start + own - self.half

                def give(way, part, rows):
                    self.stage[stage, way, part, :, first : first + SLAB - own] = rows

                place(low[:, own:], give)

        starts = range(0, 2 * self.half, SLAB)
        for start in starts:
            if start + SLAB > self.half:
                slab(start)
        self.far_copy(block).start()
        for start in starts:
            if start + SLAB <= self.half:
                slab(start)

    def absorb(self, block):
        block = jnp.int32(block)
        slot = lax.rem(block, SLOTS)
        self.far_copy(block).wait_recv()
        for way in range(2):
            chunks = pl.ds(2 * block, 2)
            self.near[way, chunks] = (
                self.near[way, chunks].astype(F32) + self.far[slot, way].astype(F32)
            ).astype(BF)

        @pl.when(block < self.chunks // 2 - SLOTS)
        def _():
            pl.semaphore_signal(
                self.far_free, inc=1, device_id={"tensor": 1 - lax.axis_index("tensor")},
                device_id_type=MESH_ID,
            )

    def pass_copy(self, way, chunk):
        piece = self.passed.at[way, chunk]
        target = self.me - 1 if way == 0 else self.me + 1
        return send(
            piece, piece, self.pass_send.at[way, chunk], self.pass_recv.at[way, chunk], dp=target
        )

    def part_rows(self, peer):
        size = self.rows // self.tasks
        return pl.ds(pl.multiple_of(peer * size, size), size)

    def part_copy(self, way, block, shift, peer):
        chunks = pl.ds(2 * block, 2)
        return send(
            self.passed.at[way, chunks, self.part_rows(peer)], self.parts.at[self.task, chunks],
            self.part_send.at[block, shift], self.part_recv.at[block, shift], task=peer,
        )

    def hops(self, way):
        return self.depth - 1 - self.me if way == 0 else self.me

    def units(self):
        return self.chunks + LAG * (self.depth - 1)

    def unit(self, index):
        for way in range(2):
            chunk = index - LAG * self.hops(way)

            @pl.when((chunk >= 0) & (chunk < self.chunks))
            def _(way=way, chunk=chunk):
                self.chunk_step(way, chunk)

    def chunk_step(self, way, chunk):
        first, last = self.hops(way) == 0, self.hops(way) == self.depth - 1
        block = chunk // 2
        own = self.near[way, chunk]

        @pl.when(first)
        def _():
            self.passed[way, chunk] = own

        @pl.when(jnp.logical_not(first))
        def _():
            self.pass_copy(way, chunk).wait_recv()
            self.passed[way, chunk] = (
                own.astype(F32) + self.passed[way, chunk].astype(F32)
            ).astype(BF)

        @pl.when(jnp.logical_not(last))
        def _():
            self.pass_copy(way, chunk).start()

        @pl.when(last & (chunk == 2 * block + 1))
        def _():
            for shift, peer in enumerate(task_peers(self.tasks)):
                self.part_copy(way, block, shift, peer).start()
            own_rows = self.part_rows(self.task)
            self.parts[self.task, chunk - 1] = self.passed[way, chunk - 1, own_rows]
            self.parts[self.task, chunk] = self.passed[way, chunk, own_rows]

    def wait_parts(self, block):
        for shift, peer in enumerate(task_senders(self.tasks)):
            landed = self.parts.at[peer, pl.ds(2 * block, 2)]
            send(
                landed, landed, self.part_send.at[block, shift], self.part_recv.at[block, shift],
                task=peer,
            ).wait_recv()

    def finish(self):
        def blocks(block, carry):
            for way in range(2):

                @pl.when(self.hops(way) != self.depth - 1)
                def _(way=way):
                    for part in range(2):
                        self.pass_copy(way, 2 * block + part).wait_send()

                @pl.when(self.hops(way) == self.depth - 1)
                def _(way=way):
                    for shift, peer in enumerate(task_peers(self.tasks)):
                        self.part_copy(way, block, shift, peer).wait_send()

            return carry

        lax.fori_loop(0, self.chunks // 2, blocks, 0)


def pairs_of(tasks):
    return [(a, b) for a in range(tasks) for b in range(a, tasks)]


def weights_of(gram, order_ref, tasks):
    totals = [0.0] * tasks
    for own in range(tasks):
        coeffs = [jnp.full_like(gram[0, 0], 1.0 if t == own else 0.0) for t in range(tasks)]
        for position in range(tasks):
            chosen = [
                jnp.where(order_ref[position] == t, 1.0, 0.0).astype(F32) for t in range(tasks)
            ]
            column = [sum(gram[t, j] * chosen[j] for j in range(tasks)) for t in range(tasks)]
            inner = sum(coeffs[t] * column[t] for t in range(tasks))
            square = sum(chosen[t] * column[t] for t in range(tasks))
            others = 1.0 - chosen[own]
            share = others * jnp.minimum(inner, 0.0) / (square + 1e-06)
            coeffs = [coeffs[t] - share * chosen[t] for t in range(tasks)]
        totals = [total + coeff for total, coeff in zip(totals, coeffs)]
    return totals


GROUPS = 4
UNITS = 2
TILE = 240


class ContextGrad:
    def __init__(self, key_grad, value_grad, weights, result, refs):
        self.grads, self.weights, self.result = (key_grad, value_grad), weights, result
        (self.staged, self.ring, self.done, self.staged_sem, self.ring_sem, self.done_sem) = refs
        self.tile = self.done.shape[1]
        self.tiles = result.shape[0] // self.tile

    SCRATCH = 6

    @staticmethod
    def scratch(keys, width):
        dma = pltpu.SemaphoreType.DMA
        return [
            pltpu.VMEM((2, keys, SLAB), BF),
            pltpu.VMEM((2, 2, width // SLAB, TILE, SLAB), BF),
            pltpu.VMEM((2, TILE, width), BF),
            dma((2,)),
            dma((2, 2)),
            dma((2,)),
        ]

    def staged_copies(self, image, group):
        keys = self.staged.shape[1]
        rows = pl.ds(pl.multiple_of(image * keys, keys), keys)
        return [
            pltpu.make_async_copy(
                self.staged.at[which], self.grads[which].at[group, rows], self.staged_sem.at[which]
            )
            for which in range(2)
        ]

    def put(self, image, group):
        for copy in self.staged_copies(image, group):
            copy.start()

    def settle(self):
        for copy in self.staged_copies(0, 0):
            copy.wait()

    def fetches(self, index):
        slot = lax.rem(index, 2)
        rows = pl.ds(pl.multiple_of(index * self.tile, self.tile), self.tile)
        return [
            pltpu.make_async_copy(
                self.grads[which].at[:, rows], self.ring.at[slot, which],
                self.ring_sem.at[slot, which],
            )
            for which in range(2)
        ]

    def store(self, index):
        slot = lax.rem(index, 2)
        rows = pl.ds(pl.multiple_of(index * self.tile, self.tile), self.tile)
        return pltpu.make_async_copy(
            self.done.at[slot], self.result.at[rows], self.done_sem.at[slot]
        )

    def compute(self, index):
        @pl.when(index < self.tiles)
        def _():
            for copy in self.fetches(index):
                copy.wait()

            @pl.when(index + 1 < self.tiles)
            def _():
                for copy in self.fetches(index + 1):
                    copy.start()

            @pl.when(index >= 2)
            def _():
                self.store(index - 2).wait()

            slot = lax.rem(index, 2)
            parts = [
                jnp.concatenate(
                    [self.ring[slot, which, group] for group in range(self.ring.shape[2])], axis=1
                )
                for which in range(2)
            ]
            total = mm_nt(parts[0], self.weights[0]) + mm_nt(parts[1], self.weights[1])
            self.done[slot] = total.astype(BF)
            self.store(index).start()

    def finish(self):
        for index in range(self.tiles - 2, self.tiles):
            self.store(jnp.int32(index)).wait()


def back_kernel(
    depth, tasks, images, groups, valid, block_order, order_ref, context_ref, query_ref, key_ref,
    value_ref, total_ref, mixed_grad_ref, cross_mixed_ref, tokens_ref, row_ref, gain_ref, qkv_ref,
    mixed_ref, self_total_ref, sum_ref, residual_ref, small_in_ref, all_w_ref, block_ref, left_ref, right_ref,
    *refs
):
    (
        context_grad_ref, query_grad_ref, update_ref, small_out_ref, gram_ref, block_far,
        key_grad, value_grad,
    ), refs = refs[:8], refs[8:]
    (
        context, context_t, key_acc, value_acc, cross_query_grad, self_mixed_grad, qkv_grad, weights,
        block_sem, weight_sem, context_sem,
    ), refs = refs[:11], refs[11:]
    context_back = ContextGrad(
        key_grad, value_grad, weights.at[pl.ds(3, 2)], context_grad_ref,
        refs[: ContextGrad.SCRATCH],
    )
    refs = refs[ContextGrad.SCRATCH :]
    chain = Chain(depth, tasks, refs[: Chain.SCRATCH])
    refs = refs[Chain.SCRATCH :]
    gram_acc = refs[7]
    step = pl.program_id(0)
    cross_steps = images * groups
    half = chain.half
    is_end = chain.is_end
    pairs = pairs_of(tasks)

    def add_products(shares):
        for index, (a, b) in enumerate(pairs):
            product = shares[a] * shares[b]
            total = product[0:8]
            for row in range(8, product.shape[0], 8):
                total = total + product[row : row + 8]
            gram_acc[index * 8 : index * 8 + 8] += total

    def unit(index):
        chain.unit(index)
        since = index - LAG * (depth - 1) - 3
        block = since // 2

        @pl.when(is_end & (since >= 0) & (since == 2 * block))
        def _():
            chain.wait_parts(block)
            for part in range(2):
                add_products(
                    [chain.parts[t, 2 * block + part].astype(F32) for t in range(tasks)]
                )

    block_copy = send(
        block_ref, block_far, block_sem.at[0], block_sem.at[1], tensor=1 - lax.axis_index("tensor")
    )
    weight_copies = [
        pltpu.make_async_copy(all_w_ref.at[source], weights.at[target], weight_sem.at[index])
        for index, (source, target) in enumerate(
            [(pl.ds(0, 5), pl.ds(0, 5)), (pl.ds(5, 2), pl.ds(3, 2))]
        )
    ]

    def context_copy(image):
        keys = context.shape[0]
        own = lax.axis_index("tensor") * images + image
        rows = pl.ds(pl.multiple_of(own * keys, keys), keys)
        return pltpu.make_async_copy(context_ref.at[0, rows], context, context_sem)

    @pl.when(step == 0)
    def _():
        context_copy(0).start()
        weight_copies[0].start()
        greet(depth, tasks)
        block_copy.start()
        gram_acc[...] = jnp.zeros_like(gram_acc)
        refs[0][...] = small_in_ref[...]

    @pl.when(step < cross_steps)
    def _():
        image = step // groups
        group = step - image * groups

        chain.emit(step, lambda lanes: mm(left_ref[0], right_ref[0, :, lanes]))

        @pl.when(group == 0)
        def _():
            context_copy(image).wait()
            context_t[...] = context[...].T

            @pl.when(image + 1 < images)
            def _():
                context_copy(image + 1).start()

        def cross_unit(part):
            if part == 0:
                chain.absorb(step)
            unit(step * UNITS + part)

        @pl.when(step > 0)
        def _():
            context_back.settle()

        grad_query = cross_back_step(
            image, group, query_ref, key_ref, value_ref, total_ref, mixed_grad_ref, cross_mixed_ref,
            refs[0], context_t, key_acc, value_acc, context_back.staged.at[0],
            context_back.staged.at[1], cross_unit,
        )
        context_back.put(image, group)
        rows = grad_query.shape[0]
        cross_query_grad[
            pl.ds(pl.multiple_of(image * rows, rows), rows),
            pl.ds(pl.multiple_of(group * SLAB, SLAB), SLAB),
        ] = grad_query

        @pl.when(step == cross_steps - 1)
        def _():
            chain.emit(cross_steps, lambda lanes: key_acc[:, lanes])
            chain.emit(cross_steps + 1, lambda lanes: value_acc[:, lanes])

    @pl.when(step == cross_steps)
    def _():
        done = [cross_steps * UNITS]
        blocks = len(block_order)

        def self_unit():
            if done[0] % 2 == 0:
                chain.absorb(done[0] // 2)
            unit(jnp.int32(done[0]))
            done[0] += 1

        in_loop = images * groups // 2

        def loop_unit(index):
            now = cross_steps * UNITS + 2 + index // 2

            @pl.when(index % 2 == 1)
            def _():
                @pl.when(now % 2 == 0)
                def _():
                    chain.absorb(now // 2)

                unit(now)

        def used():
            done[0] += in_loop
            weight_copies[1].start()

        context_back.settle()
        for copy in context_back.fetches(jnp.int32(0)):
            copy.start()
        weight_copies[0].wait()
        query_grad_ref[...] = self_back(
            images, valid, tokens_ref, weights, row_ref, gain_ref, qkv_ref, mixed_ref,
            self_total_ref, sum_ref, residual_ref, cross_query_grad, self_mixed_grad, refs[0],
            qkv_grad, lambda block, value: chain.emit(block_order.index(block), value), self_unit,
            loop_unit, used,
        ).astype(BF)
        for block in range(-(-done[0] // 2), blocks):
            chain.absorb(block)
        weight_copies[1].wait()
        rest(
            chain, unit, context_back, done[0], order_ref, update_ref, small_out_ref, gram_ref, refs
        )
        for block in range(blocks - STAGES, blocks):
            chain.far_copy(jnp.int32(block)).wait_send()
        block_copy.wait()
        context_back.finish()


def rest(
    chain, unit, context_back, done, order_ref, update_ref, small_out_ref, gram_ref, refs
):
    (
        small, small_own, small_other, small_far, small_pass, small_all, small_both, gram_acc,
        gram_plane, gram_end, out,
        small_far_sem, small_pass_sem, small_task_sem, small_dp_sem, small_core_sem,
        gram_plane_sem, gram_dp_sem, hop_sem, out_sem, update_sem,
    ) = refs
    depth, tasks, half = chain.depth, chain.tasks, chain.half
    me, task, core = (lax.axis_index(axis) for axis in ("dp", "task", "tensor"))
    is_end = chain.is_end
    top = me == 0
    pairs = pairs_of(tasks)
    own_lanes = pl.ds(pl.multiple_of(core * half, half), half)
    other_lanes = pl.ds(pl.multiple_of((1 - core) * half, half), half)
    small_own[0:8] = small[0:8, 0:half]
    small_own[8:] = small[8:, own_lanes]
    small_other[0:8] = small[0:8, half:]
    small_other[8:] = small[8:, other_lanes]
    small_copy = send(
        small_other, small_far, small_far_sem.at[0], small_far_sem.at[1], tensor=1 - core
    )
    small_copy.start()

    def small_hop():
        return send(
            small_pass, small_pass, small_pass_sem.at[0], small_pass_sem.at[1], dp=me - 1
        )

    def small_task_copy(shift, peer):
        return send(
            small_pass, small_all.at[task], small_task_sem.at[0, shift],
            small_task_sem.at[1, shift], task=peer,
        )

    def step(index, carry):
        unit(index)
        context_back.compute(index - done)

        @pl.when(index == done + 1 + LAG * chain.hops(0))
        def _():
            small_copy.wait_recv()
            total = small_own[...] + small_far[...]

            @pl.when(me == depth - 1)
            def _():
                small_pass[...] = total

            @pl.when(me < depth - 1)
            def _():
                small_hop().wait_recv()
                small_pass[...] += total

            @pl.when(me > 0)
            def _():
                small_hop().start()

            @pl.when(top)
            def _():
                for shift, peer in enumerate(task_peers(tasks)):
                    small_task_copy(shift, peer).start()
                small_all[task] = small_pass[...]

        return carry

    lax.fori_loop(done, max(chain.units() + 2, done + context_back.tiles), step, 0)

    @pl.when(top)
    def _():
        for shift, peer in enumerate(task_senders(tasks)):
            landed = small_all.at[peer]
            send(
                landed, landed, small_task_sem.at[0, shift], small_task_sem.at[1, shift], task=peer
            ).wait_recv()

    lanes = gram_plane.shape[2]
    plane = 2 * tasks
    mine = 2 * task + core

    def gram_copy(shift):
        to = lax.rem(mine + shift, plane)
        return send(
            gram_plane.at[mine], gram_plane.at[mine], gram_plane_sem.at[0, shift - 1],
            gram_plane_sem.at[1, shift - 1], task=to // 2, tensor=lax.rem(to, 2),
        )

    def gram_arrival(shift):
        place = lax.rem(mine + plane - shift, plane)
        return send(
            gram_plane.at[place], gram_plane.at[place], gram_plane_sem.at[0, shift - 1],
            gram_plane_sem.at[1, shift - 1], task=place // 2, tensor=lax.rem(place, 2),
        )

    def gram_dp_copy(end, shift):
        return send(
            gram_end.at[end], gram_end.at[end], gram_dp_sem.at[0, end, shift],
            gram_dp_sem.at[1, end, shift], dp=lax.rem((depth - 1) * end + shift + 1, depth),
        )

    def one_number(values):
        return jnp.sum(jnp.sum(values, axis=0, keepdims=True), axis=1, keepdims=True)

    @pl.when(top & (task == 0))
    def _():
        small_values = [small_all[t] for t in range(tasks)]
        for index, (a, b) in enumerate(pairs):
            product = small_values[a] * small_values[b]
            gram_acc[index * 8 : index * 8 + 8] += product[0:8] + product[8:16] + product[16:24]

    @pl.when(is_end)
    def _():
        gram_plane[mine] = jnp.zeros(gram_plane.shape[1:], F32)
        for index in range(len(pairs)):
            gram_plane[mine, index : index + 1] = jnp.broadcast_to(
                one_number(gram_acc[index * 8 : index * 8 + 8]), (1, lanes)
            )
        for shift in range(1, plane):
            gram_copy(shift).start()
        for shift in range(1, plane):
            gram_arrival(shift).wait_recv()

    for end in range(2):

        @pl.when(me == (depth - 1) * end)
        def _(end=end):
            total = gram_plane[0]
            for place in range(1, plane):
                total = total + gram_plane[place]
            gram_end[end] = total
            for shift in range(depth - 1):
                gram_dp_copy(end, shift).start()

    for end in range(2):
        for shift in range(depth - 1):

            @pl.when(me == ((depth - 1) * end + shift + 1) % depth)
            def _(end=end, shift=shift):
                gram_dp_copy(end, shift).wait_recv()

    gram = {}
    for index, (a, b) in enumerate(pairs):
        row = slice(index, index + 1)
        gram[a, b] = gram[b, a] = gram_end[0, row] + gram_end[1, row]
    for a in range(tasks):
        for b in range(tasks):
            gram_ref[a * tasks + b : a * tasks + b + 1] = gram[a, b]
    weights = [
        jnp.concatenate([weight] * (half // lanes), axis=1)
        for weight in weights_of(gram, order_ref, tasks)
    ]

    blocks = out.shape[0]
    group = blocks // GROUPS
    share = chain.rows // tasks
    own_share = pl.ds(pl.multiple_of(task * share, share), share)
    own_part = jnp.minimum(me, 1)

    def hop_copy(index):
        return send(
            chain.near.at[1, pl.ds(index * group, group), pl.ds(0, share)],
            out.at[pl.ds(index * group, group), own_share],
            hop_sem.at[0, index], hop_sem.at[1, index],
            dp=jnp.where(top, 1, depth - 2),
        )

    beside = [task + 1 - 2 * lax.rem(task, 2), task + 2 - 4 * (task // 2)]
    across = tasks - 1 - task

    def out_piece(index, owner):
        rows = pl.ds(pl.multiple_of(owner * share, share), share)
        return out.at[pl.ds(index * group, group), rows]

    def out_copy(index, which, owner):
        piece = out_piece(index, owner)
        peer = beside[which] if which < 2 else beside[1 if index < GROUPS // 2 else 0]
        return send(
            piece, piece, out_sem.at[0, index, which], out_sem.at[1, index, which], task=peer
        )

    def update_copy(index):
        at = pl.ds(index * group, group)
        return pltpu.make_async_copy(out.at[at], update_ref.at[at], update_sem.at[index])

    def weighted(chunk):
        total = weights[0] * chain.parts[0, chunk].astype(F32)
        for t in range(1, tasks):
            total = total + weights[t] * chain.parts[t, chunk].astype(F32)
        return total.astype(BF)

    def small_dp_copy(shift):
        return send(
            small_both.at[0], small_both.at[0], small_dp_sem.at[0, shift],
            small_dp_sem.at[1, shift], dp=shift + 1,
        )

    def small_core_copy():
        return send(
            small_both.at[0], small_both.at[1], small_core_sem.at[0], small_core_sem.at[1],
            tensor=1 - core,
        )

    @pl.when(top)
    def _():
        total = weights[0] * small_all[0]
        for t in range(1, tasks):
            total = total + weights[t] * small_all[t]
        small_both[0] = total
        for shift in range(depth - 1):
            small_dp_copy(shift).start()

    @pl.when(is_end)
    def _():
        for index in range(GROUPS):

            def other(block, carry):
                chain.near[1, block, 0:share] = weighted(2 * block + 1 - own_part)
                return carry

            lax.fori_loop(index * group, (index + 1) * group, other, 0)
            hop_copy(index).start()

            def own(block, carry):
                out[block, own_share] = weighted(2 * block + own_part)
                return carry

            lax.fori_loop(index * group, (index + 1) * group, own, 0)
            for which in range(2):
                out_copy(index, which, task).start()

    @pl.when(jnp.logical_not(is_end))
    def _():
        for index in range(GROUPS):
            hop_copy(index).wait_recv()
            for which in range(2):
                out_copy(index, which, task).start()

    for shift in range(depth - 1):

        @pl.when(me == shift + 1)
        def _(shift=shift):
            small_dp_copy(shift).wait_recv()

    small_core_copy().start()

    for index in range(GROUPS):
        for which in range(2):
            out_copy(index, which, beside[which]).wait_recv()
        out_copy(index, 2, beside[0 if index < GROUPS // 2 else 1]).start()
    for index in range(GROUPS):
        out_copy(index, 2, across).wait_recv()
        update_copy(index).start()

    small_core_copy().wait_recv()
    small_out_ref[0:8, 0:half] = small_both[0, 0:8]
    small_out_ref[0:8, half:] = small_both[1, 0:8]
    small_out_ref[8:, own_lanes] = small_both[0, 8:]
    small_out_ref[8:, other_lanes] = small_both[1, 8:]

    small_copy.wait_send()
    small_core_copy().wait_send()
    chain.finish()

    @pl.when(me > 0)
    def _():
        small_hop().wait_send()

    @pl.when(top)
    def _():
        for shift, peer in enumerate(task_peers(tasks)):
            small_task_copy(shift, peer).wait_send()
        for shift in range(depth - 1):
            small_dp_copy(shift).wait_send()

    for end in range(2):

        @pl.when(me == (depth - 1) * end)
        def _(end=end):
            for shift in range(depth - 1):
                gram_dp_copy(end, shift).wait_send()

    @pl.when(is_end)
    def _():
        for shift in range(1, plane):
            gram_copy(shift).wait_send()
        for index in range(GROUPS):
            hop_copy(index).wait_send()

    for index in range(GROUPS):
        update_copy(index).wait()
        for which in range(3):
            out_copy(index, which, task).wait_send()


def spread_kernel(
    images, valid, tasks, block_order, parts_ref, context_grad_ref, query_grad_ref, block_ref,
    block_far_ref, small_ref, gram_in_ref,
    update_ref, context_out_ref, query_out_ref, block_out_ref, head_ref, row_ref, gain_ref, gram_ref,
):
    ordered = [parts_ref[block_order.index(block)] for block in range(len(block_order))]
    update_ref[...] = jnp.swapaxes(jnp.stack(ordered), 0, 1).astype(F32)
    context_out_ref[...] = context_grad_ref[...]

    @pl.when(pl.program_id(0) == 0)
    def _():
        padded = query_grad_ref.shape[0] // images
        first = lax.axis_index("tensor") == 0

        def rows(ref, image):
            return ref[image * padded : (image + 1) * padded].astype(F32)[:valid]

        for image in range(images):
            at = slice(image * valid, (image + 1) * valid)
            after = slice((images + image) * valid, (images + image + 1) * valid)
            query_out_ref[at] = rows(query_grad_ref, image).astype(BF)
            near, far = rows(block_ref, image), rows(block_far_ref, image)
            block_out_ref[at] = jnp.where(first, near, far).astype(BF)
            block_out_ref[after] = jnp.where(first, far, near).astype(BF)
        head_ref[...] = small_ref[0:8, 0 : head_ref.shape[1]]
        for which in range(6):
            row_ref[which // 2, which % 2 : which % 2 + 1] = small_ref[8 + which : 9 + which]
        gain_ref[...] = small_ref[14:17]
        for a in range(tasks):
            for b in range(tasks):
                at = a * tasks + b
                gram_ref[a : a + 1, b : b + 1] = gram_in_ref[at : at + 1, 0:1]


def gram_kernel(parts_ref, gram_ref):
    tasks = parts_ref.shape[0]

    @pl.when(pl.program_id(0) == 0)
    def _():
        gram_ref[...] = jnp.zeros_like(gram_ref)

    shares = [parts_ref[task, 0].astype(F32) for task in range(tasks)]
    for a in range(tasks):
        for b in range(a, tasks):
            gram_ref[a * tasks + b : a * tasks + b + 1] += rows_sum(shares[a] * shares[b])


def update_kernel(weights_ref, parts_ref, update_ref):
    tasks, blocks = parts_ref.shape[:2]
    for block in range(blocks):
        total = weights_ref[0] * parts_ref[0, block].astype(F32)
        for task in range(1, tasks):
            total += weights_ref[task] * parts_ref[task, block].astype(F32)
        update_ref[:, block, :] = total


def body(
    queries, memory, cotangent, matches, counts, task_order, params, head_bias, row_bias, norm_gain
):
    all_images = matches.shape[1]
    valid = matches.shape[2]
    width = queries.shape[2]
    half = params.shape[2]
    block_count = params.shape[1]
    blocks = (block_count - 8) // 2
    cores = lax.axis_size("tensor")
    images = all_images // cores
    keys = memory.shape[1] // all_images
    padded = -(-valid // 16) * 16
    rows = images * padded
    groups = width // SLAB
    stack = GROUP * padded
    core = lax.axis_index("tensor")

    def const(shape, *index):
        return pl.BlockSpec(shape, lambda *_: index)

    total_shape = jax.ShapeDtypeStruct((images * groups, 8, stack), F32)
    low_rows = jax.ShapeDtypeStruct((rows, width), BF)
    full_rows = jax.ShapeDtypeStruct((rows, width), F32)
    small_shape = jax.ShapeDtypeStruct((24, width), F32)
    one_block = jax.ShapeDtypeStruct((width, width), BF)
    small_spec = const((24, width), 0, 0)
    row_spec = const(row_bias.shape, 0, 0, 0)
    gain_spec = const(norm_gain.shape, 0, 0)
    head_spec = const((16, width), 0, 0)
    rows_spec = const((rows, width), 0, 0)

    parts = 4
    part_blocks = block_count // 2
    raw_spec = const((None, *queries.shape[1:]), 0, 0, 0)
    (
        weights, head_rows, tokens, own_cotangent, qkv, self_mixed, self_total, first_sum,
        cross_query,
    ) = pl.pallas_call(
        functools.partial(start_kernel, images, valid),
        grid=(2 * parts,),
        out_shape=(
            jax.ShapeDtypeStruct((block_count, width, cores * half), BF),
            jax.ShapeDtypeStruct((16, cores * half), BF),
            low_rows, low_rows,
            jax.ShapeDtypeStruct((3, rows, width), BF), low_rows, total_shape, full_rows, low_rows,
        ),
        in_specs=[
            pl.BlockSpec((width // parts, part_blocks, half), lambda s: (s % parts, s // parts, 0)),
            const((8, half), 0, 0), raw_spec, raw_spec, row_spec, gain_spec,
        ],
        out_specs=(
            any_spec(), head_spec, rows_spec, rows_spec,
            const((3, rows, width), 0, 0, 0), rows_spec, const(total_shape.shape, 0, 0, 0),
            rows_spec, rows_spec,
        ),
        scratch_shapes=[
            pltpu.VMEM((part_blocks, width, cores * half), BF),
            pltpu.VMEM((part_blocks, width, half), BF),
            pltpu.VMEM((16, half), BF),
            pltpu.VMEM((16, cores * half), BF),
            pltpu.SemaphoreType.DMA((2 * parts + 1,)),
            pltpu.SemaphoreType.DMA((2 * parts + 1,)),
            pltpu.SemaphoreType.DMA((2 * parts,)),
            pltpu.SemaphoreType.DMA(()),
        ],
        compiler_params=params_for(collective_id=0, has_side_effects=True),
        name="start",
    )(params, head_bias, queries, cotangent, row_bias, norm_gain)

    def own_image(i, g):
        return 0, lax.axis_index("tensor") * images + i, 0

    context_all = pl.BlockSpec((None, keys, width), own_image)
    slab_q = pl.BlockSpec((padded, SLAB), lambda i, g: (i, g))
    slab_k = pl.BlockSpec((keys, SLAB), lambda i, g: (i, g))
    slab_t = pl.BlockSpec((1, 8, stack), lambda i, g: (i * groups + g, 0, 0))
    image_q = pl.BlockSpec((padded, width), lambda i: (i, 0))
    image_k = pl.BlockSpec((keys, width), lambda i: (i, 0))

    def slab_w(block):
        return pl.BlockSpec((1, width, SLAB), lambda i, g: (block, 0, g))

    key_rows = jax.ShapeDtypeStruct((images * keys, width), BF)
    key_slabs = jax.ShapeDtypeStruct((groups, images * keys, SLAB), BF)
    keys_act, values_act, cross_mixed, cross_total = pl.pallas_call(
        cross_kernel,
        grid=(images,),
        in_specs=[
            pl.BlockSpec((None, keys, width), lambda i: own_image(i, 0)),
            image_q, const((1, width, width), 5, 0, 0), const((1, width, width), 6, 0, 0), head_spec,
        ],
        out_specs=(
            image_k, image_k, image_q, pl.BlockSpec((groups, 8, stack), lambda i: (i, 0, 0)),
        ),
        out_shape=(key_rows, key_rows, low_rows, total_shape),
        compiler_params=params_for(),
        name="cross_forward",
    )(memory, cross_query, weights, weights, head_rows)

    per = 2 if blocks % 2 == 0 else 1
    block_rows, left, right, mixed_grad, second_grad, ffn_small = pl.pallas_call(
        functools.partial(ffn_kernel, images, blocks, per),
        grid=(2 * blocks // per,),
        out_shape=(
            low_rows,
            jax.ShapeDtypeStruct((3, width, rows), BF),
            jax.ShapeDtypeStruct((2 * blocks + 1, rows, width), BF),
            low_rows, full_rows, small_shape,
        ),
        in_specs=[
            rows_spec, rows_spec, rows_spec,
            const(matches.shape, 0, 0, 0),
            pl.BlockSpec(memory_space=pltpu.SMEM),
            const((1, width, width), 7, 0, 0),
            any_spec(), head_spec, row_spec, gain_spec,
        ],
        out_specs=(rows_spec, any_spec(), any_spec(), rows_spec, rows_spec, small_spec),
        scratch_shapes=[
            pltpu.VMEM((rows, width), F32),
            pltpu.VMEM((rows, width), BF),
            pltpu.VMEM((3, width, rows), BF),
            pltpu.VMEM((2 * blocks, rows, width), BF),
            pltpu.VMEM((blocks, rows, width), F32),
            pltpu.VMEM((rows, width), F32),
            pltpu.VMEM((rows, width), F32),
            pltpu.VMEM((8, width), F32),
            pltpu.VMEM((2, blocks, width, width), BF),
            pltpu.SemaphoreType.DMA((3,)),
            pltpu.SemaphoreType.DMA((2 * blocks + 1,)),
            pltpu.SemaphoreType.DMA((2, blocks // per)),
        ],
        compiler_params=params_for(),
        name="ffn",
    )(
        first_sum, cross_mixed, own_cotangent, matches, counts, weights, weights, head_rows, row_bias,
        norm_gain,
    )

    depth, tasks = lax.axis_size("dp"), lax.axis_size("task")
    by_chain = depth == 4 and tasks == 4 and cores == 2

    if by_chain:
        block_order = [*range(8, block_count), 7, 5, 6, 4, 3, 0, 1, 2]
        chain_rows = width // depth
        pair_rows = 8 * len(pairs_of(tasks))
        dma = pltpu.SemaphoreType.DMA
        last = images * groups - 1

        def at_step(make):
            def index_map(step):
                now = jnp.minimum(step, last)
                return make(now // groups, now - groups * (now // groups))

            return index_map

        def product(step):
            return jnp.minimum(step, 2 * blocks)

        def once(shape):
            return pl.BlockSpec(
                shape, lambda step: (0,) * len(shape), pipeline_mode=pl.Buffered(1)
            )

        step_q = pl.BlockSpec((padded, SLAB), at_step(lambda i, g: (i, g)))
        step_k = pl.BlockSpec((keys, SLAB), at_step(lambda i, g: (i, g)))

        small_half = pltpu.VMEM((24, half), F32)
        (
            context_grad, token_grad, update_parts, small_out, gram_rows, block_far, *_,
        ) = pl.pallas_call(
            functools.partial(
                back_kernel, depth, tasks, images, groups, valid, block_order
            ),
            grid=(images * groups + 1,),
            out_shape=(
                key_rows, low_rows,
                jax.ShapeDtypeStruct((block_count, chain_rows, half), BF),
                small_shape,
                jax.ShapeDtypeStruct((16, 128), F32),
                low_rows,
                key_slabs, key_slabs,
            ),
            in_specs=[
                pl.BlockSpec(memory_space=pltpu.SMEM),
                any_spec(), step_q, step_k, step_k,
                pl.BlockSpec((1, 8, stack), at_step(lambda i, g: (i * groups + g, 0, 0))),
                step_q, step_q,
                once((rows, width)), once(row_bias.shape), once(norm_gain.shape),
                once((3, rows, width)), once((rows, width)), once(total_shape.shape),
                once((rows, width)), once((rows, width)), once((24, width)),
                any_spec(), any_spec(),
                pl.BlockSpec((1, width, rows), lambda step: (product(step) // blocks, 0, 0)),
                pl.BlockSpec((1, rows, width), lambda step: (product(step), 0, 0)),
            ],
            out_specs=(
                any_spec(), once((rows, width)), any_spec(), once((24, width)), once((16, 128)),
                *[any_spec()] * 3,
            ),
            scratch_shapes=[
                pltpu.VMEM((keys, width), BF),
                pltpu.VMEM((width, keys), BF),
                pltpu.VMEM((width, width), F32),
                pltpu.VMEM((width, width), F32),
                pltpu.VMEM((rows, width), BF),
                pltpu.VMEM((rows, width), BF),
                pltpu.VMEM((3, rows, width), BF),
                pltpu.VMEM((5, width, width), BF),
                dma((2,)),
                dma((2,)),
                dma(()),
                *ContextGrad.scratch(keys, width),
                *Chain.scratch(block_count, chain_rows, half, tasks),
                pltpu.VMEM((24, width), F32),
                small_half, small_half, small_half, small_half,
                pltpu.VMEM((tasks, 24, half), F32),
                pltpu.VMEM((2, 24, half), F32),
                pltpu.VMEM((pair_rows, half), F32),
                pltpu.VMEM((2 * tasks, 16, 128), F32),
                pltpu.VMEM((2, 16, 128), F32),
                pltpu.VMEM((block_count, chain_rows, half), BF),
                dma((2,)),
                dma((2,)),
                dma((2, tasks - 1)),
                dma((2, depth - 1)),
                dma((2,)),
                dma((2, 2 * tasks - 1)),
                dma((2, 2, depth - 1)),
                dma((2, GROUPS)),
                dma((2, GROUPS, tasks - 1)),
                dma((GROUPS,)),
            ],
            compiler_params=params_for(collective_id=1, has_side_effects=True),
            name="backward",
        )(
            task_order, memory, cross_query, keys_act, values_act, cross_total, mixed_grad,
            cross_mixed, tokens, row_bias, norm_gain, qkv, self_mixed, self_total, first_sum,
            second_grad, ffn_small, weights, block_rows, left, right,
        )
        tile = chain_rows // images
        (
            param_update, memory_grad, query_grad, block_out, head_update, row_update, gain_update,
            gram,
        ) = pl.pallas_call(
            functools.partial(spread_kernel, images, valid, tasks, block_order),
            grid=(images,),
            out_shape=(
                jax.ShapeDtypeStruct((chain_rows, block_count, half), F32),
                key_rows,
                jax.ShapeDtypeStruct((images * valid, width), BF),
                jax.ShapeDtypeStruct((all_images * valid, width), BF),
                jax.ShapeDtypeStruct((8, half), F32),
                jax.ShapeDtypeStruct((3, 2, width), F32),
                jax.ShapeDtypeStruct((3, width), F32),
                jax.ShapeDtypeStruct((tasks, tasks), F32),
            ),
            in_specs=[
                pl.BlockSpec((block_count, tile, half), lambda r: (0, r, 0)),
                pl.BlockSpec((keys, width), lambda r: (r, 0)),
                rows_spec, rows_spec, rows_spec, small_spec, const((16, 128), 0, 0),
            ],
            out_specs=(
                pl.BlockSpec((tile, block_count, half), lambda r: (r, 0, 0)),
                pl.BlockSpec((keys, width), lambda r: (r, 0)),
                const((images * valid, width), 0, 0),
                const((all_images * valid, width), 0, 0),
                const((8, half), 0, 0), const((3, 2, width), 0, 0, 0),
                const((3, width), 0, 0), const((tasks, tasks), 0, 0),
            ),
            compiler_params=params_for(),
            name="spread",
        )(update_parts, context_grad, token_grad, block_rows, block_far, small_out, gram_rows)
        return (
            block_out[None], query_grad[None], memory_grad[None], param_update, head_update,
            row_update, gain_update, gram,
        )

    def unpad(array):
        return array.reshape(images, padded, width)[:, :valid].reshape(1, images * valid, width)

    block_out = lax.all_gather(unpad(block_rows), "tensor", axis=1, tiled=True)
    cross_query_grad, context_grad, key_wg, value_wg, cross_small = pl.pallas_call(
        cross_back_kernel,
        grid=(images, groups),
        in_specs=[
            context_all, slab_q, slab_k, slab_k, slab_t, slab_q, slab_q, slab_w(5), slab_w(6),
        ],
        out_specs=(
            slab_q,
            pl.BlockSpec((keys, width), lambda i, g: (i, 0)),
            const((width, width), 0, 0), const((width, width), 0, 0), small_spec,
        ),
        scratch_shapes=[
            pltpu.VMEM((width, keys), BF),
            pltpu.VMEM((keys, width), F32),
            pltpu.VMEM((width, width), F32),
            pltpu.VMEM((width, width), F32),
            pltpu.VMEM((keys, SLAB), BF),
            pltpu.VMEM((keys, SLAB), BF),
        ],
        out_shape=(low_rows, key_rows, one_block, one_block, small_shape),
        compiler_params=params_for(),
        name="cross_backward",
    )(
        memory, cross_query, keys_act, values_act, cross_total, mixed_grad, cross_mixed, weights,
        weights,
    )

    token_grad, self_wg, self_small = pl.pallas_call(
        functools.partial(self_back_kernel, images, valid),
        grid=(1,),
        out_shape=(
            low_rows, jax.ShapeDtypeStruct((5, width, width), BF), small_shape,
        ),
        in_specs=[
            rows_spec, const((5, width, width), 0, 0, 0), row_spec, gain_spec,
            const((3, rows, width), 0, 0, 0), rows_spec, const(total_shape.shape, 0, 0, 0),
            rows_spec, rows_spec, rows_spec,
        ],
        out_specs=(
            rows_spec, const((5, width, width), 0, 0, 0), small_spec,
        ),
        scratch_shapes=[pltpu.VMEM((3, rows, width), BF), pltpu.VMEM((rows, width), BF)],
        compiler_params=params_for(),
        name="self_backward",
    )(
        tokens, weights, row_bias, norm_gain, qkv, self_mixed, self_total, first_sum, second_grad,
        cross_query_grad,
    )

    query_grad = unpad(token_grad)
    memory_grad = context_grad[None]

    small = self_small + cross_small + ffn_small
    product = functools.partial(jnp.einsum, "dr,jre->jde", preferred_element_type=F32)
    grad_in = product(left[0], right[:blocks]).astype(BF)
    grad_out = product(left[1], right[blocks : 2 * blocks]).astype(BF)
    cross_out_wg = product(left[2], right[2 * blocks :])[0].astype(BF)
    grads = jnp.concatenate(
        [self_wg, jnp.stack([key_wg, value_wg, cross_out_wg]), grad_in, grad_out], axis=0
    )
    swap = [(0, 1), (1, 0)]
    grads = (
        grads[:, :, :half].astype(F32) + lax.ppermute(grads[:, :, half:], "tensor", swap).astype(F32)
    ).astype(BF)
    head_small = small[:8, :half] + lax.ppermute(small[:8, half:], "tensor", swap)
    row_small = lax.psum(small[8:17], ("dp", "tensor"))
    head_small = lax.psum(head_small, "dp")
    shard = lax.psum_scatter(grads, "dp", scatter_dimension=1, tiled=True)
    all_shards = lax.all_gather(shard, "task", axis=0, tiled=False)
    all_head = lax.all_gather(head_small, "task", axis=0, tiled=False)
    all_row = lax.all_gather(row_small, "task", axis=0, tiled=False)
    tasks = all_shards.shape[0]
    share_rows = shard.shape[1]
    sums = pl.pallas_call(
        gram_kernel,
        grid=(block_count,),
        out_shape=jax.ShapeDtypeStruct((tasks * tasks, half), F32),
        in_specs=[pl.BlockSpec((tasks, 1, share_rows, half), lambda k: (0, k, 0, 0))],
        out_specs=const((tasks * tasks, half), 0, 0),
        compiler_params=params_for(),
        name="gram",
    )(all_shards)
    upper = jnp.sum(sums, axis=1).reshape(tasks, tasks)
    gram_weights = upper + upper.T - jnp.diag(jnp.diag(upper))
    gram_weights = lax.psum(gram_weights, ("dp", "tensor"))
    gram_heads = jnp.einsum("axy,bxy->ab", all_head, all_head, precision=highest)
    gram_heads = lax.psum(gram_heads, "tensor")
    gram = gram_weights + gram_heads + jnp.einsum(
        "axy,bxy->ab", all_row, all_row, precision=highest
    )
    task_weights = combine_weights(gram, task_order)
    tile = 64 if share_rows % 64 == 0 else share_rows
    param_update = pl.pallas_call(
        update_kernel,
        grid=(share_rows // tile,),
        out_shape=jax.ShapeDtypeStruct((share_rows, block_count, half), F32),
        in_specs=[
            pl.BlockSpec(memory_space=pltpu.SMEM),
            pl.BlockSpec((tasks, block_count, tile, half), lambda r: (0, 0, r, 0)),
        ],
        out_specs=pl.BlockSpec((tile, block_count, half), lambda r: (r, 0, 0)),
        compiler_params=params_for(),
        name="update",
    )(task_weights, all_shards)
    head_bias_update = jnp.einsum("a,axy->xy", task_weights, all_head, precision=highest)
    row_update = jnp.einsum("a,axy->xy", task_weights, all_row, precision=highest)
    return (
        block_out, query_grad, memory_grad, param_update, head_bias_update,
        row_update[:6].reshape(3, 2, width), row_update[6:9], gram,
    )


def solution(mesh):
    return jax.shard_map(
        body,
        mesh=mesh,
        in_specs=(
            P("task", "dp", None),
            P("task", "dp", None),
            P("task", "dp", None),
            P("task", "dp", None),
            P("task", "dp"),
            P(),
            P(None, None, "tensor"),
            P(None, "tensor"),
            P(),
            P(),
        ),
        out_specs=(
            P("task", "dp", None),
            P("task", ("dp", "tensor"), None),
            P("task", ("dp", "tensor"), None),
            P("dp", None, "tensor"),
            P(None, "tensor"),
            P(),
            P(),
            P(),
        ),
        check_vma=False,
    )
```

```python
import functools

import jax
import jax.numpy as jnp
from jax import lax
from jax.experimental import pallas as pl
from jax.experimental.pallas import tpu as pltpu
from jax.sharding import PartitionSpec as P

HD = 64
GROUP = 4
SLAB = GROUP * HD
BF = jnp.bfloat16
F32 = jnp.float32
MESH_ID = pl.DeviceIdType.MESH
highest = lax.Precision.HIGHEST
VMEM_LIMIT = 63 * 2**20


def combine_weights(gram_matrix, order_list):
    task_count = gram_matrix.shape[0]
    task_index = jnp.arange(task_count, dtype=jnp.int32)
    summed = jnp.zeros((task_count,), F32)
    for own_task in range(task_count):
        coeffs = (task_index == own_task).astype(F32)
        for position in range(task_count):
            chosen = (task_index == order_list[position]).astype(F32)
            column = jnp.sum(gram_matrix * chosen[None, :], axis=1)
            inner_dot = jnp.sum(coeffs * column)
            square = jnp.sum(chosen * column)
            others = (order_list[position] != own_task).astype(F32)
            coeffs = coeffs - others * jnp.minimum(inner_dot, 0.0) / (square + 1e-06) * chosen
        summed = summed + coeffs
    return summed


def mm(a, b):
    return jnp.dot(a, b, preferred_element_type=F32)


def mm_nt(a, b):
    return lax.dot_general(a, b, (((1,), (1,)), ((), ())), preferred_element_type=F32)


def mm_tn(a, b):
    return lax.dot_general(a, b, (((0,), (0,)), ((), ())), preferred_element_type=F32)


def row_of(row_ref, which):
    return row_ref[which // 2, which % 2 : which % 2 + 1].astype(F32)


def gain_of(gain_ref, which):
    return gain_ref[which : which + 1].astype(F32)


def norm_parts(residual):
    row_mean = jnp.mean(residual, axis=-1, keepdims=True)
    centred = residual - row_mean
    variance = jnp.mean(centred * centred, axis=-1, keepdims=True)
    scale = lax.rsqrt(variance + 1e-05)
    return centred * scale, scale


def norm_back(normed, scale, gain_row, grad):
    scaled = grad * gain_row
    first = jnp.mean(scaled, axis=-1, keepdims=True)
    second = jnp.mean(scaled * normed, axis=-1, keepdims=True)
    return scale * (scaled - first - normed * second)


def rows_sum(value):
    return jnp.sum(value, axis=0, keepdims=True)


def gelu_tanh(hidden):
    square = hidden * hidden
    tanh = jnp.tanh(hidden * (0.7978845608028654 + 0.7978845608028654 * 0.044715 * square))
    half = 0.5 * (1.0 + tanh)
    inner = 0.7978845608028654 + 0.7978845608028654 * 3 * 0.044715 * square
    return hidden * half, half + 0.5 * hidden * (1.0 - tanh * tanh) * inner


def head_mask(head, rows, dtype):
    lane = lax.broadcasted_iota(jnp.int32, (rows, SLAB), 1)
    return (lane // HD == head).astype(F32).astype(dtype)


def stack_heads(slab):
    return jnp.concatenate(
        [slab * head_mask(head, slab.shape[0], slab.dtype) for head in range(GROUP)], axis=0
    )


def unstack_heads(stacked):
    rows = stacked.shape[0] // GROUP
    total = None
    for head in range(GROUP):
        part = stacked[head * rows : (head + 1) * rows] * head_mask(head, rows, stacked.dtype)
        total = part if total is None else total + part
    return total


def scores_of(query_stack, key_slab, valid):
    scores = mm_nt(key_slab, query_stack)
    if valid < key_slab.shape[0]:
        row = lax.broadcasted_iota(jnp.int32, scores.shape, 0)
        scores = jnp.where(row < valid, scores, -1e30)
    return scores


def attend(query_slab, key_slab, value_slab, valid):
    scores = scores_of(stack_heads(query_slab * HD ** (-0.5)), key_slab, valid)
    row_max = jnp.max(scores, axis=0, keepdims=True)
    exps = jnp.exp(scores - row_max)
    total = jnp.sum(exps, axis=0, keepdims=True)
    probs = (exps * (1.0 / total)).astype(BF)
    mixed = unstack_heads(mm_tn(value_slab, probs).T)
    return mixed, row_max + jnp.log(total)


def attend_back(query_slab, key_slab, value_slab, log_total, grad_slab, valid):
    query_stack = stack_heads(query_slab * HD ** (-0.5))
    grad_stack = stack_heads(grad_slab)
    probs = jnp.exp(scores_of(query_stack, key_slab, valid) - log_total)
    grad_value = mm(probs.astype(BF), grad_stack)
    grad_probs = mm_nt(value_slab, grad_stack)
    inner = jnp.sum(probs * grad_probs, axis=0, keepdims=True)
    grad_scores = (probs * (grad_probs - inner)).astype(BF)
    grad_key = mm(grad_scores, query_stack)
    grad_query = unstack_heads(mm_tn(key_slab, grad_scores).T) * HD ** (-0.5)
    return grad_query.astype(BF), grad_key.astype(BF), grad_value.astype(BF)


KEY_TILE = 400


def attend_back_tiles(
    query_slab, key_ref, value_ref, log_total, grad_slab, mixed_slab, key_grad_ref, value_grad_ref
):
    query_stack = stack_heads(query_slab * HD ** (-0.5))
    grad_stack = stack_heads(grad_slab)
    product = stack_heads(grad_slab.astype(F32) * mixed_slab.astype(F32))
    high = product.astype(BF)
    low = (product - high.astype(F32)).astype(BF)
    ones = jnp.ones((8, SLAB), BF)
    inner = (mm_nt(ones, high) + mm_nt(ones, low))[0:1]
    keys = key_ref.shape[0]
    size = KEY_TILE if keys % KEY_TILE == 0 else keys

    def tile(index, grad_query):
        rows = pl.ds(pl.multiple_of(index * size, size), size)
        key, value = key_ref[rows], value_ref[rows]
        probs = jnp.exp(mm_nt(key, query_stack) - log_total)
        grad_scores = (probs * (mm_nt(value, grad_stack) - inner)).astype(BF)
        value_grad_ref[rows] = mm(probs.astype(BF), grad_stack).astype(BF)
        key_grad_ref[rows] = mm(grad_scores, query_stack).astype(BF)
        return grad_query + mm_tn(key, grad_scores)

    grad_query = lax.fori_loop(
        0, keys // size, tile, jnp.zeros((SLAB, query_stack.shape[0]), F32)
    )
    return (unstack_heads(grad_query.T) * HD ** (-0.5)).astype(BF)


def pad_rows(source_ref, target_ref, images, valid):
    first = lax.axis_index("tensor") == 0
    padded = target_ref.shape[0] // images
    for image in range(images):
        here, there = (
            source_ref[(core * images + image) * valid : (core * images + image + 1) * valid]
            for core in range(2)
        )
        rows = jnp.where(first, here.astype(F32), there.astype(F32))
        fill = jnp.zeros((padded - valid, rows.shape[1]), F32)
        target_ref[image * padded : (image + 1) * padded] = jnp.concatenate(
            [rows, fill], axis=0
        ).astype(target_ref.dtype)


def send(source, target, send_sem, recv_sem, **device):
    return pltpu.make_async_remote_copy(
        source, target, send_sem, recv_sem, device_id=device, device_id_type=MESH_ID
    )


def start_kernel(
    images, valid, own_ref, bias_ref, queries_ref, cotangent_ref, row_ref, gain_ref,
    full_ref, head_ref, tokens_ref, own_cotangent_ref, qkv_ref, mixed_ref, total_ref, sum_ref,
    cross_query_ref, first, second, bias_own, bias_all, remote_send, remote_recv, local_sem, far_sem,
):
    step, steps = pl.program_id(0), pl.num_programs(0)
    other = 1 - lax.axis_index("tensor")
    rows, blocks, width = own_ref.shape
    parts = steps // 2
    near, far = pl.ds(0, width), pl.ds(width, width)
    lower, upper = pl.ds(0, blocks), pl.ds(blocks, blocks)

    def rows_of(part):
        return pl.ds(pl.multiple_of(part * rows, rows), rows)

    def first_copies(part):
        at = rows_of(part)
        return (
            send(
                first.at[:, at, near], first.at[:, at, far], remote_send.at[part],
                remote_recv.at[part], tensor=other,
            ),
            pltpu.make_async_copy(
                first.at[:, at, near], full_ref.at[lower, at, near], local_sem.at[part]
            ),
        )

    def second_copies(part):
        at = rows_of(part)
        return (
            send(
                second.at[:, at], full_ref.at[upper, at, far], remote_send.at[parts + part],
                remote_recv.at[parts + part], tensor=other,
            ),
            pltpu.make_async_copy(
                second.at[:, at], full_ref.at[upper, at, near], local_sem.at[parts + part]
            ),
        )

    bias_copy = send(
        bias_own, bias_all.at[:, far], remote_send.at[steps], remote_recv.at[steps], tensor=other
    )
    far_copy = pltpu.make_async_copy(first.at[:, :, far], full_ref.at[lower, :, far], far_sem)

    @pl.when(step == 0)
    def _():
        barrier = pltpu.get_barrier_semaphore()
        pl.semaphore_signal(barrier, inc=1, device_id={"tensor": other}, device_id_type=MESH_ID)
        pl.semaphore_wait(barrier, 1)
        bias_own[...] = jnp.zeros_like(bias_own)
        bias_own[0 : bias_ref.shape[0]] = bias_ref[...]
        bias_copy.start()
        bias_all[:, near] = bias_own[...]

    @pl.when(step < parts)
    def _():
        first[:, rows_of(step), near] = jnp.swapaxes(own_ref[...], 0, 1)
        for copy in first_copies(step):
            copy.start()

    @pl.when(step >= parts)
    def _():
        second[:, rows_of(step - parts)] = jnp.swapaxes(own_ref[...], 0, 1)
        for copy in second_copies(step - parts):
            copy.start()

    @pl.when(step == steps - 1)
    def _():
        pad_rows(queries_ref, tokens_ref, images, valid)
        pad_rows(cotangent_ref, own_cotangent_ref, images, valid)
        bias_copy.wait()
        head_ref[...] = bias_all[...]
        for part in range(parts):
            first_copies(part)[0].wait_recv()
        far_copy.start()
        self_forward(
            images, valid, tokens_ref, first, head_ref, row_ref, gain_ref, qkv_ref, mixed_ref,
            total_ref, sum_ref, cross_query_ref,
        )
        far_copy.wait()
        for part in range(parts):
            remote, local = first_copies(part)
            remote.wait_send()
            local.wait()
            for copy in second_copies(part):
                copy.wait()


def any_spec():
    return pl.BlockSpec(memory_space=pl.ANY)


def whole_spec():
    return pl.BlockSpec(memory_space=pltpu.VMEM)


def params_for(**keys):
    return pltpu.CompilerParams(vmem_limit_bytes=VMEM_LIMIT, **keys)


def place_of(index, groups, rows):
    image = index // groups
    group = index - image * groups
    if isinstance(index, int):
        return pl.ds(image * rows, rows), pl.ds(group * SLAB, SLAB)
    return (
        pl.ds(pl.multiple_of(image * rows, rows), rows),
        pl.ds(pl.multiple_of(group * SLAB, SLAB), SLAB),
    )


def self_forward(images, valid, tokens_ref, weight_ref, head_ref, row_ref, gain_ref, qkv_ref,
                 mixed_ref, total_ref, sum_ref, cross_query_ref):
    tokens = tokens_ref[...]
    rows = tokens.shape[0] // images
    width = tokens.shape[1]
    qkv_ref[0] = (mm(tokens, weight_ref[0]) + head_ref[0:1].astype(F32)).astype(BF)
    qkv_ref[1] = mm(tokens, weight_ref[1]).astype(BF)
    qkv_ref[2] = (mm(tokens, weight_ref[2]) + head_ref[1:2].astype(F32)).astype(BF)
    groups = width // SLAB

    for index in range(images * groups):
        at, lanes = place_of(index, groups, rows)
        mixed, log_total = attend(
            qkv_ref[0, at, lanes], qkv_ref[1, at, lanes], qkv_ref[2, at, lanes], valid
        )
        mixed_ref[at, lanes] = mixed.astype(BF)
        total_ref[index] = jnp.broadcast_to(log_total, total_ref.shape[1:])
    first_sum = tokens.astype(F32) + mm_nt(mixed_ref[...], weight_ref[3]) + row_of(row_ref, 0)
    sum_ref[...] = first_sum
    first_low = (norm_parts(first_sum)[0] * gain_of(gain_ref, 0) + row_of(row_ref, 1)).astype(BF)
    cross_query_ref[...] = (mm(first_low, weight_ref[4]) + head_ref[2:3].astype(F32)).astype(BF)


def cross_kernel(context_ref, query_ref, key_w_ref, value_w_ref, head_ref, key_ref, value_ref,
                 mixed_ref, total_ref):
    context = context_ref[...]
    for group in range(key_ref.shape[1] // SLAB):
        lanes = slice(group * SLAB, (group + 1) * SLAB)
        key_ref[:, lanes] = mm(context, key_w_ref[0, :, lanes]).astype(BF)
        value_ref[:, lanes] = (
            mm(context, value_w_ref[0, :, lanes]) + head_ref[3:4, lanes].astype(F32)
        ).astype(BF)
        mixed, log_total = attend(
            query_ref[:, lanes], key_ref[:, lanes], value_ref[:, lanes], key_ref.shape[0]
        )
        mixed_ref[:, lanes] = mixed.astype(BF)
        total_ref[group] = jnp.broadcast_to(log_total, total_ref.shape[1:])


def ffn_kernel(
    images, blocks, per, sum_ref, mixed_ref, cotangent_ref, matches_ref, counts_ref, cross_w_ref,
    weight_ref, head_ref, row_ref, gain_ref,
    block_ref, left_ref, right_ref, mixed_grad_ref, residual_ref, small_ref,
    second_sum, second_low, left, right, slope, branch, third_grad, hidden_bias, weights, left_sem,
    right_sem, weight_sem,
):
    step = pl.program_id(0)
    half_steps = blocks // per

    def weight_copies(first):
        at = pl.ds(first, per)
        return [
            pltpu.make_async_copy(
                weight_ref.at[pl.ds(8 + which * blocks + first, per)], weights.at[which, at],
                weight_sem.at[which, first // per],
            )
            for which in range(2)
        ]
    rows = sum_ref.shape[0] // images

    def left_copy(which):
        return pltpu.make_async_copy(left.at[which], left_ref.at[which], left_sem.at[which])

    def right_copy(which):
        return pltpu.make_async_copy(right.at[which], right_ref.at[which], right_sem.at[which])

    mixed_copy = pltpu.make_async_copy(
        mixed_ref, right_ref.at[2 * blocks], right_sem.at[2 * blocks]
    )

    @pl.when(step == 0)
    def _():
        for copy in weight_copies(0):
            copy.start()
        mixed_copy.start()
        first_out = norm_parts(sum_ref[...])[0] * gain_of(gain_ref, 0) + row_of(row_ref, 1)
        second = first_out + mm_nt(mixed_ref[...], cross_w_ref[0]) + row_of(row_ref, 2)
        second_sum[...] = second
        second_low[...] = (
            norm_parts(second)[0] * gain_of(gain_ref, 1) + row_of(row_ref, 3)
        ).astype(BF)
        branch[...] = jnp.zeros_like(branch)
        small_ref[...] = jnp.zeros_like(small_ref)
        hidden_bias[0:blocks] = head_ref[4 : 4 + blocks].astype(F32)
        left[0] = second_low[...].T
        left_copy(0).start()

    @pl.when(step < half_steps)
    def _():
        low = second_low[...]
        first = step * per
        copies = weight_copies(first)
        copies[0].wait()
        copies[1].wait()

        @pl.when(step + 1 < half_steps)
        def _():
            for copy in weight_copies(first + per):
                copy.start()

        pres = [
            mm(low, weights[0, first + k]) + hidden_bias[pl.ds(first + k, 1)] for k in range(per)
        ]
        total = branch[...]
        for k in range(per):
            act, grad = gelu_tanh(pres[k])
            act = act.astype(BF)
            slope[first + k] = grad
            right[blocks + first + k] = act
            right_copy(blocks + first + k).start()
            total = total + mm_nt(act, weights[1, first + k])
        branch[...] = total

    @pl.when(step == half_steps - 1)
    def _():
        second = norm_parts(second_sum[...])[0] * gain_of(gain_ref, 1) + row_of(row_ref, 3)
        third_sum = second + branch[...] + row_of(row_ref, 4)
        normed, scale = norm_parts(third_sum)
        block_ref[...] = (normed * gain_of(gain_ref, 2) + row_of(row_ref, 5)).astype(BF)
        count = matches_ref.shape[2]
        slot = lax.broadcasted_iota(jnp.int32, (rows, count), 0)
        box = lax.broadcasted_iota(jnp.int32, (rows, count), 1)
        grads = []
        for image in range(images):
            own = lax.axis_index("tensor") * images + image
            live = (matches_ref[0, pl.ds(own, 1)] == slot) & (box < counts_ref[0, own])
            mask = jnp.sum(jnp.where(live, 1.0, 0.0), axis=1, keepdims=True)
            cot = cotangent_ref[image * rows : (image + 1) * rows].astype(F32)
            grads.append(cot * mask)
        out_grad = jnp.concatenate(grads, axis=0)
        grad = norm_back(normed, scale, gain_of(gain_ref, 2), out_grad)
        third_grad[...] = grad
        left[1] = grad.astype(BF).T
        left_copy(1).start()
        small_ref[12:13] = rows_sum(grad)
        small_ref[13:14] = rows_sum(out_grad)
        small_ref[16:17] = rows_sum(out_grad * normed)
        branch[...] = jnp.zeros_like(branch)

    @pl.when(step >= half_steps)
    def _():
        ffn_low = third_grad[...].astype(BF)
        first = (step - half_steps) * per
        grads = [mm(ffn_low, weights[1, first + k]) for k in range(per)]
        total = branch[...]
        for k in range(per):
            grad_low = (grads[k] * slope[first + k]).astype(BF)
            right[first + k] = grad_low
            right_copy(first + k).start()
            small_ref[pl.ds(4 + first + k, 1)] = rows_sum(grad_low.astype(F32))
            total = total + mm_nt(grad_low, weights[0, first + k])
        branch[...] = total

    @pl.when(step == 2 * half_steps - 1)
    def _():
        second_in = third_grad[...] + branch[...]
        normed, scale = norm_parts(second_sum[...])
        grad = norm_back(normed, scale, gain_of(gain_ref, 1), second_in)
        residual_ref[...] = grad
        small_ref[10:11] = rows_sum(grad)
        small_ref[11:12] = rows_sum(second_in)
        small_ref[15:16] = rows_sum(second_in * normed)
        cross_low = grad.astype(BF)
        left[2] = cross_low.T
        left_copy(2).start()
        mixed_grad_ref[...] = mm(cross_low, cross_w_ref[0]).astype(BF)
        mixed_copy.wait()
        for which in range(3):
            left_copy(which).wait()
        for which in range(2 * blocks):
            right_copy(which).wait()


def cross_back_step(
    image, group, query_ref, key_ref, value_ref, total_ref, mixed_grad_ref, mixed_ref, small_ref,
    context_t, key_acc, value_acc, key_grad_ref, value_grad_ref, unit,
):
    grad_query = attend_back_tiles(
        query_ref[...], key_ref, value_ref, total_ref[0, 0:1], mixed_grad_ref[...], mixed_ref[...],
        key_grad_ref, value_grad_ref,
    )
    grad_key, grad_value = key_grad_ref[...], value_grad_ref[...]
    lanes = pl.ds(pl.multiple_of(group * SLAB, SLAB), SLAB)
    small_ref[2:3, lanes] += rows_sum(grad_query.astype(F32))
    small_ref[3:4, lanes] += rows_sum(grad_value.astype(F32))
    unit(0)
    key_wg = mm(context_t[...], grad_key)
    value_wg = mm(context_t[...], grad_value)

    @pl.when(image == 0)
    def _():
        key_acc[:, lanes] = key_wg
        value_acc[:, lanes] = value_wg

    @pl.when(image > 0)
    def _():
        key_acc[:, lanes] += key_wg
        value_acc[:, lanes] += value_wg

    unit(1)
    return grad_query


def cross_back_kernel(
    context_ref, query_ref, key_ref, value_ref, total_ref, mixed_grad_ref, mixed_ref, key_w_ref,
    value_w_ref, query_grad_ref, context_grad_ref, key_wg_ref, value_wg_ref, small_ref,
    context_t, acc, key_acc, value_acc, key_grad, value_grad,
):
    image, group = pl.program_id(0), pl.program_id(1)
    images, groups = pl.num_programs(0), pl.num_programs(1)

    @pl.when((image == 0) & (group == 0))
    def _():
        small_ref[...] = jnp.zeros_like(small_ref)

    @pl.when(group == 0)
    def _():
        context_t[...] = context_ref[...].T

    query_grad_ref[...] = cross_back_step(
        image, group, query_ref, key_ref, value_ref, total_ref, mixed_grad_ref, mixed_ref,
        small_ref, context_t, key_acc, value_acc, key_grad, value_grad, lambda part: None,
    )
    context_part = mm_nt(key_grad[...], key_w_ref[0]) + mm_nt(value_grad[...], value_w_ref[0])

    @pl.when(group == 0)
    def _():
        acc[...] = context_part

    @pl.when(group > 0)
    def _():
        acc[...] += context_part

    @pl.when(group == groups - 1)
    def _():
        context_grad_ref[...] = acc[...].astype(BF)

    @pl.when((image == images - 1) & (group == groups - 1))
    def _():
        key_wg_ref[...] = key_acc[...].astype(BF)
        value_wg_ref[...] = value_acc[...].astype(BF)


def self_back(
    images, valid, tokens_ref, weight_ref, row_ref, gain_ref, qkv_ref, mixed_ref, total_ref, sum_ref,
    residual_ref, cross_query_grad_ref, mixed_grad_ref, small_ref, qkv_grad, emit, unit, loop_unit,
    used,
):
    tokens = tokens_ref[...]
    rows = tokens.shape[0] // images
    width = tokens.shape[1]
    normed, scale = norm_parts(sum_ref[...])
    first_low = (normed * gain_of(gain_ref, 0) + row_of(row_ref, 1)).astype(BF)
    cross_query_grad = cross_query_grad_ref[...]
    first_low_t = first_low.T
    emit(4, lambda lanes: mm(first_low_t, cross_query_grad_ref[:, lanes]))
    unit()
    first_in = residual_ref[...] + mm_nt(cross_query_grad, weight_ref[4])
    first_grad = norm_back(normed, scale, gain_of(gain_ref, 0), first_in)
    small_ref[8:9] = rows_sum(first_grad)
    small_ref[9:10] = rows_sum(first_in)
    small_ref[14:15] = rows_sum(first_in * normed)
    self_low = first_grad.astype(BF)
    self_low_t = self_low.T
    emit(3, lambda lanes: mm(self_low_t, mixed_ref[:, lanes]))
    unit()
    mixed_grad_ref[...] = mm(self_low, weight_ref[3]).astype(BF)
    used()
    groups = width // SLAB

    def one(index, carry):
        at, lanes = place_of(index, groups, rows)
        grads = attend_back(
            qkv_ref[0, at, lanes], qkv_ref[1, at, lanes], qkv_ref[2, at, lanes],
            total_ref[index, 0:1], mixed_grad_ref[at, lanes], valid,
        )
        for which in range(3):
            qkv_grad[which, at, lanes] = grads[which]
        loop_unit(index)
        return carry

    lax.fori_loop(0, images * groups, one, 0)
    tokens_t = tokens.T
    total = first_grad
    for which in range(3):
        grad = qkv_grad[which]
        emit(which, lambda lanes, which=which: mm(tokens_t, qkv_grad[which, :, lanes]))
        if which != 1:
            unit()
        total = total + mm_nt(grad, weight_ref[which])
    small_ref[0:1] = rows_sum(qkv_grad[0].astype(F32))
    small_ref[1:2] = rows_sum(qkv_grad[2].astype(F32))
    return total


def self_back_kernel(
    images, valid, tokens_ref, weight_ref, row_ref, gain_ref, qkv_ref, mixed_ref, total_ref, sum_ref,
    residual_ref, cross_query_grad_ref, query_grad_ref, wg_ref, small_ref, qkv_grad, mixed_grad,
):
    small_ref[...] = jnp.zeros_like(small_ref)

    def emit(block, value):
        for lane in range(0, wg_ref.shape[2], SLAB):
            lanes = slice(lane, lane + SLAB)
            wg_ref[block, :, lanes] = value(lanes).astype(BF)

    query_grad_ref[...] = self_back(
        images, valid, tokens_ref, weight_ref, row_ref, gain_ref, qkv_ref, mixed_ref, total_ref,
        sum_ref, residual_ref, cross_query_grad_ref, mixed_grad, small_ref, qkv_grad, emit,
        lambda: None, lambda index: None, lambda: None,
    ).astype(BF)


def task_peers(tasks):
    me = lax.axis_index("task")
    return [lax.rem(me + shift, tasks) for shift in range(1, tasks)]


def task_senders(tasks):
    me = lax.axis_index("task")
    return [lax.rem(me + tasks - shift, tasks) for shift in range(1, tasks)]


def greet(depth, tasks):
    me = lax.axis_index("dp")
    barrier = pltpu.get_barrier_semaphore()
    other = 1 - lax.axis_index("tensor")
    for peer in task_peers(tasks):
        pl.semaphore_signal(barrier, inc=1, device_id={"task": peer}, device_id_type=MESH_ID)
        pl.semaphore_signal(
            barrier, inc=1, device_id={"task": peer, "tensor": other}, device_id_type=MESH_ID
        )
    for shift in range(1, depth):
        pl.semaphore_signal(
            barrier, inc=1, device_id={"dp": lax.rem(me + shift, depth)}, device_id_type=MESH_ID
        )
    pl.semaphore_signal(barrier, inc=1, device_id={"tensor": other}, device_id_type=MESH_ID)
    pl.semaphore_wait(barrier, 2 * (tasks - 1) + depth)


LAG = 2
SLOTS = 3
STAGES = 2


class Chain:
    def __init__(self, depth, tasks, refs):
        self.depth, self.tasks = depth, tasks
        (self.near, self.far, self.stage, self.passed, self.parts,
         self.far_send, self.far_recv, self.far_free, self.pass_send, self.pass_recv,
         self.part_send, self.part_recv) = refs
        self.chunks = self.passed.shape[1]
        self.rows, self.half = self.passed.shape[2:]
        self.me = lax.axis_index("dp")
        self.task = lax.axis_index("task")
        self.is_end = (self.me == 0) | (self.me == depth - 1)

    SCRATCH = 12

    @staticmethod
    def scratch(blocks, rows, half, tasks):
        chunks = 2 * blocks
        dma = pltpu.SemaphoreType.DMA
        return [
            pltpu.VMEM((2, chunks, rows, half), BF),
            pltpu.VMEM((SLOTS, 2, 2, rows, half), BF),
            pltpu.VMEM((STAGES, 2, 2, rows, half), BF),
            pltpu.VMEM((2, chunks, rows, half), BF),
            pltpu.VMEM((tasks, chunks, rows // tasks, half), BF),
            dma((STAGES,)),
            dma((SLOTS,)),
            pltpu.SemaphoreType.REGULAR,
            dma((2, chunks)),
            dma((2, chunks)),
            dma((blocks, tasks - 1)),
            dma((blocks, tasks - 1)),
        ]

    def far_copy(self, block):
        slot, stage = lax.rem(block, SLOTS), lax.rem(block, STAGES)
        return send(
            self.stage.at[stage], self.far.at[slot], self.far_send.at[stage], self.far_recv.at[slot],
            tensor=1 - lax.axis_index("tensor"),
        )

    def emit(self, block, value):
        block = jnp.int32(block)
        stage = lax.rem(block, STAGES)

        @pl.when(block >= STAGES)
        def _():
            self.far_copy(block).wait_send()

        @pl.when(block >= SLOTS)
        def _():
            pl.semaphore_wait(self.far_free, 1)

        def place(low, target):
            for way in range(2):
                for part in range(2):
                    row = (2 * way + part) * self.rows
                    target(way, part, low[row : row + self.rows])

        def slab(start):
            low = value(slice(start, start + SLAB)).astype(BF)
            own = max(min(self.half - start, SLAB), 0)
            if own:

                def keep(way, part, rows):
                    self.near[way, 2 * block + part, :, start : start + own] = rows

                place(low[:, :own], keep)
            if own < SLAB:
                first = start + own - self.half

                def give(way, part, rows):
                    self.stage[stage, way, part, :, first : first + SLAB - own] = rows

                place(low[:, own:], give)

        starts = range(0, 2 * self.half, SLAB)
        for start in starts:
            if start + SLAB > self.half:
                slab(start)
        self.far_copy(block).start()
        for start in starts:
            if start + SLAB <= self.half:
                slab(start)

    def absorb(self, block):
        block = jnp.int32(block)
        slot = lax.rem(block, SLOTS)
        self.far_copy(block).wait_recv()
        for way in range(2):
            chunks = pl.ds(2 * block, 2)
            self.near[way, chunks] = self.near[way, chunks] + self.far[slot, way]

        @pl.when(block < self.chunks // 2 - SLOTS)
        def _():
            pl.semaphore_signal(
                self.far_free, inc=1, device_id={"tensor": 1 - lax.axis_index("tensor")},
                device_id_type=MESH_ID,
            )

    def pass_copy(self, way, chunk):
        piece = self.passed.at[way, chunk]
        target = self.me - 1 if way == 0 else self.me + 1
        return send(
            piece, piece, self.pass_send.at[way, chunk], self.pass_recv.at[way, chunk], dp=target
        )

    def part_rows(self, peer):
        size = self.rows // self.tasks
        return pl.ds(pl.multiple_of(peer * size, size), size)

    def part_copy(self, way, block, shift, peer):
        chunks = pl.ds(2 * block, 2)
        return send(
            self.passed.at[way, chunks, self.part_rows(peer)], self.parts.at[self.task, chunks],
            self.part_send.at[block, shift], self.part_recv.at[block, shift], task=peer,
        )

    def hops(self, way):
        return self.depth - 1 - self.me if way == 0 else self.me

    def units(self):
        return self.chunks + LAG * (self.depth - 1)

    def unit(self, index):
        for way in range(2):
            chunk = index - LAG * self.hops(way)

            @pl.when((chunk >= 0) & (chunk < self.chunks))
            def _(way=way, chunk=chunk):
                self.chunk_step(way, chunk)

    def chunk_step(self, way, chunk):
        first, last = self.hops(way) == 0, self.hops(way) == self.depth - 1
        block = chunk // 2
        own = self.near[way, chunk]

        @pl.when(first)
        def _():
            self.passed[way, chunk] = own

        @pl.when(jnp.logical_not(first))
        def _():
            self.pass_copy(way, chunk).wait_recv()
            self.passed[way, chunk] = own + self.passed[way, chunk]

        @pl.when(jnp.logical_not(last))
        def _():
            self.pass_copy(way, chunk).start()

        @pl.when(last & (chunk == 2 * block + 1))
        def _():
            for shift, peer in enumerate(task_peers(self.tasks)):
                self.part_copy(way, block, shift, peer).start()
            own_rows = self.part_rows(self.task)
            self.parts[self.task, chunk - 1] = self.passed[way, chunk - 1, own_rows]
            self.parts[self.task, chunk] = self.passed[way, chunk, own_rows]

    def wait_parts(self, block):
        for shift, peer in enumerate(task_senders(self.tasks)):
            landed = self.parts.at[peer, pl.ds(2 * block, 2)]
            send(
                landed, landed, self.part_send.at[block, shift], self.part_recv.at[block, shift],
                task=peer,
            ).wait_recv()

    def finish(self):
        def blocks(block, carry):
            for way in range(2):

                @pl.when(self.hops(way) != self.depth - 1)
                def _(way=way):
                    for part in range(2):
                        self.pass_copy(way, 2 * block + part).wait_send()

                @pl.when(self.hops(way) == self.depth - 1)
                def _(way=way):
                    for shift, peer in enumerate(task_peers(self.tasks)):
                        self.part_copy(way, block, shift, peer).wait_send()

            return carry

        lax.fori_loop(0, self.chunks // 2, blocks, 0)


def pairs_of(tasks):
    return [(a, b) for a in range(tasks) for b in range(a, tasks)]


def weights_of(gram, order_ref, tasks):
    totals = [0.0] * tasks
    for own in range(tasks):
        coeffs = [jnp.full_like(gram[0, 0], 1.0 if t == own else 0.0) for t in range(tasks)]
        for position in range(tasks):
            chosen = [
                jnp.where(order_ref[position] == t, 1.0, 0.0).astype(F32) for t in range(tasks)
            ]
            column = [sum(gram[t, j] * chosen[j] for j in range(tasks)) for t in range(tasks)]
            inner = sum(coeffs[t] * column[t] for t in range(tasks))
            square = sum(chosen[t] * column[t] for t in range(tasks))
            others = 1.0 - chosen[own]
            share = others * jnp.minimum(inner, 0.0) / (square + 1e-06)
            coeffs = [coeffs[t] - share * chosen[t] for t in range(tasks)]
        totals = [total + coeff for total, coeff in zip(totals, coeffs)]
    return totals


GROUPS = 8
UNITS = 2
TILE = 240


class ContextGrad:
    def __init__(self, key_grad, value_grad, weights, result, refs):
        self.grads, self.weights, self.result = (key_grad, value_grad), weights, result
        (self.staged, self.ring, self.done, self.staged_sem, self.ring_sem, self.done_sem) = refs
        self.tile = self.done.shape[1]
        self.tiles = result.shape[0] // self.tile

    SCRATCH = 6

    @staticmethod
    def scratch(keys, width):
        dma = pltpu.SemaphoreType.DMA
        return [
            pltpu.VMEM((2, keys, SLAB), BF),
            pltpu.VMEM((2, 2, width // SLAB, TILE, SLAB), BF),
            pltpu.VMEM((2, TILE, width), BF),
            dma((2,)),
            dma((2, 2)),
            dma((2,)),
        ]

    def staged_copies(self, image, group):
        keys = self.staged.shape[1]
        rows = pl.ds(pl.multiple_of(image * keys, keys), keys)
        return [
            pltpu.make_async_copy(
                self.staged.at[which], self.grads[which].at[group, rows], self.staged_sem.at[which]
            )
            for which in range(2)
        ]

    def put(self, image, group):
        for copy in self.staged_copies(image, group):
            copy.start()

    def settle(self):
        for copy in self.staged_copies(0, 0):
            copy.wait()

    def fetches(self, index):
        slot = lax.rem(index, 2)
        rows = pl.ds(pl.multiple_of(index * self.tile, self.tile), self.tile)
        return [
            pltpu.make_async_copy(
                self.grads[which].at[:, rows], self.ring.at[slot, which],
                self.ring_sem.at[slot, which],
            )
            for which in range(2)
        ]

    def store(self, index):
        slot = lax.rem(index, 2)
        rows = pl.ds(pl.multiple_of(index * self.tile, self.tile), self.tile)
        return pltpu.make_async_copy(
            self.done.at[slot], self.result.at[rows], self.done_sem.at[slot]
        )

    def compute(self, index):
        @pl.when(index < self.tiles)
        def _():
            for copy in self.fetches(index):
                copy.wait()

            @pl.when(index + 1 < self.tiles)
            def _():
                for copy in self.fetches(index + 1):
                    copy.start()

            @pl.when(index >= 2)
            def _():
                self.store(index - 2).wait()

            slot = lax.rem(index, 2)
            parts = [
                jnp.concatenate(
                    [self.ring[slot, which, group] for group in range(self.ring.shape[2])], axis=1
                )
                for which in range(2)
            ]
            total = mm_nt(parts[0], self.weights[0]) + mm_nt(parts[1], self.weights[1])
            self.done[slot] = total.astype(BF)
            self.store(index).start()

    def finish(self):
        for index in range(self.tiles - 2, self.tiles):
            self.store(jnp.int32(index)).wait()


def back_kernel(
    depth, tasks, images, groups, valid, block_order, order_ref, context_ref, query_ref, key_ref,
    value_ref, total_ref, mixed_grad_ref, cross_mixed_ref, tokens_ref, row_ref, gain_ref, qkv_ref,
    mixed_ref, self_total_ref, sum_ref, residual_ref, small_in_ref, all_w_ref, block_ref, left_ref, right_ref,
    *refs
):
    (
        context_grad_ref, query_grad_ref, update_ref, small_out_ref, gram_ref, block_far,
        key_grad, value_grad,
    ), refs = refs[:8], refs[8:]
    (
        context, context_t, key_acc, value_acc, cross_query_grad, self_mixed_grad, qkv_grad, weights,
        block_sem, weight_sem, context_sem,
    ), refs = refs[:11], refs[11:]
    context_back = ContextGrad(
        key_grad, value_grad, weights.at[pl.ds(3, 2)], context_grad_ref,
        refs[: ContextGrad.SCRATCH],
    )
    refs = refs[ContextGrad.SCRATCH :]
    chain = Chain(depth, tasks, refs[: Chain.SCRATCH])
    refs = refs[Chain.SCRATCH :]
    gram_acc = refs[7]
    step = pl.program_id(0)
    cross_steps = images * groups
    half = chain.half
    is_end = chain.is_end
    pairs = pairs_of(tasks)

    block_copy = send(
        block_ref, block_far, block_sem.at[0], block_sem.at[1], tensor=1 - lax.axis_index("tensor")
    )
    weight_copies = [
        pltpu.make_async_copy(all_w_ref.at[source], weights.at[target], weight_sem.at[index])
        for index, (source, target) in enumerate(
            [(pl.ds(0, 5), pl.ds(0, 5)), (pl.ds(5, 2), pl.ds(3, 2))]
        )
    ]

    def context_copy(image):
        keys = context.shape[0]
        own = lax.axis_index("tensor") * images + image
        rows = pl.ds(pl.multiple_of(own * keys, keys), keys)
        return pltpu.make_async_copy(context_ref.at[0, rows], context, context_sem)

    @pl.when(step == 0)
    def _():
        context_copy(0).start()
        weight_copies[0].start()
        greet(depth, tasks)
        block_copy.start()
        gram_acc[...] = jnp.zeros_like(gram_acc)
        refs[0][...] = small_in_ref[...]

    @pl.when(step < cross_steps)
    def _():
        image = step // groups
        group = step - image * groups

        chain.emit(step, lambda lanes: mm(left_ref[0], right_ref[0, :, lanes]))

        @pl.when(group == 0)
        def _():
            context_copy(image).wait()
            context_t[...] = context[...].T

            @pl.when(image + 1 < images)
            def _():
                context_copy(image + 1).start()

        def cross_unit(part):
            if part == 0:
                chain.absorb(step)
            chain.unit(step * UNITS + part)

        @pl.when(step > 0)
        def _():
            context_back.settle()

        grad_query = cross_back_step(
            image, group, query_ref, key_ref, value_ref, total_ref, mixed_grad_ref, cross_mixed_ref,
            refs[0], context_t, key_acc, value_acc, context_back.staged.at[0],
            context_back.staged.at[1], cross_unit,
        )
        context_back.put(image, group)
        rows = grad_query.shape[0]
        cross_query_grad[
            pl.ds(pl.multiple_of(image * rows, rows), rows),
            pl.ds(pl.multiple_of(group * SLAB, SLAB), SLAB),
        ] = grad_query

        @pl.when(step == cross_steps - 1)
        def _():
            chain.emit(cross_steps, lambda lanes: key_acc[:, lanes])
            chain.emit(cross_steps + 1, lambda lanes: value_acc[:, lanes])

    @pl.when(step == cross_steps)
    def _():
        done = [cross_steps * UNITS]
        blocks = len(block_order)

        def self_unit():
            if done[0] % 2 == 0:
                chain.absorb(done[0] // 2)
            chain.unit(jnp.int32(done[0]))
            done[0] += 1

        in_loop = images * groups // 2

        def loop_unit(index):
            now = cross_steps * UNITS + 2 + index // 2

            @pl.when(index % 2 == 1)
            def _():
                @pl.when(now % 2 == 0)
                def _():
                    chain.absorb(now // 2)

                chain.unit(now)

        def used():
            done[0] += in_loop
            weight_copies[1].start()

        context_back.settle()
        for copy in context_back.fetches(jnp.int32(0)):
            copy.start()
        weight_copies[0].wait()
        query_grad_ref[...] = self_back(
            images, valid, tokens_ref, weights, row_ref, gain_ref, qkv_ref, mixed_ref,
            self_total_ref, sum_ref, residual_ref, cross_query_grad, self_mixed_grad, refs[0],
            qkv_grad, lambda block, value: chain.emit(block_order.index(block), value), self_unit,
            loop_unit, used,
        ).astype(BF)
        for block in range(-(-done[0] // 2), blocks):
            chain.absorb(block)
        weight_copies[1].wait()
        rest(
            chain, context_back, done[0], order_ref, update_ref, small_out_ref, gram_ref, refs
        )
        for block in range(blocks - STAGES, blocks):
            chain.far_copy(jnp.int32(block)).wait_send()
        block_copy.wait()
        context_back.finish()


def rest(
    chain, context_back, done, order_ref, update_ref, small_out_ref, gram_ref, refs
):
    (
        small, small_own, small_other, small_far, small_pass, small_all, small_both, gram_acc,
        gram_plane, gram_end, out,
        small_far_sem, small_pass_sem, small_task_sem, small_dp_sem, small_core_sem,
        gram_plane_sem, gram_dp_sem, hop_sem, out_sem, update_sem,
    ) = refs
    depth, tasks, half = chain.depth, chain.tasks, chain.half
    me, task, core = (lax.axis_index(axis) for axis in ("dp", "task", "tensor"))
    is_end = chain.is_end
    top = me == 0
    pairs = pairs_of(tasks)
    own_lanes = pl.ds(pl.multiple_of(core * half, half), half)
    other_lanes = pl.ds(pl.multiple_of((1 - core) * half, half), half)
    small_own[0:8] = small[0:8, 0:half]
    small_own[8:] = small[8:, own_lanes]
    small_other[0:8] = small[0:8, half:]
    small_other[8:] = small[8:, other_lanes]
    small_copy = send(
        small_other, small_far, small_far_sem.at[0], small_far_sem.at[1], tensor=1 - core
    )
    small_copy.start()

    def small_hop():
        return send(
            small_pass, small_pass, small_pass_sem.at[0], small_pass_sem.at[1], dp=me - 1
        )

    def small_task_copy(shift, peer):
        return send(
            small_pass, small_all.at[task], small_task_sem.at[0, shift],
            small_task_sem.at[1, shift], task=peer,
        )

    def add_products(shares):
        for index, (a, b) in enumerate(pairs):
            product = shares[a] * shares[b]
            total = product[0:8]
            for row in range(8, product.shape[0], 8):
                total = total + product[row : row + 8]
            gram_acc[index * 8 : index * 8 + 8] += total

    blocks = chain.chunks // 2
    late = LAG * (depth - 1) + 3

    def products_of(block):
        @pl.when((block >= 0) & (block < blocks))
        def _():
            chain.wait_parts(block)

            def part(which, carry):
                add_products(
                    [chain.parts[t, 2 * block + which].astype(F32) for t in range(tasks)]
                )
                return carry

            lax.fori_loop(0, 2, part, 0)

    def step(index, carry):
        chain.unit(index)
        context_back.compute(index - done)
        since = index - late

        @pl.when(is_end)
        def _():
            early = (done - late) // 2 + 1
            products_of(jnp.where(index - done < early, index - done, -1))
            products_of(jnp.where(since == 2 * (since // 2), since // 2, -1))

        @pl.when(index == done + 1 + LAG * chain.hops(0))
        def _():
            small_copy.wait_recv()
            total = small_own[...] + small_far[...]

            @pl.when(me == depth - 1)
            def _():
                small_pass[...] = total

            @pl.when(me < depth - 1)
            def _():
                small_hop().wait_recv()
                small_pass[...] += total

            @pl.when(me > 0)
            def _():
                small_hop().start()

            @pl.when(top)
            def _():
                for shift, peer in enumerate(task_peers(tasks)):
                    small_task_copy(shift, peer).start()
                small_all[task] = small_pass[...]

        return carry

    lax.fori_loop(done, max(chain.units() + 2, done + context_back.tiles), step, 0)

    @pl.when(top)
    def _():
        for shift, peer in enumerate(task_senders(tasks)):
            landed = small_all.at[peer]
            send(
                landed, landed, small_task_sem.at[0, shift], small_task_sem.at[1, shift], task=peer
            ).wait_recv()

    lanes = gram_plane.shape[2]
    plane = 2 * tasks
    mine = 2 * task + core

    def gram_copy(shift):
        to = lax.rem(mine + shift, plane)
        return send(
            gram_plane.at[mine], gram_plane.at[mine], gram_plane_sem.at[0, shift - 1],
            gram_plane_sem.at[1, shift - 1], task=to // 2, tensor=lax.rem(to, 2),
        )

    def gram_arrival(shift):
        place = lax.rem(mine + plane - shift, plane)
        return send(
            gram_plane.at[place], gram_plane.at[place], gram_plane_sem.at[0, shift - 1],
            gram_plane_sem.at[1, shift - 1], task=place // 2, tensor=lax.rem(place, 2),
        )

    def gram_dp_copy(end, shift):
        return send(
            gram_end.at[end], gram_end.at[end], gram_dp_sem.at[0, end, shift],
            gram_dp_sem.at[1, end, shift], dp=lax.rem((depth - 1) * end + shift + 1, depth),
        )

    def one_number(values):
        return jnp.sum(jnp.sum(values, axis=0, keepdims=True), axis=1, keepdims=True)

    @pl.when(top & (task == 0))
    def _():
        small_values = [small_all[t] for t in range(tasks)]
        for index, (a, b) in enumerate(pairs):
            product = small_values[a] * small_values[b]
            gram_acc[index * 8 : index * 8 + 8] += product[0:8] + product[8:16] + product[16:24]

    @pl.when(is_end)
    def _():
        gram_plane[mine] = jnp.zeros(gram_plane.shape[1:], F32)
        for index in range(len(pairs)):
            gram_plane[mine, index : index + 1] = jnp.broadcast_to(
                one_number(gram_acc[index * 8 : index * 8 + 8]), (1, lanes)
            )
        for shift in range(1, plane):
            gram_copy(shift).start()
        for shift in range(1, plane):
            gram_arrival(shift).wait_recv()

    for end in range(2):

        @pl.when(me == (depth - 1) * end)
        def _(end=end):
            total = gram_plane[0]
            for place in range(1, plane):
                total = total + gram_plane[place]
            gram_end[end] = total
            for shift in range(depth - 1):
                gram_dp_copy(end, shift).start()

    for end in range(2):
        for shift in range(depth - 1):

            @pl.when(me == ((depth - 1) * end + shift + 1) % depth)
            def _(end=end, shift=shift):
                gram_dp_copy(end, shift).wait_recv()

    gram = {}
    for index, (a, b) in enumerate(pairs):
        row = slice(index, index + 1)
        gram[a, b] = gram[b, a] = gram_end[0, row] + gram_end[1, row]
    for a in range(tasks):
        for b in range(tasks):
            gram_ref[a * tasks + b : a * tasks + b + 1] = gram[a, b]
    weights = [
        jnp.concatenate([weight] * (half // lanes), axis=1)
        for weight in weights_of(gram, order_ref, tasks)
    ]

    group = blocks // GROUPS
    share = chain.rows // tasks
    own_share = pl.ds(pl.multiple_of(task * share, share), share)
    own_part = jnp.minimum(me, 1)

    def hop_copy(index):
        return send(
            chain.near.at[1, pl.ds(index * group, group), pl.ds(0, share)],
            out.at[pl.ds(index * group, group), own_share],
            hop_sem.at[0, index], hop_sem.at[1, index],
            dp=jnp.where(top, 1, depth - 2),
        )

    beside = [task + 1 - 2 * lax.rem(task, 2), task + 2 - 4 * (task // 2)]
    across = tasks - 1 - task

    def out_piece(index, owner):
        rows = pl.ds(pl.multiple_of(owner * share, share), share)
        return out.at[pl.ds(index * group, group), rows]

    def out_copy(index, which, owner):
        piece = out_piece(index, owner)
        peer = beside[which] if which < 2 else beside[1 if index < GROUPS // 2 else 0]
        return send(
            piece, piece, out_sem.at[0, index, which], out_sem.at[1, index, which], task=peer
        )

    def update_copy(index):
        at = pl.ds(index * group, group)
        return pltpu.make_async_copy(out.at[at], update_ref.at[at], update_sem.at[index])

    def weighted(chunk):
        total = weights[0] * chain.parts[0, chunk].astype(F32)
        for t in range(1, tasks):
            total = total + weights[t] * chain.parts[t, chunk].astype(F32)
        return total.astype(BF)

    def small_dp_copy(shift):
        return send(
            small_both.at[0], small_both.at[0], small_dp_sem.at[0, shift],
            small_dp_sem.at[1, shift], dp=shift + 1,
        )

    def small_core_copy():
        return send(
            small_both.at[0], small_both.at[1], small_core_sem.at[0], small_core_sem.at[1],
            tensor=1 - core,
        )

    @pl.when(top)
    def _():
        total = weights[0] * small_all[0]
        for t in range(1, tasks):
            total = total + weights[t] * small_all[t]
        small_both[0] = total
        for shift in range(depth - 1):
            small_dp_copy(shift).start()

    @pl.when(is_end)
    def _():
        for index in range(GROUPS):

            def other(block, carry):
                chain.near[1, block, 0:share] = weighted(2 * block + 1 - own_part)
                return carry

            lax.fori_loop(index * group, (index + 1) * group, other, 0)
            hop_copy(index).start()

            def own(block, carry):
                out[block, own_share] = weighted(2 * block + own_part)
                return carry

            lax.fori_loop(index * group, (index + 1) * group, own, 0)
            for which in range(2):
                out_copy(index, which, task).start()

    @pl.when(jnp.logical_not(is_end))
    def _():
        for index in range(GROUPS):
            hop_copy(index).wait_recv()
            for which in range(2):
                out_copy(index, which, task).start()

    for shift in range(depth - 1):

        @pl.when(me == shift + 1)
        def _(shift=shift):
            small_dp_copy(shift).wait_recv()

    small_core_copy().start()

    for index in range(GROUPS):
        for which in range(2):
            out_copy(index, which, beside[which]).wait_recv()
        out_copy(index, 2, beside[0 if index < GROUPS // 2 else 1]).start()
    for index in range(GROUPS):
        out_copy(index, 2, across).wait_recv()
        update_copy(index).start()

    small_core_copy().wait_recv()
    small_out_ref[0:8, 0:half] = small_both[0, 0:8]
    small_out_ref[0:8, half:] = small_both[1, 0:8]
    small_out_ref[8:, own_lanes] = small_both[0, 8:]
    small_out_ref[8:, other_lanes] = small_both[1, 8:]

    small_copy.wait_send()
    small_core_copy().wait_send()
    chain.finish()

    @pl.when(me > 0)
    def _():
        small_hop().wait_send()

    @pl.when(top)
    def _():
        for shift, peer in enumerate(task_peers(tasks)):
            small_task_copy(shift, peer).wait_send()
        for shift in range(depth - 1):
            small_dp_copy(shift).wait_send()

    for end in range(2):

        @pl.when(me == (depth - 1) * end)
        def _(end=end):
            for shift in range(depth - 1):
                gram_dp_copy(end, shift).wait_send()

    @pl.when(is_end)
    def _():
        for shift in range(1, plane):
            gram_copy(shift).wait_send()
        for index in range(GROUPS):
            hop_copy(index).wait_send()

    for index in range(GROUPS):
        update_copy(index).wait()
        for which in range(3):
            out_copy(index, which, task).wait_send()


def spread_kernel(
    images, valid, tasks, block_order, parts_ref, context_grad_ref, query_grad_ref, block_ref,
    block_far_ref, small_ref, gram_in_ref,
    update_ref, context_out_ref, query_out_ref, block_out_ref, head_ref, row_ref, gain_ref, gram_ref,
):
    ordered = [parts_ref[block_order.index(block)] for block in range(len(block_order))]
    update_ref[...] = jnp.swapaxes(jnp.stack(ordered), 0, 1).astype(F32)
    context_out_ref[...] = context_grad_ref[...]

    @pl.when(pl.program_id(0) == 0)
    def _():
        padded = query_grad_ref.shape[0] // images
        first = lax.axis_index("tensor") == 0

        def rows(ref, image):
            return ref[image * padded : (image + 1) * padded].astype(F32)[:valid]

        for image in range(images):
            at = slice(image * valid, (image + 1) * valid)
            after = slice((images + image) * valid, (images + image + 1) * valid)
            query_out_ref[at] = rows(query_grad_ref, image).astype(BF)
            near, far = rows(block_ref, image), rows(block_far_ref, image)
            block_out_ref[at] = jnp.where(first, near, far).astype(BF)
            block_out_ref[after] = jnp.where(first, far, near).astype(BF)
        head_ref[...] = small_ref[0:8, 0 : head_ref.shape[1]]
        for which in range(6):
            row_ref[which // 2, which % 2 : which % 2 + 1] = small_ref[8 + which : 9 + which]
        gain_ref[...] = small_ref[14:17]
        for a in range(tasks):
            for b in range(tasks):
                at = a * tasks + b
                gram_ref[a : a + 1, b : b + 1] = gram_in_ref[at : at + 1, 0:1]


def gram_kernel(parts_ref, gram_ref):
    tasks = parts_ref.shape[0]

    @pl.when(pl.program_id(0) == 0)
    def _():
        gram_ref[...] = jnp.zeros_like(gram_ref)

    shares = [parts_ref[task, 0].astype(F32) for task in range(tasks)]
    for a in range(tasks):
        for b in range(a, tasks):
            gram_ref[a * tasks + b : a * tasks + b + 1] += rows_sum(shares[a] * shares[b])


def update_kernel(weights_ref, parts_ref, update_ref):
    tasks, blocks = parts_ref.shape[:2]
    for block in range(blocks):
        total = weights_ref[0] * parts_ref[0, block].astype(F32)
        for task in range(1, tasks):
            total += weights_ref[task] * parts_ref[task, block].astype(F32)
        update_ref[:, block, :] = total


def body(
    queries, memory, cotangent, matches, counts, task_order, params, head_bias, row_bias, norm_gain
):
    all_images = matches.shape[1]
    valid = matches.shape[2]
    width = queries.shape[2]
    half = params.shape[2]
    block_count = params.shape[1]
    blocks = (block_count - 8) // 2
    cores = lax.axis_size("tensor")
    images = all_images // cores
    keys = memory.shape[1] // all_images
    padded = -(-valid // 16) * 16
    rows = images * padded
    groups = width // SLAB
    stack = GROUP * padded
    core = lax.axis_index("tensor")

    def const(shape, *index):
        return pl.BlockSpec(shape, lambda *_: index)

    total_shape = jax.ShapeDtypeStruct((images * groups, 8, stack), F32)
    low_rows = jax.ShapeDtypeStruct((rows, width), BF)
    full_rows = jax.ShapeDtypeStruct((rows, width), F32)
    small_shape = jax.ShapeDtypeStruct((24, width), F32)
    one_block = jax.ShapeDtypeStruct((width, width), BF)
    small_spec = const((24, width), 0, 0)
    row_spec = const(row_bias.shape, 0, 0, 0)
    gain_spec = const(norm_gain.shape, 0, 0)
    head_spec = const((16, width), 0, 0)
    rows_spec = const((rows, width), 0, 0)

    parts = 4
    part_blocks = block_count // 2
    raw_spec = const((None, *queries.shape[1:]), 0, 0, 0)
    (
        weights, head_rows, tokens, own_cotangent, qkv, self_mixed, self_total, first_sum,
        cross_query,
    ) = pl.pallas_call(
        functools.partial(start_kernel, images, valid),
        grid=(2 * parts,),
        out_shape=(
            jax.ShapeDtypeStruct((block_count, width, cores * half), BF),
            jax.ShapeDtypeStruct((16, cores * half), BF),
            low_rows, low_rows,
            jax.ShapeDtypeStruct((3, rows, width), BF), low_rows, total_shape, full_rows, low_rows,
        ),
        in_specs=[
            pl.BlockSpec((width // parts, part_blocks, half), lambda s: (s % parts, s // parts, 0)),
            const((8, half), 0, 0), raw_spec, raw_spec, row_spec, gain_spec,
        ],
        out_specs=(
            any_spec(), head_spec, rows_spec, rows_spec,
            const((3, rows, width), 0, 0, 0), rows_spec, const(total_shape.shape, 0, 0, 0),
            rows_spec, rows_spec,
        ),
        scratch_shapes=[
            pltpu.VMEM((part_blocks, width, cores * half), BF),
            pltpu.VMEM((part_blocks, width, half), BF),
            pltpu.VMEM((16, half), BF),
            pltpu.VMEM((16, cores * half), BF),
            pltpu.SemaphoreType.DMA((2 * parts + 1,)),
            pltpu.SemaphoreType.DMA((2 * parts + 1,)),
            pltpu.SemaphoreType.DMA((2 * parts,)),
            pltpu.SemaphoreType.DMA(()),
        ],
        compiler_params=params_for(collective_id=0, has_side_effects=True),
        name="start",
    )(params, head_bias, queries, cotangent, row_bias, norm_gain)

    def own_image(i, g):
        return 0, lax.axis_index("tensor") * images + i, 0

    context_all = pl.BlockSpec((None, keys, width), own_image)
    slab_q = pl.BlockSpec((padded, SLAB), lambda i, g: (i, g))
    slab_k = pl.BlockSpec((keys, SLAB), lambda i, g: (i, g))
    slab_t = pl.BlockSpec((1, 8, stack), lambda i, g: (i * groups + g, 0, 0))
    image_q = pl.BlockSpec((padded, width), lambda i: (i, 0))
    image_k = pl.BlockSpec((keys, width), lambda i: (i, 0))

    def slab_w(block):
        return pl.BlockSpec((1, width, SLAB), lambda i, g: (block, 0, g))

    key_rows = jax.ShapeDtypeStruct((images * keys, width), BF)
    key_slabs = jax.ShapeDtypeStruct((groups, images * keys, SLAB), BF)
    keys_act, values_act, cross_mixed, cross_total = pl.pallas_call(
        cross_kernel,
        grid=(images,),
        in_specs=[
            pl.BlockSpec((None, keys, width), lambda i: own_image(i, 0)),
            image_q, const((1, width, width), 5, 0, 0), const((1, width, width), 6, 0, 0), head_spec,
        ],
        out_specs=(
            image_k, image_k, image_q, pl.BlockSpec((groups, 8, stack), lambda i: (i, 0, 0)),
        ),
        out_shape=(key_rows, key_rows, low_rows, total_shape),
        compiler_params=params_for(),
        name="cross_forward",
    )(memory, cross_query, weights, weights, head_rows)

    per = 2 if blocks % 2 == 0 else 1
    block_rows, left, right, mixed_grad, second_grad, ffn_small = pl.pallas_call(
        functools.partial(ffn_kernel, images, blocks, per),
        grid=(2 * blocks // per,),
        out_shape=(
            low_rows,
            jax.ShapeDtypeStruct((3, width, rows), BF),
            jax.ShapeDtypeStruct((2 * blocks + 1, rows, width), BF),
            low_rows, full_rows, small_shape,
        ),
        in_specs=[
            rows_spec, rows_spec, rows_spec,
            const(matches.shape, 0, 0, 0),
            pl.BlockSpec(memory_space=pltpu.SMEM),
            const((1, width, width), 7, 0, 0),
            any_spec(), head_spec, row_spec, gain_spec,
        ],
        out_specs=(rows_spec, any_spec(), any_spec(), rows_spec, rows_spec, small_spec),
        scratch_shapes=[
            pltpu.VMEM((rows, width), F32),
            pltpu.VMEM((rows, width), BF),
            pltpu.VMEM((3, width, rows), BF),
            pltpu.VMEM((2 * blocks, rows, width), BF),
            pltpu.VMEM((blocks, rows, width), F32),
            pltpu.VMEM((rows, width), F32),
            pltpu.VMEM((rows, width), F32),
            pltpu.VMEM((8, width), F32),
            pltpu.VMEM((2, blocks, width, width), BF),
            pltpu.SemaphoreType.DMA((3,)),
            pltpu.SemaphoreType.DMA((2 * blocks + 1,)),
            pltpu.SemaphoreType.DMA((2, blocks // per)),
        ],
        compiler_params=params_for(),
        name="ffn",
    )(
        first_sum, cross_mixed, own_cotangent, matches, counts, weights, weights, head_rows, row_bias,
        norm_gain,
    )

    depth, tasks = lax.axis_size("dp"), lax.axis_size("task")
    by_chain = depth == 4 and tasks == 4 and cores == 2

    if by_chain:
        block_order = [*range(8, block_count), 7, 5, 6, 4, 3, 0, 1, 2]
        chain_rows = width // depth
        pair_rows = 8 * len(pairs_of(tasks))
        dma = pltpu.SemaphoreType.DMA
        last = images * groups - 1

        def at_step(make):
            def index_map(step):
                now = jnp.minimum(step, last)
                return make(now // groups, now - groups * (now // groups))

            return index_map

        def product(step):
            return jnp.minimum(step, 2 * blocks)

        def once(shape):
            return pl.BlockSpec(
                shape, lambda step: (0,) * len(shape), pipeline_mode=pl.Buffered(1)
            )

        step_q = pl.BlockSpec((padded, SLAB), at_step(lambda i, g: (i, g)))
        step_k = pl.BlockSpec((keys, SLAB), at_step(lambda i, g: (i, g)))

        small_half = pltpu.VMEM((24, half), F32)
        (
            context_grad, token_grad, update_parts, small_out, gram_rows, block_far, *_,
        ) = pl.pallas_call(
            functools.partial(
                back_kernel, depth, tasks, images, groups, valid, block_order
            ),
            grid=(images * groups + 1,),
            out_shape=(
                key_rows, low_rows,
                jax.ShapeDtypeStruct((block_count, chain_rows, half), BF),
                small_shape,
                jax.ShapeDtypeStruct((16, 128), F32),
                low_rows,
                key_slabs, key_slabs,
            ),
            in_specs=[
                pl.BlockSpec(memory_space=pltpu.SMEM),
                any_spec(), step_q, step_k, step_k,
                pl.BlockSpec((1, 8, stack), at_step(lambda i, g: (i * groups + g, 0, 0))),
                step_q, step_q,
                once((rows, width)), once(row_bias.shape), once(norm_gain.shape),
                once((3, rows, width)), once((rows, width)), once(total_shape.shape),
                once((rows, width)), once((rows, width)), once((24, width)),
                any_spec(), any_spec(),
                pl.BlockSpec((1, width, rows), lambda step: (product(step) // blocks, 0, 0)),
                pl.BlockSpec((1, rows, width), lambda step: (product(step), 0, 0)),
            ],
            out_specs=(
                any_spec(), once((rows, width)), any_spec(), once((24, width)), once((16, 128)),
                *[any_spec()] * 3,
            ),
            scratch_shapes=[
                pltpu.VMEM((keys, width), BF),
                pltpu.VMEM((width, keys), BF),
                pltpu.VMEM((width, width), F32),
                pltpu.VMEM((width, width), F32),
                pltpu.VMEM((rows, width), BF),
                pltpu.VMEM((rows, width), BF),
                pltpu.VMEM((3, rows, width), BF),
                pltpu.VMEM((5, width, width), BF),
                dma((2,)),
                dma((2,)),
                dma(()),
                *ContextGrad.scratch(keys, width),
                *Chain.scratch(block_count, chain_rows, half, tasks),
                pltpu.VMEM((24, width), F32),
                small_half, small_half, small_half, small_half,
                pltpu.VMEM((tasks, 24, half), F32),
                pltpu.VMEM((2, 24, half), F32),
                pltpu.VMEM((pair_rows, half), F32),
                pltpu.VMEM((2 * tasks, 16, 128), F32),
                pltpu.VMEM((2, 16, 128), F32),
                pltpu.VMEM((block_count, chain_rows, half), BF),
                dma((2,)),
                dma((2,)),
                dma((2, tasks - 1)),
                dma((2, depth - 1)),
                dma((2,)),
                dma((2, 2 * tasks - 1)),
                dma((2, 2, depth - 1)),
                dma((2, GROUPS)),
                dma((2, GROUPS, tasks - 1)),
                dma((GROUPS,)),
            ],
            compiler_params=params_for(collective_id=1, has_side_effects=True),
            name="backward",
        )(
            task_order, memory, cross_query, keys_act, values_act, cross_total, mixed_grad,
            cross_mixed, tokens, row_bias, norm_gain, qkv, self_mixed, self_total, first_sum,
            second_grad, ffn_small, weights, block_rows, left, right,
        )
        tile = chain_rows // images
        (
            param_update, memory_grad, query_grad, block_out, head_update, row_update, gain_update,
            gram,
        ) = pl.pallas_call(
            functools.partial(spread_kernel, images, valid, tasks, block_order),
            grid=(images,),
            out_shape=(
                jax.ShapeDtypeStruct((chain_rows, block_count, half), F32),
                key_rows,
                jax.ShapeDtypeStruct((images * valid, width), BF),
                jax.ShapeDtypeStruct((all_images * valid, width), BF),
                jax.ShapeDtypeStruct((8, half), F32),
                jax.ShapeDtypeStruct((3, 2, width), F32),
                jax.ShapeDtypeStruct((3, width), F32),
                jax.ShapeDtypeStruct((tasks, tasks), F32),
            ),
            in_specs=[
                pl.BlockSpec((block_count, tile, half), lambda r: (0, r, 0)),
                pl.BlockSpec((keys, width), lambda r: (r, 0)),
                rows_spec, rows_spec, rows_spec, small_spec, const((16, 128), 0, 0),
            ],
            out_specs=(
                pl.BlockSpec((tile, block_count, half), lambda r: (r, 0, 0)),
                pl.BlockSpec((keys, width), lambda r: (r, 0)),
                const((images * valid, width), 0, 0),
                const((all_images * valid, width), 0, 0),
                const((8, half), 0, 0), const((3, 2, width), 0, 0, 0),
                const((3, width), 0, 0), const((tasks, tasks), 0, 0),
            ),
            compiler_params=params_for(),
            name="spread",
        )(update_parts, context_grad, token_grad, block_rows, block_far, small_out, gram_rows)
        return (
            block_out[None], query_grad[None], memory_grad[None], param_update, head_update,
            row_update, gain_update, gram,
        )

    def unpad(array):
        return array.reshape(images, padded, width)[:, :valid].reshape(1, images * valid, width)

    block_out = lax.all_gather(unpad(block_rows), "tensor", axis=1, tiled=True)
    cross_query_grad, context_grad, key_wg, value_wg, cross_small = pl.pallas_call(
        cross_back_kernel,
        grid=(images, groups),
        in_specs=[
            context_all, slab_q, slab_k, slab_k, slab_t, slab_q, slab_q, slab_w(5), slab_w(6),
        ],
        out_specs=(
            slab_q,
            pl.BlockSpec((keys, width), lambda i, g: (i, 0)),
            const((width, width), 0, 0), const((width, width), 0, 0), small_spec,
        ),
        scratch_shapes=[
            pltpu.VMEM((width, keys), BF),
            pltpu.VMEM((keys, width), F32),
            pltpu.VMEM((width, width), F32),
            pltpu.VMEM((width, width), F32),
            pltpu.VMEM((keys, SLAB), BF),
            pltpu.VMEM((keys, SLAB), BF),
        ],
        out_shape=(low_rows, key_rows, one_block, one_block, small_shape),
        compiler_params=params_for(),
        name="cross_backward",
    )(
        memory, cross_query, keys_act, values_act, cross_total, mixed_grad, cross_mixed, weights,
        weights,
    )

    token_grad, self_wg, self_small = pl.pallas_call(
        functools.partial(self_back_kernel, images, valid),
        grid=(1,),
        out_shape=(
            low_rows, jax.ShapeDtypeStruct((5, width, width), BF), small_shape,
        ),
        in_specs=[
            rows_spec, const((5, width, width), 0, 0, 0), row_spec, gain_spec,
            const((3, rows, width), 0, 0, 0), rows_spec, const(total_shape.shape, 0, 0, 0),
            rows_spec, rows_spec, rows_spec,
        ],
        out_specs=(
            rows_spec, const((5, width, width), 0, 0, 0), small_spec,
        ),
        scratch_shapes=[pltpu.VMEM((3, rows, width), BF), pltpu.VMEM((rows, width), BF)],
        compiler_params=params_for(),
        name="self_backward",
    )(
        tokens, weights, row_bias, norm_gain, qkv, self_mixed, self_total, first_sum, second_grad,
        cross_query_grad,
    )

    query_grad = unpad(token_grad)
    memory_grad = context_grad[None]

    small = self_small + cross_small + ffn_small
    product = functools.partial(jnp.einsum, "dr,jre->jde", preferred_element_type=F32)
    grad_in = product(left[0], right[:blocks]).astype(BF)
    grad_out = product(left[1], right[blocks : 2 * blocks]).astype(BF)
    cross_out_wg = product(left[2], right[2 * blocks :])[0].astype(BF)
    grads = jnp.concatenate(
        [self_wg, jnp.stack([key_wg, value_wg, cross_out_wg]), grad_in, grad_out], axis=0
    )
    swap = [(0, 1), (1, 0)]
    grads = (
        grads[:, :, :half].astype(F32) + lax.ppermute(grads[:, :, half:], "tensor", swap).astype(F32)
    ).astype(BF)
    head_small = small[:8, :half] + lax.ppermute(small[:8, half:], "tensor", swap)
    row_small = lax.psum(small[8:17], ("dp", "tensor"))
    head_small = lax.psum(head_small, "dp")
    shard = lax.psum_scatter(grads, "dp", scatter_dimension=1, tiled=True)
    all_shards = lax.all_gather(shard, "task", axis=0, tiled=False)
    all_head = lax.all_gather(head_small, "task", axis=0, tiled=False)
    all_row = lax.all_gather(row_small, "task", axis=0, tiled=False)
    tasks = all_shards.shape[0]
    share_rows = shard.shape[1]
    sums = pl.pallas_call(
        gram_kernel,
        grid=(block_count,),
        out_shape=jax.ShapeDtypeStruct((tasks * tasks, half), F32),
        in_specs=[pl.BlockSpec((tasks, 1, share_rows, half), lambda k: (0, k, 0, 0))],
        out_specs=const((tasks * tasks, half), 0, 0),
        compiler_params=params_for(),
        name="gram",
    )(all_shards)
    upper = jnp.sum(sums, axis=1).reshape(tasks, tasks)
    gram_weights = upper + upper.T - jnp.diag(jnp.diag(upper))
    gram_weights = lax.psum(gram_weights, ("dp", "tensor"))
    gram_heads = jnp.einsum("axy,bxy->ab", all_head, all_head, precision=highest)
    gram_heads = lax.psum(gram_heads, "tensor")
    gram = gram_weights + gram_heads + jnp.einsum(
        "axy,bxy->ab", all_row, all_row, precision=highest
    )
    task_weights = combine_weights(gram, task_order)
    tile = 64 if share_rows % 64 == 0 else share_rows
    param_update = pl.pallas_call(
        update_kernel,
        grid=(share_rows // tile,),
        out_shape=jax.ShapeDtypeStruct((share_rows, block_count, half), F32),
        in_specs=[
            pl.BlockSpec(memory_space=pltpu.SMEM),
            pl.BlockSpec((tasks, block_count, tile, half), lambda r: (0, 0, r, 0)),
        ],
        out_specs=pl.BlockSpec((tile, block_count, half), lambda r: (r, 0, 0)),
        compiler_params=params_for(),
        name="update",
    )(task_weights, all_shards)
    head_bias_update = jnp.einsum("a,axy->xy", task_weights, all_head, precision=highest)
    row_update = jnp.einsum("a,axy->xy", task_weights, all_row, precision=highest)
    return (
        block_out, query_grad, memory_grad, param_update, head_bias_update,
        row_update[:6].reshape(3, 2, width), row_update[6:9], gram,
    )


def solution(mesh):
    return jax.shard_map(
        body,
        mesh=mesh,
        in_specs=(
            P("task", "dp", None),
            P("task", "dp", None),
            P("task", "dp", None),
            P("task", "dp", None),
            P("task", "dp"),
            P(),
            P(None, None, "tensor"),
            P(None, "tensor"),
            P(),
            P(),
        ),
        out_specs=(
            P("task", "dp", None),
            P("task", ("dp", "tensor"), None),
            P("task", ("dp", "tensor"), None),
            P("dp", None, "tensor"),
            P(None, "tensor"),
            P(),
            P(),
            P(),
        ),
        check_vma=False,
    )
```

```python
import functools

import jax
import jax.numpy as jnp
from jax import lax
from jax.experimental import pallas as pl
from jax.experimental.pallas import tpu as pltpu
from jax.sharding import PartitionSpec as P

HD = 64
GROUP = 4
SLAB = GROUP * HD
BF = jnp.bfloat16
F32 = jnp.float32
MESH_ID = pl.DeviceIdType.MESH
highest = lax.Precision.HIGHEST
VMEM_LIMIT = 63 * 2**20


def combine_weights(gram_matrix, order_list):
    task_count = gram_matrix.shape[0]
    task_index = jnp.arange(task_count, dtype=jnp.int32)
    summed = jnp.zeros((task_count,), F32)
    for own_task in range(task_count):
        coeffs = (task_index == own_task).astype(F32)
        for position in range(task_count):
            chosen = (task_index == order_list[position]).astype(F32)
            column = jnp.sum(gram_matrix * chosen[None, :], axis=1)
            inner_dot = jnp.sum(coeffs * column)
            square = jnp.sum(chosen * column)
            others = (order_list[position] != own_task).astype(F32)
            coeffs = coeffs - others * jnp.minimum(inner_dot, 0.0) / (square + 1e-06) * chosen
        summed = summed + coeffs
    return summed


def mm(a, b):
    return jnp.dot(a, b, preferred_element_type=F32)


def mm_nt(a, b):
    return lax.dot_general(a, b, (((1,), (1,)), ((), ())), preferred_element_type=F32)


def mm_tn(a, b):
    return lax.dot_general(a, b, (((0,), (0,)), ((), ())), preferred_element_type=F32)


def row_of(row_ref, which):
    return row_ref[which // 2, which % 2 : which % 2 + 1].astype(F32)


def gain_of(gain_ref, which):
    return gain_ref[which : which + 1].astype(F32)


def norm_parts(residual):
    row_mean = jnp.mean(residual, axis=-1, keepdims=True)
    centred = residual - row_mean
    variance = jnp.mean(centred * centred, axis=-1, keepdims=True)
    scale = lax.rsqrt(variance + 1e-05)
    return centred * scale, scale


def norm_back(normed, scale, gain_row, grad):
    scaled = grad * gain_row
    first = jnp.mean(scaled, axis=-1, keepdims=True)
    second = jnp.mean(scaled * normed, axis=-1, keepdims=True)
    return scale * (scaled - first - normed * second)


def rows_sum(value):
    return jnp.sum(value, axis=0, keepdims=True)


def gelu_tanh(hidden):
    square = hidden * hidden
    tanh = jnp.tanh(hidden * (0.7978845608028654 + 0.7978845608028654 * 0.044715 * square))
    half = 0.5 * (1.0 + tanh)
    inner = 0.7978845608028654 + 0.7978845608028654 * 3 * 0.044715 * square
    return hidden * half, half + 0.5 * hidden * (1.0 - tanh * tanh) * inner


def head_mask(head, rows, dtype):
    lane = lax.broadcasted_iota(jnp.int32, (rows, SLAB), 1)
    return (lane // HD == head).astype(F32).astype(dtype)


def stack_heads(slab):
    return jnp.concatenate(
        [slab * head_mask(head, slab.shape[0], slab.dtype) for head in range(GROUP)], axis=0
    )


def unstack_heads(stacked):
    rows = stacked.shape[0] // GROUP
    total = None
    for head in range(GROUP):
        part = stacked[head * rows : (head + 1) * rows] * head_mask(head, rows, stacked.dtype)
        total = part if total is None else total + part
    return total


def scores_of(query_stack, key_slab, valid):
    scores = mm_nt(key_slab, query_stack)
    if valid < key_slab.shape[0]:
        row = lax.broadcasted_iota(jnp.int32, scores.shape, 0)
        scores = jnp.where(row < valid, scores, -1e30)
    return scores


def attend(query_slab, key_slab, value_slab, valid):
    scores = scores_of(stack_heads(query_slab * HD ** (-0.5)), key_slab, valid)
    row_max = jnp.max(scores, axis=0, keepdims=True)
    exps = jnp.exp(scores - row_max)
    total = jnp.sum(exps, axis=0, keepdims=True)
    probs = (exps * (1.0 / total)).astype(BF)
    mixed = unstack_heads(mm_tn(value_slab, probs).T)
    return mixed, row_max + jnp.log(total)


def attend_back(query_slab, key_slab, value_slab, log_total, grad_slab, valid):
    query_stack = stack_heads(query_slab * HD ** (-0.5))
    grad_stack = stack_heads(grad_slab)
    probs = jnp.exp(scores_of(query_stack, key_slab, valid) - log_total)
    grad_value = mm(probs.astype(BF), grad_stack)
    grad_probs = mm_nt(value_slab, grad_stack)
    inner = jnp.sum(probs * grad_probs, axis=0, keepdims=True)
    grad_scores = (probs * (grad_probs - inner)).astype(BF)
    grad_key = mm(grad_scores, query_stack)
    grad_query = unstack_heads(mm_tn(key_slab, grad_scores).T) * HD ** (-0.5)
    return grad_query.astype(BF), grad_key.astype(BF), grad_value.astype(BF)


KEY_TILE = 1200


def attend_back_tiles(
    query_slab, key_ref, value_ref, log_total, grad_slab, mixed_slab, key_grad_ref, value_grad_ref
):
    query_stack = stack_heads(query_slab * HD ** (-0.5))
    grad_stack = stack_heads(grad_slab)
    product = stack_heads(grad_slab.astype(F32) * mixed_slab.astype(F32))
    high = product.astype(BF)
    low = (product - high.astype(F32)).astype(BF)
    ones = jnp.ones((8, SLAB), BF)
    inner = (mm_nt(ones, high) + mm_nt(ones, low))[0:1]
    keys = key_ref.shape[0]
    size = KEY_TILE if keys % KEY_TILE == 0 else keys

    def tile(index, grad_query):
        rows = pl.ds(pl.multiple_of(index * size, size), size)
        key, value = key_ref[rows], value_ref[rows]
        probs = jnp.exp(mm_nt(key, query_stack) - log_total)
        grad_scores = (probs * (mm_nt(value, grad_stack) - inner)).astype(BF)
        value_grad_ref[rows] = mm(probs.astype(BF), grad_stack).astype(BF)
        key_grad_ref[rows] = mm(grad_scores, query_stack).astype(BF)
        return grad_query + mm_tn(key, grad_scores)

    grad_query = lax.fori_loop(
        0, keys // size, tile, jnp.zeros((SLAB, query_stack.shape[0]), F32)
    )
    return (unstack_heads(grad_query.T) * HD ** (-0.5)).astype(BF)


def pad_rows(source_ref, target_ref, images, valid):
    first = lax.axis_index("tensor") == 0
    padded = target_ref.shape[0] // images
    for image in range(images):
        here, there = (
            source_ref[(core * images + image) * valid : (core * images + image + 1) * valid]
            for core in range(2)
        )
        rows = jnp.where(first, here.astype(F32), there.astype(F32))
        fill = jnp.zeros((padded - valid, rows.shape[1]), F32)
        target_ref[image * padded : (image + 1) * padded] = jnp.concatenate(
            [rows, fill], axis=0
        ).astype(target_ref.dtype)


def send(source, target, send_sem, recv_sem, **device):
    return pltpu.make_async_remote_copy(
        source, target, send_sem, recv_sem, device_id=device, device_id_type=MESH_ID
    )


def start_kernel(
    images, valid, own_ref, bias_ref, queries_ref, cotangent_ref, row_ref, gain_ref,
    full_ref, head_ref, tokens_ref, own_cotangent_ref, qkv_ref, mixed_ref, total_ref, sum_ref,
    cross_query_ref, first, second, bias_own, bias_all, remote_send, remote_recv, local_sem, far_sem,
):
    step, steps = pl.program_id(0), pl.num_programs(0)
    other = 1 - lax.axis_index("tensor")
    rows, blocks, width = own_ref.shape
    parts = steps // 2
    near, far = pl.ds(0, width), pl.ds(width, width)
    lower, upper = pl.ds(0, blocks), pl.ds(blocks, blocks)

    def rows_of(part):
        return pl.ds(pl.multiple_of(part * rows, rows), rows)

    def first_copies(part):
        at = rows_of(part)
        return (
            send(
                first.at[:, at, near], first.at[:, at, far], remote_send.at[part],
                remote_recv.at[part], tensor=other,
            ),
            pltpu.make_async_copy(
                first.at[:, at, near], full_ref.at[lower, at, near], local_sem.at[part]
            ),
        )

    def second_copies(part):
        at = rows_of(part)
        return (
            send(
                second.at[:, at], full_ref.at[upper, at, far], remote_send.at[parts + part],
                remote_recv.at[parts + part], tensor=other,
            ),
            pltpu.make_async_copy(
                second.at[:, at], full_ref.at[upper, at, near], local_sem.at[parts + part]
            ),
        )

    bias_copy = send(
        bias_own, bias_all.at[:, far], remote_send.at[steps], remote_recv.at[steps], tensor=other
    )
    far_copy = pltpu.make_async_copy(first.at[:, :, far], full_ref.at[lower, :, far], far_sem)

    @pl.when(step == 0)
    def _():
        barrier = pltpu.get_barrier_semaphore()
        pl.semaphore_signal(barrier, inc=1, device_id={"tensor": other}, device_id_type=MESH_ID)
        pl.semaphore_wait(barrier, 1)
        bias_own[...] = jnp.zeros_like(bias_own)
        bias_own[0 : bias_ref.shape[0]] = bias_ref[...]
        bias_copy.start()
        bias_all[:, near] = bias_own[...]

    @pl.when(step < parts)
    def _():
        first[:, rows_of(step), near] = jnp.swapaxes(own_ref[...], 0, 1)
        for copy in first_copies(step):
            copy.start()

    @pl.when(step >= parts)
    def _():
        second[:, rows_of(step - parts)] = jnp.swapaxes(own_ref[...], 0, 1)
        for copy in second_copies(step - parts):
            copy.start()

    @pl.when(step == steps - 1)
    def _():
        pad_rows(queries_ref, tokens_ref, images, valid)
        pad_rows(cotangent_ref, own_cotangent_ref, images, valid)
        bias_copy.wait()
        head_ref[...] = bias_all[...]
        for part in range(parts):
            first_copies(part)[0].wait_recv()
        far_copy.start()
        self_forward(
            images, valid, tokens_ref, first, head_ref, row_ref, gain_ref, qkv_ref, mixed_ref,
            total_ref, sum_ref, cross_query_ref,
        )
        far_copy.wait()
        for part in range(parts):
            remote, local = first_copies(part)
            remote.wait_send()
            local.wait()
            for copy in second_copies(part):
                copy.wait()


def any_spec():
    return pl.BlockSpec(memory_space=pl.ANY)


def whole_spec():
    return pl.BlockSpec(memory_space=pltpu.VMEM)


def params_for(**keys):
    return pltpu.CompilerParams(vmem_limit_bytes=VMEM_LIMIT, **keys)


def place_of(index, groups, rows):
    image = index // groups
    group = index - image * groups
    if isinstance(index, int):
        return pl.ds(image * rows, rows), pl.ds(group * SLAB, SLAB)
    return (
        pl.ds(pl.multiple_of(image * rows, rows), rows),
        pl.ds(pl.multiple_of(group * SLAB, SLAB), SLAB),
    )


def self_forward(images, valid, tokens_ref, weight_ref, head_ref, row_ref, gain_ref, qkv_ref,
                 mixed_ref, total_ref, sum_ref, cross_query_ref):
    tokens = tokens_ref[...]
    rows = tokens.shape[0] // images
    width = tokens.shape[1]
    qkv_ref[0] = (mm(tokens, weight_ref[0]) + head_ref[0:1].astype(F32)).astype(BF)
    qkv_ref[1] = mm(tokens, weight_ref[1]).astype(BF)
    qkv_ref[2] = (mm(tokens, weight_ref[2]) + head_ref[1:2].astype(F32)).astype(BF)
    groups = width // SLAB

    for index in range(images * groups):
        at, lanes = place_of(index, groups, rows)
        mixed, log_total = attend(
            qkv_ref[0, at, lanes], qkv_ref[1, at, lanes], qkv_ref[2, at, lanes], valid
        )
        mixed_ref[at, lanes] = mixed.astype(BF)
        total_ref[index] = jnp.broadcast_to(log_total, total_ref.shape[1:])
    first_sum = tokens.astype(F32) + mm_nt(mixed_ref[...], weight_ref[3]) + row_of(row_ref, 0)
    sum_ref[...] = first_sum
    first_low = (norm_parts(first_sum)[0] * gain_of(gain_ref, 0) + row_of(row_ref, 1)).astype(BF)
    cross_query_ref[...] = (mm(first_low, weight_ref[4]) + head_ref[2:3].astype(F32)).astype(BF)


def cross_kernel(context_ref, query_ref, key_w_ref, value_w_ref, head_ref, key_ref, value_ref,
                 mixed_ref, total_ref):
    context = context_ref[...]
    for group in range(key_ref.shape[1] // SLAB):
        lanes = slice(group * SLAB, (group + 1) * SLAB)
        key_ref[:, lanes] = mm(context, key_w_ref[0, :, lanes]).astype(BF)
        value_ref[:, lanes] = (
            mm(context, value_w_ref[0, :, lanes]) + head_ref[3:4, lanes].astype(F32)
        ).astype(BF)
        mixed, log_total = attend(
            query_ref[:, lanes], key_ref[:, lanes], value_ref[:, lanes], key_ref.shape[0]
        )
        mixed_ref[:, lanes] = mixed.astype(BF)
        total_ref[group] = jnp.broadcast_to(log_total, total_ref.shape[1:])


def ffn_kernel(
    images, blocks, per, sum_ref, mixed_ref, cotangent_ref, matches_ref, counts_ref, cross_w_ref,
    weight_ref, head_ref, row_ref, gain_ref,
    block_ref, left_ref, right_ref, mixed_grad_ref, residual_ref, small_ref,
    second_sum, second_low, left, right, slope, branch, third_grad, hidden_bias, weights, left_sem,
    right_sem, weight_sem,
):
    step = pl.program_id(0)
    half_steps = blocks // per

    def weight_copies(first):
        at = pl.ds(first, per)
        return [
            pltpu.make_async_copy(
                weight_ref.at[pl.ds(8 + which * blocks + first, per)], weights.at[which, at],
                weight_sem.at[which, first // per],
            )
            for which in range(2)
        ]
    rows = sum_ref.shape[0] // images

    def left_copy(which):
        return pltpu.make_async_copy(left.at[which], left_ref.at[which], left_sem.at[which])

    def right_copy(which):
        return pltpu.make_async_copy(right.at[which], right_ref.at[which], right_sem.at[which])

    mixed_copy = pltpu.make_async_copy(
        mixed_ref, right_ref.at[2 * blocks], right_sem.at[2 * blocks]
    )

    @pl.when(step == 0)
    def _():
        for copy in weight_copies(0):
            copy.start()
        mixed_copy.start()
        first_out = norm_parts(sum_ref[...])[0] * gain_of(gain_ref, 0) + row_of(row_ref, 1)
        second = first_out + mm_nt(mixed_ref[...], cross_w_ref[0]) + row_of(row_ref, 2)
        second_sum[...] = second
        second_low[...] = (
            norm_parts(second)[0] * gain_of(gain_ref, 1) + row_of(row_ref, 3)
        ).astype(BF)
        branch[...] = jnp.zeros_like(branch)
        small_ref[...] = jnp.zeros_like(small_ref)
        hidden_bias[0:blocks] = head_ref[4 : 4 + blocks].astype(F32)
        left[0] = second_low[...].T
        left_copy(0).start()

    @pl.when(step < half_steps)
    def _():
        low = second_low[...]
        first = step * per
        copies = weight_copies(first)
        copies[0].wait()
        copies[1].wait()

        @pl.when(step + 1 < half_steps)
        def _():
            for copy in weight_copies(first + per):
                copy.start()

        pres = [
            mm(low, weights[0, first + k]) + hidden_bias[pl.ds(first + k, 1)] for k in range(per)
        ]
        total = branch[...]
        for k in range(per):
            act, grad = gelu_tanh(pres[k])
            act = act.astype(BF)
            slope[first + k] = grad
            right[blocks + first + k] = act
            right_copy(blocks + first + k).start()
            total = total + mm_nt(act, weights[1, first + k])
        branch[...] = total

    @pl.when(step == half_steps - 1)
    def _():
        second = norm_parts(second_sum[...])[0] * gain_of(gain_ref, 1) + row_of(row_ref, 3)
        third_sum = second + branch[...] + row_of(row_ref, 4)
        normed, scale = norm_parts(third_sum)
        block_ref[...] = (normed * gain_of(gain_ref, 2) + row_of(row_ref, 5)).astype(BF)
        count = matches_ref.shape[2]
        slot = lax.broadcasted_iota(jnp.int32, (rows, count), 0)
        box = lax.broadcasted_iota(jnp.int32, (rows, count), 1)
        grads = []
        for image in range(images):
            own = lax.axis_index("tensor") * images + image
            live = (matches_ref[own] == slot) & (box < counts_ref[0, own])
            mask = jnp.sum(jnp.where(live, 1.0, 0.0), axis=1, keepdims=True)
            cot = cotangent_ref[image * rows : (image + 1) * rows].astype(F32)
            grads.append(cot * mask)
        out_grad = jnp.concatenate(grads, axis=0)
        grad = norm_back(normed, scale, gain_of(gain_ref, 2), out_grad)
        third_grad[...] = grad
        left[1] = grad.astype(BF).T
        left_copy(1).start()
        small_ref[12:13] = rows_sum(grad)
        small_ref[13:14] = rows_sum(out_grad)
        small_ref[16:17] = rows_sum(out_grad * normed)
        branch[...] = jnp.zeros_like(branch)

    @pl.when(step >= half_steps)
    def _():
        ffn_low = third_grad[...].astype(BF)
        first = (step - half_steps) * per
        grads = [mm(ffn_low, weights[1, first + k]) for k in range(per)]
        total = branch[...]
        for k in range(per):
            grad_low = (grads[k] * slope[first + k]).astype(BF)
            right[first + k] = grad_low
            right_copy(first + k).start()
            small_ref[pl.ds(4 + first + k, 1)] = rows_sum(grad_low.astype(F32))
            total = total + mm_nt(grad_low, weights[0, first + k])
        branch[...] = total

    @pl.when(step == 2 * half_steps - 1)
    def _():
        second_in = third_grad[...] + branch[...]
        normed, scale = norm_parts(second_sum[...])
        grad = norm_back(normed, scale, gain_of(gain_ref, 1), second_in)
        residual_ref[...] = grad
        small_ref[10:11] = rows_sum(grad)
        small_ref[11:12] = rows_sum(second_in)
        small_ref[15:16] = rows_sum(second_in * normed)
        cross_low = grad.astype(BF)
        left[2] = cross_low.T
        left_copy(2).start()
        mixed_grad_ref[...] = mm(cross_low, cross_w_ref[0]).astype(BF)
        mixed_copy.wait()
        for which in range(3):
            left_copy(which).wait()
        for which in range(2 * blocks):
            right_copy(which).wait()


def cross_back_step(
    image, group, query_ref, key_ref, value_ref, total_ref, mixed_grad_ref, mixed_ref, small_ref,
    context_t, key_acc, value_acc, key_grad_ref, value_grad_ref, unit,
):
    grad_query = attend_back_tiles(
        query_ref[...], key_ref, value_ref, total_ref[0, 0:1], mixed_grad_ref[...], mixed_ref[...],
        key_grad_ref, value_grad_ref,
    )
    grad_key, grad_value = key_grad_ref[...], value_grad_ref[...]
    lanes = pl.ds(pl.multiple_of(group * SLAB, SLAB), SLAB)
    small_ref[2:3, lanes] += rows_sum(grad_query.astype(F32))
    small_ref[3:4, lanes] += rows_sum(grad_value.astype(F32))
    unit(0)
    key_wg = mm(context_t[...], grad_key)
    value_wg = mm(context_t[...], grad_value)

    @pl.when(image == 0)
    def _():
        key_acc[:, lanes] = key_wg
        value_acc[:, lanes] = value_wg

    @pl.when(image > 0)
    def _():
        key_acc[:, lanes] += key_wg
        value_acc[:, lanes] += value_wg

    unit(1)
    return grad_query


def cross_back_kernel(
    context_ref, query_ref, key_ref, value_ref, total_ref, mixed_grad_ref, mixed_ref, key_w_ref,
    value_w_ref, query_grad_ref, context_grad_ref, key_wg_ref, value_wg_ref, small_ref,
    context_t, acc, key_acc, value_acc, key_grad, value_grad,
):
    image, group = pl.program_id(0), pl.program_id(1)
    images, groups = pl.num_programs(0), pl.num_programs(1)

    @pl.when((image == 0) & (group == 0))
    def _():
        small_ref[...] = jnp.zeros_like(small_ref)

    @pl.when(group == 0)
    def _():
        context_t[...] = context_ref[...].T

    query_grad_ref[...] = cross_back_step(
        image, group, query_ref, key_ref, value_ref, total_ref, mixed_grad_ref, mixed_ref,
        small_ref, context_t, key_acc, value_acc, key_grad, value_grad, lambda part: None,
    )
    context_part = mm_nt(key_grad[...], key_w_ref[0]) + mm_nt(value_grad[...], value_w_ref[0])

    @pl.when(group == 0)
    def _():
        acc[...] = context_part

    @pl.when(group > 0)
    def _():
        acc[...] += context_part

    @pl.when(group == groups - 1)
    def _():
        context_grad_ref[...] = acc[...].astype(BF)

    @pl.when((image == images - 1) & (group == groups - 1))
    def _():
        key_wg_ref[...] = key_acc[...].astype(BF)
        value_wg_ref[...] = value_acc[...].astype(BF)


def self_back(
    images, valid, tokens_ref, weight_ref, row_ref, gain_ref, qkv_ref, mixed_ref, total_ref, sum_ref,
    residual_ref, cross_query_grad_ref, mixed_grad_ref, small_ref, qkv_grad, emit, unit, loop_unit,
    used,
):
    tokens = tokens_ref[...]
    rows = tokens.shape[0] // images
    width = tokens.shape[1]
    normed, scale = norm_parts(sum_ref[...])
    first_low = (normed * gain_of(gain_ref, 0) + row_of(row_ref, 1)).astype(BF)
    cross_query_grad = cross_query_grad_ref[...]
    first_low_t = first_low.T
    emit(4, lambda lanes: mm(first_low_t, cross_query_grad_ref[:, lanes]))
    unit()
    first_in = residual_ref[...] + mm_nt(cross_query_grad, weight_ref[4])
    first_grad = norm_back(normed, scale, gain_of(gain_ref, 0), first_in)
    small_ref[8:9] = rows_sum(first_grad)
    small_ref[9:10] = rows_sum(first_in)
    small_ref[14:15] = rows_sum(first_in * normed)
    self_low = first_grad.astype(BF)
    self_low_t = self_low.T
    emit(3, lambda lanes: mm(self_low_t, mixed_ref[:, lanes]))
    unit()
    mixed_grad_ref[...] = mm(self_low, weight_ref[3]).astype(BF)
    used()
    groups = width // SLAB

    def one(index, carry):
        at, lanes = place_of(index, groups, rows)
        grads = attend_back(
            qkv_ref[0, at, lanes], qkv_ref[1, at, lanes], qkv_ref[2, at, lanes],
            total_ref[index, 0:1], mixed_grad_ref[at, lanes], valid,
        )
        for which in range(3):
            qkv_grad[which, at, lanes] = grads[which]
        loop_unit(index)
        return carry

    lax.fori_loop(0, images * groups, one, 0)
    tokens_t = tokens.T
    total = first_grad
    for which in range(3):
        grad = qkv_grad[which]
        emit(which, lambda lanes, which=which: mm(tokens_t, qkv_grad[which, :, lanes]))
        if which != 1:
            unit()
        total = total + mm_nt(grad, weight_ref[which])
    small_ref[0:1] = rows_sum(qkv_grad[0].astype(F32))
    small_ref[1:2] = rows_sum(qkv_grad[2].astype(F32))
    return total


def self_back_kernel(
    images, valid, tokens_ref, weight_ref, row_ref, gain_ref, qkv_ref, mixed_ref, total_ref, sum_ref,
    residual_ref, cross_query_grad_ref, query_grad_ref, wg_ref, small_ref, qkv_grad, mixed_grad,
):
    small_ref[...] = jnp.zeros_like(small_ref)

    def emit(block, value):
        for lane in range(0, wg_ref.shape[2], SLAB):
            lanes = slice(lane, lane + SLAB)
            wg_ref[block, :, lanes] = value(lanes).astype(BF)

    query_grad_ref[...] = self_back(
        images, valid, tokens_ref, weight_ref, row_ref, gain_ref, qkv_ref, mixed_ref, total_ref,
        sum_ref, residual_ref, cross_query_grad_ref, mixed_grad, small_ref, qkv_grad, emit,
        lambda: None, lambda index: None, lambda: None,
    ).astype(BF)


def task_peers(tasks):
    me = lax.axis_index("task")
    return [lax.rem(me + shift, tasks) for shift in range(1, tasks)]


def task_senders(tasks):
    me = lax.axis_index("task")
    return [lax.rem(me + tasks - shift, tasks) for shift in range(1, tasks)]


def greet(depth, tasks):
    me = lax.axis_index("dp")
    barrier = pltpu.get_barrier_semaphore()
    other = 1 - lax.axis_index("tensor")
    for peer in task_peers(tasks):
        pl.semaphore_signal(barrier, inc=1, device_id={"task": peer}, device_id_type=MESH_ID)
        pl.semaphore_signal(
            barrier, inc=1, device_id={"task": peer, "tensor": other}, device_id_type=MESH_ID
        )
    for shift in range(1, depth):
        pl.semaphore_signal(
            barrier, inc=1, device_id={"dp": lax.rem(me + shift, depth)}, device_id_type=MESH_ID
        )
    pl.semaphore_signal(barrier, inc=1, device_id={"tensor": other}, device_id_type=MESH_ID)
    pl.semaphore_wait(barrier, 2 * (tasks - 1) + depth)


LAG = 2
SLOTS = 3
STAGES = 2


class Chain:
    def __init__(self, depth, tasks, refs):
        self.depth, self.tasks = depth, tasks
        (self.near, self.far, self.stage, self.passed, self.parts,
         self.far_send, self.far_recv, self.far_free, self.pass_send, self.pass_recv,
         self.part_send, self.part_recv) = refs
        self.chunks = self.passed.shape[1]
        self.rows, self.half = self.passed.shape[2:]
        self.me = lax.axis_index("dp")
        self.task = lax.axis_index("task")
        self.is_end = (self.me == 0) | (self.me == depth - 1)

    SCRATCH = 12

    @staticmethod
    def scratch(blocks, rows, half, tasks):
        chunks = 2 * blocks
        dma = pltpu.SemaphoreType.DMA
        return [
            pltpu.VMEM((2, chunks, rows, half), BF),
            pltpu.VMEM((SLOTS, 2, 2, rows, half), BF),
            pltpu.VMEM((STAGES, 2, 2, rows, half), BF),
            pltpu.VMEM((2, chunks, rows, half), BF),
            pltpu.VMEM((tasks, chunks, rows // tasks, half), BF),
            dma((STAGES,)),
            dma((SLOTS,)),
            pltpu.SemaphoreType.REGULAR,
            dma((2, chunks)),
            dma((2, chunks)),
            dma((blocks, tasks - 1)),
            dma((blocks, tasks - 1)),
        ]

    def far_copy(self, block):
        slot, stage = lax.rem(block, SLOTS), lax.rem(block, STAGES)
        return send(
            self.stage.at[stage], self.far.at[slot], self.far_send.at[stage], self.far_recv.at[slot],
            tensor=1 - lax.axis_index("tensor"),
        )

    def emit(self, block, value):
        block = jnp.int32(block)
        stage = lax.rem(block, STAGES)

        @pl.when(block >= STAGES)
        def _():
            self.far_copy(block).wait_send()

        @pl.when(block >= SLOTS)
        def _():
            pl.semaphore_wait(self.far_free, 1)

        def place(low, target):
            for way in range(2):
                for part in range(2):
                    row = (2 * way + part) * self.rows
                    target(way, part, low[row : row + self.rows])

        def slab(start):
            low = value(slice(start, start + SLAB)).astype(BF)
            own = max(min(self.half - start, SLAB), 0)
            if own:

                def keep(way, part, rows):
                    self.near[way, 2 * block + part, :, start : start + own] = rows

                place(low[:, :own], keep)
            if own < SLAB:
                first = start + own - self.half

                def give(way, part, rows):
                    self.stage[stage, way, part, :, first : first + SLAB - own] = rows

                place(low[:, own:], give)

        starts = range(0, 2 * self.half, SLAB)
        for start in starts:
            if start + SLAB > self.half:
                slab(start)
        self.far_copy(block).start()
        for start in starts:
            if start + SLAB <= self.half:
                slab(start)

    def absorb(self, block):
        block = jnp.int32(block)
        slot = lax.rem(block, SLOTS)
        self.far_copy(block).wait_recv()
        for way in range(2):
            chunks = pl.ds(2 * block, 2)
            self.near[way, chunks] = self.near[way, chunks] + self.far[slot, way]

        @pl.when(block < self.chunks // 2 - SLOTS)
        def _():
            pl.semaphore_signal(
                self.far_free, inc=1, device_id={"tensor": 1 - lax.axis_index("tensor")},
                device_id_type=MESH_ID,
            )

    def pass_copy(self, way, chunk):
        piece = self.passed.at[way, chunk]
        target = self.me - 1 if way == 0 else self.me + 1
        return send(
            piece, piece, self.pass_send.at[way, chunk], self.pass_recv.at[way, chunk], dp=target
        )

    def part_rows(self, peer):
        size = self.rows // self.tasks
        return pl.ds(pl.multiple_of(peer * size, size), size)

    def part_copy(self, way, block, shift, peer):
        chunks = pl.ds(2 * block, 2)
        return send(
            self.passed.at[way, chunks, self.part_rows(peer)], self.parts.at[self.task, chunks],
            self.part_send.at[block, shift], self.part_recv.at[block, shift], task=peer,
        )

    def hops(self, way):
        return self.depth - 1 - self.me if way == 0 else self.me

    def units(self):
        return self.chunks + LAG * (self.depth - 1)

    def unit(self, index):
        for way in range(2):
            chunk = index - LAG * self.hops(way)

            @pl.when((chunk >= 0) & (chunk < self.chunks))
            def _(way=way, chunk=chunk):
                self.chunk_step(way, chunk)

    def chunk_step(self, way, chunk):
        first, last = self.hops(way) == 0, self.hops(way) == self.depth - 1
        block = chunk // 2
        own = self.near[way, chunk]

        @pl.when(first)
        def _():
            self.passed[way, chunk] = own

        @pl.when(jnp.logical_not(first))
        def _():
            self.pass_copy(way, chunk).wait_recv()
            self.passed[way, chunk] = own + self.passed[way, chunk]

        @pl.when(jnp.logical_not(last))
        def _():
            self.pass_copy(way, chunk).start()

        @pl.when(last & (chunk == 2 * block + 1))
        def _():
            for shift, peer in enumerate(task_peers(self.tasks)):
                self.part_copy(way, block, shift, peer).start()
            own_rows = self.part_rows(self.task)
            self.parts[self.task, chunk - 1] = self.passed[way, chunk - 1, own_rows]
            self.parts[self.task, chunk] = self.passed[way, chunk, own_rows]

    def wait_parts(self, block):
        for shift, peer in enumerate(task_senders(self.tasks)):
            landed = self.parts.at[peer, pl.ds(2 * block, 2)]
            send(
                landed, landed, self.part_send.at[block, shift], self.part_recv.at[block, shift],
                task=peer,
            ).wait_recv()

    def finish(self):
        def blocks(block, carry):
            for way in range(2):

                @pl.when(self.hops(way) != self.depth - 1)
                def _(way=way):
                    for part in range(2):
                        self.pass_copy(way, 2 * block + part).wait_send()

                @pl.when(self.hops(way) == self.depth - 1)
                def _(way=way):
                    for shift, peer in enumerate(task_peers(self.tasks)):
                        self.part_copy(way, block, shift, peer).wait_send()

            return carry

        lax.fori_loop(0, self.chunks // 2, blocks, 0)


def pairs_of(tasks):
    return [(a, b) for a in range(tasks) for b in range(a, tasks)]


def weights_of(gram, order_ref, tasks):
    totals = [0.0] * tasks
    for own in range(tasks):
        coeffs = [jnp.full_like(gram[0, 0], 1.0 if t == own else 0.0) for t in range(tasks)]
        for position in range(tasks):
            chosen = [
                jnp.where(order_ref[position] == t, 1.0, 0.0).astype(F32) for t in range(tasks)
            ]
            column = [sum(gram[t, j] * chosen[j] for j in range(tasks)) for t in range(tasks)]
            inner = sum(coeffs[t] * column[t] for t in range(tasks))
            square = sum(chosen[t] * column[t] for t in range(tasks))
            others = 1.0 - chosen[own]
            share = others * jnp.minimum(inner, 0.0) / (square + 1e-06)
            coeffs = [coeffs[t] - share * chosen[t] for t in range(tasks)]
        totals = [total + coeff for total, coeff in zip(totals, coeffs)]
    return totals


GROUPS = 8
UNITS = 2
TILE = 240


class ContextGrad:
    def __init__(self, key_grad, value_grad, weights, result, refs):
        self.grads, self.weights, self.result = (key_grad, value_grad), weights, result
        (self.staged, self.ring, self.done, self.staged_sem, self.ring_sem, self.done_sem) = refs
        self.tile = self.done.shape[1]
        self.tiles = result.shape[0] // self.tile

    SCRATCH = 6

    @staticmethod
    def scratch(keys, width):
        dma = pltpu.SemaphoreType.DMA
        return [
            pltpu.VMEM((2, keys, SLAB), BF),
            pltpu.VMEM((2, 2, width // SLAB, TILE, SLAB), BF),
            pltpu.VMEM((2, TILE, width), BF),
            dma((2,)),
            dma((2, 2)),
            dma((2,)),
        ]

    def staged_copies(self, image, group):
        keys = self.staged.shape[1]
        rows = pl.ds(pl.multiple_of(image * keys, keys), keys)
        return [
            pltpu.make_async_copy(
                self.staged.at[which], self.grads[which].at[group, rows], self.staged_sem.at[which]
            )
            for which in range(2)
        ]

    def put(self, image, group):
        for copy in self.staged_copies(image, group):
            copy.start()

    def settle(self):
        for copy in self.staged_copies(0, 0):
            copy.wait()

    def fetches(self, index):
        slot = lax.rem(index, 2)
        rows = pl.ds(pl.multiple_of(index * self.tile, self.tile), self.tile)
        return [
            pltpu.make_async_copy(
                self.grads[which].at[:, rows], self.ring.at[slot, which],
                self.ring_sem.at[slot, which],
            )
            for which in range(2)
        ]

    def store(self, index):
        slot = lax.rem(index, 2)
        rows = pl.ds(pl.multiple_of(index * self.tile, self.tile), self.tile)
        return pltpu.make_async_copy(
            self.done.at[slot], self.result.at[rows], self.done_sem.at[slot]
        )

    def compute(self, index):
        @pl.when(index < self.tiles)
        def _():
            for copy in self.fetches(index):
                copy.wait()

            @pl.when(index + 1 < self.tiles)
            def _():
                for copy in self.fetches(index + 1):
                    copy.start()

            @pl.when(index >= 2)
            def _():
                self.store(index - 2).wait()

            slot = lax.rem(index, 2)
            parts = [
                jnp.concatenate(
                    [self.ring[slot, which, group] for group in range(self.ring.shape[2])], axis=1
                )
                for which in range(2)
            ]
            total = mm_nt(parts[0], self.weights[0]) + mm_nt(parts[1], self.weights[1])
            self.done[slot] = total.astype(BF)
            self.store(index).start()

    def finish(self):
        for index in range(self.tiles - 2, self.tiles):
            self.store(jnp.int32(index)).wait()


def back_kernel(
    depth, tasks, images, groups, valid, block_order, order_ref, context_ref, query_ref, key_ref,
    value_ref, total_ref, mixed_grad_ref, cross_mixed_ref, tokens_ref, row_ref, gain_ref, qkv_ref,
    mixed_ref, self_total_ref, sum_ref, residual_ref, small_in_ref, all_w_ref, block_ref, left_ref, right_ref,
    *refs
):
    (
        context_grad_ref, query_grad_ref, update_ref, small_out_ref, gram_ref, block_far,
        key_grad, value_grad,
    ), refs = refs[:8], refs[8:]
    (
        context, context_t, key_acc, value_acc, cross_query_grad, self_mixed_grad, qkv_grad, weights,
        block_sem, weight_sem, context_sem,
    ), refs = refs[:11], refs[11:]
    context_back = ContextGrad(
        key_grad, value_grad, weights.at[pl.ds(3, 2)], context_grad_ref,
        refs[: ContextGrad.SCRATCH],
    )
    refs = refs[ContextGrad.SCRATCH :]
    chain = Chain(depth, tasks, refs[: Chain.SCRATCH])
    refs = refs[Chain.SCRATCH :]
    gram_acc = refs[7]
    step = pl.program_id(0)
    cross_steps = images * groups
    half = chain.half
    is_end = chain.is_end
    pairs = pairs_of(tasks)

    block_copy = send(
        block_ref, block_far, block_sem.at[0], block_sem.at[1], tensor=1 - lax.axis_index("tensor")
    )
    weight_copies = [
        pltpu.make_async_copy(all_w_ref.at[source], weights.at[target], weight_sem.at[index])
        for index, (source, target) in enumerate(
            [(pl.ds(0, 5), pl.ds(0, 5)), (pl.ds(5, 2), pl.ds(3, 2))]
        )
    ]

    def context_copy(image):
        keys = context.shape[0]
        own = lax.axis_index("tensor") * images + image
        rows = pl.ds(pl.multiple_of(own * keys, keys), keys)
        return pltpu.make_async_copy(context_ref.at[0, rows], context, context_sem)

    @pl.when(step == 0)
    def _():
        context_copy(0).start()
        weight_copies[0].start()
        greet(depth, tasks)
        block_copy.start()
        gram_acc[...] = jnp.zeros_like(gram_acc)
        refs[0][...] = small_in_ref[...]

    @pl.when(step < cross_steps)
    def _():
        image = step // groups
        group = step - image * groups

        chain.emit(step, lambda lanes: mm(left_ref[0], right_ref[0, :, lanes]))

        @pl.when(group == 0)
        def _():
            context_copy(image).wait()
            context_t[...] = context[...].T

            @pl.when(image + 1 < images)
            def _():
                context_copy(image + 1).start()

        def cross_unit(part):
            if part == 0:
                context_back.put(image, group)
                chain.absorb(step)
            chain.unit(step * UNITS + part)

        @pl.when(step > 0)
        def _():
            context_back.settle()

        grad_query = cross_back_step(
            image, group, query_ref, key_ref, value_ref, total_ref, mixed_grad_ref, cross_mixed_ref,
            refs[0], context_t, key_acc, value_acc, context_back.staged.at[0],
            context_back.staged.at[1], cross_unit,
        )
        rows = grad_query.shape[0]
        cross_query_grad[
            pl.ds(pl.multiple_of(image * rows, rows), rows),
            pl.ds(pl.multiple_of(group * SLAB, SLAB), SLAB),
        ] = grad_query

        @pl.when(step == cross_steps - 1)
        def _():
            chain.emit(cross_steps, lambda lanes: key_acc[:, lanes])
            chain.emit(cross_steps + 1, lambda lanes: value_acc[:, lanes])

    @pl.when(step == cross_steps)
    def _():
        done = [cross_steps * UNITS]
        blocks = len(block_order)

        def self_unit():
            if done[0] % 2 == 0:
                chain.absorb(done[0] // 2)
            chain.unit(jnp.int32(done[0]))
            done[0] += 1

        in_loop = images * groups // 2

        def loop_unit(index):
            now = cross_steps * UNITS + 2 + index // 2

            @pl.when(index % 2 == 1)
            def _():
                @pl.when(now % 2 == 0)
                def _():
                    chain.absorb(now // 2)

                chain.unit(now)

        def used():
            done[0] += in_loop
            weight_copies[1].start()

        context_back.settle()
        for copy in context_back.fetches(jnp.int32(0)):
            copy.start()
        weight_copies[0].wait()
        query_grad_ref[...] = self_back(
            images, valid, tokens_ref, weights, row_ref, gain_ref, qkv_ref, mixed_ref,
            self_total_ref, sum_ref, residual_ref, cross_query_grad, self_mixed_grad, refs[0],
            qkv_grad, lambda block, value: chain.emit(block_order.index(block), value), self_unit,
            loop_unit, used,
        ).astype(BF)
        for block in range(-(-done[0] // 2), blocks):
            chain.absorb(block)
        weight_copies[1].wait()
        rest(
            chain, context_back, done[0], order_ref, update_ref, small_out_ref, gram_ref, refs
        )
        for block in range(blocks - STAGES, blocks):
            chain.far_copy(jnp.int32(block)).wait_send()
        block_copy.wait()
        context_back.finish()


def rest(
    chain, context_back, done, order_ref, update_ref, small_out_ref, gram_ref, refs
):
    (
        small, small_own, small_other, small_far, small_pass, small_all, small_both, gram_acc,
        gram_plane, gram_end, out,
        small_far_sem, small_pass_sem, small_task_sem, small_dp_sem, small_core_sem,
        gram_plane_sem, gram_dp_sem, hop_sem, out_sem, update_sem,
    ) = refs
    depth, tasks, half = chain.depth, chain.tasks, chain.half
    me, task, core = (lax.axis_index(axis) for axis in ("dp", "task", "tensor"))
    is_end = chain.is_end
    top = me == 0
    pairs = pairs_of(tasks)
    own_lanes = pl.ds(pl.multiple_of(core * half, half), half)
    other_lanes = pl.ds(pl.multiple_of((1 - core) * half, half), half)
    small_own[0:8] = small[0:8, 0:half]
    small_own[8:] = small[8:, own_lanes]
    small_other[0:8] = small[0:8, half:]
    small_other[8:] = small[8:, other_lanes]
    small_copy = send(
        small_other, small_far, small_far_sem.at[0], small_far_sem.at[1], tensor=1 - core
    )
    small_copy.start()

    def small_hop():
        return send(
            small_pass, small_pass, small_pass_sem.at[0], small_pass_sem.at[1], dp=me - 1
        )

    def small_task_copy(shift, peer):
        return send(
            small_pass, small_all.at[task], small_task_sem.at[0, shift],
            small_task_sem.at[1, shift], task=peer,
        )

    def add_products(shares):
        for index, (a, b) in enumerate(pairs):
            product = shares[a] * shares[b]
            total = product[0:8]
            for row in range(8, product.shape[0], 8):
                total = total + product[row : row + 8]
            gram_acc[index * 8 : index * 8 + 8] += total

    blocks = chain.chunks // 2
    late = LAG * (depth - 1) + 3

    def products_of(block):
        @pl.when((block >= 0) & (block < blocks))
        def _():
            chain.wait_parts(block)

            def part(which, carry):
                add_products(
                    [chain.parts[t, 2 * block + which].astype(F32) for t in range(tasks)]
                )
                return carry

            lax.fori_loop(0, 2, part, 0)

    def step(index, carry):
        chain.unit(index)
        context_back.compute(index - done)
        since = index - late

        @pl.when(is_end)
        def _():
            early = (done - late) // 2 + 1
            products_of(jnp.where(index - done < early, index - done, -1))
            products_of(jnp.where(since == 2 * (since // 2), since // 2, -1))

        @pl.when(index == done + 1 + LAG * chain.hops(0))
        def _():
            small_copy.wait_recv()
            total = small_own[...] + small_far[...]

            @pl.when(me == depth - 1)
            def _():
                small_pass[...] = total

            @pl.when(me < depth - 1)
            def _():
                small_hop().wait_recv()
                small_pass[...] += total

            @pl.when(me > 0)
            def _():
                small_hop().start()

            @pl.when(top)
            def _():
                for shift, peer in enumerate(task_peers(tasks)):
                    small_task_copy(shift, peer).start()
                small_all[task] = small_pass[...]

        return carry

    lax.fori_loop(done, max(chain.units() + 2, done + context_back.tiles), step, 0)

    @pl.when(top)
    def _():
        for shift, peer in enumerate(task_senders(tasks)):
            landed = small_all.at[peer]
            send(
                landed, landed, small_task_sem.at[0, shift], small_task_sem.at[1, shift], task=peer
            ).wait_recv()

    lanes = gram_plane.shape[2]
    plane = 2 * tasks
    mine = 2 * task + core

    def gram_copy(shift):
        to = lax.rem(mine + shift, plane)
        return send(
            gram_plane.at[mine], gram_plane.at[mine], gram_plane_sem.at[0, shift - 1],
            gram_plane_sem.at[1, shift - 1], task=to // 2, tensor=lax.rem(to, 2),
        )

    def gram_arrival(shift):
        place = lax.rem(mine + plane - shift, plane)
        return send(
            gram_plane.at[place], gram_plane.at[place], gram_plane_sem.at[0, shift - 1],
            gram_plane_sem.at[1, shift - 1], task=place // 2, tensor=lax.rem(place, 2),
        )

    def gram_dp_copy(end, shift):
        return send(
            gram_end.at[end], gram_end.at[end], gram_dp_sem.at[0, end, shift],
            gram_dp_sem.at[1, end, shift], dp=lax.rem((depth - 1) * end + shift + 1, depth),
        )

    def one_number(values):
        return jnp.sum(jnp.sum(values, axis=0, keepdims=True), axis=1, keepdims=True)

    @pl.when(top & (task == 0))
    def _():
        small_values = [small_all[t] for t in range(tasks)]
        for index, (a, b) in enumerate(pairs):
            product = small_values[a] * small_values[b]
            gram_acc[index * 8 : index * 8 + 8] += product[0:8] + product[8:16] + product[16:24]

    @pl.when(is_end)
    def _():
        gram_plane[mine] = jnp.zeros(gram_plane.shape[1:], F32)
        for index in range(len(pairs)):
            gram_plane[mine, index : index + 1] = jnp.broadcast_to(
                one_number(gram_acc[index * 8 : index * 8 + 8]), (1, lanes)
            )
        for shift in range(1, plane):
            gram_copy(shift).start()
        for shift in range(1, plane):
            gram_arrival(shift).wait_recv()

    for end in range(2):

        @pl.when(me == (depth - 1) * end)
        def _(end=end):
            total = gram_plane[0]
            for place in range(1, plane):
                total = total + gram_plane[place]
            gram_end[end] = total
            for shift in range(depth - 1):
                gram_dp_copy(end, shift).start()

    for end in range(2):
        for shift in range(depth - 1):

            @pl.when(me == ((depth - 1) * end + shift + 1) % depth)
            def _(end=end, shift=shift):
                gram_dp_copy(end, shift).wait_recv()

    gram = {}
    for index, (a, b) in enumerate(pairs):
        row = slice(index, index + 1)
        gram[a, b] = gram[b, a] = gram_end[0, row] + gram_end[1, row]
    for a in range(tasks):
        for b in range(tasks):
            gram_ref[a * tasks + b : a * tasks + b + 1] = gram[a, b]
    weights = [
        jnp.concatenate([weight] * (half // lanes), axis=1)
        for weight in weights_of(gram, order_ref, tasks)
    ]

    group = blocks // GROUPS
    share = chain.rows // tasks
    own_share = pl.ds(pl.multiple_of(task * share, share), share)
    own_part = jnp.minimum(me, 1)

    def hop_copy(index):
        return send(
            chain.near.at[1, pl.ds(index * group, group), pl.ds(0, share)],
            out.at[pl.ds(index * group, group), own_share],
            hop_sem.at[0, index], hop_sem.at[1, index],
            dp=jnp.where(top, 1, depth - 2),
        )

    beside = [task + 1 - 2 * lax.rem(task, 2), task + 2 - 4 * (task // 2)]
    across = tasks - 1 - task

    def out_piece(index, owner):
        rows = pl.ds(pl.multiple_of(owner * share, share), share)
        return out.at[pl.ds(index * group, group), rows]

    def out_copy(index, which, owner):
        piece = out_piece(index, owner)
        peer = beside[which] if which < 2 else beside[1 if index < GROUPS // 2 else 0]
        return send(
            piece, piece, out_sem.at[0, index, which], out_sem.at[1, index, which], task=peer
        )

    def update_copy(index):
        at = pl.ds(index * group, group)
        return pltpu.make_async_copy(out.at[at], update_ref.at[at], update_sem.at[index])

    def weighted(chunk):
        total = weights[0] * chain.parts[0, chunk].astype(F32)
        for t in range(1, tasks):
            total = total + weights[t] * chain.parts[t, chunk].astype(F32)
        return total.astype(BF)

    def small_dp_copy(shift):
        return send(
            small_both.at[0], small_both.at[0], small_dp_sem.at[0, shift],
            small_dp_sem.at[1, shift], dp=shift + 1,
        )

    def small_core_copy():
        return send(
            small_both.at[0], small_both.at[1], small_core_sem.at[0], small_core_sem.at[1],
            tensor=1 - core,
        )

    @pl.when(top)
    def _():
        total = weights[0] * small_all[0]
        for t in range(1, tasks):
            total = total + weights[t] * small_all[t]
        small_both[0] = total
        for shift in range(depth - 1):
            small_dp_copy(shift).start()

    @pl.when(is_end)
    def _():
        for index in range(GROUPS):

            def other(block, carry):
                chain.near[1, block, 0:share] = weighted(2 * block + 1 - own_part)
                return carry

            lax.fori_loop(index * group, (index + 1) * group, other, 0)
            hop_copy(index).start()

            def own(block, carry):
                out[block, own_share] = weighted(2 * block + own_part)
                return carry

            lax.fori_loop(index * group, (index + 1) * group, own, 0)
            for which in range(2):
                out_copy(index, which, task).start()

    @pl.when(jnp.logical_not(is_end))
    def _():
        for index in range(GROUPS):
            hop_copy(index).wait_recv()
            for which in range(2):
                out_copy(index, which, task).start()

    for shift in range(depth - 1):

        @pl.when(me == shift + 1)
        def _(shift=shift):
            small_dp_copy(shift).wait_recv()

    small_core_copy().start()

    for index in range(GROUPS):
        for which in range(2):
            out_copy(index, which, beside[which]).wait_recv()
        out_copy(index, 2, beside[0 if index < GROUPS // 2 else 1]).start()
    for index in range(GROUPS):
        out_copy(index, 2, across).wait_recv()
        update_copy(index).start()

    small_core_copy().wait_recv()
    small_out_ref[0:8, 0:half] = small_both[0, 0:8]
    small_out_ref[0:8, half:] = small_both[1, 0:8]
    small_out_ref[8:, own_lanes] = small_both[0, 8:]
    small_out_ref[8:, other_lanes] = small_both[1, 8:]

    small_copy.wait_send()
    small_core_copy().wait_send()
    chain.finish()

    @pl.when(me > 0)
    def _():
        small_hop().wait_send()

    @pl.when(top)
    def _():
        for shift, peer in enumerate(task_peers(tasks)):
            small_task_copy(shift, peer).wait_send()
        for shift in range(depth - 1):
            small_dp_copy(shift).wait_send()

    for end in range(2):

        @pl.when(me == (depth - 1) * end)
        def _(end=end):
            for shift in range(depth - 1):
                gram_dp_copy(end, shift).wait_send()

    @pl.when(is_end)
    def _():
        for shift in range(1, plane):
            gram_copy(shift).wait_send()
        for index in range(GROUPS):
            hop_copy(index).wait_send()

    for index in range(GROUPS):
        update_copy(index).wait()
        for which in range(3):
            out_copy(index, which, task).wait_send()


def spread_kernel(
    images, valid, tasks, block_order, parts_ref, context_grad_ref, query_grad_ref, block_ref,
    block_far_ref, small_ref, gram_in_ref,
    update_ref, context_out_ref, query_out_ref, block_out_ref, head_ref, row_ref, gain_ref, gram_ref,
):
    ordered = [parts_ref[block_order.index(block)] for block in range(len(block_order))]
    update_ref[...] = jnp.swapaxes(jnp.stack(ordered), 0, 1).astype(F32)
    context_out_ref[...] = context_grad_ref[...]

    @pl.when(pl.program_id(0) == 0)
    def _():
        padded = query_grad_ref.shape[0] // images
        first = lax.axis_index("tensor") == 0

        def rows(ref, image):
            return ref[image * padded : (image + 1) * padded].astype(F32)[:valid]

        for image in range(images):
            at = slice(image * valid, (image + 1) * valid)
            after = slice((images + image) * valid, (images + image + 1) * valid)
            query_out_ref[at] = rows(query_grad_ref, image).astype(BF)
            near, far = rows(block_ref, image), rows(block_far_ref, image)
            block_out_ref[at] = jnp.where(first, near, far).astype(BF)
            block_out_ref[after] = jnp.where(first, far, near).astype(BF)
        head_ref[...] = small_ref[0:8, 0 : head_ref.shape[1]]
        for which in range(6):
            row_ref[which // 2, which % 2 : which % 2 + 1] = small_ref[8 + which : 9 + which]
        gain_ref[...] = small_ref[14:17]
        for a in range(tasks):
            for b in range(tasks):
                at = a * tasks + b
                gram_ref[a : a + 1, b : b + 1] = gram_in_ref[at : at + 1, 0:1]


def gram_kernel(parts_ref, gram_ref):
    tasks = parts_ref.shape[0]

    @pl.when(pl.program_id(0) == 0)
    def _():
        gram_ref[...] = jnp.zeros_like(gram_ref)

    shares = [parts_ref[task, 0].astype(F32) for task in range(tasks)]
    for a in range(tasks):
        for b in range(a, tasks):
            gram_ref[a * tasks + b : a * tasks + b + 1] += rows_sum(shares[a] * shares[b])


def update_kernel(weights_ref, parts_ref, update_ref):
    tasks, blocks = parts_ref.shape[:2]
    for block in range(blocks):
        total = weights_ref[0] * parts_ref[0, block].astype(F32)
        for task in range(1, tasks):
            total += weights_ref[task] * parts_ref[task, block].astype(F32)
        update_ref[:, block, :] = total


def body(
    queries, memory, cotangent, matches, counts, task_order, params, head_bias, row_bias, norm_gain
):
    all_images = matches.shape[1]
    valid = matches.shape[2]
    width = queries.shape[2]
    half = params.shape[2]
    block_count = params.shape[1]
    blocks = (block_count - 8) // 2
    cores = lax.axis_size("tensor")
    images = all_images // cores
    keys = memory.shape[1] // all_images
    padded = -(-valid // 16) * 16
    rows = images * padded
    groups = width // SLAB
    stack = GROUP * padded
    core = lax.axis_index("tensor")

    def const(shape, *index):
        return pl.BlockSpec(shape, lambda *_: index)

    total_shape = jax.ShapeDtypeStruct((images * groups, 8, stack), F32)
    low_rows = jax.ShapeDtypeStruct((rows, width), BF)
    full_rows = jax.ShapeDtypeStruct((rows, width), F32)
    small_shape = jax.ShapeDtypeStruct((24, width), F32)
    one_block = jax.ShapeDtypeStruct((width, width), BF)
    small_spec = const((24, width), 0, 0)
    row_spec = const(row_bias.shape, 0, 0, 0)
    gain_spec = const(norm_gain.shape, 0, 0)
    head_spec = const((16, width), 0, 0)
    rows_spec = const((rows, width), 0, 0)

    parts = 4
    part_blocks = block_count // 2
    raw_spec = const((None, *queries.shape[1:]), 0, 0, 0)
    (
        weights, head_rows, tokens, own_cotangent, qkv, self_mixed, self_total, first_sum,
        cross_query,
    ) = pl.pallas_call(
        functools.partial(start_kernel, images, valid),
        grid=(2 * parts,),
        out_shape=(
            jax.ShapeDtypeStruct((block_count, width, cores * half), BF),
            jax.ShapeDtypeStruct((16, cores * half), BF),
            low_rows, low_rows,
            jax.ShapeDtypeStruct((3, rows, width), BF), low_rows, total_shape, full_rows, low_rows,
        ),
        in_specs=[
            pl.BlockSpec((width // parts, part_blocks, half), lambda s: (s % parts, s // parts, 0)),
            const((8, half), 0, 0), raw_spec, raw_spec, row_spec, gain_spec,
        ],
        out_specs=(
            any_spec(), head_spec, rows_spec, rows_spec,
            const((3, rows, width), 0, 0, 0), rows_spec, const(total_shape.shape, 0, 0, 0),
            rows_spec, rows_spec,
        ),
        scratch_shapes=[
            pltpu.VMEM((part_blocks, width, cores * half), BF),
            pltpu.VMEM((part_blocks, width, half), BF),
            pltpu.VMEM((16, half), BF),
            pltpu.VMEM((16, cores * half), BF),
            pltpu.SemaphoreType.DMA((2 * parts + 1,)),
            pltpu.SemaphoreType.DMA((2 * parts + 1,)),
            pltpu.SemaphoreType.DMA((2 * parts,)),
            pltpu.SemaphoreType.DMA(()),
        ],
        compiler_params=params_for(collective_id=0, has_side_effects=True),
        name="start",
    )(params, head_bias, queries, cotangent, row_bias, norm_gain)

    def own_image(i, g):
        return 0, lax.axis_index("tensor") * images + i, 0

    context_all = pl.BlockSpec((None, keys, width), own_image)
    slab_q = pl.BlockSpec((padded, SLAB), lambda i, g: (i, g))
    slab_k = pl.BlockSpec((keys, SLAB), lambda i, g: (i, g))
    slab_t = pl.BlockSpec((1, 8, stack), lambda i, g: (i * groups + g, 0, 0))
    image_q = pl.BlockSpec((padded, width), lambda i: (i, 0))
    image_k = pl.BlockSpec((keys, width), lambda i: (i, 0))

    def slab_w(block):
        return pl.BlockSpec((1, width, SLAB), lambda i, g: (block, 0, g))

    key_rows = jax.ShapeDtypeStruct((images * keys, width), BF)
    key_slabs = jax.ShapeDtypeStruct((groups, images * keys, SLAB), BF)
    keys_act, values_act, cross_mixed, cross_total = pl.pallas_call(
        cross_kernel,
        grid=(images,),
        in_specs=[
            pl.BlockSpec((None, keys, width), lambda i: own_image(i, 0)),
            image_q, const((1, width, width), 5, 0, 0), const((1, width, width), 6, 0, 0), head_spec,
        ],
        out_specs=(
            image_k, image_k, image_q, pl.BlockSpec((groups, 8, stack), lambda i: (i, 0, 0)),
        ),
        out_shape=(key_rows, key_rows, low_rows, total_shape),
        compiler_params=params_for(),
        name="cross_forward",
    )(memory, cross_query, weights, weights, head_rows)

    per = 2 if blocks % 2 == 0 else 1
    block_rows, left, right, mixed_grad, second_grad, ffn_small = pl.pallas_call(
        functools.partial(ffn_kernel, images, blocks, per),
        grid=(2 * blocks // per,),
        out_shape=(
            low_rows,
            jax.ShapeDtypeStruct((3, width, rows), BF),
            jax.ShapeDtypeStruct((2 * blocks + 1, rows, width), BF),
            low_rows, full_rows, small_shape,
        ),
        in_specs=[
            rows_spec, rows_spec, rows_spec,
            const((all_images, 1, valid), 0, 0, 0),
            pl.BlockSpec(memory_space=pltpu.SMEM),
            const((1, width, width), 7, 0, 0),
            any_spec(), head_spec, row_spec, gain_spec,
        ],
        out_specs=(rows_spec, any_spec(), any_spec(), rows_spec, rows_spec, small_spec),
        scratch_shapes=[
            pltpu.VMEM((rows, width), F32),
            pltpu.VMEM((rows, width), BF),
            pltpu.VMEM((3, width, rows), BF),
            pltpu.VMEM((2 * blocks, rows, width), BF),
            pltpu.VMEM((blocks, rows, width), F32),
            pltpu.VMEM((rows, width), F32),
            pltpu.VMEM((rows, width), F32),
            pltpu.VMEM((8, width), F32),
            pltpu.VMEM((2, blocks, width, width), BF),
            pltpu.SemaphoreType.DMA((3,)),
            pltpu.SemaphoreType.DMA((2 * blocks + 1,)),
            pltpu.SemaphoreType.DMA((2, blocks // per)),
        ],
        compiler_params=params_for(),
        name="ffn",
    )(
        first_sum, cross_mixed, own_cotangent, jnp.transpose(matches, (1, 0, 2)), counts, weights, weights, head_rows, row_bias,
        norm_gain,
    )

    depth, tasks = lax.axis_size("dp"), lax.axis_size("task")
    by_chain = depth == 4 and tasks == 4 and cores == 2

    if by_chain:
        block_order = [*range(8, block_count), 7, 5, 6, 4, 3, 0, 1, 2]
        chain_rows = width // depth
        pair_rows = 8 * len(pairs_of(tasks))
        dma = pltpu.SemaphoreType.DMA
        last = images * groups - 1

        def at_step(make):
            def index_map(step):
                now = jnp.minimum(step, last)
                return make(now // groups, now - groups * (now // groups))

            return index_map

        def product(step):
            return jnp.minimum(step, 2 * blocks)

        def once(shape):
            return pl.BlockSpec(
                shape, lambda step: (0,) * len(shape), pipeline_mode=pl.Buffered(1)
            )

        step_q = pl.BlockSpec((padded, SLAB), at_step(lambda i, g: (i, g)))
        step_k = pl.BlockSpec((keys, SLAB), at_step(lambda i, g: (i, g)))

        small_half = pltpu.VMEM((24, half), F32)
        (
            context_grad, token_grad, update_parts, small_out, gram_rows, block_far, *_,
        ) = pl.pallas_call(
            functools.partial(
                back_kernel, depth, tasks, images, groups, valid, block_order
            ),
            grid=(images * groups + 1,),
            out_shape=(
                key_rows, low_rows,
                jax.ShapeDtypeStruct((block_count, chain_rows, half), BF),
                small_shape,
                jax.ShapeDtypeStruct((16, 128), F32),
                low_rows,
                key_slabs, key_slabs,
            ),
            in_specs=[
                pl.BlockSpec(memory_space=pltpu.SMEM),
                any_spec(), step_q, step_k, step_k,
                pl.BlockSpec((1, 8, stack), at_step(lambda i, g: (i * groups + g, 0, 0))),
                step_q, step_q,
                once((rows, width)), once(row_bias.shape), once(norm_gain.shape),
                once((3, rows, width)), once((rows, width)), once(total_shape.shape),
                once((rows, width)), once((rows, width)), once((24, width)),
                any_spec(), any_spec(),
                pl.BlockSpec((1, width, rows), lambda step: (product(step) // blocks, 0, 0)),
                pl.BlockSpec((1, rows, width), lambda step: (product(step), 0, 0)),
            ],
            out_specs=(
                any_spec(), once((rows, width)), any_spec(), once((24, width)), once((16, 128)),
                *[any_spec()] * 3,
            ),
            scratch_shapes=[
                pltpu.VMEM((keys, width), BF),
                pltpu.VMEM((width, keys), BF),
                pltpu.VMEM((width, width), F32),
                pltpu.VMEM((width, width), F32),
                pltpu.VMEM((rows, width), BF),
                pltpu.VMEM((rows, width), BF),
                pltpu.VMEM((3, rows, width), BF),
                pltpu.VMEM((5, width, width), BF),
                dma((2,)),
                dma((2,)),
                dma(()),
                *ContextGrad.scratch(keys, width),
                *Chain.scratch(block_count, chain_rows, half, tasks),
                pltpu.VMEM((24, width), F32),
                small_half, small_half, small_half, small_half,
                pltpu.VMEM((tasks, 24, half), F32),
                pltpu.VMEM((2, 24, half), F32),
                pltpu.VMEM((pair_rows, half), F32),
                pltpu.VMEM((2 * tasks, 16, 128), F32),
                pltpu.VMEM((2, 16, 128), F32),
                pltpu.VMEM((block_count, chain_rows, half), BF),
                dma((2,)),
                dma((2,)),
                dma((2, tasks - 1)),
                dma((2, depth - 1)),
                dma((2,)),
                dma((2, 2 * tasks - 1)),
                dma((2, 2, depth - 1)),
                dma((2, GROUPS)),
                dma((2, GROUPS, tasks - 1)),
                dma((GROUPS,)),
            ],
            compiler_params=params_for(collective_id=1, has_side_effects=True),
            name="backward",
        )(
            task_order, memory, cross_query, keys_act, values_act, cross_total, mixed_grad,
            cross_mixed, tokens, row_bias, norm_gain, qkv, self_mixed, self_total, first_sum,
            second_grad, ffn_small, weights, block_rows, left, right,
        )
        tile = chain_rows // images
        (
            param_update, memory_grad, query_grad, block_out, head_update, row_update, gain_update,
            gram,
        ) = pl.pallas_call(
            functools.partial(spread_kernel, images, valid, tasks, block_order),
            grid=(images,),
            out_shape=(
                jax.ShapeDtypeStruct((chain_rows, block_count, half), F32),
                key_rows,
                jax.ShapeDtypeStruct((images * valid, width), BF),
                jax.ShapeDtypeStruct((all_images * valid, width), BF),
                jax.ShapeDtypeStruct((8, half), F32),
                jax.ShapeDtypeStruct((3, 2, width), F32),
                jax.ShapeDtypeStruct((3, width), F32),
                jax.ShapeDtypeStruct((tasks, tasks), F32),
            ),
            in_specs=[
                pl.BlockSpec((block_count, tile, half), lambda r: (0, r, 0)),
                pl.BlockSpec((keys, width), lambda r: (r, 0)),
                rows_spec, rows_spec, rows_spec, small_spec, const((16, 128), 0, 0),
            ],
            out_specs=(
                pl.BlockSpec((tile, block_count, half), lambda r: (r, 0, 0)),
                pl.BlockSpec((keys, width), lambda r: (r, 0)),
                const((images * valid, width), 0, 0),
                const((all_images * valid, width), 0, 0),
                const((8, half), 0, 0), const((3, 2, width), 0, 0, 0),
                const((3, width), 0, 0), const((tasks, tasks), 0, 0),
            ),
            compiler_params=params_for(),
            name="spread",
        )(update_parts, context_grad, token_grad, block_rows, block_far, small_out, gram_rows)
        return (
            block_out[None], query_grad[None], memory_grad[None], param_update, head_update,
            row_update, gain_update, gram,
        )

    def unpad(array):
        return array.reshape(images, padded, width)[:, :valid].reshape(1, images * valid, width)

    block_out = lax.all_gather(unpad(block_rows), "tensor", axis=1, tiled=True)
    cross_query_grad, context_grad, key_wg, value_wg, cross_small = pl.pallas_call(
        cross_back_kernel,
        grid=(images, groups),
        in_specs=[
            context_all, slab_q, slab_k, slab_k, slab_t, slab_q, slab_q, slab_w(5), slab_w(6),
        ],
        out_specs=(
            slab_q,
            pl.BlockSpec((keys, width), lambda i, g: (i, 0)),
            const((width, width), 0, 0), const((width, width), 0, 0), small_spec,
        ),
        scratch_shapes=[
            pltpu.VMEM((width, keys), BF),
            pltpu.VMEM((keys, width), F32),
            pltpu.VMEM((width, width), F32),
            pltpu.VMEM((width, width), F32),
            pltpu.VMEM((keys, SLAB), BF),
            pltpu.VMEM((keys, SLAB), BF),
        ],
        out_shape=(low_rows, key_rows, one_block, one_block, small_shape),
        compiler_params=params_for(),
        name="cross_backward",
    )(
        memory, cross_query, keys_act, values_act, cross_total, mixed_grad, cross_mixed, weights,
        weights,
    )

    token_grad, self_wg, self_small = pl.pallas_call(
        functools.partial(self_back_kernel, images, valid),
        grid=(1,),
        out_shape=(
            low_rows, jax.ShapeDtypeStruct((5, width, width), BF), small_shape,
        ),
        in_specs=[
            rows_spec, const((5, width, width), 0, 0, 0), row_spec, gain_spec,
            const((3, rows, width), 0, 0, 0), rows_spec, const(total_shape.shape, 0, 0, 0),
            rows_spec, rows_spec, rows_spec,
        ],
        out_specs=(
            rows_spec, const((5, width, width), 0, 0, 0), small_spec,
        ),
        scratch_shapes=[pltpu.VMEM((3, rows, width), BF), pltpu.VMEM((rows, width), BF)],
        compiler_params=params_for(),
        name="self_backward",
    )(
        tokens, weights, row_bias, norm_gain, qkv, self_mixed, self_total, first_sum, second_grad,
        cross_query_grad,
    )

    query_grad = unpad(token_grad)
    memory_grad = context_grad[None]

    small = self_small + cross_small + ffn_small
    product = functools.partial(jnp.einsum, "dr,jre->jde", preferred_element_type=F32)
    grad_in = product(left[0], right[:blocks]).astype(BF)
    grad_out = product(left[1], right[blocks : 2 * blocks]).astype(BF)
    cross_out_wg = product(left[2], right[2 * blocks :])[0].astype(BF)
    grads = jnp.concatenate(
        [self_wg, jnp.stack([key_wg, value_wg, cross_out_wg]), grad_in, grad_out], axis=0
    )
    swap = [(0, 1), (1, 0)]
    grads = (
        grads[:, :, :half].astype(F32) + lax.ppermute(grads[:, :, half:], "tensor", swap).astype(F32)
    ).astype(BF)
    head_small = small[:8, :half] + lax.ppermute(small[:8, half:], "tensor", swap)
    row_small = lax.psum(small[8:17], ("dp", "tensor"))
    head_small = lax.psum(head_small, "dp")
    shard = lax.psum_scatter(grads, "dp", scatter_dimension=1, tiled=True)
    all_shards = lax.all_gather(shard, "task", axis=0, tiled=False)
    all_head = lax.all_gather(head_small, "task", axis=0, tiled=False)
    all_row = lax.all_gather(row_small, "task", axis=0, tiled=False)
    tasks = all_shards.shape[0]
    share_rows = shard.shape[1]
    sums = pl.pallas_call(
        gram_kernel,
        grid=(block_count,),
        out_shape=jax.ShapeDtypeStruct((tasks * tasks, half), F32),
        in_specs=[pl.BlockSpec((tasks, 1, share_rows, half), lambda k: (0, k, 0, 0))],
        out_specs=const((tasks * tasks, half), 0, 0),
        compiler_params=params_for(),
        name="gram",
    )(all_shards)
    upper = jnp.sum(sums, axis=1).reshape(tasks, tasks)
    gram_weights = upper + upper.T - jnp.diag(jnp.diag(upper))
    gram_weights = lax.psum(gram_weights, ("dp", "tensor"))
    gram_heads = jnp.einsum("axy,bxy->ab", all_head, all_head, precision=highest)
    gram_heads = lax.psum(gram_heads, "tensor")
    gram = gram_weights + gram_heads + jnp.einsum(
        "axy,bxy->ab", all_row, all_row, precision=highest
    )
    task_weights = combine_weights(gram, task_order)
    tile = 64 if share_rows % 64 == 0 else share_rows
    param_update = pl.pallas_call(
        update_kernel,
        grid=(share_rows // tile,),
        out_shape=jax.ShapeDtypeStruct((share_rows, block_count, half), F32),
        in_specs=[
            pl.BlockSpec(memory_space=pltpu.SMEM),
            pl.BlockSpec((tasks, block_count, tile, half), lambda r: (0, 0, r, 0)),
        ],
        out_specs=pl.BlockSpec((tile, block_count, half), lambda r: (r, 0, 0)),
        compiler_params=params_for(),
        name="update",
    )(task_weights, all_shards)
    head_bias_update = jnp.einsum("a,axy->xy", task_weights, all_head, precision=highest)
    row_update = jnp.einsum("a,axy->xy", task_weights, all_row, precision=highest)
    return (
        block_out, query_grad, memory_grad, param_update, head_bias_update,
        row_update[:6].reshape(3, 2, width), row_update[6:9], gram,
    )


def solution(mesh):
    return jax.shard_map(
        body,
        mesh=mesh,
        in_specs=(
            P("task", "dp", None),
            P("task", "dp", None),
            P("task", "dp", None),
            P("task", "dp", None),
            P("task", "dp"),
            P(),
            P(None, None, "tensor"),
            P(None, "tensor"),
            P(),
            P(),
        ),
        out_specs=(
            P("task", "dp", None),
            P("task", ("dp", "tensor"), None),
            P("task", ("dp", "tensor"), None),
            P("dp", None, "tensor"),
            P(None, "tensor"),
            P(),
            P(),
            P(),
        ),
        check_vma=False,
    )
```

```python
import functools

import jax
import jax.numpy as jnp
from jax import lax
from jax.experimental import pallas as pl
from jax.experimental.pallas import tpu as pltpu
from jax.sharding import PartitionSpec as P

HD = 64
GROUP = 4
SLAB = GROUP * HD
BF = jnp.bfloat16
F32 = jnp.float32
MESH_ID = pl.DeviceIdType.MESH
highest = lax.Precision.HIGHEST
VMEM_LIMIT = 63 * 2**20


def combine_weights(gram_matrix, order_list):
    task_count = gram_matrix.shape[0]
    task_index = jnp.arange(task_count, dtype=jnp.int32)
    summed = jnp.zeros((task_count,), F32)
    for own_task in range(task_count):
        coeffs = (task_index == own_task).astype(F32)
        for position in range(task_count):
            chosen = (task_index == order_list[position]).astype(F32)
            column = jnp.sum(gram_matrix * chosen[None, :], axis=1)
            inner_dot = jnp.sum(coeffs * column)
            square = jnp.sum(chosen * column)
            others = (order_list[position] != own_task).astype(F32)
            coeffs = coeffs - others * jnp.minimum(inner_dot, 0.0) / (square + 1e-06) * chosen
        summed = summed + coeffs
    return summed


def mm(a, b):
    return jnp.dot(a, b, preferred_element_type=F32)


def mm_nt(a, b):
    return lax.dot_general(a, b, (((1,), (1,)), ((), ())), preferred_element_type=F32)


def mm_tn(a, b):
    return lax.dot_general(a, b, (((0,), (0,)), ((), ())), preferred_element_type=F32)


def row_of(row_ref, which):
    return row_ref[which // 2, which % 2 : which % 2 + 1].astype(F32)


def gain_of(gain_ref, which):
    return gain_ref[which : which + 1].astype(F32)


def norm_parts(residual):
    row_mean = jnp.mean(residual, axis=-1, keepdims=True)
    centred = residual - row_mean
    variance = jnp.mean(centred * centred, axis=-1, keepdims=True)
    scale = lax.rsqrt(variance + 1e-05)
    return centred * scale, scale


def norm_back(normed, scale, gain_row, grad):
    scaled = grad * gain_row
    first = jnp.mean(scaled, axis=-1, keepdims=True)
    second = jnp.mean(scaled * normed, axis=-1, keepdims=True)
    return scale * (scaled - first - normed * second)


def rows_sum(value):
    return jnp.sum(value, axis=0, keepdims=True)


def gelu_tanh(hidden):
    square = hidden * hidden
    tanh = jnp.tanh(hidden * (0.7978845608028654 + 0.7978845608028654 * 0.044715 * square))
    half = 0.5 * (1.0 + tanh)
    inner = 0.7978845608028654 + 0.7978845608028654 * 3 * 0.044715 * square
    return hidden * half, half + 0.5 * hidden * (1.0 - tanh * tanh) * inner


def head_mask(head, rows, dtype):
    lane = lax.broadcasted_iota(jnp.int32, (rows, SLAB), 1)
    return (lane // HD == head).astype(F32).astype(dtype)


def stack_heads(slab):
    return jnp.concatenate(
        [slab * head_mask(head, slab.shape[0], slab.dtype) for head in range(GROUP)], axis=0
    )


def unstack_heads(stacked):
    rows = stacked.shape[0] // GROUP
    total = None
    for head in range(GROUP):
        part = stacked[head * rows : (head + 1) * rows] * head_mask(head, rows, stacked.dtype)
        total = part if total is None else total + part
    return total


def scores_of(query_stack, key_slab, valid):
    scores = mm_nt(key_slab, query_stack)
    if valid < key_slab.shape[0]:
        row = lax.broadcasted_iota(jnp.int32, scores.shape, 0)
        scores = jnp.where(row < valid, scores, -1e30)
    return scores


def attend(query_slab, key_slab, value_slab, valid):
    scores = scores_of(stack_heads(query_slab * HD ** (-0.5)), key_slab, valid)
    row_max = jnp.max(scores, axis=0, keepdims=True)
    exps = jnp.exp(scores - row_max)
    total = jnp.sum(exps, axis=0, keepdims=True)
    probs = (exps * (1.0 / total)).astype(BF)
    mixed = unstack_heads(mm_tn(value_slab, probs).T)
    return mixed, row_max + jnp.log(total)


def attend_back(query_slab, key_slab, value_slab, log_total, grad_slab, valid):
    query_stack = stack_heads(query_slab * HD ** (-0.5))
    grad_stack = stack_heads(grad_slab)
    probs = jnp.exp(scores_of(query_stack, key_slab, valid) - log_total)
    grad_value = mm(probs.astype(BF), grad_stack)
    grad_probs = mm_nt(value_slab, grad_stack)
    inner = jnp.sum(probs * grad_probs, axis=0, keepdims=True)
    grad_scores = (probs * (grad_probs - inner)).astype(BF)
    grad_key = mm(grad_scores, query_stack)
    grad_query = unstack_heads(mm_tn(key_slab, grad_scores).T) * HD ** (-0.5)
    return grad_query.astype(BF), grad_key.astype(BF), grad_value.astype(BF)


KEY_TILE = 1200


def attend_back_tiles(
    query_slab, key_ref, value_ref, log_total, grad_slab, mixed_slab, key_grad_ref, value_grad_ref
):
    query_stack = stack_heads(query_slab * HD ** (-0.5))
    grad_stack = stack_heads(grad_slab)
    product = stack_heads(grad_slab.astype(F32) * mixed_slab.astype(F32))
    high = product.astype(BF)
    low = (product - high.astype(F32)).astype(BF)
    ones = jnp.ones((8, SLAB), BF)
    inner = (mm_nt(ones, high) + mm_nt(ones, low))[0:1]
    keys = key_ref.shape[0]
    size = KEY_TILE if keys % KEY_TILE == 0 else keys

    def tile(index, grad_query):
        rows = pl.ds(pl.multiple_of(index * size, size), size)
        key, value = key_ref[rows], value_ref[rows]
        probs = jnp.exp(mm_nt(key, query_stack) - log_total)
        grad_scores = (probs * (mm_nt(value, grad_stack) - inner)).astype(BF)
        value_grad_ref[rows] = mm(probs.astype(BF), grad_stack).astype(BF)
        key_grad_ref[rows] = mm(grad_scores, query_stack).astype(BF)
        return grad_query + mm_tn(key, grad_scores)

    grad_query = lax.fori_loop(
        0, keys // size, tile, jnp.zeros((SLAB, query_stack.shape[0]), F32)
    )
    return (unstack_heads(grad_query.T) * HD ** (-0.5)).astype(BF)


def pad_rows(source_ref, target_ref, images, valid):
    first = lax.axis_index("tensor") == 0
    padded = target_ref.shape[0] // images
    for image in range(images):
        here, there = (
            source_ref[(core * images + image) * valid : (core * images + image + 1) * valid]
            for core in range(2)
        )
        rows = jnp.where(first, here.astype(F32), there.astype(F32))
        fill = jnp.zeros((padded - valid, rows.shape[1]), F32)
        target_ref[image * padded : (image + 1) * padded] = jnp.concatenate(
            [rows, fill], axis=0
        ).astype(target_ref.dtype)


def send(source, target, send_sem, recv_sem, **device):
    return pltpu.make_async_remote_copy(
        source, target, send_sem, recv_sem, device_id=device, device_id_type=MESH_ID
    )


def start_kernel(
    images, valid, own_ref, bias_ref, queries_ref, cotangent_ref, row_ref, gain_ref,
    full_ref, head_ref, tokens_ref, own_cotangent_ref, qkv_ref, mixed_ref, total_ref, sum_ref,
    cross_query_ref, first, second, bias_own, bias_all, remote_send, remote_recv, local_sem, far_sem,
):
    step, steps = pl.program_id(0), pl.num_programs(0)
    other = 1 - lax.axis_index("tensor")
    rows, blocks, width = own_ref.shape
    parts = steps // 2
    near, far = pl.ds(0, width), pl.ds(width, width)
    lower, upper = pl.ds(0, blocks), pl.ds(blocks, blocks)

    def rows_of(part):
        return pl.ds(pl.multiple_of(part * rows, rows), rows)

    def first_copies(part):
        at = rows_of(part)
        return (
            send(
                first.at[:, at, near], first.at[:, at, far], remote_send.at[part],
                remote_recv.at[part], tensor=other,
            ),
            pltpu.make_async_copy(
                first.at[:, at, near], full_ref.at[lower, at, near], local_sem.at[part]
            ),
        )

    def second_copies(part):
        at = rows_of(part)
        return (
            send(
                second.at[:, at], full_ref.at[upper, at, far], remote_send.at[parts + part],
                remote_recv.at[parts + part], tensor=other,
            ),
            pltpu.make_async_copy(
                second.at[:, at], full_ref.at[upper, at, near], local_sem.at[parts + part]
            ),
        )

    bias_copy = send(
        bias_own, bias_all.at[:, far], remote_send.at[steps], remote_recv.at[steps], tensor=other
    )
    far_copy = pltpu.make_async_copy(first.at[:, :, far], full_ref.at[lower, :, far], far_sem)

    @pl.when(step == 0)
    def _():
        barrier = pltpu.get_barrier_semaphore()
        pl.semaphore_signal(barrier, inc=1, device_id={"tensor": other}, device_id_type=MESH_ID)
        pl.semaphore_wait(barrier, 1)
        bias_own[...] = jnp.zeros_like(bias_own)
        bias_own[0 : bias_ref.shape[0]] = bias_ref[...]
        bias_copy.start()
        bias_all[:, near] = bias_own[...]

    @pl.when(step < parts)
    def _():
        first[:, rows_of(step), near] = jnp.swapaxes(own_ref[...], 0, 1)
        for copy in first_copies(step):
            copy.start()

    @pl.when(step >= parts)
    def _():
        second[:, rows_of(step - parts)] = jnp.swapaxes(own_ref[...], 0, 1)
        for copy in second_copies(step - parts):
            copy.start()

    @pl.when(step == steps - 1)
    def _():
        pad_rows(queries_ref, tokens_ref, images, valid)
        pad_rows(cotangent_ref, own_cotangent_ref, images, valid)
        bias_copy.wait()
        head_ref[...] = bias_all[...]
        for part in range(parts):
            first_copies(part)[0].wait_recv()
        far_copy.start()
        self_forward(
            images, valid, tokens_ref, first, head_ref, row_ref, gain_ref, qkv_ref, mixed_ref,
            total_ref, sum_ref, cross_query_ref,
        )
        far_copy.wait()
        for part in range(parts):
            remote, local = first_copies(part)
            remote.wait_send()
            local.wait()
            for copy in second_copies(part):
                copy.wait()


def any_spec():
    return pl.BlockSpec(memory_space=pl.ANY)


def whole_spec():
    return pl.BlockSpec(memory_space=pltpu.VMEM)


def params_for(**keys):
    return pltpu.CompilerParams(vmem_limit_bytes=VMEM_LIMIT, **keys)


def place_of(index, groups, rows):
    image = index // groups
    group = index - image * groups
    if isinstance(index, int):
        return pl.ds(image * rows, rows), pl.ds(group * SLAB, SLAB)
    return (
        pl.ds(pl.multiple_of(image * rows, rows), rows),
        pl.ds(pl.multiple_of(group * SLAB, SLAB), SLAB),
    )


def self_forward(images, valid, tokens_ref, weight_ref, head_ref, row_ref, gain_ref, qkv_ref,
                 mixed_ref, total_ref, sum_ref, cross_query_ref):
    tokens = tokens_ref[...]
    rows = tokens.shape[0] // images
    width = tokens.shape[1]
    qkv_ref[0] = (mm(tokens, weight_ref[0]) + head_ref[0:1].astype(F32)).astype(BF)
    qkv_ref[1] = mm(tokens, weight_ref[1]).astype(BF)
    qkv_ref[2] = (mm(tokens, weight_ref[2]) + head_ref[1:2].astype(F32)).astype(BF)
    groups = width // SLAB

    for index in range(images * groups):
        at, lanes = place_of(index, groups, rows)
        mixed, log_total = attend(
            qkv_ref[0, at, lanes], qkv_ref[1, at, lanes], qkv_ref[2, at, lanes], valid
        )
        mixed_ref[at, lanes] = mixed.astype(BF)
        total_ref[index] = jnp.broadcast_to(log_total, total_ref.shape[1:])
    first_sum = tokens.astype(F32) + mm_nt(mixed_ref[...], weight_ref[3]) + row_of(row_ref, 0)
    sum_ref[...] = first_sum
    first_low = (norm_parts(first_sum)[0] * gain_of(gain_ref, 0) + row_of(row_ref, 1)).astype(BF)
    cross_query_ref[...] = (mm(first_low, weight_ref[4]) + head_ref[2:3].astype(F32)).astype(BF)


def cross_kernel(context_ref, query_ref, key_w_ref, value_w_ref, head_ref, key_ref, value_ref,
                 mixed_ref, total_ref):
    context = context_ref[...]
    for group in range(key_ref.shape[1] // SLAB):
        lanes = slice(group * SLAB, (group + 1) * SLAB)
        key_ref[:, lanes] = mm(context, key_w_ref[0, :, lanes]).astype(BF)
        value_ref[:, lanes] = (
            mm(context, value_w_ref[0, :, lanes]) + head_ref[3:4, lanes].astype(F32)
        ).astype(BF)
        mixed, log_total = attend(
            query_ref[:, lanes], key_ref[:, lanes], value_ref[:, lanes], key_ref.shape[0]
        )
        mixed_ref[:, lanes] = mixed.astype(BF)
        total_ref[group] = jnp.broadcast_to(log_total, total_ref.shape[1:])


def ffn_kernel(
    images, blocks, per, sum_ref, mixed_ref, cotangent_ref, matches_ref, counts_ref, cross_w_ref,
    weight_ref, head_ref, row_ref, gain_ref,
    block_ref, left_ref, right_ref, mixed_grad_ref, residual_ref, small_ref,
    second_sum, second_low, left, right, slope, branch, third_grad, hidden_bias, weights, left_sem,
    right_sem, weight_sem,
):
    step = pl.program_id(0)
    half_steps = blocks // per

    def weight_copies(first):
        at = pl.ds(first, per)
        return [
            pltpu.make_async_copy(
                weight_ref.at[pl.ds(8 + which * blocks + first, per)], weights.at[which, at],
                weight_sem.at[which, first // per],
            )
            for which in range(2)
        ]
    rows = sum_ref.shape[0] // images

    def left_copy(which):
        return pltpu.make_async_copy(left.at[which], left_ref.at[which], left_sem.at[which])

    def right_copy(which):
        return pltpu.make_async_copy(right.at[which], right_ref.at[which], right_sem.at[which])

    mixed_copy = pltpu.make_async_copy(
        mixed_ref, right_ref.at[2 * blocks], right_sem.at[2 * blocks]
    )

    @pl.when(step == 0)
    def _():
        for copy in weight_copies(0):
            copy.start()
        mixed_copy.start()
        first_out = norm_parts(sum_ref[...])[0] * gain_of(gain_ref, 0) + row_of(row_ref, 1)
        second = first_out + mm_nt(mixed_ref[...], cross_w_ref[0]) + row_of(row_ref, 2)
        second_sum[...] = second
        second_low[...] = (
            norm_parts(second)[0] * gain_of(gain_ref, 1) + row_of(row_ref, 3)
        ).astype(BF)
        branch[...] = jnp.zeros_like(branch)
        small_ref[...] = jnp.zeros_like(small_ref)
        hidden_bias[0:blocks] = head_ref[4 : 4 + blocks].astype(F32)
        left[0] = second_low[...].T
        left_copy(0).start()

    @pl.when(step < half_steps)
    def _():
        low = second_low[...]
        first = step * per
        copies = weight_copies(first)
        copies[0].wait()
        copies[1].wait()

        @pl.when(step + 1 < half_steps)
        def _():
            for copy in weight_copies(first + per):
                copy.start()

        pres = [
            mm(low, weights[0, first + k]) + hidden_bias[pl.ds(first + k, 1)] for k in range(per)
        ]
        total = branch[...]
        for k in range(per):
            act, grad = gelu_tanh(pres[k])
            act = act.astype(BF)
            slope[first + k] = grad
            right[blocks + first + k] = act
            right_copy(blocks + first + k).start()
            total = total + mm_nt(act, weights[1, first + k])
        branch[...] = total

    @pl.when(step == half_steps - 1)
    def _():
        second = norm_parts(second_sum[...])[0] * gain_of(gain_ref, 1) + row_of(row_ref, 3)
        third_sum = second + branch[...] + row_of(row_ref, 4)
        normed, scale = norm_parts(third_sum)
        block_ref[...] = (normed * gain_of(gain_ref, 2) + row_of(row_ref, 5)).astype(BF)
        count = matches_ref.shape[2]
        slot = lax.broadcasted_iota(jnp.int32, (rows, count), 0)
        box = lax.broadcasted_iota(jnp.int32, (rows, count), 1)
        grads = []
        for image in range(images):
            own = lax.axis_index("tensor") * images + image
            live = (matches_ref[own] == slot) & (box < counts_ref[0, own])
            mask = jnp.sum(jnp.where(live, 1.0, 0.0), axis=1, keepdims=True)
            cot = cotangent_ref[image * rows : (image + 1) * rows].astype(F32)
            grads.append(cot * mask)
        out_grad = jnp.concatenate(grads, axis=0)
        grad = norm_back(normed, scale, gain_of(gain_ref, 2), out_grad)
        third_grad[...] = grad
        left[1] = grad.astype(BF).T
        left_copy(1).start()
        small_ref[12:13] = rows_sum(grad)
        small_ref[13:14] = rows_sum(out_grad)
        small_ref[16:17] = rows_sum(out_grad * normed)
        branch[...] = jnp.zeros_like(branch)

    @pl.when(step >= half_steps)
    def _():
        ffn_low = third_grad[...].astype(BF)
        first = (step - half_steps) * per
        grads = [mm(ffn_low, weights[1, first + k]) for k in range(per)]
        total = branch[...]
        for k in range(per):
            grad_low = (grads[k] * slope[first + k]).astype(BF)
            right[first + k] = grad_low
            right_copy(first + k).start()
            small_ref[pl.ds(4 + first + k, 1)] = rows_sum(grad_low.astype(F32))
            total = total + mm_nt(grad_low, weights[0, first + k])
        branch[...] = total

    @pl.when(step == 2 * half_steps - 1)
    def _():
        second_in = third_grad[...] + branch[...]
        normed, scale = norm_parts(second_sum[...])
        grad = norm_back(normed, scale, gain_of(gain_ref, 1), second_in)
        residual_ref[...] = grad
        small_ref[10:11] = rows_sum(grad)
        small_ref[11:12] = rows_sum(second_in)
        small_ref[15:16] = rows_sum(second_in * normed)
        cross_low = grad.astype(BF)
        left[2] = cross_low.T
        left_copy(2).start()
        mixed_grad_ref[...] = mm(cross_low, cross_w_ref[0]).astype(BF)
        mixed_copy.wait()
        for which in range(3):
            left_copy(which).wait()
        for which in range(2 * blocks):
            right_copy(which).wait()


def cross_back_step(
    image, group, query_ref, key_ref, value_ref, total_ref, mixed_grad_ref, mixed_ref, small_ref,
    context_t, key_acc, value_acc, key_grad_ref, value_grad_ref, unit,
):
    grad_query = attend_back_tiles(
        query_ref[...], key_ref, value_ref, total_ref[0, 0:1], mixed_grad_ref[...], mixed_ref[...],
        key_grad_ref, value_grad_ref,
    )
    grad_key, grad_value = key_grad_ref[...], value_grad_ref[...]
    lanes = pl.ds(pl.multiple_of(group * SLAB, SLAB), SLAB)
    small_ref[2:3, lanes] += rows_sum(grad_query.astype(F32))
    small_ref[3:4, lanes] += rows_sum(grad_value.astype(F32))
    unit(0)
    key_wg = mm(context_t[...], grad_key)
    value_wg = mm(context_t[...], grad_value)

    @pl.when(image == 0)
    def _():
        key_acc[:, lanes] = key_wg
        value_acc[:, lanes] = value_wg

    @pl.when(image > 0)
    def _():
        key_acc[:, lanes] += key_wg
        value_acc[:, lanes] += value_wg

    unit(1)
    return grad_query


def cross_back_kernel(
    context_ref, query_ref, key_ref, value_ref, total_ref, mixed_grad_ref, mixed_ref, key_w_ref,
    value_w_ref, query_grad_ref, context_grad_ref, key_wg_ref, value_wg_ref, small_ref,
    context_t, acc, key_acc, value_acc, key_grad, value_grad,
):
    image, group = pl.program_id(0), pl.program_id(1)
    images, groups = pl.num_programs(0), pl.num_programs(1)

    @pl.when((image == 0) & (group == 0))
    def _():
        small_ref[...] = jnp.zeros_like(small_ref)

    @pl.when(group == 0)
    def _():
        context_t[...] = context_ref[...].T

    query_grad_ref[...] = cross_back_step(
        image, group, query_ref, key_ref, value_ref, total_ref, mixed_grad_ref, mixed_ref,
        small_ref, context_t, key_acc, value_acc, key_grad, value_grad, lambda part: None,
    )
    context_part = mm_nt(key_grad[...], key_w_ref[0]) + mm_nt(value_grad[...], value_w_ref[0])

    @pl.when(group == 0)
    def _():
        acc[...] = context_part

    @pl.when(group > 0)
    def _():
        acc[...] += context_part

    @pl.when(group == groups - 1)
    def _():
        context_grad_ref[...] = acc[...].astype(BF)

    @pl.when((image == images - 1) & (group == groups - 1))
    def _():
        key_wg_ref[...] = key_acc[...].astype(BF)
        value_wg_ref[...] = value_acc[...].astype(BF)


def self_back(
    images, valid, tokens_ref, weight_ref, row_ref, gain_ref, qkv_ref, mixed_ref, total_ref, sum_ref,
    residual_ref, cross_query_grad_ref, mixed_grad_ref, small_ref, qkv_grad, emit, unit, loop_unit,
    used,
):
    tokens = tokens_ref[...]
    rows = tokens.shape[0] // images
    width = tokens.shape[1]
    normed, scale = norm_parts(sum_ref[...])
    first_low = (normed * gain_of(gain_ref, 0) + row_of(row_ref, 1)).astype(BF)
    cross_query_grad = cross_query_grad_ref[...]
    first_low_t = first_low.T
    emit(4, lambda lanes: mm(first_low_t, cross_query_grad_ref[:, lanes]))
    unit()
    first_in = residual_ref[...] + mm_nt(cross_query_grad, weight_ref[4])
    first_grad = norm_back(normed, scale, gain_of(gain_ref, 0), first_in)
    small_ref[8:9] = rows_sum(first_grad)
    small_ref[9:10] = rows_sum(first_in)
    small_ref[14:15] = rows_sum(first_in * normed)
    self_low = first_grad.astype(BF)
    self_low_t = self_low.T
    emit(3, lambda lanes: mm(self_low_t, mixed_ref[:, lanes]))
    unit()
    mixed_grad_ref[...] = mm(self_low, weight_ref[3]).astype(BF)
    used()
    groups = width // SLAB

    def one(index, carry):
        at, lanes = place_of(index, groups, rows)
        grads = attend_back(
            qkv_ref[0, at, lanes], qkv_ref[1, at, lanes], qkv_ref[2, at, lanes],
            total_ref[index, 0:1], mixed_grad_ref[at, lanes], valid,
        )
        for which in range(3):
            qkv_grad[which, at, lanes] = grads[which]
        loop_unit(index)
        return carry

    lax.fori_loop(0, images * groups, one, 0)
    tokens_t = tokens.T
    total = first_grad
    for which in range(3):
        grad = qkv_grad[which]
        emit(which, lambda lanes, which=which: mm(tokens_t, qkv_grad[which, :, lanes]))
        if which != 1:
            unit()
        total = total + mm_nt(grad, weight_ref[which])
    small_ref[0:1] = rows_sum(qkv_grad[0].astype(F32))
    small_ref[1:2] = rows_sum(qkv_grad[2].astype(F32))
    return total


def self_back_kernel(
    images, valid, tokens_ref, weight_ref, row_ref, gain_ref, qkv_ref, mixed_ref, total_ref, sum_ref,
    residual_ref, cross_query_grad_ref, query_grad_ref, wg_ref, small_ref, qkv_grad, mixed_grad,
):
    small_ref[...] = jnp.zeros_like(small_ref)

    def emit(block, value):
        for lane in range(0, wg_ref.shape[2], SLAB):
            lanes = slice(lane, lane + SLAB)
            wg_ref[block, :, lanes] = value(lanes).astype(BF)

    query_grad_ref[...] = self_back(
        images, valid, tokens_ref, weight_ref, row_ref, gain_ref, qkv_ref, mixed_ref, total_ref,
        sum_ref, residual_ref, cross_query_grad_ref, mixed_grad, small_ref, qkv_grad, emit,
        lambda: None, lambda index: None, lambda: None,
    ).astype(BF)


def task_peers(tasks):
    me = lax.axis_index("task")
    return [lax.rem(me + shift, tasks) for shift in range(1, tasks)]


def task_senders(tasks):
    me = lax.axis_index("task")
    return [lax.rem(me + tasks - shift, tasks) for shift in range(1, tasks)]


def greet(depth, tasks):
    me = lax.axis_index("dp")
    barrier = pltpu.get_barrier_semaphore()
    other = 1 - lax.axis_index("tensor")
    for peer in task_peers(tasks):
        pl.semaphore_signal(barrier, inc=1, device_id={"task": peer}, device_id_type=MESH_ID)
        pl.semaphore_signal(
            barrier, inc=1, device_id={"task": peer, "tensor": other}, device_id_type=MESH_ID
        )
    for shift in range(1, depth):
        pl.semaphore_signal(
            barrier, inc=1, device_id={"dp": lax.rem(me + shift, depth)}, device_id_type=MESH_ID
        )
    pl.semaphore_signal(barrier, inc=1, device_id={"tensor": other}, device_id_type=MESH_ID)
    pl.semaphore_wait(barrier, 2 * (tasks - 1) + depth)


LAG = 2
SLOTS = 3
STAGES = 2


class Chain:
    def __init__(self, depth, tasks, refs):
        self.depth, self.tasks = depth, tasks
        (self.near, self.far, self.stage, self.passed, self.parts,
         self.far_send, self.far_recv, self.far_free, self.pass_send, self.pass_recv,
         self.part_send, self.part_recv) = refs
        self.chunks = self.passed.shape[1]
        self.rows, self.half = self.passed.shape[2:]
        self.me = lax.axis_index("dp")
        self.task = lax.axis_index("task")
        self.is_end = (self.me == 0) | (self.me == depth - 1)

    SCRATCH = 12

    @staticmethod
    def scratch(blocks, rows, half, tasks):
        chunks = 2 * blocks
        dma = pltpu.SemaphoreType.DMA
        return [
            pltpu.VMEM((2, chunks, rows, half), BF),
            pltpu.VMEM((SLOTS, 2, 2, rows, half), BF),
            pltpu.VMEM((STAGES, 2, 2, rows, half), BF),
            pltpu.VMEM((2, chunks, rows, half), BF),
            pltpu.VMEM((tasks, chunks, rows // tasks, half), BF),
            dma((STAGES,)),
            dma((SLOTS,)),
            pltpu.SemaphoreType.REGULAR,
            dma((2, chunks)),
            dma((2, chunks)),
            dma((blocks, tasks - 1)),
            dma((blocks, tasks - 1)),
        ]

    def far_copy(self, block):
        slot, stage = lax.rem(block, SLOTS), lax.rem(block, STAGES)
        return send(
            self.stage.at[stage], self.far.at[slot], self.far_send.at[stage], self.far_recv.at[slot],
            tensor=1 - lax.axis_index("tensor"),
        )

    def emit(self, block, value):
        block = jnp.int32(block)
        stage = lax.rem(block, STAGES)

        @pl.when(block >= STAGES)
        def _():
            self.far_copy(block).wait_send()

        @pl.when(block >= SLOTS)
        def _():
            pl.semaphore_wait(self.far_free, 1)

        def place(low, target):
            for way in range(2):
                for part in range(2):
                    row = (2 * way + part) * self.rows
                    target(way, part, low[row : row + self.rows])

        def slab(start):
            low = value(slice(start, start + SLAB)).astype(BF)
            own = max(min(self.half - start, SLAB), 0)
            if own:

                def keep(way, part, rows):
                    self.near[way, 2 * block + part, :, start : start + own] = rows

                place(low[:, :own], keep)
            if own < SLAB:
                first = start + own - self.half

                def give(way, part, rows):
                    self.stage[stage, way, part, :, first : first + SLAB - own] = rows

                place(low[:, own:], give)

        starts = range(0, 2 * self.half, SLAB)
        for start in starts:
            if start + SLAB > self.half:
                slab(start)
        self.far_copy(block).start()
        for start in starts:
            if start + SLAB <= self.half:
                slab(start)

    def absorb(self, block):
        block = jnp.int32(block)
        slot = lax.rem(block, SLOTS)
        self.far_copy(block).wait_recv()
        for way in range(2):
            chunks = pl.ds(2 * block, 2)
            self.near[way, chunks] = self.near[way, chunks] + self.far[slot, way]

        @pl.when(block < self.chunks // 2 - SLOTS)
        def _():
            pl.semaphore_signal(
                self.far_free, inc=1, device_id={"tensor": 1 - lax.axis_index("tensor")},
                device_id_type=MESH_ID,
            )

    def pass_copy(self, way, chunk):
        piece = self.passed.at[way, chunk]
        target = self.me - 1 if way == 0 else self.me + 1
        return send(
            piece, piece, self.pass_send.at[way, chunk], self.pass_recv.at[way, chunk], dp=target
        )

    def part_rows(self, peer):
        size = self.rows // self.tasks
        return pl.ds(pl.multiple_of(peer * size, size), size)

    def part_copy(self, way, block, shift, peer):
        chunks = pl.ds(2 * block, 2)
        return send(
            self.passed.at[way, chunks, self.part_rows(peer)], self.parts.at[self.task, chunks],
            self.part_send.at[block, shift], self.part_recv.at[block, shift], task=peer,
        )

    def hops(self, way):
        return self.depth - 1 - self.me if way == 0 else self.me

    def units(self):
        return self.chunks + LAG * (self.depth - 1)

    def unit(self, index):
        for way in range(2):
            chunk = index - LAG * self.hops(way)

            @pl.when((chunk >= 0) & (chunk < self.chunks))
            def _(way=way, chunk=chunk):
                self.chunk_step(way, chunk)

    def chunk_step(self, way, chunk):
        first, last = self.hops(way) == 0, self.hops(way) == self.depth - 1
        block = chunk // 2
        own = self.near[way, chunk]

        @pl.when(first)
        def _():
            self.passed[way, chunk] = own

        @pl.when(jnp.logical_not(first))
        def _():
            self.pass_copy(way, chunk).wait_recv()
            self.passed[way, chunk] = own + self.passed[way, chunk]

        @pl.when(jnp.logical_not(last))
        def _():
            self.pass_copy(way, chunk).start()

        @pl.when(last & (chunk == 2 * block + 1))
        def _():
            for shift, peer in enumerate(task_peers(self.tasks)):
                self.part_copy(way, block, shift, peer).start()
            own_rows = self.part_rows(self.task)
            self.parts[self.task, chunk - 1] = self.passed[way, chunk - 1, own_rows]
            self.parts[self.task, chunk] = self.passed[way, chunk, own_rows]

    def wait_parts(self, block):
        for shift, peer in enumerate(task_senders(self.tasks)):
            landed = self.parts.at[peer, pl.ds(2 * block, 2)]
            send(
                landed, landed, self.part_send.at[block, shift], self.part_recv.at[block, shift],
                task=peer,
            ).wait_recv()

    def finish(self):
        def blocks(block, carry):
            for way in range(2):

                @pl.when(self.hops(way) != self.depth - 1)
                def _(way=way):
                    for part in range(2):
                        self.pass_copy(way, 2 * block + part).wait_send()

                @pl.when(self.hops(way) == self.depth - 1)
                def _(way=way):
                    for shift, peer in enumerate(task_peers(self.tasks)):
                        self.part_copy(way, block, shift, peer).wait_send()

            return carry

        lax.fori_loop(0, self.chunks // 2, blocks, 0)


def pairs_of(tasks):
    return [(a, b) for a in range(tasks) for b in range(a, tasks)]


def weights_of(gram, order_ref, tasks):
    totals = [0.0] * tasks
    for own in range(tasks):
        coeffs = [jnp.full_like(gram[0, 0], 1.0 if t == own else 0.0) for t in range(tasks)]
        for position in range(tasks):
            chosen = [
                jnp.where(order_ref[position] == t, 1.0, 0.0).astype(F32) for t in range(tasks)
            ]
            column = [sum(gram[t, j] * chosen[j] for j in range(tasks)) for t in range(tasks)]
            inner = sum(coeffs[t] * column[t] for t in range(tasks))
            square = sum(chosen[t] * column[t] for t in range(tasks))
            others = 1.0 - chosen[own]
            share = others * jnp.minimum(inner, 0.0) / (square + 1e-06)
            coeffs = [coeffs[t] - share * chosen[t] for t in range(tasks)]
        totals = [total + coeff for total, coeff in zip(totals, coeffs)]
    return totals


GROUPS = 16
UNITS = 2
TILE = 240


class ContextGrad:
    def __init__(self, key_grad, value_grad, weights, result, refs):
        self.grads, self.weights, self.result = (key_grad, value_grad), weights, result
        (self.staged, self.ring, self.done, self.staged_sem, self.ring_sem, self.done_sem) = refs
        self.tile = self.done.shape[1]
        self.tiles = result.shape[0] // self.tile

    SCRATCH = 6

    @staticmethod
    def scratch(keys, width):
        dma = pltpu.SemaphoreType.DMA
        return [
            pltpu.VMEM((2, keys, SLAB), BF),
            pltpu.VMEM((2, 2, width // SLAB, TILE, SLAB), BF),
            pltpu.VMEM((2, TILE, width), BF),
            dma((2,)),
            dma((2, 2)),
            dma((2,)),
        ]

    def staged_copies(self, image, group):
        keys = self.staged.shape[1]
        rows = pl.ds(pl.multiple_of(image * keys, keys), keys)
        return [
            pltpu.make_async_copy(
                self.staged.at[which], self.grads[which].at[group, rows], self.staged_sem.at[which]
            )
            for which in range(2)
        ]

    def put(self, image, group):
        for copy in self.staged_copies(image, group):
            copy.start()

    def settle(self):
        for copy in self.staged_copies(0, 0):
            copy.wait()

    def fetches(self, index):
        slot = lax.rem(index, 2)
        rows = pl.ds(pl.multiple_of(index * self.tile, self.tile), self.tile)
        return [
            pltpu.make_async_copy(
                self.grads[which].at[:, rows], self.ring.at[slot, which],
                self.ring_sem.at[slot, which],
            )
            for which in range(2)
        ]

    def store(self, index):
        slot = lax.rem(index, 2)
        rows = pl.ds(pl.multiple_of(index * self.tile, self.tile), self.tile)
        return pltpu.make_async_copy(
            self.done.at[slot], self.result.at[rows], self.done_sem.at[slot]
        )

    def compute(self, index):
        @pl.when(index < self.tiles)
        def _():
            for copy in self.fetches(index):
                copy.wait()

            @pl.when(index + 1 < self.tiles)
            def _():
                for copy in self.fetches(index + 1):
                    copy.start()

            @pl.when(index >= 2)
            def _():
                self.store(index - 2).wait()

            slot = lax.rem(index, 2)
            parts = [
                jnp.concatenate(
                    [self.ring[slot, which, group] for group in range(self.ring.shape[2])], axis=1
                )
                for which in range(2)
            ]
            total = mm_nt(parts[0], self.weights[0]) + mm_nt(parts[1], self.weights[1])
            self.done[slot] = total.astype(BF)
            self.store(index).start()

    def finish(self):
        for index in range(self.tiles - 2, self.tiles):
            self.store(jnp.int32(index)).wait()


def back_kernel(
    depth, tasks, images, groups, valid, block_order, order_ref, context_ref, query_ref, key_ref,
    value_ref, total_ref, mixed_grad_ref, cross_mixed_ref, tokens_ref, row_ref, gain_ref, qkv_ref,
    mixed_ref, self_total_ref, sum_ref, residual_ref, small_in_ref, all_w_ref, block_ref, left_ref, right_ref,
    *refs
):
    (
        context_grad_ref, query_grad_ref, update_ref, small_out_ref, gram_ref, block_far,
        key_grad, value_grad,
    ), refs = refs[:8], refs[8:]
    (
        context, context_t, key_acc, value_acc, cross_query_grad, self_mixed_grad, qkv_grad, weights,
        block_sem, weight_sem, context_sem,
    ), refs = refs[:11], refs[11:]
    context_back = ContextGrad(
        key_grad, value_grad, weights.at[pl.ds(3, 2)], context_grad_ref,
        refs[: ContextGrad.SCRATCH],
    )
    refs = refs[ContextGrad.SCRATCH :]
    chain = Chain(depth, tasks, refs[: Chain.SCRATCH])
    refs = refs[Chain.SCRATCH :]
    gram_acc = refs[7]
    step = pl.program_id(0)
    cross_steps = images * groups
    half = chain.half
    is_end = chain.is_end
    pairs = pairs_of(tasks)

    block_copy = send(
        block_ref, block_far, block_sem.at[0], block_sem.at[1], tensor=1 - lax.axis_index("tensor")
    )
    weight_copies = [
        pltpu.make_async_copy(all_w_ref.at[source], weights.at[target], weight_sem.at[index])
        for index, (source, target) in enumerate(
            [(pl.ds(0, 5), pl.ds(0, 5)), (pl.ds(5, 2), pl.ds(3, 2))]
        )
    ]

    def context_copy(image):
        keys = context.shape[0]
        own = lax.axis_index("tensor") * images + image
        rows = pl.ds(pl.multiple_of(own * keys, keys), keys)
        return pltpu.make_async_copy(context_ref.at[0, rows], context, context_sem)

    @pl.when(step == 0)
    def _():
        context_copy(0).start()
        weight_copies[0].start()
        greet(depth, tasks)
        block_copy.start()
        gram_acc[...] = jnp.zeros_like(gram_acc)
        refs[0][...] = small_in_ref[...]

    @pl.when(step < cross_steps)
    def _():
        image = step // groups
        group = step - image * groups

        chain.emit(step, lambda lanes: mm(left_ref[0], right_ref[0, :, lanes]))

        @pl.when(group == 0)
        def _():
            context_copy(image).wait()
            context_t[...] = context[...].T

            @pl.when(image + 1 < images)
            def _():
                context_copy(image + 1).start()

        def cross_unit(part):
            if part == 0:
                context_back.put(image, group)
                chain.absorb(step)
            chain.unit(step * UNITS + part)

        @pl.when(step > 0)
        def _():
            context_back.settle()

        grad_query = cross_back_step(
            image, group, query_ref, key_ref, value_ref, total_ref, mixed_grad_ref, cross_mixed_ref,
            refs[0], context_t, key_acc, value_acc, context_back.staged.at[0],
            context_back.staged.at[1], cross_unit,
        )
        rows = grad_query.shape[0]
        cross_query_grad[
            pl.ds(pl.multiple_of(image * rows, rows), rows),
            pl.ds(pl.multiple_of(group * SLAB, SLAB), SLAB),
        ] = grad_query

        @pl.when(step == cross_steps - 1)
        def _():
            chain.emit(cross_steps, lambda lanes: key_acc[:, lanes])
            chain.emit(cross_steps + 1, lambda lanes: value_acc[:, lanes])

    @pl.when(step == cross_steps)
    def _():
        done = [cross_steps * UNITS]
        blocks = len(block_order)

        def self_unit():
            if done[0] % 2 == 0:
                chain.absorb(done[0] // 2)
            chain.unit(jnp.int32(done[0]))
            done[0] += 1

        in_loop = images * groups // 2

        def loop_unit(index):
            now = cross_steps * UNITS + 2 + index // 2

            @pl.when(index % 2 == 1)
            def _():
                @pl.when(now % 2 == 0)
                def _():
                    chain.absorb(now // 2)

                chain.unit(now)

        def used():
            done[0] += in_loop
            weight_copies[1].start()

        context_back.settle()
        for copy in context_back.fetches(jnp.int32(0)):
            copy.start()
        weight_copies[0].wait()
        query_grad_ref[...] = self_back(
            images, valid, tokens_ref, weights, row_ref, gain_ref, qkv_ref, mixed_ref,
            self_total_ref, sum_ref, residual_ref, cross_query_grad, self_mixed_grad, refs[0],
            qkv_grad, lambda block, value: chain.emit(block_order.index(block), value), self_unit,
            loop_unit, used,
        ).astype(BF)
        for block in range(-(-done[0] // 2), blocks):
            chain.absorb(block)
        weight_copies[1].wait()
        rest(
            chain, context_back, done[0], order_ref, update_ref, small_out_ref, gram_ref, refs
        )
        for block in range(blocks - STAGES, blocks):
            chain.far_copy(jnp.int32(block)).wait_send()
        block_copy.wait()
        context_back.finish()


def rest(
    chain, context_back, done, order_ref, update_ref, small_out_ref, gram_ref, refs
):
    (
        small, small_own, small_other, small_far, small_pass, small_all, small_both, gram_acc,
        gram_plane, gram_end, out,
        small_far_sem, small_pass_sem, small_task_sem, small_dp_sem, small_core_sem,
        gram_plane_sem, gram_dp_sem, hop_sem, out_sem, update_sem,
    ) = refs
    depth, tasks, half = chain.depth, chain.tasks, chain.half
    me, task, core = (lax.axis_index(axis) for axis in ("dp", "task", "tensor"))
    is_end = chain.is_end
    top = me == 0
    pairs = pairs_of(tasks)
    own_lanes = pl.ds(pl.multiple_of(core * half, half), half)
    other_lanes = pl.ds(pl.multiple_of((1 - core) * half, half), half)
    small_own[0:8] = small[0:8, 0:half]
    small_own[8:] = small[8:, own_lanes]
    small_other[0:8] = small[0:8, half:]
    small_other[8:] = small[8:, other_lanes]
    small_copy = send(
        small_other, small_far, small_far_sem.at[0], small_far_sem.at[1], tensor=1 - core
    )
    small_copy.start()

    def small_hop():
        return send(
            small_pass, small_pass, small_pass_sem.at[0], small_pass_sem.at[1], dp=me - 1
        )

    def small_task_copy(shift, peer):
        return send(
            small_pass, small_all.at[task], small_task_sem.at[0, shift],
            small_task_sem.at[1, shift], task=peer,
        )

    def add_products(shares):
        for index, (a, b) in enumerate(pairs):
            product = shares[a] * shares[b]
            total = product[0:8]
            for row in range(8, product.shape[0], 8):
                total = total + product[row : row + 8]
            gram_acc[index * 8 : index * 8 + 8] += total

    blocks = chain.chunks // 2
    late = LAG * (depth - 1) + 3

    def products_of(block):
        @pl.when((block >= 0) & (block < blocks))
        def _():
            chain.wait_parts(block)

            def part(which, carry):
                add_products(
                    [chain.parts[t, 2 * block + which].astype(F32) for t in range(tasks)]
                )
                return carry

            lax.fori_loop(0, 2, part, 0)

    def step(index, carry):
        chain.unit(index)
        context_back.compute(index - done)
        since = index - late

        @pl.when(is_end)
        def _():
            early = (done - late) // 2 + 1
            products_of(jnp.where(index - done < early, index - done, -1))
            products_of(jnp.where(since == 2 * (since // 2), since // 2, -1))

        @pl.when(index == done + 1 + LAG * chain.hops(0))
        def _():
            small_copy.wait_recv()
            total = small_own[...] + small_far[...]

            @pl.when(me == depth - 1)
            def _():
                small_pass[...] = total

            @pl.when(me < depth - 1)
            def _():
                small_hop().wait_recv()
                small_pass[...] += total

            @pl.when(me > 0)
            def _():
                small_hop().start()

            @pl.when(top)
            def _():
                for shift, peer in enumerate(task_peers(tasks)):
                    small_task_copy(shift, peer).start()
                small_all[task] = small_pass[...]

        return carry

    lax.fori_loop(done, max(chain.units() + 2, done + context_back.tiles), step, 0)

    @pl.when(top)
    def _():
        for shift, peer in enumerate(task_senders(tasks)):
            landed = small_all.at[peer]
            send(
                landed, landed, small_task_sem.at[0, shift], small_task_sem.at[1, shift], task=peer
            ).wait_recv()

    lanes = gram_plane.shape[2]
    plane = 2 * tasks
    mine = 2 * task + core

    def gram_copy(shift):
        to = lax.rem(mine + shift, plane)
        return send(
            gram_plane.at[mine], gram_plane.at[mine], gram_plane_sem.at[0, shift - 1],
            gram_plane_sem.at[1, shift - 1], task=to // 2, tensor=lax.rem(to, 2),
        )

    def gram_arrival(shift):
        place = lax.rem(mine + plane - shift, plane)
        return send(
            gram_plane.at[place], gram_plane.at[place], gram_plane_sem.at[0, shift - 1],
            gram_plane_sem.at[1, shift - 1], task=place // 2, tensor=lax.rem(place, 2),
        )

    def gram_dp_copy(end, shift):
        return send(
            gram_end.at[end], gram_end.at[end], gram_dp_sem.at[0, end, shift],
            gram_dp_sem.at[1, end, shift], dp=lax.rem((depth - 1) * end + shift + 1, depth),
        )

    def one_number(values):
        return jnp.sum(jnp.sum(values, axis=0, keepdims=True), axis=1, keepdims=True)

    @pl.when(top & (task == 0))
    def _():
        small_values = [small_all[t] for t in range(tasks)]
        for index, (a, b) in enumerate(pairs):
            product = small_values[a] * small_values[b]
            gram_acc[index * 8 : index * 8 + 8] += product[0:8] + product[8:16] + product[16:24]

    @pl.when(is_end)
    def _():
        gram_plane[mine] = jnp.zeros(gram_plane.shape[1:], F32)
        for index in range(len(pairs)):
            gram_plane[mine, index : index + 1] = jnp.broadcast_to(
                one_number(gram_acc[index * 8 : index * 8 + 8]), (1, lanes)
            )
        for shift in range(1, plane):
            gram_copy(shift).start()
        for shift in range(1, plane):
            gram_arrival(shift).wait_recv()

    for end in range(2):

        @pl.when(me == (depth - 1) * end)
        def _(end=end):
            total = gram_plane[0]
            for place in range(1, plane):
                total = total + gram_plane[place]
            gram_end[end] = total
            for shift in range(depth - 1):
                gram_dp_copy(end, shift).start()

    for end in range(2):
        for shift in range(depth - 1):

            @pl.when(me == ((depth - 1) * end + shift + 1) % depth)
            def _(end=end, shift=shift):
                gram_dp_copy(end, shift).wait_recv()

    gram = {}
    for index, (a, b) in enumerate(pairs):
        row = slice(index, index + 1)
        gram[a, b] = gram[b, a] = gram_end[0, row] + gram_end[1, row]
    for a in range(tasks):
        for b in range(tasks):
            gram_ref[a * tasks + b : a * tasks + b + 1] = gram[a, b]
    weights = [
        jnp.concatenate([weight] * (half // lanes), axis=1)
        for weight in weights_of(gram, order_ref, tasks)
    ]

    group = blocks // GROUPS
    share = chain.rows // tasks
    own_share = pl.ds(pl.multiple_of(task * share, share), share)
    own_part = jnp.minimum(me, 1)

    def hop_copy(index):
        return send(
            chain.near.at[1, pl.ds(index * group, group), pl.ds(0, share)],
            out.at[pl.ds(index * group, group), own_share],
            hop_sem.at[0, index], hop_sem.at[1, index],
            dp=jnp.where(top, 1, depth - 2),
        )

    beside = [task + 1 - 2 * lax.rem(task, 2), task + 2 - 4 * (task // 2)]
    across = tasks - 1 - task

    def out_piece(index, owner):
        rows = pl.ds(pl.multiple_of(owner * share, share), share)
        return out.at[pl.ds(index * group, group), rows]

    def out_copy(index, which, owner):
        piece = out_piece(index, owner)
        peer = beside[which] if which < 2 else beside[1 if index < GROUPS // 2 else 0]
        return send(
            piece, piece, out_sem.at[0, index, which], out_sem.at[1, index, which], task=peer
        )

    def update_copy(index):
        at = pl.ds(index * group, group)
        return pltpu.make_async_copy(out.at[at], update_ref.at[at], update_sem.at[index])

    def weighted(chunk):
        total = weights[0] * chain.parts[0, chunk].astype(F32)
        for t in range(1, tasks):
            total = total + weights[t] * chain.parts[t, chunk].astype(F32)
        return total.astype(BF)

    def small_dp_copy(shift):
        return send(
            small_both.at[0], small_both.at[0], small_dp_sem.at[0, shift],
            small_dp_sem.at[1, shift], dp=shift + 1,
        )

    def small_core_copy():
        return send(
            small_both.at[0], small_both.at[1], small_core_sem.at[0], small_core_sem.at[1],
            tensor=1 - core,
        )

    @pl.when(top)
    def _():
        total = weights[0] * small_all[0]
        for t in range(1, tasks):
            total = total + weights[t] * small_all[t]
        small_both[0] = total
        for shift in range(depth - 1):
            small_dp_copy(shift).start()

    @pl.when(is_end)
    def _():
        for index in range(GROUPS):

            def other(block, carry):
                chain.near[1, block, 0:share] = weighted(2 * block + 1 - own_part)
                return carry

            lax.fori_loop(index * group, (index + 1) * group, other, 0)
            hop_copy(index).start()

            def own(block, carry):
                out[block, own_share] = weighted(2 * block + own_part)
                return carry

            lax.fori_loop(index * group, (index + 1) * group, own, 0)
            for which in range(2):
                out_copy(index, which, task).start()

    @pl.when(jnp.logical_not(is_end))
    def _():
        for index in range(GROUPS):
            hop_copy(index).wait_recv()
            for which in range(2):
                out_copy(index, which, task).start()

    for shift in range(depth - 1):

        @pl.when(me == shift + 1)
        def _(shift=shift):
            small_dp_copy(shift).wait_recv()

    small_core_copy().start()

    for index in range(GROUPS):
        for which in range(2):
            out_copy(index, which, beside[which]).wait_recv()
        out_copy(index, 2, beside[0 if index < GROUPS // 2 else 1]).start()
    for index in range(GROUPS):
        out_copy(index, 2, across).wait_recv()
        update_copy(index).start()

    small_core_copy().wait_recv()
    small_out_ref[0:8, 0:half] = small_both[0, 0:8]
    small_out_ref[0:8, half:] = small_both[1, 0:8]
    small_out_ref[8:, own_lanes] = small_both[0, 8:]
    small_out_ref[8:, other_lanes] = small_both[1, 8:]

    small_copy.wait_send()
    small_core_copy().wait_send()
    chain.finish()

    @pl.when(me > 0)
    def _():
        small_hop().wait_send()

    @pl.when(top)
    def _():
        for shift, peer in enumerate(task_peers(tasks)):
            small_task_copy(shift, peer).wait_send()
        for shift in range(depth - 1):
            small_dp_copy(shift).wait_send()

    for end in range(2):

        @pl.when(me == (depth - 1) * end)
        def _(end=end):
            for shift in range(depth - 1):
                gram_dp_copy(end, shift).wait_send()

    @pl.when(is_end)
    def _():
        for shift in range(1, plane):
            gram_copy(shift).wait_send()
        for index in range(GROUPS):
            hop_copy(index).wait_send()

    for index in range(GROUPS):
        update_copy(index).wait()
        for which in range(3):
            out_copy(index, which, task).wait_send()


def spread_kernel(
    images, valid, tasks, block_order, parts_ref, context_grad_ref, query_grad_ref, block_ref,
    block_far_ref, small_ref, gram_in_ref,
    update_ref, context_out_ref, query_out_ref, block_out_ref, head_ref, row_ref, gain_ref, gram_ref,
):
    ordered = [parts_ref[block_order.index(block)] for block in range(len(block_order))]
    update_ref[...] = jnp.swapaxes(jnp.stack(ordered), 0, 1).astype(F32)
    context_out_ref[...] = context_grad_ref[...]

    @pl.when(pl.program_id(0) == 0)
    def _():
        padded = query_grad_ref.shape[0] // images
        first = lax.axis_index("tensor") == 0

        def rows(ref, image):
            return ref[image * padded : (image + 1) * padded].astype(F32)[:valid]

        for image in range(images):
            at = slice(image * valid, (image + 1) * valid)
            after = slice((images + image) * valid, (images + image + 1) * valid)
            query_out_ref[at] = rows(query_grad_ref, image).astype(BF)
            near, far = rows(block_ref, image), rows(block_far_ref, image)
            block_out_ref[at] = jnp.where(first, near, far).astype(BF)
            block_out_ref[after] = jnp.where(first, far, near).astype(BF)
        head_ref[...] = small_ref[0:8, 0 : head_ref.shape[1]]
        for which in range(6):
            row_ref[which // 2, which % 2 : which % 2 + 1] = small_ref[8 + which : 9 + which]
        gain_ref[...] = small_ref[14:17]
        for a in range(tasks):
            for b in range(tasks):
                at = a * tasks + b
                gram_ref[a : a + 1, b : b + 1] = gram_in_ref[at : at + 1, 0:1]


def gram_kernel(parts_ref, gram_ref):
    tasks = parts_ref.shape[0]

    @pl.when(pl.program_id(0) == 0)
    def _():
        gram_ref[...] = jnp.zeros_like(gram_ref)

    shares = [parts_ref[task, 0].astype(F32) for task in range(tasks)]
    for a in range(tasks):
        for b in range(a, tasks):
            gram_ref[a * tasks + b : a * tasks + b + 1] += rows_sum(shares[a] * shares[b])


def update_kernel(weights_ref, parts_ref, update_ref):
    tasks, blocks = parts_ref.shape[:2]
    for block in range(blocks):
        total = weights_ref[0] * parts_ref[0, block].astype(F32)
        for task in range(1, tasks):
            total += weights_ref[task] * parts_ref[task, block].astype(F32)
        update_ref[:, block, :] = total


def body(
    queries, memory, cotangent, matches, counts, task_order, params, head_bias, row_bias, norm_gain
):
    all_images = matches.shape[1]
    valid = matches.shape[2]
    width = queries.shape[2]
    half = params.shape[2]
    block_count = params.shape[1]
    blocks = (block_count - 8) // 2
    cores = lax.axis_size("tensor")
    images = all_images // cores
    keys = memory.shape[1] // all_images
    padded = -(-valid // 16) * 16
    rows = images * padded
    groups = width // SLAB
    stack = GROUP * padded
    core = lax.axis_index("tensor")

    def const(shape, *index):
        return pl.BlockSpec(shape, lambda *_: index)

    total_shape = jax.ShapeDtypeStruct((images * groups, 8, stack), F32)
    low_rows = jax.ShapeDtypeStruct((rows, width), BF)
    full_rows = jax.ShapeDtypeStruct((rows, width), F32)
    small_shape = jax.ShapeDtypeStruct((24, width), F32)
    one_block = jax.ShapeDtypeStruct((width, width), BF)
    small_spec = const((24, width), 0, 0)
    row_spec = const(row_bias.shape, 0, 0, 0)
    gain_spec = const(norm_gain.shape, 0, 0)
    head_spec = const((16, width), 0, 0)
    rows_spec = const((rows, width), 0, 0)

    parts = 4
    part_blocks = block_count // 2
    raw_spec = const((None, *queries.shape[1:]), 0, 0, 0)
    (
        weights, head_rows, tokens, own_cotangent, qkv, self_mixed, self_total, first_sum,
        cross_query,
    ) = pl.pallas_call(
        functools.partial(start_kernel, images, valid),
        grid=(2 * parts,),
        out_shape=(
            jax.ShapeDtypeStruct((block_count, width, cores * half), BF),
            jax.ShapeDtypeStruct((16, cores * half), BF),
            low_rows, low_rows,
            jax.ShapeDtypeStruct((3, rows, width), BF), low_rows, total_shape, full_rows, low_rows,
        ),
        in_specs=[
            pl.BlockSpec((width // parts, part_blocks, half), lambda s: (s % parts, s // parts, 0)),
            const((8, half), 0, 0), raw_spec, raw_spec, row_spec, gain_spec,
        ],
        out_specs=(
            any_spec(), head_spec, rows_spec, rows_spec,
            const((3, rows, width), 0, 0, 0), rows_spec, const(total_shape.shape, 0, 0, 0),
            rows_spec, rows_spec,
        ),
        scratch_shapes=[
            pltpu.VMEM((part_blocks, width, cores * half), BF),
            pltpu.VMEM((part_blocks, width, half), BF),
            pltpu.VMEM((16, half), BF),
            pltpu.VMEM((16, cores * half), BF),
            pltpu.SemaphoreType.DMA((2 * parts + 1,)),
            pltpu.SemaphoreType.DMA((2 * parts + 1,)),
            pltpu.SemaphoreType.DMA((2 * parts,)),
            pltpu.SemaphoreType.DMA(()),
        ],
        compiler_params=params_for(collective_id=0, has_side_effects=True),
        name="start",
    )(params, head_bias, queries, cotangent, row_bias, norm_gain)

    def own_image(i, g):
        return 0, lax.axis_index("tensor") * images + i, 0

    context_all = pl.BlockSpec((None, keys, width), own_image)
    slab_q = pl.BlockSpec((padded, SLAB), lambda i, g: (i, g))
    slab_k = pl.BlockSpec((keys, SLAB), lambda i, g: (i, g))
    slab_t = pl.BlockSpec((1, 8, stack), lambda i, g: (i * groups + g, 0, 0))
    image_q = pl.BlockSpec((padded, width), lambda i: (i, 0))
    image_k = pl.BlockSpec((keys, width), lambda i: (i, 0))

    def slab_w(block):
        return pl.BlockSpec((1, width, SLAB), lambda i, g: (block, 0, g))

    key_rows = jax.ShapeDtypeStruct((images * keys, width), BF)
    key_slabs = jax.ShapeDtypeStruct((groups, images * keys, SLAB), BF)
    keys_act, values_act, cross_mixed, cross_total = pl.pallas_call(
        cross_kernel,
        grid=(images,),
        in_specs=[
            pl.BlockSpec((None, keys, width), lambda i: own_image(i, 0)),
            image_q, const((1, width, width), 5, 0, 0), const((1, width, width), 6, 0, 0), head_spec,
        ],
        out_specs=(
            image_k, image_k, image_q, pl.BlockSpec((groups, 8, stack), lambda i: (i, 0, 0)),
        ),
        out_shape=(key_rows, key_rows, low_rows, total_shape),
        compiler_params=params_for(),
        name="cross_forward",
    )(memory, cross_query, weights, weights, head_rows)

    per = 2 if blocks % 2 == 0 else 1
    block_rows, left, right, mixed_grad, second_grad, ffn_small = pl.pallas_call(
        functools.partial(ffn_kernel, images, blocks, per),
        grid=(2 * blocks // per,),
        out_shape=(
            low_rows,
            jax.ShapeDtypeStruct((3, width, rows), BF),
            jax.ShapeDtypeStruct((2 * blocks + 1, rows, width), BF),
            low_rows, full_rows, small_shape,
        ),
        in_specs=[
            rows_spec, rows_spec, rows_spec,
            const((all_images, 1, valid), 0, 0, 0),
            pl.BlockSpec(memory_space=pltpu.SMEM),
            const((1, width, width), 7, 0, 0),
            any_spec(), head_spec, row_spec, gain_spec,
        ],
        out_specs=(rows_spec, any_spec(), any_spec(), rows_spec, rows_spec, small_spec),
        scratch_shapes=[
            pltpu.VMEM((rows, width), F32),
            pltpu.VMEM((rows, width), BF),
            pltpu.VMEM((3, width, rows), BF),
            pltpu.VMEM((2 * blocks, rows, width), BF),
            pltpu.VMEM((blocks, rows, width), F32),
            pltpu.VMEM((rows, width), F32),
            pltpu.VMEM((rows, width), F32),
            pltpu.VMEM((8, width), F32),
            pltpu.VMEM((2, blocks, width, width), BF),
            pltpu.SemaphoreType.DMA((3,)),
            pltpu.SemaphoreType.DMA((2 * blocks + 1,)),
            pltpu.SemaphoreType.DMA((2, blocks // per)),
        ],
        compiler_params=params_for(),
        name="ffn",
    )(
        first_sum, cross_mixed, own_cotangent, jnp.transpose(matches, (1, 0, 2)), counts, weights, weights, head_rows, row_bias,
        norm_gain,
    )

    depth, tasks = lax.axis_size("dp"), lax.axis_size("task")
    by_chain = depth == 4 and tasks == 4 and cores == 2

    if by_chain:
        block_order = [*range(8, block_count), 7, 5, 6, 4, 3, 0, 1, 2]
        chain_rows = width // depth
        pair_rows = 8 * len(pairs_of(tasks))
        dma = pltpu.SemaphoreType.DMA
        last = images * groups - 1

        def at_step(make):
            def index_map(step):
                now = jnp.minimum(step, last)
                return make(now // groups, now - groups * (now // groups))

            return index_map

        def product(step):
            return jnp.minimum(step, 2 * blocks)

        def once(shape):
            return pl.BlockSpec(
                shape, lambda step: (0,) * len(shape), pipeline_mode=pl.Buffered(1)
            )

        step_q = pl.BlockSpec((padded, SLAB), at_step(lambda i, g: (i, g)))
        step_k = pl.BlockSpec((keys, SLAB), at_step(lambda i, g: (i, g)))

        small_half = pltpu.VMEM((24, half), F32)
        (
            context_grad, token_grad, update_parts, small_out, gram_rows, block_far, *_,
        ) = pl.pallas_call(
            functools.partial(
                back_kernel, depth, tasks, images, groups, valid, block_order
            ),
            grid=(images * groups + 1,),
            out_shape=(
                key_rows, low_rows,
                jax.ShapeDtypeStruct((block_count, chain_rows, half), BF),
                small_shape,
                jax.ShapeDtypeStruct((16, 128), F32),
                low_rows,
                key_slabs, key_slabs,
            ),
            in_specs=[
                pl.BlockSpec(memory_space=pltpu.SMEM),
                any_spec(), step_q, step_k, step_k,
                pl.BlockSpec((1, 8, stack), at_step(lambda i, g: (i * groups + g, 0, 0))),
                step_q, step_q,
                once((rows, width)), once(row_bias.shape), once(norm_gain.shape),
                once((3, rows, width)), once((rows, width)), once(total_shape.shape),
                once((rows, width)), once((rows, width)), once((24, width)),
                any_spec(), any_spec(),
                pl.BlockSpec((1, width, rows), lambda step: (product(step) // blocks, 0, 0)),
                pl.BlockSpec((1, rows, width), lambda step: (product(step), 0, 0)),
            ],
            out_specs=(
                any_spec(), once((rows, width)), any_spec(), once((24, width)), once((16, 128)),
                *[any_spec()] * 3,
            ),
            scratch_shapes=[
                pltpu.VMEM((keys, width), BF),
                pltpu.VMEM((width, keys), BF),
                pltpu.VMEM((width, width), F32),
                pltpu.VMEM((width, width), F32),
                pltpu.VMEM((rows, width), BF),
                pltpu.VMEM((rows, width), BF),
                pltpu.VMEM((3, rows, width), BF),
                pltpu.VMEM((5, width, width), BF),
                dma((2,)),
                dma((2,)),
                dma(()),
                *ContextGrad.scratch(keys, width),
                *Chain.scratch(block_count, chain_rows, half, tasks),
                pltpu.VMEM((24, width), F32),
                small_half, small_half, small_half, small_half,
                pltpu.VMEM((tasks, 24, half), F32),
                pltpu.VMEM((2, 24, half), F32),
                pltpu.VMEM((pair_rows, half), F32),
                pltpu.VMEM((2 * tasks, 16, 128), F32),
                pltpu.VMEM((2, 16, 128), F32),
                pltpu.VMEM((block_count, chain_rows, half), BF),
                dma((2,)),
                dma((2,)),
                dma((2, tasks - 1)),
                dma((2, depth - 1)),
                dma((2,)),
                dma((2, 2 * tasks - 1)),
                dma((2, 2, depth - 1)),
                dma((2, GROUPS)),
                dma((2, GROUPS, tasks - 1)),
                dma((GROUPS,)),
            ],
            compiler_params=params_for(collective_id=1, has_side_effects=True),
            name="backward",
        )(
            task_order, memory, cross_query, keys_act, values_act, cross_total, mixed_grad,
            cross_mixed, tokens, row_bias, norm_gain, qkv, self_mixed, self_total, first_sum,
            second_grad, ffn_small, weights, block_rows, left, right,
        )
        tile = chain_rows // images
        (
            param_update, memory_grad, query_grad, block_out, head_update, row_update, gain_update,
            gram,
        ) = pl.pallas_call(
            functools.partial(spread_kernel, images, valid, tasks, block_order),
            grid=(images,),
            out_shape=(
                jax.ShapeDtypeStruct((chain_rows, block_count, half), F32),
                key_rows,
                jax.ShapeDtypeStruct((images * valid, width), BF),
                jax.ShapeDtypeStruct((all_images * valid, width), BF),
                jax.ShapeDtypeStruct((8, half), F32),
                jax.ShapeDtypeStruct((3, 2, width), F32),
                jax.ShapeDtypeStruct((3, width), F32),
                jax.ShapeDtypeStruct((tasks, tasks), F32),
            ),
            in_specs=[
                pl.BlockSpec((block_count, tile, half), lambda r: (0, r, 0)),
                pl.BlockSpec((keys, width), lambda r: (r, 0)),
                rows_spec, rows_spec, rows_spec, small_spec, const((16, 128), 0, 0),
            ],
            out_specs=(
                pl.BlockSpec((tile, block_count, half), lambda r: (r, 0, 0)),
                pl.BlockSpec((keys, width), lambda r: (r, 0)),
                const((images * valid, width), 0, 0),
                const((all_images * valid, width), 0, 0),
                const((8, half), 0, 0), const((3, 2, width), 0, 0, 0),
                const((3, width), 0, 0), const((tasks, tasks), 0, 0),
            ),
            compiler_params=params_for(),
            name="spread",
        )(update_parts, context_grad, token_grad, block_rows, block_far, small_out, gram_rows)
        return (
            block_out[None], query_grad[None], memory_grad[None], param_update, head_update,
            row_update, gain_update, gram,
        )

    def unpad(array):
        return array.reshape(images, padded, width)[:, :valid].reshape(1, images * valid, width)

    block_out = lax.all_gather(unpad(block_rows), "tensor", axis=1, tiled=True)
    cross_query_grad, context_grad, key_wg, value_wg, cross_small = pl.pallas_call(
        cross_back_kernel,
        grid=(images, groups),
        in_specs=[
            context_all, slab_q, slab_k, slab_k, slab_t, slab_q, slab_q, slab_w(5), slab_w(6),
        ],
        out_specs=(
            slab_q,
            pl.BlockSpec((keys, width), lambda i, g: (i, 0)),
            const((width, width), 0, 0), const((width, width), 0, 0), small_spec,
        ),
        scratch_shapes=[
            pltpu.VMEM((width, keys), BF),
            pltpu.VMEM((keys, width), F32),
            pltpu.VMEM((width, width), F32),
            pltpu.VMEM((width, width), F32),
            pltpu.VMEM((keys, SLAB), BF),
            pltpu.VMEM((keys, SLAB), BF),
        ],
        out_shape=(low_rows, key_rows, one_block, one_block, small_shape),
        compiler_params=params_for(),
        name="cross_backward",
    )(
        memory, cross_query, keys_act, values_act, cross_total, mixed_grad, cross_mixed, weights,
        weights,
    )

    token_grad, self_wg, self_small = pl.pallas_call(
        functools.partial(self_back_kernel, images, valid),
        grid=(1,),
        out_shape=(
            low_rows, jax.ShapeDtypeStruct((5, width, width), BF), small_shape,
        ),
        in_specs=[
            rows_spec, const((5, width, width), 0, 0, 0), row_spec, gain_spec,
            const((3, rows, width), 0, 0, 0), rows_spec, const(total_shape.shape, 0, 0, 0),
            rows_spec, rows_spec, rows_spec,
        ],
        out_specs=(
            rows_spec, const((5, width, width), 0, 0, 0), small_spec,
        ),
        scratch_shapes=[pltpu.VMEM((3, rows, width), BF), pltpu.VMEM((rows, width), BF)],
        compiler_params=params_for(),
        name="self_backward",
    )(
        tokens, weights, row_bias, norm_gain, qkv, self_mixed, self_total, first_sum, second_grad,
        cross_query_grad,
    )

    query_grad = unpad(token_grad)
    memory_grad = context_grad[None]

    small = self_small + cross_small + ffn_small
    product = functools.partial(jnp.einsum, "dr,jre->jde", preferred_element_type=F32)
    grad_in = product(left[0], right[:blocks]).astype(BF)
    grad_out = product(left[1], right[blocks : 2 * blocks]).astype(BF)
    cross_out_wg = product(left[2], right[2 * blocks :])[0].astype(BF)
    grads = jnp.concatenate(
        [self_wg, jnp.stack([key_wg, value_wg, cross_out_wg]), grad_in, grad_out], axis=0
    )
    swap = [(0, 1), (1, 0)]
    grads = (
        grads[:, :, :half].astype(F32) + lax.ppermute(grads[:, :, half:], "tensor", swap).astype(F32)
    ).astype(BF)
    head_small = small[:8, :half] + lax.ppermute(small[:8, half:], "tensor", swap)
    row_small = lax.psum(small[8:17], ("dp", "tensor"))
    head_small = lax.psum(head_small, "dp")
    shard = lax.psum_scatter(grads, "dp", scatter_dimension=1, tiled=True)
    all_shards = lax.all_gather(shard, "task", axis=0, tiled=False)
    all_head = lax.all_gather(head_small, "task", axis=0, tiled=False)
    all_row = lax.all_gather(row_small, "task", axis=0, tiled=False)
    tasks = all_shards.shape[0]
    share_rows = shard.shape[1]
    sums = pl.pallas_call(
        gram_kernel,
        grid=(block_count,),
        out_shape=jax.ShapeDtypeStruct((tasks * tasks, half), F32),
        in_specs=[pl.BlockSpec((tasks, 1, share_rows, half), lambda k: (0, k, 0, 0))],
        out_specs=const((tasks * tasks, half), 0, 0),
        compiler_params=params_for(),
        name="gram",
    )(all_shards)
    upper = jnp.sum(sums, axis=1).reshape(tasks, tasks)
    gram_weights = upper + upper.T - jnp.diag(jnp.diag(upper))
    gram_weights = lax.psum(gram_weights, ("dp", "tensor"))
    gram_heads = jnp.einsum("axy,bxy->ab", all_head, all_head, precision=highest)
    gram_heads = lax.psum(gram_heads, "tensor")
    gram = gram_weights + gram_heads + jnp.einsum(
        "axy,bxy->ab", all_row, all_row, precision=highest
    )
    task_weights = combine_weights(gram, task_order)
    tile = 64 if share_rows % 64 == 0 else share_rows
    param_update = pl.pallas_call(
        update_kernel,
        grid=(share_rows // tile,),
        out_shape=jax.ShapeDtypeStruct((share_rows, block_count, half), F32),
        in_specs=[
            pl.BlockSpec(memory_space=pltpu.SMEM),
            pl.BlockSpec((tasks, block_count, tile, half), lambda r: (0, 0, r, 0)),
        ],
        out_specs=pl.BlockSpec((tile, block_count, half), lambda r: (r, 0, 0)),
        compiler_params=params_for(),
        name="update",
    )(task_weights, all_shards)
    head_bias_update = jnp.einsum("a,axy->xy", task_weights, all_head, precision=highest)
    row_update = jnp.einsum("a,axy->xy", task_weights, all_row, precision=highest)
    return (
        block_out, query_grad, memory_grad, param_update, head_bias_update,
        row_update[:6].reshape(3, 2, width), row_update[6:9], gram,
    )


def solution(mesh):
    return jax.shard_map(
        body,
        mesh=mesh,
        in_specs=(
            P("task", "dp", None),
            P("task", "dp", None),
            P("task", "dp", None),
            P("task", "dp", None),
            P("task", "dp"),
            P(),
            P(None, None, "tensor"),
            P(None, "tensor"),
            P(),
            P(),
        ),
        out_specs=(
            P("task", "dp", None),
            P("task", ("dp", "tensor"), None),
            P("task", ("dp", "tensor"), None),
            P("dp", None, "tensor"),
            P(None, "tensor"),
            P(),
            P(),
            P(),
        ),
        check_vma=False,
    )
```
